32 devices in a mesh: dp: 4 (over y, x), seq: 8 (over z, core).
Axes of the slice: x: 2, y: 2, z: 4, core: 2. Of those that a mesh axis runs over, the one named last changes fastest.
Arguments:
- hidden: bfloat16 [4, 1024, 2048], P('dp', 'seq'), may hold values from -6 to 6
- token_document_numbers: int32 [4, 1024], P('dp', 'seq'), may hold values from 0 to 1023, as said below
- sequence_adapter_index: int32 [4], P('dp'), may hold values from 0 to 3, each once
- cotangent: bfloat16 [4, 1024, 2048], P('dp', 'seq'), may hold values from -6 to 6
- attention_norm_gain: float32 [2048], replicated, may hold values from 0.25 to 1.75
- feedforward_norm_gain: float32 [2048], replicated, may hold values from 0.25 to 1.75
- query_weight: bfloat16 [2048, 2048], P(('dp', 'seq')), may hold values from -0.5 to 0.5
- key_weight: bfloat16 [2048, 512], P(('dp', 'seq')), may hold values from -0.5 to 0.5
- value_weight: bfloat16 [2048, 512], P(('dp', 'seq')), may hold values from -0.125 to 0.125
- attention_output_weight: bfloat16 [2048, 2048], P(('dp', 'seq')), may hold values from -1.5 to 1.5
- gate_weight: bfloat16 [2048, 8192], P(('dp', 'seq')), may hold values from -0.125 to 0.125
- up_weight: bfloat16 [2048, 8192], P(('dp', 'seq')), may hold values from -0.125 to 0.125
- down_weight: bfloat16 [8192, 2048], P(('dp', 'seq')), may hold values from -0.5 to 0.5
- adapter_query_key_value_input: bfloat16 [4, 2048, 48], replicated, may hold values from -0.125 to 0.125
- adapter_query_output: bfloat16 [4, 16, 2048], replicated, may hold values from -1.5 to 1.5
- adapter_key_value_output: bfloat16 [4, 16, 1024], replicated, may hold values from -1.5 to 1.5
- adapter_projection_input: bfloat16 [4, 2048, 16], replicated, may hold values from -0.125 to 0.125
- adapter_projection_output: bfloat16 [4, 16, 2048], replicated, may hold values from -1.5 to 1.5
- adapter_gate_up_input: bfloat16 [4, 2048, 32], replicated, may hold values from -0.125 to 0.125
- adapter_gate_up_output: bfloat16 [4, 16, 16384], replicated, may hold values from -1.5 to 1.5
- adapter_down_input: bfloat16 [4, 8192, 16], replicated, may hold values from -0.0625 to 0.0625
- adapter_down_output: bfloat16 [4, 16, 2048], replicated, may hold values from -1.5 to 1.5
Outputs:
- mixed: bfloat16 [4, 1024, 2048], P('dp', 'seq')
- grad_hidden: bfloat16 [4, 1024, 2048], P('dp', 'seq')
- grad_lora_qkv_in: float32 [4, 2048, 48], P(None, ('dp', 'seq'))
- grad_lora_q_out: float32 [4, 16, 2048], P(None, None, ('dp', 'seq'))
- grad_lora_kv_out: float32 [4, 16, 1024], P(None, None, ('dp', 'seq'))
- grad_lora_o_in: float32 [4, 2048, 16], P(None, ('dp', 'seq'))
- grad_lora_o_out: float32 [4, 16, 2048], P(None, None, ('dp', 'seq'))
- grad_lora_gu_in: float32 [4, 2048, 32], P(None, ('dp', 'seq'))
- grad_lora_gu_out: float32 [4, 16, 16384], P(None, None, ('dp', 'seq'))
- grad_lora_down_in: float32 [4, 8192, 16], P(None, ('dp', 'seq'))
- grad_lora_down_out: float32 [4, 16, 2048], P(None, None, ('dp', 'seq'))
The draws below stay inside these ranges and needn't reach their ends.
Inputs may be any that keep to these rules, and one draw needn't show every extreme that they name: `token_document_numbers`: along each sequence the ids start at 0 and never fall; the last segment of every sequence is padding of 1 to 64 tokens and has the id 1024 - 1. `sequence_adapter_index`: every adapter is used by exactly one sequence.
All inputs are finite; a program needn't handle non-finite values.
Results may differ from the reference program's by a relative error of at most 0.02.
Values may be sent and summed in bfloat16 or wider, within the bound.
A program may use at most 320 MiB of HBM per device.

```python
import math
import jax
import jax.numpy as jnp
from jax import lax

MODEL_WIDTH = 2048
NH = 32
KVH = 8
HD = 64
HIDDEN_UNITS = 8192
ADAPTER_RANK = 16
SP = 1
TOK = 128
KEY_VALUE_WIDTH = 512
SEQS = 4
ADAPTER_COUNT = 4
LENGTH = 1024


def draw_token_document_numbers(key, part):
    key = jax.random.fold_in(key, 7)
    rate_key, flag_key, pad_key, long_key = jax.random.split(key, 4)
    places = jnp.arange(LENGTH, dtype=jnp.int32)[None, :]
    levels = jax.random.randint(rate_key, (SEQS, LENGTH // TOK), 0, 3)
    levels = jnp.repeat(levels, TOK, axis=1)
    limits = jnp.where(levels == 0, 2 ** 17, jnp.where(levels == 1, 2 ** 14, 2 ** 10))
    starts = (jax.random.randint(flag_key, (SEQS, LENGTH), 0, 2 ** 20) < limits).astype(jnp.int32)
    chosen = jax.random.randint(long_key, (SEQS // SP,), 0, SP)
    row_ids = jnp.arange(SEQS, dtype=jnp.int32)
    is_long = row_ids % SP == jnp.repeat(chosen, SP)
    inside = (places >= TOK) & (places <= LENGTH - TOK)
    starts = jnp.where(is_long[:, None] & inside, 0, starts)
    pad_len = jax.random.randint(pad_key, (SEQS, 1), 1, TOK // 2 + 1)
    pad_start = LENGTH - pad_len
    starts = jnp.where(places >= pad_start, 0, starts)
    starts = jnp.where(places == 0, 0, starts)
    counted = jnp.cumsum(starts, axis=1).astype(jnp.int32)
    return jnp.where(places >= pad_start, LENGTH - 1, counted).astype(jnp.int32)


def level_of(key, extent, cuts, least, largest):
    factor_of, own = 1.0, jax.random.fold_in(key, 6)
    for position, parts in cuts:
        draws = jnp.exp(jax.random.uniform(jax.random.fold_in(own, position), (parts,), jnp.float32, least / len(cuts), largest / len(cuts)))
        factor_of = factor_of * jnp.repeat(draws, extent[position] // parts).reshape([-1 if axis == position else 1 for axis in range(len(extent))])
    return factor_of


def bell_draw(stream_key, shape, deviation, bound, pieces=(), kind=jnp.bfloat16):
    entries = deviation * jax.random.normal(stream_key, shape, jnp.float32)
    if pieces:
        entries = entries * level_of(stream_key, shape, pieces, -0.22, 0.18)
    return jnp.clip(entries, -bound, bound).astype(kind)


def setup_inputs(seed: int = 0) -> dict:
    seeds = jax.random.split(jax.random.key(seed), 23)
    hidden = bell_draw(seeds[0], (SEQS, LENGTH, MODEL_WIDTH), 1.0, 6.0, ((0, 4), (1, 8)))
    token_document_numbers = draw_token_document_numbers(jax.random.fold_in(seeds[22], 71), 0)
    sequence_adapter_index = jax.random.permutation(seeds[2], SEQS).astype(jnp.int32)
    cotangent = bell_draw(seeds[3], (SEQS, LENGTH, MODEL_WIDTH), 1.0, 6.0, ((0, 4), (1, 8)))
    attention_norm_gain = jnp.clip(1.0 + 0.15 * jax.random.normal(seeds[4], (MODEL_WIDTH,), jnp.float32), 0.25, 1.75)
    feedforward_norm_gain = jnp.clip(1.0 + 0.15 * jax.random.normal(seeds[5], (MODEL_WIDTH,), jnp.float32), 0.25, 1.75)
    query_weight = bell_draw(seeds[6], (MODEL_WIDTH, MODEL_WIDTH), 128 ** -0.5, 0.5, ((0, 32),))
    key_weight = bell_draw(seeds[7], (MODEL_WIDTH, KEY_VALUE_WIDTH), 128 ** -0.5, 0.5, ((0, 32),))
    value_weight = bell_draw(seeds[8], (MODEL_WIDTH, KEY_VALUE_WIDTH), MODEL_WIDTH ** -0.5, 0.125, ((0, 32),))
    attention_output_weight = bell_draw(seeds[9], (MODEL_WIDTH, MODEL_WIDTH), 16 ** -0.5, 1.5, ((0, 32),))
    gate_weight = bell_draw(seeds[10], (MODEL_WIDTH, HIDDEN_UNITS), MODEL_WIDTH ** -0.5, 0.125, ((0, 32),))
    up_weight = bell_draw(seeds[11], (MODEL_WIDTH, HIDDEN_UNITS), MODEL_WIDTH ** -0.5, 0.125, ((0, 32),))
    down_weight = bell_draw(seeds[12], (HIDDEN_UNITS, MODEL_WIDTH), 128 ** -0.5, 0.5, ((0, 32),))
    adapter_query_key_value_input = bell_draw(seeds[13], (ADAPTER_COUNT, MODEL_WIDTH, 3 * ADAPTER_RANK), MODEL_WIDTH ** -0.5, 0.125)
    adapter_query_output = bell_draw(seeds[14], (ADAPTER_COUNT, ADAPTER_RANK, MODEL_WIDTH), ADAPTER_RANK ** -0.5, 1.5)
    adapter_key_value_output = bell_draw(seeds[15], (ADAPTER_COUNT, ADAPTER_RANK, 2 * KEY_VALUE_WIDTH), ADAPTER_RANK ** -0.5, 1.5)
    adapter_projection_input = bell_draw(seeds[16], (ADAPTER_COUNT, MODEL_WIDTH, ADAPTER_RANK), MODEL_WIDTH ** -0.5, 0.125)
    adapter_projection_output = bell_draw(seeds[17], (ADAPTER_COUNT, ADAPTER_RANK, MODEL_WIDTH), ADAPTER_RANK ** -0.5, 1.5)
    adapter_gate_up_input = bell_draw(seeds[18], (ADAPTER_COUNT, MODEL_WIDTH, 2 * ADAPTER_RANK), MODEL_WIDTH ** -0.5, 0.125)
    adapter_gate_up_output = bell_draw(seeds[19], (ADAPTER_COUNT, ADAPTER_RANK, 2 * HIDDEN_UNITS), ADAPTER_RANK ** -0.5, 1.5)
    adapter_down_input = bell_draw(seeds[20], (ADAPTER_COUNT, HIDDEN_UNITS, ADAPTER_RANK), HIDDEN_UNITS ** -0.5, 0.0625)
    adapter_down_output = bell_draw(seeds[21], (ADAPTER_COUNT, ADAPTER_RANK, MODEL_WIDTH), ADAPTER_RANK ** -0.5, 1.5)
    return dict(hidden=hidden, token_document_numbers=token_document_numbers, sequence_adapter_index=sequence_adapter_index, cotangent=cotangent, attention_norm_gain=attention_norm_gain, feedforward_norm_gain=feedforward_norm_gain, query_weight=query_weight, key_weight=key_weight, value_weight=value_weight, attention_output_weight=attention_output_weight, gate_weight=gate_weight, up_weight=up_weight, down_weight=down_weight, adapter_query_key_value_input=adapter_query_key_value_input, adapter_query_output=adapter_query_output, adapter_key_value_output=adapter_key_value_output, adapter_projection_input=adapter_projection_input, adapter_projection_output=adapter_projection_output, adapter_gate_up_input=adapter_gate_up_input, adapter_gate_up_output=adapter_gate_up_output, adapter_down_input=adapter_down_input, adapter_down_output=adapter_down_output)


@jax.custom_vjp
def low(v):
    return lax.optimization_barrier(v.astype(jnp.bfloat16)).astype(jnp.float32)

@jax.custom_vjp
def low_back(v):
    return v

def low_keep(v):
    return (low(v), None)

def low_pass(kept, grad):
    return (grad,)

def back_keep(v):
    return (v, None)

def back_low(kept, grad):
    return (low(grad),)
low.defvjp(low_keep, low_pass)
low_back.defvjp(back_keep, back_low)
EPSILON = 1e-05
RESIDUAL_SCALE = 0.22
SCORE_SCALE = 1.0 / 64.0
ROPE_BASE = 10000000.0
HIGHEST = lax.Precision.HIGHEST

def matmul(operand, matrix):
    return jnp.dot(operand, matrix, precision=HIGHEST)

def rms_scale(values, gain):
    mean_square = lax.optimization_barrier(jnp.mean(values * values, axis=-1, keepdims=True))
    return values * lax.rsqrt(mean_square + EPSILON) * gain

def rotate(values, cos_table, sin_table):
    half_width = values.shape[-1] // 2
    first_half = values[..., :half_width]
    second_half = values[..., half_width:]
    cos_part = cos_table[:, None, :]
    sin_part = sin_table[:, None, :]
    return jnp.concatenate([first_half * cos_part - second_half * sin_part, second_half * cos_part + first_half * sin_part], axis=-1)

def angle_tables(positions, head_size):
    steps = jnp.arange(head_size // 2).astype(jnp.float32)
    frequency = jnp.exp(steps * (-2.0 * math.log(ROPE_BASE) / head_size))
    angles = positions[:, None] * frequency[None, :]
    return (jnp.cos(angles), jnp.sin(angles))

def attention(query, keys, values, segments):
    block_rows = min(512, LENGTH)
    key_pos = jnp.arange(LENGTH, dtype=jnp.int32)

    def one_block(block_index):
        start_row = (block_index * block_rows).astype(jnp.int32)
        query_block = lax.dynamic_slice_in_dim(query, start_row, block_rows, 0)
        seg_block = lax.dynamic_slice_in_dim(segments, start_row, block_rows, 0)
        query_pos = start_row + jnp.arange(block_rows, dtype=jnp.int32)
        scores = jnp.einsum('qhd,khd->hqk', query_block, keys, precision=HIGHEST) * SCORE_SCALE
        scores = low_back(scores)
        allowed = (key_pos[None, :] <= query_pos[:, None]) & (seg_block[:, None] == segments[None, :])
        scores = jnp.where(allowed[None], scores, -1e+30)
        weights = low(jax.nn.softmax(scores, axis=-1))
        return jnp.einsum('hqk,khd->qhd', weights, values, precision=HIGHEST)
    outputs = lax.map(jax.checkpoint(one_block), jnp.arange(LENGTH // block_rows, dtype=jnp.int32))
    return outputs.reshape(LENGTH, NH, HD)

def forward_pass(input_tokens_all, adapter_weights, frozen_weights, token_document_numbers, sequence_adapter_index):
    query_key_value_input_map, query_output_map, key_value_output_map, projection_input_map, projection_output_map, gate_up_input_map, gate_up_output_map, down_input_map, down_output_map = adapter_weights
    attention_norm_gain, feedforward_norm_gain, query_weight, key_weight, value_weight, attention_output_weight, gate_weight, up_weight, down_weight = frozen_weights
    positions = jnp.arange(LENGTH).astype(jnp.float32)
    cos_table, sin_table = angle_tables(positions, HD)
    groups = NH // KVH

    def one_sequence(x_seq, segments, adapter):
        norm_one = low(rms_scale(x_seq, attention_norm_gain))
        low_qkv = low(low_back(matmul(norm_one, query_key_value_input_map[adapter])))
        query_pre = matmul(norm_one, query_weight) + matmul(low_qkv[:, :ADAPTER_RANK], query_output_map[adapter])
        key_pre = matmul(norm_one, key_weight) + matmul(low_qkv[:, ADAPTER_RANK:2 * ADAPTER_RANK], key_value_output_map[adapter][:, :KEY_VALUE_WIDTH])
        value_pre = matmul(norm_one, value_weight) + matmul(low_qkv[:, 2 * ADAPTER_RANK:], key_value_output_map[adapter][:, KEY_VALUE_WIDTH:])
        query = rotate(low_back(query_pre).reshape(LENGTH, NH, HD), cos_table, sin_table)
        query = low_back(low(query))
        keys = low(rotate(low_back(key_pre).reshape(LENGTH, KVH, HD), cos_table, sin_table))
        keys = low_back(jnp.repeat(keys, groups, axis=1))
        values = low(low_back(value_pre)).reshape(LENGTH, KVH, HD)
        values = low_back(jnp.repeat(values, groups, axis=1))
        attn = attention(query, keys, values, segments).reshape(LENGTH, MODEL_WIDTH)
        attn = low_back(low(attn))
        low_out = low(low_back(matmul(attn, projection_input_map[adapter])))
        branch = low_back(matmul(attn, attention_output_weight) + matmul(low_out, projection_output_map[adapter]))
        middle = x_seq + RESIDUAL_SCALE * branch
        norm_two = low(rms_scale(middle, feedforward_norm_gain))
        low_gu = low(low_back(matmul(norm_two, gate_up_input_map[adapter])))
        gate = low_back(matmul(norm_two, gate_weight) + matmul(low_gu[:, :ADAPTER_RANK], gate_up_output_map[adapter][:, :HIDDEN_UNITS]))
        up_proj = low_back(matmul(norm_two, up_weight) + matmul(low_gu[:, ADAPTER_RANK:], gate_up_output_map[adapter][:, HIDDEN_UNITS:]))
        activation = low(jax.nn.silu(gate) * up_proj)
        low_down = low(low_back(matmul(activation, down_input_map[adapter])))
        ffn = low_back(matmul(activation, down_weight) + matmul(low_down, down_output_map[adapter]))
        return middle + RESIDUAL_SCALE * ffn
    step_fn = jax.checkpoint(one_sequence)

    def scan_step(carry, items):
        return (carry, step_fn(items[0], items[1], items[2]))
    _, outputs = lax.scan(scan_step, jnp.zeros((), jnp.float32), (input_tokens_all, token_document_numbers, sequence_adapter_index))
    return outputs

def reference(hidden, token_document_numbers, sequence_adapter_index, cotangent, attention_norm_gain, feedforward_norm_gain, query_weight, key_weight, value_weight, attention_output_weight, gate_weight, up_weight, down_weight, adapter_query_key_value_input, adapter_query_output, adapter_key_value_output, adapter_projection_input, adapter_projection_output, adapter_gate_up_input, adapter_gate_up_output, adapter_down_input, adapter_down_output):
    frozen_weights = tuple((single_item.astype(jnp.float32) for single_item in (attention_norm_gain, feedforward_norm_gain, query_weight, key_weight, value_weight, attention_output_weight, gate_weight, up_weight, down_weight)))
    adapter_weights = tuple((single_item.astype(jnp.float32) for single_item in (adapter_query_key_value_input, adapter_query_output, adapter_key_value_output, adapter_projection_input, adapter_projection_output, adapter_gate_up_input, adapter_gate_up_output, adapter_down_input, adapter_down_output)))
    input_tokens_all = hidden.astype(jnp.float32)

    def wrapped_layer(input_token_values, adapter_arrays):
        return forward_pass(input_token_values, adapter_arrays, frozen_weights, token_document_numbers, sequence_adapter_index)
    mixed, backward_pullback_fn = jax.vjp(wrapped_layer, input_tokens_all, adapter_weights)
    input_gradient, adapter_gradients = backward_pullback_fn(cotangent.astype(jnp.float32))
    return (mixed.astype(jnp.bfloat16), input_gradient.astype(jnp.bfloat16), adapter_gradients[0], adapter_gradients[1], adapter_gradients[2], adapter_gradients[3], adapter_gradients[4], adapter_gradients[5], adapter_gradients[6], adapter_gradients[7], adapter_gradients[8])
```

```python
import math

import jax
import jax.numpy as jnp
from jax import lax
from jax.sharding import PartitionSpec as P

NH = 32
KVH = 8
HD = 64

EPSILON = 1e-05
RESIDUAL_SCALE = 0.22
SCORE_SCALE = 1.0 / 64.0
ROPE_BASE = 10000000.0
BF16 = jnp.bfloat16
F32 = jnp.float32


def mm(a, b):
    return jnp.dot(a, b, preferred_element_type=F32)


def mm_t(a, b):
    return lax.dot_general(a, b, (((1,), (1,)), ((), ())), preferred_element_type=F32)


def t_mm(a, b):
    return lax.dot_general(a, b, (((0,), (0,)), ((), ())), preferred_element_type=F32)


def rms_scale(values, gain):
    mean_square = jnp.mean(values * values, axis=-1, keepdims=True)
    return values * lax.rsqrt(mean_square + EPSILON) * gain


def rms_back(values, gain, grad):
    r = lax.rsqrt(jnp.mean(values * values, axis=-1, keepdims=True) + EPSILON)
    z = grad * gain
    return r * z - r * r * r * values * jnp.mean(z * values, axis=-1, keepdims=True)


def angle_tables(positions, head_size):
    steps = jnp.arange(head_size // 2).astype(F32)
    frequency = jnp.exp(steps * (-2.0 * math.log(ROPE_BASE) / head_size))
    angles = positions[:, None] * frequency[None, :]
    return (jnp.cos(angles), jnp.sin(angles))


def rotate(values, cos_table, sin_table):
    half_width = values.shape[-1] // 2
    first_half = values[..., :half_width]
    second_half = values[..., half_width:]
    cos_part = cos_table[:, None, :]
    sin_part = sin_table[:, None, :]
    return jnp.concatenate(
        [
            first_half * cos_part - second_half * sin_part,
            second_half * cos_part + first_half * sin_part,
        ],
        axis=-1,
    )


def masked_scores(query_block, keys, seg_block, segments, start_row):
    key_pos = jnp.arange(keys.shape[0], dtype=jnp.int32)
    query_pos = start_row + jnp.arange(query_block.shape[0], dtype=jnp.int32)
    scores = jnp.einsum("qhd,kd->hqk", query_block, keys, preferred_element_type=F32) * SCORE_SCALE
    allowed = (key_pos[None, :] <= query_pos[:, None]) & (seg_block[:, None] == segments[None, :])
    return jnp.where(allowed[None], scores, -1e30)


def attend_forward(query, keys, values, segments):
    length, heads, head_size = query.shape
    rows = min(512, length)

    def one_block(index):
        start = index * rows
        query_block = lax.dynamic_slice_in_dim(query, start, rows, 0)
        seg_block = lax.dynamic_slice_in_dim(segments, start, rows, 0)
        scores = masked_scores(query_block, keys, seg_block, segments, start)
        row_max = jnp.max(scores, axis=-1, keepdims=True)
        weights = jnp.exp(scores - row_max)
        totals = jnp.sum(weights, axis=-1, keepdims=True)
        low = (weights / totals).astype(BF16)
        output = jnp.einsum("hqk,kd->qhd", low, values, preferred_element_type=F32)
        return (output.astype(BF16), (row_max + jnp.log(totals))[..., 0])

    outputs, log_totals = lax.map(one_block, jnp.arange(length // rows, dtype=jnp.int32))
    return (outputs.reshape(length, heads * head_size), log_totals)


def attend_backward(query, keys, values, segments, log_totals, grad):
    length, heads, head_size = query.shape
    rows = min(512, length)

    def one_block(carry, index):
        grad_keys, grad_values = carry
        start = index * rows
        query_block = lax.dynamic_slice_in_dim(query, start, rows, 0)
        seg_block = lax.dynamic_slice_in_dim(segments, start, rows, 0)
        grad_block = lax.dynamic_slice_in_dim(grad, start, rows, 0)
        scores = masked_scores(query_block, keys, seg_block, segments, start)
        weights = jnp.exp(scores - log_totals[index][..., None])
        grad_weights = jnp.einsum("qhd,kd->hqk", grad_block, values, preferred_element_type=F32)
        row_dot = jnp.sum(weights * grad_weights, axis=-1, keepdims=True)
        grad_scores = (weights * (grad_weights - row_dot)).astype(BF16)
        grad_query = jnp.einsum("hqk,kd->qhd", grad_scores, keys, preferred_element_type=F32)
        grad_keys = grad_keys + jnp.einsum(
            "hqk,qhd->kd", grad_scores, query_block, preferred_element_type=F32
        )
        grad_values = grad_values + jnp.einsum(
            "hqk,qhd->kd", weights.astype(BF16), grad_block, preferred_element_type=F32
        )
        return ((grad_keys, grad_values), (grad_query * SCORE_SCALE).astype(BF16))

    zero = jnp.zeros(keys.shape, F32)
    (grad_keys, grad_values), grad_query = lax.scan(
        one_block, (zero, zero), jnp.arange(length // rows, dtype=jnp.int32)
    )
    return (grad_query.reshape(length, heads, head_size), grad_keys * SCORE_SCALE, grad_values)


def make_local(dp_size, seq_size):
    devices = dp_size * seq_size
    heads = NH // seq_size
    kv_repeat = max(1, seq_size // KVH)

    def local(
        hidden,
        token_document_numbers,
        sequence_adapter_index,
        cotangent,
        attention_norm_gain,
        feedforward_norm_gain,
        query_weight,
        key_weight,
        value_weight,
        attention_output_weight,
        gate_weight,
        up_weight,
        down_weight,
        adapter_query_key_value_input,
        adapter_query_output,
        adapter_key_value_output,
        adapter_projection_input,
        adapter_projection_output,
        adapter_gate_up_input,
        adapter_gate_up_output,
        adapter_down_input,
        adapter_down_output,
    ):
        tokens, width = hidden.shape[1:]
        length = tokens * seq_size
        rows = query_weight.shape[0]
        key_width = key_weight.shape[1]
        ff_width = gate_weight.shape[1]
        ff_block = ff_width // devices
        rank = adapter_projection_input.shape[2]
        adapters = adapter_projection_input.shape[0]
        me = lax.axis_index("seq")
        q_width = heads * HD

        def across(piece):
            return lax.all_to_all(piece, "seq", split_axis=0, concat_axis=0, tiled=True)

        def gather_dp(block):
            return lax.all_gather(block, "dp", axis=0, tiled=True)

        def gather_seq(block):
            return lax.all_gather(block, "seq", axis=0, tiled=True)

        def scatter_seq(total):
            return lax.psum_scatter(total, "seq", scatter_dimension=0, tiled=True)

        def by_owner(columns):
            return columns.reshape(columns.shape[0], dp_size, seq_size, ff_block)

        hidden_own = hidden[0].astype(F32)
        hidden_all = gather_seq(hidden[0])
        segments = gather_seq(token_document_numbers[0])
        kv = jnp.stack([key_weight.reshape(rows, KVH, HD), value_weight.reshape(rows, KVH, HD)], 2)
        kv = jnp.repeat(kv.reshape(rows, KVH, 2 * HD), kv_repeat, axis=1)
        qkv = jnp.concatenate([query_weight.reshape(rows, seq_size, q_width), kv], axis=2)
        qkv = across(jnp.swapaxes(qkv, 0, 1)).reshape(seq_size * rows, q_width + 2 * HD)
        qkv = gather_dp(qkv)
        gate_up = jnp.concatenate([by_owner(gate_weight), by_owner(up_weight)], axis=1)
        gate_up = across(jnp.transpose(gate_up, (2, 0, 1, 3)))
        gate_up = gather_dp(gate_up.reshape(seq_size * rows, 2 * dp_size * ff_block))
        down = gather_dp(down_weight)
        out_full = lax.all_gather(attention_output_weight, ("dp", "seq"), axis=0, tiled=True)
        ff_own = dp_size * ff_block

        adapter = sequence_adapter_index[0]
        qkv_in = adapter_query_key_value_input[adapter]
        q_out = lax.dynamic_slice_in_dim(adapter_query_output[adapter], me * q_width, q_width, 1)
        kv_out = adapter_key_value_output[adapter]
        kv_start = (me // kv_repeat) * HD
        k_out = lax.dynamic_slice_in_dim(kv_out, kv_start, HD, 1)
        v_out = lax.dynamic_slice_in_dim(kv_out, key_width + kv_start, HD, 1)
        o_in = adapter_projection_input[adapter]
        o_out = adapter_projection_output[adapter]
        gu_in = adapter_gate_up_input[adapter]
        gu_all = adapter_gate_up_output[adapter].reshape(rank, 2, dp_size, seq_size, ff_block)
        gu_out = lax.dynamic_index_in_dim(gu_all, me, 3, keepdims=False)
        g_out, u_out = gu_out[:, 0].reshape(rank, ff_own), gu_out[:, 1].reshape(rank, ff_own)
        down_all = adapter_down_input[adapter].reshape(dp_size, seq_size, ff_block, rank)
        down_in = lax.dynamic_index_in_dim(down_all, me, 1, keepdims=False).reshape(ff_own, rank)
        down_out = adapter_down_output[adapter]

        norm_one = rms_scale(hidden_all.astype(F32), attention_norm_gain).astype(BF16)
        low_qkv = mm(norm_one, qkv_in).astype(BF16)
        pre = mm(norm_one, qkv)
        query_pre = pre[:, :q_width] + mm(low_qkv[:, :rank], q_out)
        key_pre = pre[:, q_width : q_width + HD] + mm(low_qkv[:, rank : 2 * rank], k_out)
        value_pre = pre[:, q_width + HD :] + mm(low_qkv[:, 2 * rank :], v_out)
        cos_table, sin_table = angle_tables(jnp.arange(length, dtype=jnp.int32).astype(F32), HD)
        query = rotate(query_pre.reshape(length, heads, HD), cos_table, sin_table).astype(BF16)
        keys = rotate(key_pre.reshape(length, 1, HD), cos_table, sin_table).astype(BF16)[:, 0]
        values = value_pre.astype(BF16)
        attn_heads, log_totals = attend_forward(query, keys, values, segments)
        attn = lax.all_gather(attn_heads, "seq", axis=1, tiled=True)
        low_out = mm(attn, o_in).astype(BF16)
        branch = mm(attn, out_full) + mm(low_out, o_out)
        middle = hidden_all.astype(F32) + RESIDUAL_SCALE * branch
        own_row = me * tokens
        middle_own = lax.dynamic_slice_in_dim(middle, own_row, tokens, 0)
        norm_two = rms_scale(middle, feedforward_norm_gain).astype(BF16)
        low_gu = mm(norm_two, gu_in).astype(BF16)
        wide = mm(norm_two, gate_up)
        gate = wide[:, :ff_own] + mm(low_gu[:, :rank], g_out)
        up_proj = wide[:, ff_own:] + mm(low_gu[:, rank:], u_out)
        sigma = jax.nn.sigmoid(gate)
        activation = (gate * sigma * up_proj).astype(BF16)
        low_down = mm(activation, down_in).astype(BF16)
        ffn = scatter_seq((mm(activation, down) + mm(low_down, down_out)).astype(BF16))
        mixed = (middle_own + RESIDUAL_SCALE * ffn.astype(F32)).astype(BF16)

        grad_ffn = gather_seq((RESIDUAL_SCALE * cotangent[0].astype(F32)).astype(BF16))
        grad_low_down = mm_t(grad_ffn, down_out).astype(BF16)
        grad_act = mm_t(grad_ffn, down) + mm_t(grad_low_down, down_in)
        grad_gate = (grad_act * up_proj * sigma * (1.0 + gate * (1.0 - sigma))).astype(BF16)
        grad_up = (grad_act * gate * sigma).astype(BF16)
        grad_low_gu = jnp.concatenate([mm_t(grad_gate, g_out), mm_t(grad_up, u_out)], axis=1)
        grad_low_gu = grad_low_gu.astype(BF16)
        grad_norm_two = scatter_seq(
            (
                mm_t(jnp.concatenate([grad_gate, grad_up], axis=1), gate_up)
                + mm_t(grad_low_gu, gu_in)
            ).astype(BF16)
        )
        grad_middle = cotangent[0].astype(F32) + rms_back(
            middle_own, feedforward_norm_gain, grad_norm_two.astype(F32)
        )
        grad_branch = (RESIDUAL_SCALE * grad_middle).astype(BF16)
        grad_low_out = mm_t(grad_branch, o_out).astype(BF16)
        grad_attn = (mm_t(grad_branch, out_full) + mm_t(grad_low_out, o_in)).astype(BF16)
        grad_heads = lax.all_to_all(
            jnp.swapaxes(grad_attn.reshape(tokens, seq_size, q_width), 0, 1),
            "seq",
            split_axis=0,
            concat_axis=0,
            tiled=True,
        ).reshape(length, heads, HD)
        grad_q, grad_k, grad_v = attend_backward(
            query, keys, values, segments, log_totals, grad_heads
        )
        grad_query = rotate(grad_q.astype(F32), cos_table, -sin_table)
        grad_query = grad_query.reshape(length, q_width).astype(BF16)
        grad_key = rotate(grad_k[:, None], cos_table, -sin_table)[:, 0].astype(BF16)
        grad_value = grad_v.astype(BF16)
        grad_low_qkv = jnp.concatenate(
            [mm_t(grad_query, q_out), mm_t(grad_key, k_out), mm_t(grad_value, v_out)], axis=1
        ).astype(BF16)
        grad_qkv = jnp.concatenate([grad_query, grad_key, grad_value], axis=1)
        grad_norm_one = scatter_seq((mm_t(grad_qkv, qkv) + mm_t(grad_low_qkv, qkv_in)).astype(BF16))
        grad_hidden = grad_middle + rms_back(
            hidden_own, attention_norm_gain, grad_norm_one.astype(F32)
        )

        attn_own = lax.dynamic_slice_in_dim(attn, own_row, tokens, 0)
        low_out_own = lax.dynamic_slice_in_dim(low_out, own_row, tokens, 0)
        partial = jnp.concatenate(
            [
                t_mm(norm_one, grad_low_qkv),
                t_mm(attn_own, grad_low_out),
                t_mm(grad_branch, low_out_own),
                t_mm(norm_two, grad_low_gu),
                t_mm(grad_ffn, low_down),
            ],
            axis=1,
        ).reshape(dp_size, seq_size, rows, 8 * rank)
        own_q = t_mm(grad_query, low_qkv[:, :rank])
        own_k = t_mm(grad_key, low_qkv[:, rank : 2 * rank])
        own_v = t_mm(grad_value, low_qkv[:, 2 * rank :])
        own_g = t_mm(grad_gate, low_gu[:, :rank]).reshape(dp_size, ff_block, rank)
        own_u = t_mm(grad_up, low_gu[:, rank:]).reshape(dp_size, ff_block, rank)
        own_d = t_mm(activation, grad_low_down).reshape(dp_size, ff_block, rank)

        def placed(block, total, start, axis):
            empty = list(block.shape)
            empty[axis] = total
            return lax.dynamic_update_slice_in_dim(jnp.zeros(empty, F32), block, start, axis)

        def by_target(whole):
            return whole.reshape(dp_size, seq_size, -1)

        full_q = placed(own_q, width, me * q_width, 0)
        full_kv = jnp.concatenate(
            [placed(own_k, key_width, kv_start, 0), placed(own_v, key_width, kv_start, 0)], axis=0
        )
        spot = [placed(v[:, None], seq_size, me, 1) for v in (own_g, own_u, own_d)]
        full_gu = jnp.concatenate([spot[0].reshape(ff_width, rank), spot[1].reshape(ff_width, rank)])
        pieces = [by_target(v) for v in (partial, full_q, full_kv, full_gu, spot[2])]
        send = jnp.concatenate(pieces, axis=2)
        send = jnp.swapaxes(send, 0, 1).reshape(seq_size, -1)
        mine = lax.psum_scatter(send, "seq", scatter_dimension=0, tiled=True)
        mine = lax.all_to_all(
            mine.reshape(dp_size, -1), "dp", split_axis=0, concat_axis=0, tiled=True
        )
        owners = lax.all_gather(sequence_adapter_index, "dp", axis=0, tiled=True)
        numbers = jnp.arange(adapters, dtype=jnp.int32)
        chooser = (owners[:, None] == numbers[None, :]).astype(F32)
        mine = jnp.einsum("sa,si->ai", chooser, mine, precision=lax.Precision.HIGHEST)
        sizes = [v.shape[2] for v in pieces]
        cuts = [sum(sizes[:i]) for i in range(1, len(sizes))]
        got, got_q, got_kv, got_gu, got_d = jnp.split(mine, cuts, axis=1)
        got = got.reshape(adapters, rows, 8 * rank)

        def turned(flat):
            return jnp.swapaxes(flat.reshape(adapters, -1, rank), 1, 2)

        return (
            mixed[None],
            grad_hidden.astype(BF16)[None],
            got[:, :, : 3 * rank],
            turned(got_q),
            turned(got_kv),
            got[:, :, 3 * rank : 4 * rank],
            jnp.swapaxes(got[:, :, 4 * rank : 5 * rank], 1, 2),
            got[:, :, 5 * rank : 7 * rank],
            turned(got_gu),
            got_d.reshape(adapters, ff_block, rank),
            jnp.swapaxes(got[:, :, 7 * rank :], 1, 2),
        )

    return local


def solution(mesh):
    both = ("dp", "seq")
    tokens = P("dp", "seq", None)
    weight = P(both, None)
    in_specs = (
        (tokens, P("dp", "seq"), P("dp"), tokens, P(), P()) + (weight,) * 7 + (P(),) * 9
    )
    by_row, by_column = P(None, both, None), P(None, None, both)
    out_specs = (
        tokens,
        tokens,
        by_row,
        by_column,
        by_column,
        by_row,
        by_column,
        by_row,
        by_column,
        by_row,
        by_column,
    )
    local = make_local(mesh.shape["dp"], mesh.shape["seq"])
    return jax.shard_map(local, mesh=mesh, in_specs=in_specs, out_specs=out_specs, check_vma=False)
```

```python
import functools
import math

import jax
import jax.numpy as jnp
from jax import lax
from jax.experimental import pallas as pl
from jax.experimental.pallas import tpu as pltpu
from jax.sharding import PartitionSpec as P

NH = 32
KVH = 8
HD = 64

EPSILON = 1e-05
RESIDUAL_SCALE = 0.22
SCORE_SCALE = 1.0 / 64.0
ROPE_BASE = 10000000.0
BF16 = jnp.bfloat16
F32 = jnp.float32


def mm(a, b):
    return jnp.dot(a, b, preferred_element_type=F32)


def mm_t(a, b):
    return lax.dot_general(a, b, (((1,), (1,)), ((), ())), preferred_element_type=F32)


def t_mm(a, b):
    return lax.dot_general(a, b, (((0,), (0,)), ((), ())), preferred_element_type=F32)


def rms_scale(values, gain):
    mean_square = jnp.mean(values * values, axis=-1, keepdims=True)
    return values * lax.rsqrt(mean_square + EPSILON) * gain


def rms_back(values, gain, grad):
    r = lax.rsqrt(jnp.mean(values * values, axis=-1, keepdims=True) + EPSILON)
    z = grad * gain
    return r * z - r * r * r * values * jnp.mean(z * values, axis=-1, keepdims=True)


def angle_tables(positions, head_size):
    steps = jnp.arange(head_size // 2).astype(F32)
    frequency = jnp.exp(steps * (-2.0 * math.log(ROPE_BASE) / head_size))
    angles = positions[:, None] * frequency[None, :]
    return (jnp.cos(angles), jnp.sin(angles))


def rotate(values, cos_table, sin_table):
    half_width = values.shape[-1] // 2
    first_half = values[..., :half_width]
    second_half = values[..., half_width:]
    cos_part = cos_table[:, None, :]
    sin_part = sin_table[:, None, :]
    return jnp.concatenate(
        [
            first_half * cos_part - second_half * sin_part,
            second_half * cos_part + first_half * sin_part,
        ],
        axis=-1,
    )


def masked_scores(query_block, keys, seg_block, segments, start_row):
    key_pos = jnp.arange(keys.shape[0], dtype=jnp.int32)
    query_pos = start_row + jnp.arange(query_block.shape[0], dtype=jnp.int32)
    scores = jnp.einsum("qhd,kd->hqk", query_block, keys, preferred_element_type=F32) * SCORE_SCALE
    allowed = (key_pos[None, :] <= query_pos[:, None]) & (seg_block[:, None] == segments[None, :])
    return jnp.where(allowed[None], scores, -1e30)


def attend_forward(query, keys, values, segments):
    length, heads, head_size = query.shape
    rows = min(512, length)

    def one_block(index):
        start = index * rows
        query_block = lax.dynamic_slice_in_dim(query, start, rows, 0)
        seg_block = lax.dynamic_slice_in_dim(segments, start, rows, 0)
        scores = masked_scores(query_block, keys, seg_block, segments, start)
        row_max = jnp.max(scores, axis=-1, keepdims=True)
        weights = jnp.exp(scores - row_max)
        totals = jnp.sum(weights, axis=-1, keepdims=True)
        low = (weights / totals).astype(BF16)
        output = jnp.einsum("hqk,kd->qhd", low, values, preferred_element_type=F32)
        return (output.astype(BF16), (row_max + jnp.log(totals))[..., 0])

    outputs, log_totals = lax.map(one_block, jnp.arange(length // rows, dtype=jnp.int32))
    return (outputs.reshape(length, heads * head_size), log_totals)


def attend_backward(query, keys, values, segments, log_totals, grad):
    length, heads, head_size = query.shape
    rows = min(512, length)

    def one_block(carry, index):
        grad_keys, grad_values = carry
        start = index * rows
        query_block = lax.dynamic_slice_in_dim(query, start, rows, 0)
        seg_block = lax.dynamic_slice_in_dim(segments, start, rows, 0)
        grad_block = lax.dynamic_slice_in_dim(grad, start, rows, 0)
        scores = masked_scores(query_block, keys, seg_block, segments, start)
        weights = jnp.exp(scores - log_totals[index][..., None])
        grad_weights = jnp.einsum("qhd,kd->hqk", grad_block, values, preferred_element_type=F32)
        row_dot = jnp.sum(weights * grad_weights, axis=-1, keepdims=True)
        grad_scores = (weights * (grad_weights - row_dot)).astype(BF16)
        grad_query = jnp.einsum("hqk,kd->qhd", grad_scores, keys, preferred_element_type=F32)
        grad_keys = grad_keys + jnp.einsum(
            "hqk,qhd->kd", grad_scores, query_block, preferred_element_type=F32
        )
        grad_values = grad_values + jnp.einsum(
            "hqk,qhd->kd", weights.astype(BF16), grad_block, preferred_element_type=F32
        )
        return ((grad_keys, grad_values), (grad_query * SCORE_SCALE).astype(BF16))

    zero = jnp.zeros(keys.shape, F32)
    (grad_keys, grad_values), grad_query = lax.scan(
        one_block, (zero, zero), jnp.arange(length // rows, dtype=jnp.int32)
    )
    return (grad_query.reshape(length, heads, head_size), grad_keys * SCORE_SCALE, grad_values)


MESH = pl.DeviceIdType.MESH


def remote(src, dst, send_sem, recv_sem, device):
    return pltpu.make_async_remote_copy(
        src_ref=src,
        dst_ref=dst,
        send_sem=send_sem,
        recv_sem=recv_sem,
        device_id=device,
        device_id_type=MESH,
    )


class Place:
    def __init__(self, seq_size):
        self.d = lax.axis_index("dp")
        self.s = lax.axis_index("seq")
        self.seq_size = seq_size
        self.chips = seq_size // 2
        self.z = self.s // 2
        self.c = self.s % 2
        self.dx = self.d + 1 - 2 * (self.d % 2)
        self.dy = lax.rem(self.d + 2, 4)
        self.dd = lax.rem(self.dx + 2, 4)
        self.sib = self.s + 1 - 2 * self.c

    def seq(self, s):
        return (self.d, s)

    def dp(self, d):
        return (d, self.s)

    def peer(self, step):
        return lax.rem(self.s + step, self.seq_size)

    def greet(self, seq_steps, dp_peers):
        barrier = pltpu.get_barrier_semaphore()
        for step in seq_steps:
            pl.semaphore_signal(
                barrier, 1, device_id=self.seq(self.peer(step)), device_id_type=MESH
            )
        for d in dp_peers:
            pl.semaphore_signal(barrier, 1, device_id=self.dp(d), device_id_type=MESH)
        pl.semaphore_wait(barrier, len(seq_steps) + len(dp_peers))


class Chain:
    def __init__(self, place, own, slot, sems):
        self.p, self.own, self.slot = place, own, slot
        self.up, self.down, self.side, self.got = (sems.at[i] for i in range(4))

    def _up(self, src, i):
        return remote(src, self.slot(i), self.up.at[i], self.got.at[i], self.p.seq(self.p.s + 2))

    def _down(self, src, i):
        return remote(src, self.slot(i), self.down.at[i], self.got.at[i], self.p.seq(self.p.s - 2))

    def _side(self, src, i):
        return remote(src, self.slot(i), self.side.at[i], self.got.at[i], self.p.seq(self.p.sib))

    def start(self):
        p = self.p

        @pl.when(p.z < p.chips - 1)
        def _():
            self._up(self.own, p.s).start()

        @pl.when(p.z > 0)
        def _():
            self._down(self.own, p.s).start()

        self._side(self.own, p.s).start()

    def step(self, k):
        p = self.p
        low, high = p.s - 2 * k, p.s + 2 * k

        @pl.when(p.z >= k)
        def _():
            self._side(self.slot(low), low).wait_recv()

            @pl.when(p.z < p.chips - 1)
            def _():
                self._up(self.slot(low), low).start()

            self._side(self.slot(low), low).start()

        @pl.when(p.z + k < p.chips)
        def _():
            self._side(self.slot(high), high).wait_recv()

            @pl.when(p.z > 0)
            def _():
                self._down(self.slot(high), high).start()

            self._side(self.slot(high), high).start()

    def side_recv(self, z):
        other = 2 * z + 1 - self.p.c
        self._side(self.slot(other), other).wait_recv()

    def finish(self):
        p = self.p

        @pl.when(p.z < p.chips - 1)
        def _():
            self._up(self.own, p.s).wait_send()

        @pl.when(p.z > 0)
        def _():
            self._down(self.own, p.s).wait_send()

        self._side(self.own, p.s).wait_send()
        for k in range(1, p.chips):
            low, high = p.s - 2 * k, p.s + 2 * k

            @pl.when(p.z >= k)
            def _():
                @pl.when(p.z < p.chips - 1)
                def _():
                    self._up(self.slot(low), low).wait_send()

                self._side(self.slot(low), low).wait_send()

            @pl.when(p.z + k < p.chips)
            def _():
                @pl.when(p.z > 0)
                def _():
                    self._down(self.slot(high), high).wait_send()

                self._side(self.slot(high), high).wait_send()


class Plane:
    def __init__(self, place, block, half, sems):
        self.p, self.block, self.half, self.sems = place, block, half, sems

    def _copy(self, ref, i, d):
        return remote(ref, ref, self.sems.at[0, i], self.sems.at[1, i], self.p.dp(d))

    def _all(self):
        p = self.p
        return (
            (self.block(p.d), p.dx),
            (self.block(p.d), p.dy),
            (self.half(p.dx, 0), p.dy),
            (self.half(p.dy, 1), p.dx),
        )

    def start(self):
        for i, (ref, d) in enumerate(self._all()[:2]):
            self._copy(ref, i, d).start()

    def forward(self):
        p = self.p
        everything = self._all()
        for i, came in ((0, p.dx), (1, p.dy)):
            self._copy(self.block(came), i, came).wait_recv()
            ref, d = everything[2 + i]
            self._copy(ref, 2 + i, d).start()

    def recv(self):
        p = self.p
        self._copy(self.half(p.dd, 0), 2, p.dy).wait_recv()
        self._copy(self.half(p.dd, 1), 3, p.dx).wait_recv()

    def finish(self):
        for i, (ref, d) in enumerate(self._all()):
            self._copy(ref, i, d).wait_send()


class Spread:
    def __init__(self, place, pairs, whole, send_sem, recv_sem):
        self.p, self.pairs, self.whole = place, pairs, whole
        self.send_sem, self.recv_sem = send_sem, recv_sem

    def start(self):
        p = self.p
        for step in (1, 2, 3, 4, 5, 6, 7):
            j = p.peer(step)
            for src, dst in self.pairs(j):
                remote(src, dst, self.send_sem, self.recv_sem, p.seq(j)).start()

    def recv(self):
        p = self.p
        for whole in self.whole:
            remote(whole, whole, self.send_sem, self.recv_sem, p.seq(p.sib)).wait_recv()

    def finish(self):
        p = self.p
        for whole in self.whole:
            remote(whole, whole, self.send_sem, self.recv_sem, p.seq(p.sib)).wait_send()


PIECES = 4


def gather_kernel(
    seq_size,
    hidden,
    cotangent,
    documents,
    adapter_row,
    query_w,
    kv_w,
    out_w,
    gate_w,
    up_w,
    down_w,
    hidden_all,
    cotangent_all,
    documents_all,
    adapters_all,
    qkv_all,
    out_all,
    gu_all,
    down_all,
    chain_sems,
    plane_sems,
    local_sems,
    spread_sems,
    small_sems,
    side_sems,
    hidden_v,
    cotangent_v,
    out_v,
    down_v,
    qkv_v,
    gu_v,
):
    p = Place(seq_size)
    d, s, z, c = p.d, p.s, p.z, p.c
    rows = query_w.shape[0]
    part = down_w.shape[0]
    half_rows = seq_size * rows // 2

    landing = pl.ds(pl.multiple_of(rows * s, rows), rows)
    q_width = query_w.shape[1] // seq_size

    def column_block(number, size):
        return pl.ds(pl.multiple_of(number * size, size), size)

    stage = [
        (hidden, hidden_v),
        (cotangent, cotangent_v),
        (out_w, out_v),
        (down_w, down_v),
        (query_w.at[:, column_block(s, q_width)], qkv_v.at[:, pl.ds(0, q_width)]),
        (kv_w.at[s], qkv_v.at[:, pl.ds(q_width, kv_w.shape[2])]),
    ]
    for i in range(8):
        matrix = (gate_w, up_w)[i // 4]
        block = matrix.at[:, column_block(seq_size * (i % 4) + s, part)]
        stage.append((block, gu_v.at[:, pl.ds(part * i, part)]))
    stage = [
        pltpu.make_async_copy(src, dst, local_sems.at[0, i]) for i, (src, dst) in enumerate(stage)
    ]
    keep = [
        pltpu.make_async_copy(src, dst, local_sems.at[1, i])
        for i, (src, dst) in enumerate(
            (
                (hidden_v, hidden_all.at[s]),
                (cotangent_v, cotangent_all.at[s]),
                (out_v, out_all.at[d, z, c]),
                (down_v, down_all.at[d]),
                (qkv_v, qkv_all.at[d, landing]),
                (gu_v, gu_all.at[d, landing]),
                (documents, documents_all.at[s]),
                (adapter_row, adapters_all.at[d]),
            )
        )
    ]
    for copy in stage:
        copy.start()
    p.greet(range(1, seq_size), (p.dx, p.dy, p.dd))

    hid = Chain(p, hidden, lambda i: hidden_all.at[i], chain_sems.at[0])
    cot = Chain(p, cotangent, lambda i: cotangent_all.at[i], chain_sems.at[1])
    out = Chain(p, out_w, lambda i: out_all.at[d, i // 2, i % 2], chain_sems.at[2])

    def qkv_pairs(j):
        width = query_w.shape[1] // seq_size
        columns = pl.ds(pl.multiple_of(width * j, width), width)
        return (
            (query_w.at[:, columns], qkv_all.at[d, landing, pl.ds(0, width)]),
            (kv_w.at[j], qkv_all.at[d, landing, pl.ds(width, kv_w.shape[2])]),
        )

    def gu_pairs(piece):
        matrix = (gate_w, up_w)[piece // 2]

        def pairs(j):
            found = []
            for block in (2 * (piece % 2), 2 * (piece % 2) + 1):
                columns = pl.ds(pl.multiple_of(part * (seq_size * block + j), part), part)
                at = part * (4 * (piece // 2) + block)
                found.append((matrix.at[:, columns], gu_all.at[d, landing, pl.ds(at, part)]))
            return found

        return pairs

    others = pl.ds(0, rows * (seq_size - 1))
    qkv = Spread(
        p, qkv_pairs, [qkv_all.at[d, others]], spread_sems.at[0, 0], spread_sems.at[0, 1]
    )
    gu = []
    gu_planes = []
    for i in range(PIECES):
        cut = pl.ds(2 * part * i, 2 * part)
        gu.append(
            Spread(
                p, gu_pairs(i), [gu_all.at[d, others, cut]], spread_sems.at[1 + i, 0], spread_sems.at[1 + i, 1],
            )
        )
        gu_planes.append(
            Plane(
                p,
                lambda e, cut=cut: gu_all.at[e, :, cut],
                lambda e, h, cut=cut: gu_all.at[e, pl.ds(half_rows * h, half_rows), cut],
                plane_sems.at[3 + i],
            )
        )
    qkv_plane = Plane(
        p,
        lambda e: qkv_all.at[e],
        lambda e, h: qkv_all.at[e, pl.ds(half_rows * h, half_rows)],
        plane_sems.at[0],
    )
    down = Plane(
        p,
        lambda e: down_w if e is d else down_all.at[e],
        lambda e, h: down_all.at[e, pl.ds(part // 2 * h, part // 2)],
        plane_sems.at[1],
    )
    half_chips = p.chips // 2
    out_plane = Plane(
        p,
        lambda e: out_all.at[e, :, c],
        lambda e, h: out_all.at[e, pl.ds(half_chips * h, half_chips), c],
        plane_sems.at[2],
    )

    def documents_copy(step):
        return remote(
            documents, documents_all.at[s], small_sems.at[0, step], small_sems.at[1, 0], p.seq(p.peer(step))
        )

    def adapters_copy(i, e):
        return remote(
            adapter_row, adapters_all.at[d], small_sems.at[2, i], small_sems.at[3, 0], p.dp(e)
        )

    def side_copy(i, e):
        ref = out_all.at[e, :, c]
        return remote(ref, ref, side_sems.at[0, i], side_sems.at[1, i], p.seq(p.sib))

    def side_wait(i, e):
        ref = out_all.at[e, :, 1 - c]
        remote(ref, ref, side_sems.at[0, i], side_sems.at[1, i], p.seq(p.sib)).wait_recv()

    for step in range(1, seq_size):
        documents_copy(step).start()
    for i, e in enumerate((p.dx, p.dy, p.dd)):
        adapters_copy(i, e).start()
    qkv.start()
    hid.start()
    for i, e in enumerate((p.dx, p.dy)):
        remote(
            down_w, down_all.at[d], down.sems.at[0, i], down.sems.at[1, i], p.dp(e)
        ).start()
    for copy in stage:
        copy.wait()
    for copy in keep:
        copy.start()
    for copy in keep:
        copy.wait()
    qkv.recv()
    qkv_plane.start()
    hid.step(1)
    gu[0].start()
    down.forward()
    qkv_plane.forward()
    hid.step(2)
    gu[1].start()
    gu[0].recv()
    gu_planes[0].start()
    hid.step(3)
    gu[2].start()
    qkv_plane.recv()
    out.start()
    gu[1].recv()
    gu_planes[1].start()
    gu_planes[0].forward()
    gu[3].start()
    out.step(1)
    gu[2].recv()
    gu_planes[2].start()
    gu_planes[1].forward()
    out.step(2)
    cot.start()
    gu[3].recv()
    gu_planes[3].start()
    gu_planes[2].forward()
    out.step(3)
    out_plane.start()
    cot.step(1)
    gu_planes[3].forward()
    cot.step(2)
    out_plane.forward()
    side_copy(0, p.dx).start()
    side_copy(1, p.dy).start()
    cot.step(3)
    out_plane.recv()
    side_copy(2, p.dd).start()
    for i in range(4):
        gu_planes[i].recv()
    down.recv()
    for chain in (hid, out, cot):
        for other in range(p.chips):
            chain.side_recv(other)
        chain.finish()
    side_wait(0, p.dx)
    side_wait(1, p.dy)
    side_wait(2, p.dd)
    remote(
        documents_all.at[pl.ds(0, seq_size - 1)], documents_all.at[pl.ds(0, seq_size - 1)],
        small_sems.at[0, 0], small_sems.at[1, 0], p.seq(p.sib),
    ).wait_recv()
    remote(
        adapters_all.at[pl.ds(0, 3)], adapters_all.at[pl.ds(0, 3)],
        small_sems.at[2, 3], small_sems.at[3, 0], p.dp(p.dx),
    ).wait_recv()
    for step in range(1, seq_size):
        documents_copy(step).wait_send()
    for i, e in enumerate((p.dx, p.dy, p.dd)):
        adapters_copy(i, e).wait_send()
        side_copy(i, e).wait_send()
    for group in [qkv, *gu, qkv_plane, down, out_plane, *gu_planes]:
        group.finish()


def gather_all(
    seq_size, hidden, cotangent, documents, adapter_row, query_w, kv_w, out_w, gate_w, up_w, down_w
):
    tokens, width = hidden.shape
    rows = query_w.shape[0]
    part = down_w.shape[0]
    chips = seq_size // 2
    qkv_width = query_w.shape[1] // seq_size + kv_w.shape[2]

    def shape(*dims, dtype=BF16):
        return jax.ShapeDtypeStruct(dims, dtype)

    anywhere = pl.BlockSpec(memory_space=pl.ANY)
    return pl.pallas_call(
        functools.partial(gather_kernel, seq_size),
        out_shape=(
            shape(seq_size, tokens, width),
            shape(seq_size, tokens, width),
            shape(seq_size, 8, tokens, dtype=jnp.int32),
            shape(4, 8, 128, dtype=jnp.int32),
            shape(4, seq_size * rows, qkv_width),
            shape(4, chips, 2, rows, width),
            shape(4, seq_size * rows, 8 * part),
            shape(4, part, width),
        ),
        in_specs=[anywhere] * 10,
        out_specs=(anywhere,) * 8,
        scratch_shapes=[
            pltpu.SemaphoreType.DMA((3, 4, seq_size)),
            pltpu.SemaphoreType.DMA((3 + PIECES, 2, 4)),
            pltpu.SemaphoreType.DMA((2, 14)),
            pltpu.SemaphoreType.DMA((1 + PIECES, 2)),
            pltpu.SemaphoreType.DMA((4, seq_size)),
            pltpu.SemaphoreType.DMA((2, 3)),
            pltpu.VMEM((tokens, width), BF16),
            pltpu.VMEM((tokens, width), BF16),
            pltpu.VMEM((rows, width), BF16),
            pltpu.VMEM((part, width), BF16),
            pltpu.VMEM((rows, qkv_width), BF16),
            pltpu.VMEM((rows, 8 * part), BF16),
        ],
        compiler_params=pltpu.CompilerParams(collective_id=0, has_side_effects=True),
        cost_estimate=pl.CostEstimate(flops=0, bytes_accessed=2 * 30 * 2**20, transcendentals=0),
        name="gather_all",
    )(hidden, cotangent, documents, adapter_row, query_w, kv_w, out_w, gate_w, up_w, down_w)


def make_local(dp_size, seq_size):
    devices = dp_size * seq_size
    heads = NH // seq_size
    kv_repeat = max(1, seq_size // KVH)
    kernels = dp_size == 4 and seq_size == 8

    def local(
        hidden,
        token_document_numbers,
        sequence_adapter_index,
        cotangent,
        attention_norm_gain,
        feedforward_norm_gain,
        query_weight,
        key_weight,
        value_weight,
        attention_output_weight,
        gate_weight,
        up_weight,
        down_weight,
        adapter_query_key_value_input,
        adapter_query_output,
        adapter_key_value_output,
        adapter_projection_input,
        adapter_projection_output,
        adapter_gate_up_input,
        adapter_gate_up_output,
        adapter_down_input,
        adapter_down_output,
    ):
        tokens, width = hidden.shape[1:]
        length = tokens * seq_size
        rows = query_weight.shape[0]
        key_width = key_weight.shape[1]
        ff_width = gate_weight.shape[1]
        ff_block = ff_width // devices
        rank = adapter_projection_input.shape[2]
        adapters = adapter_projection_input.shape[0]
        me = lax.axis_index("seq")
        q_width = heads * HD

        def across(piece):
            return lax.all_to_all(piece, "seq", split_axis=0, concat_axis=0, tiled=True)

        def gather_dp(block):
            return lax.all_gather(block, "dp", axis=0, tiled=True)

        def gather_seq(block):
            return lax.all_gather(block, "seq", axis=0, tiled=True)

        def scatter_seq(total):
            return lax.psum_scatter(total, "seq", scatter_dimension=0, tiled=True)

        def by_owner(columns):
            return columns.reshape(columns.shape[0], dp_size, seq_size, ff_block)

        hidden_own = hidden[0].astype(F32)
        if kernels:
            kv = jnp.concatenate(
                [key_weight.reshape(rows, KVH, HD), value_weight.reshape(rows, KVH, HD)], axis=2
            )
            gathered = gather_all(
                seq_size,
                hidden[0],
                cotangent[0],
                jnp.broadcast_to(token_document_numbers, (8, tokens)),
                jnp.broadcast_to(sequence_adapter_index[:, None], (8, 128)),
                query_weight,
                jnp.swapaxes(kv, 0, 1),
                attention_output_weight,
                gate_weight,
                up_weight,
                down_weight,
            )
            hidden_all = gathered[0].reshape(length, width)
            cotangent_all = gathered[1].reshape(length, width)
            segments = gathered[2][:, 0].reshape(length)
            owners = gathered[3][:, 0, 0]
            qkv = gathered[4].reshape(width, -1)
            out_full = gathered[5].reshape(width, width)
            gate_up = gathered[6].reshape(width, -1)
            down = gathered[7].reshape(dp_size * ff_block, width)
        else:
            hidden_all = gather_seq(hidden[0])
            segments = gather_seq(token_document_numbers[0])
            kv = jnp.stack([key_weight.reshape(rows, KVH, HD), value_weight.reshape(rows, KVH, HD)], 2)
            kv = jnp.repeat(kv.reshape(rows, KVH, 2 * HD), kv_repeat, axis=1)
            qkv = jnp.concatenate([query_weight.reshape(rows, seq_size, q_width), kv], axis=2)
            qkv = across(jnp.swapaxes(qkv, 0, 1)).reshape(seq_size * rows, q_width + 2 * HD)
            qkv = gather_dp(qkv)
            gate_up = jnp.concatenate([by_owner(gate_weight), by_owner(up_weight)], axis=1)
            gate_up = across(jnp.transpose(gate_up, (2, 0, 1, 3)))
            gate_up = gather_dp(gate_up.reshape(seq_size * rows, 2 * dp_size * ff_block))
            down = gather_dp(down_weight)
            out_full = lax.all_gather(attention_output_weight, ("dp", "seq"), axis=0, tiled=True)
            cotangent_all = gather_seq(cotangent[0])
            owners = lax.all_gather(sequence_adapter_index, "dp", axis=0, tiled=True)
        ff_own = dp_size * ff_block

        adapter = sequence_adapter_index[0]
        qkv_in = adapter_query_key_value_input[adapter]
        q_out = lax.dynamic_slice_in_dim(adapter_query_output[adapter], me * q_width, q_width, 1)
        kv_out = adapter_key_value_output[adapter]
        kv_start = (me // kv_repeat) * HD
        k_out = lax.dynamic_slice_in_dim(kv_out, kv_start, HD, 1)
        v_out = lax.dynamic_slice_in_dim(kv_out, key_width + kv_start, HD, 1)
        o_in = adapter_projection_input[adapter]
        o_out = adapter_projection_output[adapter]
        gu_in = adapter_gate_up_input[adapter]
        gu_all = adapter_gate_up_output[adapter].reshape(rank, 2, dp_size, seq_size, ff_block)
        gu_out = lax.dynamic_index_in_dim(gu_all, me, 3, keepdims=False)
        g_out, u_out = gu_out[:, 0].reshape(rank, ff_own), gu_out[:, 1].reshape(rank, ff_own)
        down_all = adapter_down_input[adapter].reshape(dp_size, seq_size, ff_block, rank)
        down_in = lax.dynamic_index_in_dim(down_all, me, 1, keepdims=False).reshape(ff_own, rank)
        down_out = adapter_down_output[adapter]

        norm_one = rms_scale(hidden_all.astype(F32), attention_norm_gain).astype(BF16)
        low_qkv = mm(norm_one, qkv_in).astype(BF16)
        pre = mm(norm_one, qkv)
        query_pre = pre[:, :q_width] + mm(low_qkv[:, :rank], q_out)
        key_pre = pre[:, q_width : q_width + HD] + mm(low_qkv[:, rank : 2 * rank], k_out)
        value_pre = pre[:, q_width + HD :] + mm(low_qkv[:, 2 * rank :], v_out)
        cos_table, sin_table = angle_tables(jnp.arange(length, dtype=jnp.int32).astype(F32), HD)
        query = rotate(query_pre.reshape(length, heads, HD), cos_table, sin_table).astype(BF16)
        keys = rotate(key_pre.reshape(length, 1, HD), cos_table, sin_table).astype(BF16)[:, 0]
        values = value_pre.astype(BF16)
        attn_heads, log_totals = attend_forward(query, keys, values, segments)
        attn = lax.all_gather(attn_heads, "seq", axis=1, tiled=True)
        low_out = mm(attn, o_in).astype(BF16)
        branch = mm(attn, out_full) + mm(low_out, o_out)
        middle = hidden_all.astype(F32) + RESIDUAL_SCALE * branch
        own_row = me * tokens
        middle_own = lax.dynamic_slice_in_dim(middle, own_row, tokens, 0)
        norm_two = rms_scale(middle, feedforward_norm_gain).astype(BF16)
        low_gu = mm(norm_two, gu_in).astype(BF16)
        wide = mm(norm_two, gate_up)
        gate = wide[:, :ff_own] + mm(low_gu[:, :rank], g_out)
        up_proj = wide[:, ff_own:] + mm(low_gu[:, rank:], u_out)
        sigma = jax.nn.sigmoid(gate)
        activation = (gate * sigma * up_proj).astype(BF16)
        low_down = mm(activation, down_in).astype(BF16)
        ffn = scatter_seq((mm(activation, down) + mm(low_down, down_out)).astype(BF16))
        mixed = (middle_own + RESIDUAL_SCALE * ffn.astype(F32)).astype(BF16)

        grad_ffn = (RESIDUAL_SCALE * cotangent_all.astype(F32)).astype(BF16)
        grad_low_down = mm_t(grad_ffn, down_out).astype(BF16)
        grad_act = mm_t(grad_ffn, down) + mm_t(grad_low_down, down_in)
        grad_gate = (grad_act * up_proj * sigma * (1.0 + gate * (1.0 - sigma))).astype(BF16)
        grad_up = (grad_act * gate * sigma).astype(BF16)
        grad_low_gu = jnp.concatenate([mm_t(grad_gate, g_out), mm_t(grad_up, u_out)], axis=1)
        grad_low_gu = grad_low_gu.astype(BF16)
        grad_norm_two = scatter_seq(
            (
                mm_t(jnp.concatenate([grad_gate, grad_up], axis=1), gate_up)
                + mm_t(grad_low_gu, gu_in)
            ).astype(BF16)
        )
        grad_middle = cotangent[0].astype(F32) + rms_back(
            middle_own, feedforward_norm_gain, grad_norm_two.astype(F32)
        )
        grad_branch = (RESIDUAL_SCALE * grad_middle).astype(BF16)
        grad_low_out = mm_t(grad_branch, o_out).astype(BF16)
        grad_attn = (mm_t(grad_branch, out_full) + mm_t(grad_low_out, o_in)).astype(BF16)
        grad_heads = lax.all_to_all(
            jnp.swapaxes(grad_attn.reshape(tokens, seq_size, q_width), 0, 1),
            "seq",
            split_axis=0,
            concat_axis=0,
            tiled=True,
        ).reshape(length, heads, HD)
        grad_q, grad_k, grad_v = attend_backward(
            query, keys, values, segments, log_totals, grad_heads
        )
        grad_query = rotate(grad_q.astype(F32), cos_table, -sin_table)
        grad_query = grad_query.reshape(length, q_width).astype(BF16)
        grad_key = rotate(grad_k[:, None], cos_table, -sin_table)[:, 0].astype(BF16)
        grad_value = grad_v.astype(BF16)
        grad_low_qkv = jnp.concatenate(
            [mm_t(grad_query, q_out), mm_t(grad_key, k_out), mm_t(grad_value, v_out)], axis=1
        ).astype(BF16)
        grad_qkv = jnp.concatenate([grad_query, grad_key, grad_value], axis=1)
        grad_norm_one = scatter_seq((mm_t(grad_qkv, qkv) + mm_t(grad_low_qkv, qkv_in)).astype(BF16))
        grad_hidden = grad_middle + rms_back(
            hidden_own, attention_norm_gain, grad_norm_one.astype(F32)
        )

        attn_own = lax.dynamic_slice_in_dim(attn, own_row, tokens, 0)
        low_out_own = lax.dynamic_slice_in_dim(low_out, own_row, tokens, 0)
        partial = jnp.concatenate(
            [
                t_mm(norm_one, grad_low_qkv),
                t_mm(attn_own, grad_low_out),
                t_mm(grad_branch, low_out_own),
                t_mm(norm_two, grad_low_gu),
                t_mm(grad_ffn, low_down),
            ],
            axis=1,
        ).reshape(dp_size, seq_size, rows, 8 * rank)
        own_q = t_mm(grad_query, low_qkv[:, :rank])
        own_k = t_mm(grad_key, low_qkv[:, rank : 2 * rank])
        own_v = t_mm(grad_value, low_qkv[:, 2 * rank :])
        own_g = t_mm(grad_gate, low_gu[:, :rank]).reshape(dp_size, ff_block, rank)
        own_u = t_mm(grad_up, low_gu[:, rank:]).reshape(dp_size, ff_block, rank)
        own_d = t_mm(activation, grad_low_down).reshape(dp_size, ff_block, rank)

        def placed(block, total, start, axis):
            empty = list(block.shape)
            empty[axis] = total
            return lax.dynamic_update_slice_in_dim(jnp.zeros(empty, F32), block, start, axis)

        def by_target(whole):
            return whole.reshape(dp_size, seq_size, -1)

        full_q = placed(own_q, width, me * q_width, 0)
        full_kv = jnp.concatenate(
            [placed(own_k, key_width, kv_start, 0), placed(own_v, key_width, kv_start, 0)], axis=0
        )
        spot = [placed(v[:, None], seq_size, me, 1) for v in (own_g, own_u, own_d)]
        full_gu = jnp.concatenate([spot[0].reshape(ff_width, rank), spot[1].reshape(ff_width, rank)])
        pieces = [by_target(v) for v in (partial, full_q, full_kv, full_gu, spot[2])]
        send = jnp.concatenate(pieces, axis=2)
        send = jnp.swapaxes(send, 0, 1).reshape(seq_size, -1)
        mine = lax.psum_scatter(send, "seq", scatter_dimension=0, tiled=True)
        mine = lax.all_to_all(
            mine.reshape(dp_size, -1), "dp", split_axis=0, concat_axis=0, tiled=True
        )
        numbers = jnp.arange(adapters, dtype=jnp.int32)
        chooser = (owners[:, None] == numbers[None, :]).astype(F32)
        mine = jnp.einsum("sa,si->ai", chooser, mine, precision=lax.Precision.HIGHEST)
        sizes = [v.shape[2] for v in pieces]
        cuts = [sum(sizes[:i]) for i in range(1, len(sizes))]
        got, got_q, got_kv, got_gu, got_d = jnp.split(mine, cuts, axis=1)
        got = got.reshape(adapters, rows, 8 * rank)

        def turned(flat):
            return jnp.swapaxes(flat.reshape(adapters, -1, rank), 1, 2)

        return (
            mixed[None],
            grad_hidden.astype(BF16)[None],
            got[:, :, : 3 * rank],
            turned(got_q),
            turned(got_kv),
            got[:, :, 3 * rank : 4 * rank],
            jnp.swapaxes(got[:, :, 4 * rank : 5 * rank], 1, 2),
            got[:, :, 5 * rank : 7 * rank],
            turned(got_gu),
            got_d.reshape(adapters, ff_block, rank),
            jnp.swapaxes(got[:, :, 7 * rank :], 1, 2),
        )

    return local


def solution(mesh):
    both = ("dp", "seq")
    tokens = P("dp", "seq", None)
    weight = P(both, None)
    in_specs = (
        (tokens, P("dp", "seq"), P("dp"), tokens, P(), P()) + (weight,) * 7 + (P(),) * 9
    )
    by_row, by_column = P(None, both, None), P(None, None, both)
    out_specs = (
        tokens,
        tokens,
        by_row,
        by_column,
        by_column,
        by_row,
        by_column,
        by_row,
        by_column,
        by_row,
        by_column,
    )
    local = make_local(mesh.shape["dp"], mesh.shape["seq"])
    return jax.shard_map(local, mesh=mesh, in_specs=in_specs, out_specs=out_specs, check_vma=False)
```

```python
import functools
import math

import jax
import jax.numpy as jnp
from jax import lax
from jax.experimental import pallas as pl
from jax.experimental.pallas import tpu as pltpu
from jax.sharding import PartitionSpec as P

NH = 32
KVH = 8
HD = 64

EPSILON = 1e-05
RESIDUAL_SCALE = 0.22
SCORE_SCALE = 1.0 / 64.0
ROPE_BASE = 10000000.0
BF16 = jnp.bfloat16
F32 = jnp.float32


def mm(a, b):
    return jnp.dot(a, b, preferred_element_type=F32)


def mm_t(a, b):
    return lax.dot_general(a, b, (((1,), (1,)), ((), ())), preferred_element_type=F32)


def t_mm(a, b):
    return lax.dot_general(a, b, (((0,), (0,)), ((), ())), preferred_element_type=F32)


def rms_scale(values, gain):
    mean_square = jnp.mean(values * values, axis=-1, keepdims=True)
    return values * lax.rsqrt(mean_square + EPSILON) * gain


def rms_back(values, gain, grad):
    r = lax.rsqrt(jnp.mean(values * values, axis=-1, keepdims=True) + EPSILON)
    z = grad * gain
    return r * z - r * r * r * values * jnp.mean(z * values, axis=-1, keepdims=True)


def angle_tables(positions, head_size):
    steps = jnp.arange(head_size // 2).astype(F32)
    frequency = jnp.exp(steps * (-2.0 * math.log(ROPE_BASE) / head_size))
    angles = positions[:, None] * frequency[None, :]
    return (jnp.cos(angles), jnp.sin(angles))


def rotate(values, cos_table, sin_table):
    half_width = values.shape[-1] // 2
    first_half = values[..., :half_width]
    second_half = values[..., half_width:]
    cos_part = cos_table[:, None, :]
    sin_part = sin_table[:, None, :]
    return jnp.concatenate(
        [
            first_half * cos_part - second_half * sin_part,
            second_half * cos_part + first_half * sin_part,
        ],
        axis=-1,
    )


def masked_scores(query_block, keys, seg_block, segments, start_row):
    key_pos = jnp.arange(keys.shape[0], dtype=jnp.int32)
    query_pos = start_row + jnp.arange(query_block.shape[0], dtype=jnp.int32)
    scores = jnp.einsum("qhd,kd->hqk", query_block, keys, preferred_element_type=F32) * SCORE_SCALE
    allowed = (key_pos[None, :] <= query_pos[:, None]) & (seg_block[:, None] == segments[None, :])
    return jnp.where(allowed[None], scores, -1e30)


def attend_forward(query, keys, values, segments):
    length, heads, head_size = query.shape
    rows = min(512, length)

    def one_block(index):
        start = index * rows
        query_block = lax.dynamic_slice_in_dim(query, start, rows, 0)
        seg_block = lax.dynamic_slice_in_dim(segments, start, rows, 0)
        scores = masked_scores(query_block, keys, seg_block, segments, start)
        row_max = jnp.max(scores, axis=-1, keepdims=True)
        weights = jnp.exp(scores - row_max)
        totals = jnp.sum(weights, axis=-1, keepdims=True)
        low = (weights / totals).astype(BF16)
        output = jnp.einsum("hqk,kd->qhd", low, values, preferred_element_type=F32)
        return (output.astype(BF16), (row_max + jnp.log(totals))[..., 0])

    outputs, log_totals = lax.map(one_block, jnp.arange(length // rows, dtype=jnp.int32))
    return (outputs.reshape(length, heads * head_size), log_totals)


def attend_backward(query, keys, values, segments, log_totals, grad):
    length, heads, head_size = query.shape
    rows = min(512, length)

    def one_block(carry, index):
        grad_keys, grad_values = carry
        start = index * rows
        query_block = lax.dynamic_slice_in_dim(query, start, rows, 0)
        seg_block = lax.dynamic_slice_in_dim(segments, start, rows, 0)
        grad_block = lax.dynamic_slice_in_dim(grad, start, rows, 0)
        scores = masked_scores(query_block, keys, seg_block, segments, start)
        weights = jnp.exp(scores - log_totals[index][..., None])
        grad_weights = jnp.einsum("qhd,kd->hqk", grad_block, values, preferred_element_type=F32)
        row_dot = jnp.sum(weights * grad_weights, axis=-1, keepdims=True)
        grad_scores = (weights * (grad_weights - row_dot)).astype(BF16)
        grad_query = jnp.einsum("hqk,kd->qhd", grad_scores, keys, preferred_element_type=F32)
        grad_keys = grad_keys + jnp.einsum(
            "hqk,qhd->kd", grad_scores, query_block, preferred_element_type=F32
        )
        grad_values = grad_values + jnp.einsum(
            "hqk,qhd->kd", weights.astype(BF16), grad_block, preferred_element_type=F32
        )
        return ((grad_keys, grad_values), (grad_query * SCORE_SCALE).astype(BF16))

    zero = jnp.zeros(keys.shape, F32)
    (grad_keys, grad_values), grad_query = lax.scan(
        one_block, (zero, zero), jnp.arange(length // rows, dtype=jnp.int32)
    )
    return (grad_query.reshape(length, heads, head_size), grad_keys * SCORE_SCALE, grad_values)


MESH = pl.DeviceIdType.MESH


def remote(src, dst, send_sem, recv_sem, device):
    return pltpu.make_async_remote_copy(
        src_ref=src,
        dst_ref=dst,
        send_sem=send_sem,
        recv_sem=recv_sem,
        device_id=device,
        device_id_type=MESH,
    )


class Place:
    def __init__(self, seq_size):
        self.d = lax.axis_index("dp")
        self.s = lax.axis_index("seq")
        self.seq_size = seq_size
        self.chips = seq_size // 2
        self.z = self.s // 2
        self.c = self.s % 2
        self.dx = self.d + 1 - 2 * (self.d % 2)
        self.dy = lax.rem(self.d + 2, 4)
        self.dd = lax.rem(self.dx + 2, 4)
        self.sib = self.s + 1 - 2 * self.c

    def seq(self, s):
        return (self.d, s)

    def dp(self, d):
        return (d, self.s)

    def peer(self, step):
        return lax.rem(self.s + step, self.seq_size)

    def greet(self, seq_steps, dp_peers):
        barrier = pltpu.get_barrier_semaphore()
        for step in seq_steps:
            pl.semaphore_signal(
                barrier, 1, device_id=self.seq(self.peer(step)), device_id_type=MESH
            )
        for d in dp_peers:
            pl.semaphore_signal(barrier, 1, device_id=self.dp(d), device_id_type=MESH)
        pl.semaphore_wait(barrier, len(seq_steps) + len(dp_peers))


class Chain:
    def __init__(self, place, own, slot, sems):
        self.p, self.own, self.slot = place, own, slot
        self.up, self.down, self.side, self.got = (sems.at[i] for i in range(4))

    def _up(self, src, i):
        return remote(src, self.slot(i), self.up.at[i], self.got.at[i], self.p.seq(self.p.s + 2))

    def _down(self, src, i):
        return remote(src, self.slot(i), self.down.at[i], self.got.at[i], self.p.seq(self.p.s - 2))

    def _side(self, src, i):
        return remote(src, self.slot(i), self.side.at[i], self.got.at[i], self.p.seq(self.p.sib))

    def start(self):
        p = self.p

        @pl.when(p.z < p.chips - 1)
        def _():
            self._up(self.own, p.s).start()

        @pl.when(p.z > 0)
        def _():
            self._down(self.own, p.s).start()

        self._side(self.own, p.s).start()

    def step(self, k):
        p = self.p
        low, high = p.s - 2 * k, p.s + 2 * k

        @pl.when(p.z >= k)
        def _():
            self._side(self.slot(low), low).wait_recv()

            @pl.when(p.z < p.chips - 1)
            def _():
                self._up(self.slot(low), low).start()

            self._side(self.slot(low), low).start()

        @pl.when(p.z + k < p.chips)
        def _():
            self._side(self.slot(high), high).wait_recv()

            @pl.when(p.z > 0)
            def _():
                self._down(self.slot(high), high).start()

            self._side(self.slot(high), high).start()

    def side_recv(self, z):
        other = 2 * z + 1 - self.p.c
        self._side(self.slot(other), other).wait_recv()

    def finish(self):
        p = self.p

        @pl.when(p.z < p.chips - 1)
        def _():
            self._up(self.own, p.s).wait_send()

        @pl.when(p.z > 0)
        def _():
            self._down(self.own, p.s).wait_send()

        self._side(self.own, p.s).wait_send()
        for k in range(1, p.chips):
            low, high = p.s - 2 * k, p.s + 2 * k

            @pl.when(p.z >= k)
            def _():
                @pl.when(p.z < p.chips - 1)
                def _():
                    self._up(self.slot(low), low).wait_send()

                self._side(self.slot(low), low).wait_send()

            @pl.when(p.z + k < p.chips)
            def _():
                @pl.when(p.z > 0)
                def _():
                    self._down(self.slot(high), high).wait_send()

                self._side(self.slot(high), high).wait_send()


class Plane:
    def __init__(self, place, block, half, sems):
        self.p, self.block, self.half, self.sems = place, block, half, sems

    def _copy(self, ref, i, d):
        return remote(ref, ref, self.sems.at[0, i], self.sems.at[1, i], self.p.dp(d))

    def _all(self):
        p = self.p
        return (
            (self.block(p.d), p.dx),
            (self.block(p.d), p.dy),
            (self.half(p.dx, 0), p.dy),
            (self.half(p.dy, 1), p.dx),
        )

    def start(self):
        for i, (ref, d) in enumerate(self._all()[:2]):
            self._copy(ref, i, d).start()

    def forward(self):
        p = self.p
        everything = self._all()
        for i, came in ((0, p.dx), (1, p.dy)):
            self._copy(self.block(came), i, came).wait_recv()
            ref, d = everything[2 + i]
            self._copy(ref, 2 + i, d).start()

    def recv(self):
        p = self.p
        self._copy(self.half(p.dd, 0), 2, p.dy).wait_recv()
        self._copy(self.half(p.dd, 1), 3, p.dx).wait_recv()

    def finish(self):
        for i, (ref, d) in enumerate(self._all()):
            self._copy(ref, i, d).wait_send()


class Spread:
    def __init__(self, place, pairs, whole, send_sem, recv_sem):
        self.p, self.pairs, self.whole = place, pairs, whole
        self.send_sem, self.recv_sem = send_sem, recv_sem

    def start(self):
        p = self.p
        for step in (1, 2, 3, 4, 5, 6, 7):
            j = p.peer(step)
            for src, dst in self.pairs(j):
                remote(src, dst, self.send_sem, self.recv_sem, p.seq(j)).start()

    def recv(self):
        p = self.p
        for whole in self.whole:
            remote(whole, whole, self.send_sem, self.recv_sem, p.seq(p.sib)).wait_recv()

    def finish(self):
        p = self.p
        for whole in self.whole:
            remote(whole, whole, self.send_sem, self.recv_sem, p.seq(p.sib)).wait_send()


PIECES = 4


def gather_kernel(
    seq_size,
    hidden,
    cotangent,
    documents,
    adapter_row,
    query_w,
    kv_w,
    out_w,
    gate_w,
    up_w,
    down_w,
    hidden_all,
    cotangent_all,
    documents_all,
    adapters_all,
    qkv_all,
    out_all,
    gu_all,
    down_all,
    chain_sems,
    plane_sems,
    local_sems,
    spread_sems,
    small_sems,
    side_sems,
    hidden_v,
    cotangent_v,
    out_v,
    down_v,
    qkv_v,
    gu_v,
):
    p = Place(seq_size)
    d, s, z, c = p.d, p.s, p.z, p.c
    rows = query_w.shape[0]
    part = down_w.shape[0]
    half_rows = seq_size * rows // 2

    landing = pl.ds(pl.multiple_of(rows * s, rows), rows)
    q_width = query_w.shape[1] // seq_size

    def column_block(number, size):
        return pl.ds(pl.multiple_of(number * size, size), size)

    stage = [
        (hidden, hidden_v),
        (cotangent, cotangent_v),
        (out_w, out_v),
        (down_w, down_v),
        (query_w.at[:, column_block(s, q_width)], qkv_v.at[:, pl.ds(0, q_width)]),
        (kv_w.at[s], qkv_v.at[:, pl.ds(q_width, kv_w.shape[2])]),
    ]
    for i in range(8):
        matrix = (gate_w, up_w)[i // 4]
        block = matrix.at[:, column_block(seq_size * (i % 4) + s, part)]
        stage.append((block, gu_v.at[:, pl.ds(part * i, part)]))
    stage = [
        pltpu.make_async_copy(src, dst, local_sems.at[0, i]) for i, (src, dst) in enumerate(stage)
    ]
    keep = [
        pltpu.make_async_copy(src, dst, local_sems.at[1, i])
        for i, (src, dst) in enumerate(
            (
                (hidden_v, hidden_all.at[s]),
                (cotangent_v, cotangent_all.at[s]),
                (out_v, out_all.at[d, z, c]),
                (down_v, down_all.at[d]),
                (qkv_v, qkv_all.at[d, landing]),
                (gu_v, gu_all.at[d, landing]),
                (documents, documents_all.at[s]),
                (adapter_row, adapters_all.at[d]),
            )
        )
    ]
    for copy in stage:
        copy.start()
    p.greet(range(1, seq_size), (p.dx, p.dy, p.dd))

    hid = Chain(p, hidden, lambda i: hidden_all.at[i], chain_sems.at[0])
    cot = Chain(p, cotangent, lambda i: cotangent_all.at[i], chain_sems.at[1])
    out = Chain(p, out_w, lambda i: out_all.at[d, i // 2, i % 2], chain_sems.at[2])

    def qkv_pairs(j):
        width = query_w.shape[1] // seq_size
        columns = pl.ds(pl.multiple_of(width * j, width), width)
        return (
            (query_w.at[:, columns], qkv_all.at[d, landing, pl.ds(0, width)]),
            (kv_w.at[j], qkv_all.at[d, landing, pl.ds(width, kv_w.shape[2])]),
        )

    def gu_pairs(piece):
        matrix = (gate_w, up_w)[piece // 2]

        def pairs(j):
            found = []
            for block in (2 * (piece % 2), 2 * (piece % 2) + 1):
                columns = pl.ds(pl.multiple_of(part * (seq_size * block + j), part), part)
                at = part * (4 * (piece // 2) + block)
                found.append((matrix.at[:, columns], gu_all.at[d, landing, pl.ds(at, part)]))
            return found

        return pairs

    others = pl.ds(0, rows * (seq_size - 1))
    qkv = Spread(
        p, qkv_pairs, [qkv_all.at[d, others]], spread_sems.at[0, 0], spread_sems.at[0, 1]
    )
    gu = []
    gu_planes = []
    for i in range(PIECES):
        cut = pl.ds(2 * part * i, 2 * part)
        gu.append(
            Spread(
                p, gu_pairs(i), [gu_all.at[d, others, cut]], spread_sems.at[1 + i, 0], spread_sems.at[1 + i, 1],
            )
        )
        gu_planes.append(
            Plane(
                p,
                lambda e, cut=cut: gu_all.at[e, :, cut],
                lambda e, h, cut=cut: gu_all.at[e, pl.ds(half_rows * h, half_rows), cut],
                plane_sems.at[3 + i],
            )
        )
    qkv_plane = Plane(
        p,
        lambda e: qkv_all.at[e],
        lambda e, h: qkv_all.at[e, pl.ds(half_rows * h, half_rows)],
        plane_sems.at[0],
    )
    down = Plane(
        p,
        lambda e: down_w if e is d else down_all.at[e],
        lambda e, h: down_all.at[e, pl.ds(part // 2 * h, part // 2)],
        plane_sems.at[1],
    )
    half_chips = p.chips // 2
    out_plane = Plane(
        p,
        lambda e: out_all.at[e, :, c],
        lambda e, h: out_all.at[e, pl.ds(half_chips * h, half_chips), c],
        plane_sems.at[2],
    )

    def documents_copy(step):
        return remote(
            documents, documents_all.at[s], small_sems.at[0, step], small_sems.at[1, 0], p.seq(p.peer(step))
        )

    def adapters_copy(i, e):
        return remote(
            adapter_row, adapters_all.at[d], small_sems.at[2, i], small_sems.at[3, 0], p.dp(e)
        )

    def side_copy(i, e):
        ref = out_all.at[e, :, c]
        return remote(ref, ref, side_sems.at[0, i], side_sems.at[1, i], p.seq(p.sib))

    def side_wait(i, e):
        ref = out_all.at[e, :, 1 - c]
        remote(ref, ref, side_sems.at[0, i], side_sems.at[1, i], p.seq(p.sib)).wait_recv()

    for step in range(1, seq_size):
        documents_copy(step).start()
    for i, e in enumerate((p.dx, p.dy, p.dd)):
        adapters_copy(i, e).start()
    qkv.start()
    hid.start()
    for i, e in enumerate((p.dx, p.dy)):
        remote(
            down_w, down_all.at[d], down.sems.at[0, i], down.sems.at[1, i], p.dp(e)
        ).start()
    for copy in stage:
        copy.wait()
    for copy in keep:
        copy.start()
    for copy in keep:
        copy.wait()
    qkv.recv()
    qkv_plane.start()
    hid.step(1)
    gu[0].start()
    down.forward()
    qkv_plane.forward()
    hid.step(2)
    gu[1].start()
    gu[0].recv()
    gu_planes[0].start()
    hid.step(3)
    gu[2].start()
    qkv_plane.recv()
    out.start()
    gu[1].recv()
    gu_planes[1].start()
    gu_planes[0].forward()
    gu[3].start()
    out.step(1)
    gu[2].recv()
    gu_planes[2].start()
    gu_planes[1].forward()
    out.step(2)
    cot.start()
    gu[3].recv()
    gu_planes[3].start()
    gu_planes[2].forward()
    out.step(3)
    out_plane.start()
    cot.step(1)
    gu_planes[3].forward()
    cot.step(2)
    out_plane.forward()
    side_copy(0, p.dx).start()
    side_copy(1, p.dy).start()
    cot.step(3)
    out_plane.recv()
    side_copy(2, p.dd).start()
    for i in range(4):
        gu_planes[i].recv()
    down.recv()
    for chain in (hid, out, cot):
        for other in range(p.chips):
            chain.side_recv(other)
        chain.finish()
    side_wait(0, p.dx)
    side_wait(1, p.dy)
    side_wait(2, p.dd)
    remote(
        documents_all.at[pl.ds(0, seq_size - 1)], documents_all.at[pl.ds(0, seq_size - 1)],
        small_sems.at[0, 0], small_sems.at[1, 0], p.seq(p.sib),
    ).wait_recv()
    remote(
        adapters_all.at[pl.ds(0, 3)], adapters_all.at[pl.ds(0, 3)],
        small_sems.at[2, 3], small_sems.at[3, 0], p.dp(p.dx),
    ).wait_recv()
    for step in range(1, seq_size):
        documents_copy(step).wait_send()
    for i, e in enumerate((p.dx, p.dy, p.dd)):
        adapters_copy(i, e).wait_send()
        side_copy(i, e).wait_send()
    for group in [qkv, *gu, qkv_plane, down, out_plane, *gu_planes]:
        group.finish()


def gather_all(
    seq_size, hidden, cotangent, documents, adapter_row, query_w, kv_w, out_w, gate_w, up_w, down_w
):
    tokens, width = hidden.shape
    rows = query_w.shape[0]
    part = down_w.shape[0]
    chips = seq_size // 2
    qkv_width = query_w.shape[1] // seq_size + kv_w.shape[2]

    def shape(*dims, dtype=BF16):
        return jax.ShapeDtypeStruct(dims, dtype)

    anywhere = pl.BlockSpec(memory_space=pl.ANY)
    return pl.pallas_call(
        functools.partial(gather_kernel, seq_size),
        out_shape=(
            shape(seq_size, tokens, width),
            shape(seq_size, tokens, width),
            shape(seq_size, 8, tokens, dtype=jnp.int32),
            shape(4, 8, 128, dtype=jnp.int32),
            shape(4, seq_size * rows, qkv_width),
            shape(4, chips, 2, rows, width),
            shape(4, seq_size * rows, 8 * part),
            shape(4, part, width),
        ),
        in_specs=[anywhere] * 10,
        out_specs=(anywhere,) * 8,
        scratch_shapes=[
            pltpu.SemaphoreType.DMA((3, 4, seq_size)),
            pltpu.SemaphoreType.DMA((3 + PIECES, 2, 4)),
            pltpu.SemaphoreType.DMA((2, 14)),
            pltpu.SemaphoreType.DMA((1 + PIECES, 2)),
            pltpu.SemaphoreType.DMA((4, seq_size)),
            pltpu.SemaphoreType.DMA((2, 3)),
            pltpu.VMEM((tokens, width), BF16),
            pltpu.VMEM((tokens, width), BF16),
            pltpu.VMEM((rows, width), BF16),
            pltpu.VMEM((part, width), BF16),
            pltpu.VMEM((rows, qkv_width), BF16),
            pltpu.VMEM((rows, 8 * part), BF16),
        ],
        compiler_params=pltpu.CompilerParams(collective_id=0, has_side_effects=True),
        cost_estimate=pl.CostEstimate(flops=0, bytes_accessed=2 * 30 * 2**20, transcendentals=0),
        name="gather_all",
    )(hidden, cotangent, documents, adapter_row, query_w, kv_w, out_w, gate_w, up_w, down_w)


def dot_nn(a, b):
    return lax.dot_general(a, b, (((1,), (0,)), ((), ())), preferred_element_type=F32)


def dot_nt(a, b):
    return lax.dot_general(a, b, (((1,), (1,)), ((), ())), preferred_element_type=F32)


class ChainSum:
    def __init__(self, place, part, side_in, up_in, down_in, sems):
        self.p, self.part = place, part
        self.side_in, self.up_in, self.down_in = side_in, up_in, down_in
        self.sems = sems

    def _side(self, z):
        p = self.p
        return remote(
            self.part.at[2 * z + 1 - p.c], self.side_in.at[z],
            self.sems.at[0, z], self.sems.at[1, z], p.seq(p.sib),
        )

    def _up(self, z):
        p = self.p
        return remote(
            self.part.at[2 * z + p.c], self.up_in.at[z],
            self.sems.at[2, z], self.sems.at[3, z], p.seq(p.s + 2),
        )

    def _down(self, z):
        p = self.p
        return remote(
            self.part.at[2 * z + p.c], self.down_in.at[z],
            self.sems.at[4, z], self.sems.at[5, z], p.seq(p.s - 2),
        )

    def _add(self, z, incoming):
        slot = 2 * z + self.p.c
        rows = self.part.shape[1]

        @pl.loop(0, rows // 16)
        def _(i):
            cut = pl.ds(pl.multiple_of(i * 16, 16), 16)
            total = self.part[slot, cut].astype(F32) + incoming[z, cut].astype(F32)
            self.part[slot, cut] = total.astype(BF16)

    def side_start(self, z):
        self._side(z).start()

    def side_add(self, z):
        self._side(z).wait_recv()
        self._add(z, self.side_in)

    def step(self, k):
        p = self.p

        @pl.when(p.z + k < p.chips)
        def _():
            to = p.z + k
            self.side_add(to)

            @pl.when(p.z > 0)
            def _():
                self._up(to).wait_recv()
                self._add(to, self.up_in)

            self._up(to).start()

        @pl.when(p.z >= k)
        def _():
            to = p.z - k
            self.side_add(to)

            @pl.when(p.z < p.chips - 1)
            def _():
                self._down(to).wait_recv()
                self._add(to, self.down_in)

            self._down(to).start()

    def last(self):
        p = self.p
        self.side_add(p.z)

        @pl.when(p.z > 0)
        def _():
            self._up(p.z).wait_recv()
            self._add(p.z, self.up_in)

        @pl.when(p.z < p.chips - 1)
        def _():
            self._down(p.z).wait_recv()
            self._add(p.z, self.down_in)

    def finish(self):
        p = self.p
        for z in range(p.chips):
            self._side(z).wait_send()
        for k in range(1, p.chips):

            @pl.when(p.z + k < p.chips)
            def _():
                self._up(p.z + k).wait_send()

            @pl.when(p.z >= k)
            def _():
                self._down(p.z - k).wait_send()


def swap_halves(values):
    lane = lax.broadcasted_iota(jnp.int32, values.shape, 1)
    return jnp.where(
        lane % HD < HD // 2,
        pltpu.roll(values, values.shape[1] - HD // 2, 1),
        pltpu.roll(values, HD // 2, 1),
    )


def mask_bias(seg_col, seg_row, start, size):
    length = start + size
    key_pos = lax.broadcasted_iota(jnp.int32, (length, size), 0)
    query_pos = start + lax.broadcasted_iota(jnp.int32, (length, size), 1)
    same = seg_col[pl.ds(0, length), 0:1] == seg_row[0:1, pl.ds(start, size)]
    return jnp.where((key_pos <= query_pos) & same, 0.0, -1e30).astype(F32)


QB = 256


def back_kernel(
    seq_size,
    grad_attn,
    query,
    keys2,
    values2,
    keys_t,
    log_totals,
    seg_row,
    seg_col,
    cos_t,
    sin_t,
    cos_n,
    sin_n,
    qkv_w,
    qkv_in,
    low_map,
    low_qkv_t,
    norm_one,
    ffn_part,
    early_t,
    gu_grad,
    down_grad,
    owners,
    norm_sum,
    ffn_sum,
    share_out,
    gu_out,
    down_out,
    q_out,
    kv_out,
    grads,
    key_z,
    value_z,
    key_acc,
    value_acc,
    bias,
    grad_qkv,
    grad_low,
    qkv_v,
    norm_v,
    ffn_v,
    ffn_side,
    ffn_up,
    ffn_down,
    sum_v,
    sum_side,
    sum_up,
    sum_down,
    share,
    share_in,
    turned,
    gu_in,
    down_in,
    q_got,
    kv_got,
    load_sems,
    swap_sems,
    ffn_sems,
    sum_sems,
    send_sems,
    got_sems,
):
    p = Place(seq_size)
    d, s = p.d, p.s
    length = query.shape[0]
    chips = p.chips
    loads = [
        pltpu.make_async_copy(src, dst, load_sems.at[i])
        for i, (src, dst) in enumerate(
            ((ffn_part, ffn_v), (qkv_w, qkv_v), (norm_one, norm_v), (grad_attn.at[s], grads.at[s]))
        )
    ]
    for copy in loads:
        copy.start()
    barrier = pltpu.get_barrier_semaphore()
    everyone = 4 * seq_size

    def place_of(t):
        return lax.rem(d + t // seq_size, 4), lax.rem(s + lax.rem(t, seq_size), seq_size)

    @pl.loop(1, everyone)
    def _(t):
        pl.semaphore_signal(barrier, 1, device_id=place_of(t), device_id_type=MESH)

    pl.semaphore_wait(barrier, everyone - 1)

    def swap_copy(step):
        return remote(
            grad_attn.at[p.peer(step)], grads.at[s], swap_sems.at[0, step], swap_sems.at[1, 0],
            p.seq(p.peer(step)),
        )

    for step in range(1, seq_size):
        swap_copy(step).start()

    def deliver(src, dst, td, ts, i, wait):
        here = (td == d) & (ts == s)

        @pl.when(jnp.logical_not(here))
        def _():
            copy = remote(src, dst, send_sems.at[i], got_sems.at[i], (td, ts))
            if wait:
                copy.wait_send()
            else:
                copy.start()

        if not wait:

            @pl.when(here)
            def _():
                pltpu.make_async_copy(src, dst, got_sems.at[i]).start()

    def ready(buffer, i):
        remote(buffer, buffer, send_sems.at[i], got_sems.at[i], p.seq(p.sib)).wait_recv()

    block = gu_grad.shape[1] // 8

    def deliver_wide(wait):
        side = pl.ds(pl.multiple_of(block * lax.rem(s, 2), block), block)
        for e in range(4):
            for upper in range(2):
                deliver(
                    gu_grad.at[:, pl.ds((4 * upper + e) * block, block)],
                    gu_in.at[d, :, side],
                    2 * upper + e // 2,
                    lax.rem(e, 2) * (seq_size // 2) + s // 2,
                    0,
                    wait,
                )
            deliver(down_grad.at[:, pl.ds(e * block, block)], down_in.at[d], e, s, 1, wait)

    def deliver_heads(wait):
        for i in range(4):
            m = 4 * s + i
            deliver(
                turned.at[pl.ds(HD * i, HD)], q_got.at[d], m // seq_size, lax.rem(m, seq_size), 2, wait
            )
        for i in range(4):
            m = 2 * seq_size * (i // 2) + 2 * s + i % 2
            deliver(
                turned.at[pl.ds(4 * HD + HD // 2 * i, HD // 2)],
                kv_got.at[d],
                m // seq_size,
                lax.rem(m, seq_size),
                3,
                wait,
            )

    def deliver_share(wait):
        rows = share.shape[0] // everyone

        @pl.loop(0, everyone)
        def _(t):
            td, ts = place_of(t)
            start = pl.multiple_of((td * seq_size + ts) * rows, rows)
            deliver(share.at[pl.ds(start, rows)], share_in.at[d, s], td, ts, 4, wait)

    ffn = ChainSum(p, ffn_v, ffn_side, ffn_up, ffn_down, ffn_sems)
    total = ChainSum(p, sum_v, sum_side, sum_up, sum_down, sum_sems)

    low_lane = lax.broadcasted_iota(jnp.int32, (length, 2 * HD), 1) < HD
    zero = jnp.zeros((length, 2 * HD), BF16)
    key_z[0] = jnp.where(low_lane, keys2[...], zero)
    key_z[1] = jnp.where(low_lane, zero, keys2[...])
    value_z[0] = jnp.where(low_lane, values2[...], zero)
    value_z[1] = jnp.where(low_lane, zero, values2[...])
    key_acc[...] = jnp.zeros_like(key_acc)
    value_acc[...] = jnp.zeros_like(value_acc)
    for copy in loads:
        copy.wait()
    for z in range(chips):
        ffn.side_start(z)
    remote(
        grads.at[pl.ds(0, seq_size - 1)], grads.at[pl.ds(0, seq_size - 1)],
        swap_sems.at[0, 0], swap_sems.at[1, 0], p.seq(p.sib),
    ).wait_recv()
    deliver_wide(False)
    ffn.step(3)

    def query_block(i):
        start = i * QB
        span = pl.ds(0, start + QB)
        rows = pl.ds(start, QB)
        bias[span, :] = mask_bias(seg_col, seg_row, start, QB)
        slots = QB // grads.shape[1]

        for m in range(2):
            pair = pl.ds(2 * HD * m, 2 * HD)
            query_pair = query[rows, pair]
            grad_pair = grads[pl.ds(slots * i, slots), :, pair].reshape(QB, 2 * HD)
            turned_q = []
            for e in range(2):
                h = 2 * m + e
                scores = dot_nt(key_z[e, span, :], query_pair)
                weights = jnp.exp(scores * SCORE_SCALE + bias[span, :] - log_totals[h : h + 1, rows])
                grad_weights = dot_nt(value_z[e, span, :], grad_pair)
                row_dot = jnp.sum(weights * grad_weights, axis=0, keepdims=True)
                grad_scores = (weights * (grad_weights - row_dot)).astype(BF16)
                key_acc[e, span, :] += dot_nn(grad_scores, query_pair)
                value_acc[e, span, :] += dot_nn(weights.astype(BF16), grad_pair)
                grad_q = dot_nn(keys_t[:, span], grad_scores) * SCORE_SCALE
                first, second = grad_q[: HD // 2], grad_q[HD // 2 :]
                cos_part, sin_part = cos_t[:, rows], sin_t[:, rows]
                turned_q.append(first * cos_part + second * sin_part)
                turned_q.append(second * cos_part - first * sin_part)
            grad_qkv[rows, pair] = jnp.concatenate(turned_q, axis=0).T.astype(BF16)

    query_block(0)
    query_block(1)
    query_block(2)
    ffn.step(2)
    query_block(3)

    def folded(acc):
        merged = jnp.where(low_lane, acc[0], acc[1])
        return merged + pltpu.roll(merged, HD, 1)

    grad_key = folded(key_acc) * SCORE_SCALE
    grad_key = grad_key * cos_n[...] - swap_halves(grad_key) * sin_n[...]
    grad_qkv[:, pl.ds(4 * HD, 2 * HD)] = jnp.where(low_lane, grad_key, folded(value_acc)).astype(BF16)
    grad_low[...] = dot_nt(grad_qkv[...], low_map[...]).astype(BF16)
    grad_low_t = dot_nt(low_map[...], grad_qkv[...]).astype(BF16)
    ffn.step(1)

    tokens = sum_v.shape[1]

    def fill(slot):
        rows = pl.ds(pl.multiple_of(slot * tokens, tokens), tokens)
        left, low = grad_qkv[rows, :], grad_low[rows, :]
        for j in range(4):
            cut = pl.ds(512 * j, 512)
            sum_v[slot, :, cut] = (
                dot_nt(left, qkv_v[cut, :]) + dot_nt(low, qkv_in[cut, :])
            ).astype(BF16)

    for k in (3, 2, 1, 0):

        def give(to):
            fill(2 * to)
            fill(2 * to + 1)
            total.side_start(to)

        @pl.when(p.z + k < chips)
        def _():
            give(p.z + k)

        if k:

            @pl.when(p.z >= k)
            def _():
                give(p.z - k)

            total.step(k)
        if k == 2:
            outer = dot_nn(low_qkv_t[...], grad_qkv[...])
            outer = jnp.concatenate([outer, jnp.zeros((80, outer.shape[1]), F32)], axis=0)
            turned[...] = outer.T
            deliver_heads(False)
            for j in range(8):
                cut = pl.ds(256 * j, 256)
                piece = jnp.concatenate(
                    [dot_nn(grad_low_t, norm_v[:, cut]), early_t[:, cut]], axis=0
                )
                share[cut, :] = piece.T.astype(BF16)
            deliver_share(False)
    ffn.last()
    ffn_sum[...] = ffn_v[s].astype(F32)
    for buffer, i in ((gu_in, 0), (down_in, 1), (q_got, 2), (kv_got, 3), (share_in, 4)):
        ready(buffer, i)

    def by_adapter(out, value):
        values = [value(e) for e in range(4)]
        for a in range(4):
            chosen = jnp.zeros_like(values[0])
            for e in range(4):
                chosen = jnp.where(owners[e, 0:1, 0:1] == a, values[e], chosen)
            out[a] = chosen

    by_adapter(gu_out, lambda e: gu_in[e])
    by_adapter(down_out, lambda e: down_in[e])
    by_adapter(q_out, lambda e: q_got[e])
    by_adapter(kv_out, lambda e: kv_got[e])
    by_adapter(share_out, lambda e: jnp.sum(share_in[e].astype(F32), axis=0))
    total.last()
    norm_sum[...] = sum_v[s].astype(F32)
    for step in range(1, seq_size):
        swap_copy(step).wait_send()
    deliver_wide(True)
    deliver_heads(True)
    deliver_share(True)
    ffn.finish()
    total.finish()


def back_all(seq_size, ins):
    (grad_attn, query, keys2) = ins[:3]
    _, tokens, width_q = grad_attn.shape
    length = query.shape[0]
    width = ins[16].shape[1]
    qkv_width = ins[12].shape[1]
    chips = seq_size // 2
    rows = width // (4 * seq_size)
    rank = ins[19].shape[0]
    block = ins[19].shape[1] // 8

    def shape(*dims):
        return jax.ShapeDtypeStruct(dims, F32)

    vmem = pl.BlockSpec(memory_space=pltpu.VMEM)
    anywhere = pl.BlockSpec(memory_space=pl.ANY)
    far = (0, 12, 16, 17)
    outs = (
        shape(tokens, width),
        shape(tokens, width),
        shape(4, rows, 128),
        shape(4, rank, 2 * block),
        shape(4, rank, block),
        shape(4, HD, 128),
        shape(4, HD // 2, 128),
    )
    many = (seq_size, tokens, width)
    few = (chips, tokens, width)
    return pl.pallas_call(
        functools.partial(back_kernel, seq_size),
        out_shape=outs,
        in_specs=[anywhere if i in far else vmem for i in range(len(ins))],
        out_specs=(vmem,) * len(outs),
        scratch_shapes=[
            pltpu.VMEM(grad_attn.shape, BF16),
            pltpu.VMEM((2, length, 2 * HD), BF16),
            pltpu.VMEM((2, length, 2 * HD), BF16),
            pltpu.VMEM((2, length, 2 * HD), F32),
            pltpu.VMEM((2, length, 2 * HD), F32),
            pltpu.VMEM((length, QB), F32),
            pltpu.VMEM((length, qkv_width), BF16),
            pltpu.VMEM((length, 3 * rank), BF16),
            pltpu.VMEM(ins[12].shape, BF16),
            pltpu.VMEM((length, width), BF16),
            pltpu.VMEM(many, BF16),
            pltpu.VMEM(few, BF16),
            pltpu.VMEM(few, BF16),
            pltpu.VMEM(few, BF16),
            pltpu.VMEM(many, BF16),
            pltpu.VMEM(few, BF16),
            pltpu.VMEM(few, BF16),
            pltpu.VMEM(few, BF16),
            pltpu.VMEM((width, 128), BF16),
            pltpu.VMEM((4, seq_size, rows, 128), BF16),
            pltpu.VMEM((qkv_width, 128), F32),
            pltpu.VMEM((4, rank, 2 * block), F32),
            pltpu.VMEM((4, rank, block), F32),
            pltpu.VMEM((4, HD, 128), F32),
            pltpu.VMEM((4, HD // 2, 128), F32),
            pltpu.SemaphoreType.DMA((4,)),
            pltpu.SemaphoreType.DMA((2, seq_size)),
            pltpu.SemaphoreType.DMA((6, chips)),
            pltpu.SemaphoreType.DMA((6, chips)),
            pltpu.SemaphoreType.DMA((5,)),
            pltpu.SemaphoreType.DMA((5,)),
        ],
        compiler_params=pltpu.CompilerParams(
            collective_id=1, has_side_effects=True, vmem_limit_bytes=60 * 2**20
        ),
        cost_estimate=pl.CostEstimate(
            flops=10 * 10**9, bytes_accessed=20 * 2**20, transcendentals=4 * 2**20
        ),
        name="attend_back",
    )(*ins)


def make_local(dp_size, seq_size):
    devices = dp_size * seq_size
    heads = NH // seq_size
    kv_repeat = max(1, seq_size // KVH)
    kernels = dp_size == 4 and seq_size == 8

    def local(
        hidden,
        token_document_numbers,
        sequence_adapter_index,
        cotangent,
        attention_norm_gain,
        feedforward_norm_gain,
        query_weight,
        key_weight,
        value_weight,
        attention_output_weight,
        gate_weight,
        up_weight,
        down_weight,
        adapter_query_key_value_input,
        adapter_query_output,
        adapter_key_value_output,
        adapter_projection_input,
        adapter_projection_output,
        adapter_gate_up_input,
        adapter_gate_up_output,
        adapter_down_input,
        adapter_down_output,
    ):
        tokens, width = hidden.shape[1:]
        length = tokens * seq_size
        rows = query_weight.shape[0]
        key_width = key_weight.shape[1]
        ff_width = gate_weight.shape[1]
        ff_block = ff_width // devices
        rank = adapter_projection_input.shape[2]
        adapters = adapter_projection_input.shape[0]
        me = lax.axis_index("seq")
        q_width = heads * HD

        def across(piece):
            return lax.all_to_all(piece, "seq", split_axis=0, concat_axis=0, tiled=True)

        def gather_dp(block):
            return lax.all_gather(block, "dp", axis=0, tiled=True)

        def gather_seq(block):
            return lax.all_gather(block, "seq", axis=0, tiled=True)

        def scatter_seq(total):
            return lax.psum_scatter(total, "seq", scatter_dimension=0, tiled=True)

        def by_owner(columns):
            return columns.reshape(columns.shape[0], dp_size, seq_size, ff_block)

        hidden_own = hidden[0].astype(F32)
        if kernels:
            kv = jnp.concatenate(
                [key_weight.reshape(rows, KVH, HD), value_weight.reshape(rows, KVH, HD)], axis=2
            )
            gathered = gather_all(
                seq_size,
                hidden[0],
                cotangent[0],
                jnp.broadcast_to(token_document_numbers, (8, tokens)),
                jnp.broadcast_to(sequence_adapter_index[:, None], (8, 128)),
                query_weight,
                jnp.swapaxes(kv, 0, 1),
                attention_output_weight,
                gate_weight,
                up_weight,
                down_weight,
            )
            hidden_all = gathered[0].reshape(length, width)
            cotangent_all = gathered[1].reshape(length, width)
            segments = gathered[2][:, 0].reshape(length)
            owners = gathered[3][:, 0, 0]
            qkv = gathered[4].reshape(width, -1)
            out_full = gathered[5].reshape(width, width)
            gate_up = gathered[6].reshape(width, -1)
            down = gathered[7].reshape(dp_size * ff_block, width)
        else:
            hidden_all = gather_seq(hidden[0])
            segments = gather_seq(token_document_numbers[0])
            kv = jnp.stack([key_weight.reshape(rows, KVH, HD), value_weight.reshape(rows, KVH, HD)], 2)
            kv = jnp.repeat(kv.reshape(rows, KVH, 2 * HD), kv_repeat, axis=1)
            qkv = jnp.concatenate([query_weight.reshape(rows, seq_size, q_width), kv], axis=2)
            qkv = across(jnp.swapaxes(qkv, 0, 1)).reshape(seq_size * rows, q_width + 2 * HD)
            qkv = gather_dp(qkv)
            gate_up = jnp.concatenate([by_owner(gate_weight), by_owner(up_weight)], axis=1)
            gate_up = across(jnp.transpose(gate_up, (2, 0, 1, 3)))
            gate_up = gather_dp(gate_up.reshape(seq_size * rows, 2 * dp_size * ff_block))
            down = gather_dp(down_weight)
            out_full = lax.all_gather(attention_output_weight, ("dp", "seq"), axis=0, tiled=True)
            cotangent_all = gather_seq(cotangent[0])
            owners = lax.all_gather(sequence_adapter_index, "dp", axis=0, tiled=True)
        ff_own = dp_size * ff_block

        adapter = sequence_adapter_index[0]
        qkv_in = adapter_query_key_value_input[adapter]
        q_out = lax.dynamic_slice_in_dim(adapter_query_output[adapter], me * q_width, q_width, 1)
        kv_out = adapter_key_value_output[adapter]
        kv_start = (me // kv_repeat) * HD
        k_out = lax.dynamic_slice_in_dim(kv_out, kv_start, HD, 1)
        v_out = lax.dynamic_slice_in_dim(kv_out, key_width + kv_start, HD, 1)
        o_in = adapter_projection_input[adapter]
        o_out = adapter_projection_output[adapter]
        gu_in = adapter_gate_up_input[adapter]
        gu_all = adapter_gate_up_output[adapter].reshape(rank, 2, dp_size, seq_size, ff_block)
        gu_out = lax.dynamic_index_in_dim(gu_all, me, 3, keepdims=False)
        g_out, u_out = gu_out[:, 0].reshape(rank, ff_own), gu_out[:, 1].reshape(rank, ff_own)
        down_all = adapter_down_input[adapter].reshape(dp_size, seq_size, ff_block, rank)
        down_in = lax.dynamic_index_in_dim(down_all, me, 1, keepdims=False).reshape(ff_own, rank)
        down_out = adapter_down_output[adapter]

        norm_one = rms_scale(hidden_all.astype(F32), attention_norm_gain).astype(BF16)
        low_qkv = mm(norm_one, qkv_in).astype(BF16)
        pre = mm(norm_one, qkv)
        query_pre = pre[:, :q_width] + mm(low_qkv[:, :rank], q_out)
        key_pre = pre[:, q_width : q_width + HD] + mm(low_qkv[:, rank : 2 * rank], k_out)
        value_pre = pre[:, q_width + HD :] + mm(low_qkv[:, 2 * rank :], v_out)
        cos_table, sin_table = angle_tables(jnp.arange(length, dtype=jnp.int32).astype(F32), HD)
        query = rotate(query_pre.reshape(length, heads, HD), cos_table, sin_table).astype(BF16)
        keys = rotate(key_pre.reshape(length, 1, HD), cos_table, sin_table).astype(BF16)[:, 0]
        values = value_pre.astype(BF16)
        attn_heads, log_totals = attend_forward(query, keys, values, segments)
        attn = lax.all_gather(attn_heads, "seq", axis=1, tiled=True)
        low_out = mm(attn, o_in).astype(BF16)
        branch = mm(attn, out_full) + mm(low_out, o_out)
        middle = hidden_all.astype(F32) + RESIDUAL_SCALE * branch
        own_row = me * tokens
        middle_own = lax.dynamic_slice_in_dim(middle, own_row, tokens, 0)
        norm_two = rms_scale(middle, feedforward_norm_gain).astype(BF16)
        low_gu = mm(norm_two, gu_in).astype(BF16)
        wide = mm(norm_two, gate_up)
        gate = wide[:, :ff_own] + mm(low_gu[:, :rank], g_out)
        up_proj = wide[:, ff_own:] + mm(low_gu[:, rank:], u_out)
        sigma = jax.nn.sigmoid(gate)
        activation = (gate * sigma * up_proj).astype(BF16)
        low_down = mm(activation, down_in).astype(BF16)
        ffn_part = (mm(activation, down) + mm(low_down, down_out)).astype(BF16)

        grad_ffn = (RESIDUAL_SCALE * cotangent_all.astype(F32)).astype(BF16)
        grad_low_down = mm_t(grad_ffn, down_out).astype(BF16)
        grad_act = mm_t(grad_ffn, down) + mm_t(grad_low_down, down_in)
        grad_gate = (grad_act * up_proj * sigma * (1.0 + gate * (1.0 - sigma))).astype(BF16)
        grad_up = (grad_act * gate * sigma).astype(BF16)
        grad_low_gu = jnp.concatenate([mm_t(grad_gate, g_out), mm_t(grad_up, u_out)], axis=1)
        grad_low_gu = grad_low_gu.astype(BF16)
        grad_norm_two = scatter_seq(
            (
                mm_t(jnp.concatenate([grad_gate, grad_up], axis=1), gate_up)
                + mm_t(grad_low_gu, gu_in)
            ).astype(BF16)
        )
        grad_middle = cotangent[0].astype(F32) + rms_back(
            middle_own, feedforward_norm_gain, grad_norm_two.astype(F32)
        )
        grad_branch = (RESIDUAL_SCALE * grad_middle).astype(BF16)
        grad_low_out = mm_t(grad_branch, o_out).astype(BF16)
        grad_attn = (mm_t(grad_branch, out_full) + mm_t(grad_low_out, o_in)).astype(BF16)
        attn_own = lax.dynamic_slice_in_dim(attn, own_row, tokens, 0)
        low_out_own = lax.dynamic_slice_in_dim(low_out, own_row, tokens, 0)
        if kernels:
            early = jnp.concatenate(
                [
                    t_mm(grad_low_out, attn_own),
                    t_mm(low_out_own, grad_branch),
                    t_mm(grad_low_gu, norm_two),
                    t_mm(low_down, grad_ffn),
                ],
                axis=0,
            )
            gu_grad = jnp.concatenate(
                [t_mm(low_gu[:, :rank], grad_gate), t_mm(low_gu[:, rank:], grad_up)], axis=1
            )
            none_q = jnp.zeros((rank, q_width), BF16)
            none_h = jnp.zeros((rank, HD), BF16)
            low_map = jnp.concatenate(
                [
                    jnp.concatenate([q_out, none_h, none_h], axis=1),
                    jnp.concatenate([none_q, k_out, none_h], axis=1),
                    jnp.concatenate([none_q, none_h, v_out], axis=1),
                ],
                axis=0,
            )
            sums = back_all(
                seq_size,
                (
                    jnp.swapaxes(grad_attn.reshape(tokens, seq_size, q_width), 0, 1),
                    query.reshape(length, q_width),
                    jnp.concatenate([keys, keys], axis=1),
                    jnp.concatenate([values, values], axis=1),
                    keys.T,
                    jnp.swapaxes(log_totals, 0, 1).reshape(heads, length),
                    segments[None],
                    jnp.broadcast_to(segments[:, None], (length, 128)),
                    cos_table.T,
                    sin_table.T,
                    jnp.tile(cos_table, (1, 4)),
                    jnp.tile(jnp.concatenate([-sin_table, sin_table], axis=1), (1, 2)),
                    qkv,
                    qkv_in,
                    low_map,
                    low_qkv.T,
                    norm_one,
                    ffn_part.reshape(seq_size, tokens, width),
                    early,
                    gu_grad,
                    t_mm(grad_low_down, activation),
                    gathered[3],
                ),
            )
            norm_sum, ffn_sum, share, gu_got, down_got, q_got, kv_got = sums
            mixed = (middle_own + RESIDUAL_SCALE * ffn_sum).astype(BF16)
            grad_hidden = grad_middle + rms_back(hidden_own, attention_norm_gain, norm_sum)
            lower = lax.axis_index("dp") < dp_size // 2
            kv_got = jnp.where(lower, kv_got[:, :, rank : 2 * rank], kv_got[:, :, 2 * rank : 3 * rank])
            share_t = jnp.swapaxes(share, 1, 2)
            return (
                mixed[None],
                grad_hidden.astype(BF16)[None],
                share[:, :, : 3 * rank],
                jnp.swapaxes(q_got[:, :, :rank], 1, 2),
                jnp.swapaxes(kv_got, 1, 2),
                share[:, :, 3 * rank : 4 * rank],
                share_t[:, 4 * rank : 5 * rank],
                share[:, :, 5 * rank : 7 * rank],
                gu_got,
                jnp.swapaxes(down_got, 1, 2),
                share_t[:, 7 * rank :],
            )
        ffn = lax.psum_scatter(ffn_part, "seq", scatter_dimension=0, tiled=True)
        mixed = (middle_own + RESIDUAL_SCALE * ffn.astype(F32)).astype(BF16)
        grad_heads = lax.all_to_all(
            jnp.swapaxes(grad_attn.reshape(tokens, seq_size, q_width), 0, 1),
            "seq",
            split_axis=0,
            concat_axis=0,
            tiled=True,
        ).reshape(length, heads, HD)
        grad_q, grad_k, grad_v = attend_backward(
            query, keys, values, segments, log_totals, grad_heads
        )
        grad_query = rotate(grad_q.astype(F32), cos_table, -sin_table)
        grad_query = grad_query.reshape(length, q_width).astype(BF16)
        grad_key = rotate(grad_k[:, None], cos_table, -sin_table)[:, 0].astype(BF16)
        grad_value = grad_v.astype(BF16)
        grad_low_qkv = jnp.concatenate(
            [mm_t(grad_query, q_out), mm_t(grad_key, k_out), mm_t(grad_value, v_out)], axis=1
        ).astype(BF16)
        grad_qkv = jnp.concatenate([grad_query, grad_key, grad_value], axis=1)
        grad_norm_one = scatter_seq((mm_t(grad_qkv, qkv) + mm_t(grad_low_qkv, qkv_in)).astype(BF16))
        grad_hidden = grad_middle + rms_back(
            hidden_own, attention_norm_gain, grad_norm_one.astype(F32)
        )

        partial = jnp.concatenate(
            [
                t_mm(norm_one, grad_low_qkv),
                t_mm(attn_own, grad_low_out),
                t_mm(grad_branch, low_out_own),
                t_mm(norm_two, grad_low_gu),
                t_mm(grad_ffn, low_down),
            ],
            axis=1,
        ).reshape(dp_size, seq_size, rows, 8 * rank)
        own_q = t_mm(grad_query, low_qkv[:, :rank])
        own_k = t_mm(grad_key, low_qkv[:, rank : 2 * rank])
        own_v = t_mm(grad_value, low_qkv[:, 2 * rank :])
        own_g = t_mm(grad_gate, low_gu[:, :rank]).reshape(dp_size, ff_block, rank)
        own_u = t_mm(grad_up, low_gu[:, rank:]).reshape(dp_size, ff_block, rank)
        own_d = t_mm(activation, grad_low_down).reshape(dp_size, ff_block, rank)

        def placed(block, total, start, axis):
            empty = list(block.shape)
            empty[axis] = total
            return lax.dynamic_update_slice_in_dim(jnp.zeros(empty, F32), block, start, axis)

        def by_target(whole):
            return whole.reshape(dp_size, seq_size, -1)

        full_q = placed(own_q, width, me * q_width, 0)
        full_kv = jnp.concatenate(
            [placed(own_k, key_width, kv_start, 0), placed(own_v, key_width, kv_start, 0)], axis=0
        )
        spot = [placed(v[:, None], seq_size, me, 1) for v in (own_g, own_u, own_d)]
        full_gu = jnp.concatenate([spot[0].reshape(ff_width, rank), spot[1].reshape(ff_width, rank)])
        pieces = [by_target(v) for v in (partial, full_q, full_kv, full_gu, spot[2])]
        send = jnp.concatenate(pieces, axis=2)
        send = jnp.swapaxes(send, 0, 1).reshape(seq_size, -1)
        mine = lax.psum_scatter(send, "seq", scatter_dimension=0, tiled=True)
        mine = lax.all_to_all(
            mine.reshape(dp_size, -1), "dp", split_axis=0, concat_axis=0, tiled=True
        )
        numbers = jnp.arange(adapters, dtype=jnp.int32)
        chooser = (owners[:, None] == numbers[None, :]).astype(F32)
        mine = jnp.einsum("sa,si->ai", chooser, mine, precision=lax.Precision.HIGHEST)
        sizes = [v.shape[2] for v in pieces]
        cuts = [sum(sizes[:i]) for i in range(1, len(sizes))]
        got, got_q, got_kv, got_gu, got_d = jnp.split(mine, cuts, axis=1)
        got = got.reshape(adapters, rows, 8 * rank)

        def turned(flat):
            return jnp.swapaxes(flat.reshape(adapters, -1, rank), 1, 2)

        return (
            mixed[None],
            grad_hidden.astype(BF16)[None],
            got[:, :, : 3 * rank],
            turned(got_q),
            turned(got_kv),
            got[:, :, 3 * rank : 4 * rank],
            jnp.swapaxes(got[:, :, 4 * rank : 5 * rank], 1, 2),
            got[:, :, 5 * rank : 7 * rank],
            turned(got_gu),
            got_d.reshape(adapters, ff_block, rank),
            jnp.swapaxes(got[:, :, 7 * rank :], 1, 2),
        )

    return local


def solution(mesh):
    both = ("dp", "seq")
    tokens = P("dp", "seq", None)
    weight = P(both, None)
    in_specs = (
        (tokens, P("dp", "seq"), P("dp"), tokens, P(), P()) + (weight,) * 7 + (P(),) * 9
    )
    by_row, by_column = P(None, both, None), P(None, None, both)
    out_specs = (
        tokens,
        tokens,
        by_row,
        by_column,
        by_column,
        by_row,
        by_column,
        by_row,
        by_column,
        by_row,
        by_column,
    )
    local = make_local(mesh.shape["dp"], mesh.shape["seq"])
    return jax.shard_map(local, mesh=mesh, in_specs=in_specs, out_specs=out_specs, check_vma=False)
```

```python
import functools
import math

import jax
import jax.numpy as jnp
import numpy as np
from jax import lax
from jax.experimental import pallas as pl
from jax.experimental.pallas import tpu as pltpu
from jax.sharding import PartitionSpec as P

NH = 32
KVH = 8
HD = 64

EPSILON = 1e-05
RESIDUAL_SCALE = 0.22
SCORE_SCALE = 1.0 / 64.0
ROPE_BASE = 10000000.0
BF16 = jnp.bfloat16
F32 = jnp.float32


def mm(a, b):
    return jnp.dot(a, b, preferred_element_type=F32)


def mm_t(a, b):
    return lax.dot_general(a, b, (((1,), (1,)), ((), ())), preferred_element_type=F32)


def t_mm(a, b):
    return lax.dot_general(a, b, (((0,), (0,)), ((), ())), preferred_element_type=F32)


def rms_scale(values, gain):
    mean_square = jnp.mean(values * values, axis=-1, keepdims=True)
    return values * lax.rsqrt(mean_square + EPSILON) * gain


def rms_back(values, gain, grad):
    r = lax.rsqrt(jnp.mean(values * values, axis=-1, keepdims=True) + EPSILON)
    z = grad * gain
    return r * z - r * r * r * values * jnp.mean(z * values, axis=-1, keepdims=True)


def angle_tables(positions, head_size):
    steps = jnp.arange(head_size // 2).astype(F32)
    frequency = jnp.exp(steps * (-2.0 * math.log(ROPE_BASE) / head_size))
    angles = positions[:, None] * frequency[None, :]
    return (jnp.cos(angles), jnp.sin(angles))


def fixed_tables(length):
    steps = np.arange(HD // 2, dtype=np.float32)
    frequency = np.exp(steps * np.float32(-2.0 * math.log(ROPE_BASE) / HD))
    angles = np.arange(length, dtype=np.float32)[:, None] * frequency[None, :]
    return (np.cos(angles), np.sin(angles))


def rotate(values, cos_table, sin_table):
    half_width = values.shape[-1] // 2
    first_half = values[..., :half_width]
    second_half = values[..., half_width:]
    cos_part = cos_table[:, None, :]
    sin_part = sin_table[:, None, :]
    return jnp.concatenate(
        [
            first_half * cos_part - second_half * sin_part,
            second_half * cos_part + first_half * sin_part,
        ],
        axis=-1,
    )


def masked_scores(query_block, keys, seg_block, segments, start_row):
    key_pos = jnp.arange(keys.shape[0], dtype=jnp.int32)
    query_pos = start_row + jnp.arange(query_block.shape[0], dtype=jnp.int32)
    scores = jnp.einsum("qhd,kd->hqk", query_block, keys, preferred_element_type=F32) * SCORE_SCALE
    allowed = (key_pos[None, :] <= query_pos[:, None]) & (seg_block[:, None] == segments[None, :])
    return jnp.where(allowed[None], scores, -1e30)


def attend_forward(query, keys, values, segments):
    length, heads, head_size = query.shape
    rows = min(512, length)

    def one_block(index):
        start = index * rows
        query_block = lax.dynamic_slice_in_dim(query, start, rows, 0)
        seg_block = lax.dynamic_slice_in_dim(segments, start, rows, 0)
        scores = masked_scores(query_block, keys, seg_block, segments, start)
        row_max = jnp.max(scores, axis=-1, keepdims=True)
        weights = jnp.exp(scores - row_max)
        totals = jnp.sum(weights, axis=-1, keepdims=True)
        low = (weights / totals).astype(BF16)
        output = jnp.einsum("hqk,kd->qhd", low, values, preferred_element_type=F32)
        return (output.astype(BF16), (row_max + jnp.log(totals))[..., 0])

    outputs, log_totals = lax.map(one_block, jnp.arange(length // rows, dtype=jnp.int32))
    return (outputs.reshape(length, heads * head_size), log_totals)


def attend_backward(query, keys, values, segments, log_totals, grad):
    length, heads, head_size = query.shape
    rows = min(512, length)

    def one_block(carry, index):
        grad_keys, grad_values = carry
        start = index * rows
        query_block = lax.dynamic_slice_in_dim(query, start, rows, 0)
        seg_block = lax.dynamic_slice_in_dim(segments, start, rows, 0)
        grad_block = lax.dynamic_slice_in_dim(grad, start, rows, 0)
        scores = masked_scores(query_block, keys, seg_block, segments, start)
        weights = jnp.exp(scores - log_totals[index][..., None])
        grad_weights = jnp.einsum("qhd,kd->hqk", grad_block, values, preferred_element_type=F32)
        row_dot = jnp.sum(weights * grad_weights, axis=-1, keepdims=True)
        grad_scores = (weights * (grad_weights - row_dot)).astype(BF16)
        grad_query = jnp.einsum("hqk,kd->qhd", grad_scores, keys, preferred_element_type=F32)
        grad_keys = grad_keys + jnp.einsum(
            "hqk,qhd->kd", grad_scores, query_block, preferred_element_type=F32
        )
        grad_values = grad_values + jnp.einsum(
            "hqk,qhd->kd", weights.astype(BF16), grad_block, preferred_element_type=F32
        )
        return ((grad_keys, grad_values), (grad_query * SCORE_SCALE).astype(BF16))

    zero = jnp.zeros(keys.shape, F32)
    (grad_keys, grad_values), grad_query = lax.scan(
        one_block, (zero, zero), jnp.arange(length // rows, dtype=jnp.int32)
    )
    return (grad_query.reshape(length, heads, head_size), grad_keys * SCORE_SCALE, grad_values)


MESH = pl.DeviceIdType.MESH


def remote(src, dst, send_sem, recv_sem, device):
    return pltpu.make_async_remote_copy(
        src_ref=src,
        dst_ref=dst,
        send_sem=send_sem,
        recv_sem=recv_sem,
        device_id=device,
        device_id_type=MESH,
    )


class Place:
    def __init__(self, seq_size):
        self.d = lax.axis_index("dp")
        self.s = lax.axis_index("seq")
        self.seq_size = seq_size
        self.chips = seq_size // 2
        self.z = self.s // 2
        self.c = self.s % 2
        self.dx = self.d + 1 - 2 * (self.d % 2)
        self.dy = lax.rem(self.d + 2, 4)
        self.dd = lax.rem(self.dx + 2, 4)
        self.sib = self.s + 1 - 2 * self.c

    def seq(self, s):
        return (self.d, s)

    def dp(self, d):
        return (d, self.s)

    def peer(self, step):
        return lax.rem(self.s + step, self.seq_size)

    def greet(self, seq_steps, dp_peers):
        barrier = pltpu.get_barrier_semaphore()
        for step in seq_steps:
            pl.semaphore_signal(
                barrier, 1, device_id=self.seq(self.peer(step)), device_id_type=MESH
            )
        for d in dp_peers:
            pl.semaphore_signal(barrier, 1, device_id=self.dp(d), device_id_type=MESH)
        pl.semaphore_wait(barrier, len(seq_steps) + len(dp_peers))


class Chain:
    def __init__(self, place, own, slot, sems):
        self.p, self.own, self.slot = place, own, slot
        self.up, self.down, self.side, self.got = (sems.at[i] for i in range(4))

    def _up(self, src, i):
        return remote(src, self.slot(i), self.up.at[i], self.got.at[i], self.p.seq(self.p.s + 2))

    def _down(self, src, i):
        return remote(src, self.slot(i), self.down.at[i], self.got.at[i], self.p.seq(self.p.s - 2))

    def _side(self, src, i):
        return remote(src, self.slot(i), self.side.at[i], self.got.at[i], self.p.seq(self.p.sib))

    def start(self):
        p = self.p

        @pl.when(p.z < p.chips - 1)
        def _():
            self._up(self.own, p.s).start()

        @pl.when(p.z > 0)
        def _():
            self._down(self.own, p.s).start()

        self._side(self.own, p.s).start()

    def step(self, k):
        p = self.p
        low, high = p.s - 2 * k, p.s + 2 * k

        @pl.when(p.z >= k)
        def _():
            self._side(self.slot(low), low).wait_recv()

            @pl.when(p.z < p.chips - 1)
            def _():
                self._up(self.slot(low), low).start()

            self._side(self.slot(low), low).start()

        @pl.when(p.z + k < p.chips)
        def _():
            self._side(self.slot(high), high).wait_recv()

            @pl.when(p.z > 0)
            def _():
                self._down(self.slot(high), high).start()

            self._side(self.slot(high), high).start()

    def side_recv(self, z):
        other = 2 * z + 1 - self.p.c
        self._side(self.slot(other), other).wait_recv()

    def finish(self):
        p = self.p

        @pl.when(p.z < p.chips - 1)
        def _():
            self._up(self.own, p.s).wait_send()

        @pl.when(p.z > 0)
        def _():
            self._down(self.own, p.s).wait_send()

        self._side(self.own, p.s).wait_send()
        for k in range(1, p.chips):
            low, high = p.s - 2 * k, p.s + 2 * k

            @pl.when(p.z >= k)
            def _():
                @pl.when(p.z < p.chips - 1)
                def _():
                    self._up(self.slot(low), low).wait_send()

                self._side(self.slot(low), low).wait_send()

            @pl.when(p.z + k < p.chips)
            def _():
                @pl.when(p.z > 0)
                def _():
                    self._down(self.slot(high), high).wait_send()

                self._side(self.slot(high), high).wait_send()


class Plane:
    def __init__(self, place, block, half, sems):
        self.p, self.block, self.half, self.sems = place, block, half, sems

    def _copy(self, ref, i, d):
        return remote(ref, ref, self.sems.at[0, i], self.sems.at[1, i], self.p.dp(d))

    def _all(self):
        p = self.p
        return (
            (self.block(p.d), p.dx),
            (self.block(p.d), p.dy),
            (self.half(p.dx, 0), p.dy),
            (self.half(p.dy, 1), p.dx),
        )

    def start(self):
        for i, (ref, d) in enumerate(self._all()[:2]):
            self._copy(ref, i, d).start()

    def forward(self):
        p = self.p
        everything = self._all()
        for i, came in ((0, p.dx), (1, p.dy)):
            self._copy(self.block(came), i, came).wait_recv()
            ref, d = everything[2 + i]
            self._copy(ref, 2 + i, d).start()

    def recv(self):
        p = self.p
        self._copy(self.half(p.dd, 0), 2, p.dy).wait_recv()
        self._copy(self.half(p.dd, 1), 3, p.dx).wait_recv()

    def finish(self):
        for i, (ref, d) in enumerate(self._all()):
            self._copy(ref, i, d).wait_send()


class Spread:
    def __init__(self, place, pairs, whole, send_sem, recv_sem):
        self.p, self.pairs, self.whole = place, pairs, whole
        self.send_sem, self.recv_sem = send_sem, recv_sem

    def start(self):
        p = self.p
        for step in (1, 2, 3, 4, 5, 6, 7):
            j = p.peer(step)
            for src, dst in self.pairs(j):
                remote(src, dst, self.send_sem, self.recv_sem, p.seq(j)).start()

    def recv(self):
        p = self.p
        for whole in self.whole:
            remote(whole, whole, self.send_sem, self.recv_sem, p.seq(p.sib)).wait_recv()

    def finish(self):
        p = self.p
        for whole in self.whole:
            remote(whole, whole, self.send_sem, self.recv_sem, p.seq(p.sib)).wait_send()


def dot_nn(a, b):
    return lax.dot_general(a, b, (((1,), (0,)), ((), ())), preferred_element_type=F32)


def dot_nt(a, b):
    return lax.dot_general(a, b, (((1,), (1,)), ((), ())), preferred_element_type=F32)


class ChainSum:
    def __init__(self, place, part, side_in, up_in, down_in, sems):
        self.p, self.part = place, part
        self.side_in, self.up_in, self.down_in = side_in, up_in, down_in
        self.sems = sems

    def _side(self, z):
        p = self.p
        return remote(
            self.part.at[2 * z + 1 - p.c], self.side_in.at[z],
            self.sems.at[0, z], self.sems.at[1, z], p.seq(p.sib),
        )

    def _up(self, z):
        p = self.p
        return remote(
            self.part.at[2 * z + p.c], self.up_in.at[z],
            self.sems.at[2, z], self.sems.at[3, z], p.seq(p.s + 2),
        )

    def _down(self, z):
        p = self.p
        return remote(
            self.part.at[2 * z + p.c], self.down_in.at[z],
            self.sems.at[4, z], self.sems.at[5, z], p.seq(p.s - 2),
        )

    def _add(self, z, incoming):
        slot = 2 * z + self.p.c
        rows = self.part.shape[1]

        @pl.loop(0, rows // 16)
        def _(i):
            cut = pl.ds(pl.multiple_of(i * 16, 16), 16)
            total = self.part[slot, cut].astype(F32) + incoming[z, cut].astype(F32)
            self.part[slot, cut] = total.astype(BF16)

    def side_start(self, z):
        self._side(z).start()

    def side_add(self, z):
        self._side(z).wait_recv()
        self._add(z, self.side_in)

    def step(self, k):
        p = self.p

        @pl.when(p.z + k < p.chips)
        def _():
            to = p.z + k
            self.side_add(to)

            @pl.when(p.z > 0)
            def _():
                self._up(to).wait_recv()
                self._add(to, self.up_in)

            self._up(to).start()

        @pl.when(p.z >= k)
        def _():
            to = p.z - k
            self.side_add(to)

            @pl.when(p.z < p.chips - 1)
            def _():
                self._down(to).wait_recv()
                self._add(to, self.down_in)

            self._down(to).start()

    def last(self):
        p = self.p
        self.side_add(p.z)

        @pl.when(p.z > 0)
        def _():
            self._up(p.z).wait_recv()
            self._add(p.z, self.up_in)

        @pl.when(p.z < p.chips - 1)
        def _():
            self._down(p.z).wait_recv()
            self._add(p.z, self.down_in)

    def finish(self):
        p = self.p
        for z in range(p.chips):
            self._side(z).wait_send()
        for k in range(1, p.chips):

            @pl.when(p.z + k < p.chips)
            def _():
                self._up(p.z + k).wait_send()

            @pl.when(p.z >= k)
            def _():
                self._down(p.z - k).wait_send()


def swap_halves(values):
    lane = lax.broadcasted_iota(jnp.int32, values.shape, 1)
    return jnp.where(
        lane % HD < HD // 2,
        pltpu.roll(values, values.shape[1] - HD // 2, 1),
        pltpu.roll(values, HD // 2, 1),
    )


def mask_bias(seg_col, seg_row, start, size):
    length = start + size
    key_pos = lax.broadcasted_iota(jnp.int32, (length, size), 0)
    query_pos = start + lax.broadcasted_iota(jnp.int32, (length, size), 1)
    same = seg_col[pl.ds(0, length), 0:1] == seg_row[0:1, pl.ds(start, size)]
    return jnp.where((key_pos <= query_pos) & same, 0.0, -1e30).astype(F32)


PIECES = 4
QB = 256


def front_kernel(
    seq_size,
    hidden,
    cotangent,
    documents,
    adapter_row,
    query_w,
    kv_w,
    out_w,
    gate_w,
    up_w,
    down_w,
    gain,
    qkv_in,
    low_map,
    cos_n,
    sin_n,
    hidden_all,
    cotangent_all,
    adapters_all,
    qkv_all,
    out_all,
    gu_all,
    down_all,
    attn_all,
    norm_all,
    query,
    keys2,
    values2,
    keys_t,
    log_totals,
    seg_row,
    seg_col,
    low_t,
    documents_all,
    chain_sems,
    plane_sems,
    local_sems,
    spread_sems,
    small_sems,
    side_sems,
    hidden_v,
    norm_v,
    cotangent_v,
    out_v,
    down_v,
    qkv_v,
    gu_v,
    weights_v,
    key_z,
    values_t,
    bias,
    attn_v,
):
    p = Place(seq_size)
    d, s, z, c = p.d, p.s, p.z, p.c
    rows = query_w.shape[0]
    part = down_w.shape[0]
    tokens = hidden.shape[0]
    half_rows = seq_size * rows // 2
    landing = pl.ds(pl.multiple_of(rows * s, rows), rows)
    q_width = query_w.shape[1] // seq_size

    def column_block(number, size):
        return pl.ds(pl.multiple_of(number * size, size), size)

    stage = [
        (hidden, hidden_v.at[s]),
        (cotangent, cotangent_v),
        (out_w, out_v),
        (down_w, down_v),
        (query_w.at[:, column_block(s, q_width)], qkv_v.at[:, pl.ds(0, q_width)]),
        (kv_w.at[s], qkv_v.at[:, pl.ds(q_width, kv_w.shape[2])]),
        (documents, documents_all.at[s]),
        (adapter_row, adapters_all.at[d]),
    ]
    for i in range(8):
        matrix = (gate_w, up_w)[i // 4]
        block = matrix.at[:, column_block(seq_size * (i % 4) + s, part)]
        stage.append((block, gu_v.at[:, pl.ds(part * i, part)]))
    stage = [
        pltpu.make_async_copy(src, dst, local_sems.at[0, i]) for i, (src, dst) in enumerate(stage)
    ]
    keep = [
        pltpu.make_async_copy(src, dst, local_sems.at[1, i])
        for i, (src, dst) in enumerate(
            (
                (cotangent_v, cotangent_all.at[s]),
                (out_v, out_all.at[d, z, c]),
                (down_v, down_all.at[d]),
                (qkv_v, qkv_all.at[d, landing]),
                (gu_v, gu_all.at[d, landing]),
                (qkv_all, weights_v),
                (hidden_v, hidden_all),
                (norm_v, norm_all),
                (attn_v, attn_all.at[s]),
            )
        )
    ]
    for copy in stage:
        copy.start()
    p.greet(range(1, seq_size), (p.dx, p.dy, p.dd))

    hid = Chain(p, hidden, lambda i: hidden_v.at[i], chain_sems.at[0])
    cot = Chain(p, cotangent, lambda i: cotangent_all.at[i], chain_sems.at[1])
    out = Chain(p, out_w, lambda i: out_all.at[d, i // 2, i % 2], chain_sems.at[2])
    att = Chain(p, attn_v, lambda i: attn_all.at[i], chain_sems.at[3])

    def qkv_pairs(j):
        return (
            (query_w.at[:, column_block(j, q_width)], qkv_all.at[d, landing, pl.ds(0, q_width)]),
            (kv_w.at[j], qkv_all.at[d, landing, pl.ds(q_width, kv_w.shape[2])]),
        )

    def gu_pairs(piece):
        matrix = (gate_w, up_w)[piece // 2]

        def pairs(j):
            found = []
            for block in (2 * (piece % 2), 2 * (piece % 2) + 1):
                at = part * (4 * (piece // 2) + block)
                source = matrix.at[:, column_block(seq_size * block + j, part)]
                found.append((source, gu_all.at[d, landing, pl.ds(at, part)]))
            return found

        return pairs

    others = pl.ds(0, rows * (seq_size - 1))
    qkv = Spread(
        p, qkv_pairs, [qkv_all.at[d, others]], spread_sems.at[0, 0], spread_sems.at[0, 1]
    )
    gu = []
    gu_planes = []
    for i in range(PIECES):
        cut = pl.ds(2 * part * i, 2 * part)
        gu.append(
            Spread(
                p, gu_pairs(i), [gu_all.at[d, others, cut]], spread_sems.at[1 + i, 0],
                spread_sems.at[1 + i, 1],
            )
        )
        gu_planes.append(
            Plane(
                p,
                lambda e, cut=cut: gu_all.at[e, :, cut],
                lambda e, h, cut=cut: gu_all.at[e, pl.ds(half_rows * h, half_rows), cut],
                plane_sems.at[3 + i],
            )
        )
    qkv_plane = Plane(
        p,
        lambda e: qkv_all.at[e],
        lambda e, h: qkv_all.at[e, pl.ds(half_rows * h, half_rows)],
        plane_sems.at[0],
    )
    down = Plane(
        p,
        lambda e: down_all.at[e],
        lambda e, h: down_all.at[e, pl.ds(part // 2 * h, part // 2)],
        plane_sems.at[1],
    )
    half_chips = p.chips // 2
    out_plane = Plane(
        p,
        lambda e: out_all.at[e, :, c],
        lambda e, h: out_all.at[e, pl.ds(half_chips * h, half_chips), c],
        plane_sems.at[2],
    )

    def documents_copy(step):
        return remote(
            documents, documents_all.at[s], small_sems.at[0, step], small_sems.at[1, 0],
            p.seq(p.peer(step)),
        )

    def adapters_copy(i, e):
        return remote(
            adapter_row, adapters_all.at[d], small_sems.at[2, i], small_sems.at[3, 0], p.dp(e)
        )

    def side_copy(i, e):
        ref = out_all.at[e, :, c]
        return remote(ref, ref, side_sems.at[0, i], side_sems.at[1, i], p.seq(p.sib))

    def side_wait(i, e):
        ref = out_all.at[e, :, 1 - c]
        remote(ref, ref, side_sems.at[0, i], side_sems.at[1, i], p.seq(p.sib)).wait_recv()

    low_lane = lax.broadcasted_iota(jnp.int32, (tokens, 2 * HD), 1) < HD
    weights = weights_v.reshape(4 * seq_size * rows, qkv_v.shape[1])

    def process(slot):
        at = pl.ds(pl.multiple_of(slot * tokens, tokens), tokens)
        cos_part, sin_part = cos_n[at, :], sin_n[at, :]
        normed = rms_scale(hidden_v[slot].astype(F32), gain[...]).astype(BF16)
        norm_v[slot] = normed
        low = dot_nn(normed, qkv_in[...]).astype(BF16)
        pre = dot_nn(normed, weights[...]) + dot_nn(low, low_map[...])
        padded = jnp.concatenate(
            [low.astype(F32), jnp.zeros((tokens, 128 - low.shape[1]), F32)], axis=1
        )
        low_t[:, at] = padded.T[: low.shape[1]].astype(BF16)
        for m in range(2):
            pair = pre[:, 2 * HD * m : 2 * HD * (m + 1)]
            turned = pair * cos_part + swap_halves(pair) * sin_part
            query[at, pl.ds(2 * HD * m, 2 * HD)] = turned.astype(BF16)
        pair = pre[:, 4 * HD :]
        turned = pair * cos_part + swap_halves(pair) * sin_part
        both = jnp.where(low_lane, turned, pair)
        crossed = pltpu.roll(both, HD, 1)
        keys2[at, :] = jnp.where(low_lane, both, crossed).astype(BF16)
        values2[at, :] = jnp.where(low_lane, crossed, both).astype(BF16)
        zero = jnp.zeros_like(both)
        key_z[0, at, :] = jnp.where(low_lane, both, zero).astype(BF16)
        key_z[1, at, :] = jnp.where(low_lane, zero, crossed).astype(BF16)
        both_t = both.T
        keys_t[:, at] = both_t[:HD].astype(BF16)
        values_t[:, at] = both_t[HD:].astype(BF16)

    def process_distance(k):
        @pl.when(p.z >= k)
        def _():
            hid.side_recv(p.z - k)

            @pl.loop(0, 2)
            def _(core):
                process(2 * (p.z - k) + core)

        if k:

            @pl.when(p.z + k < p.chips)
            def _():
                hid.side_recv(p.z + k)

                @pl.loop(0, 2)
                def _(core):
                    process(2 * (p.z + k) + core)

    def query_block(i):
        start = i * QB
        span = pl.ds(0, start + QB)
        at = pl.ds(start, QB)
        bias[span, :] = mask_bias(seg_col, seg_row, start, QB)

        for m in range(2):
            pair = pl.ds(2 * HD * m, 2 * HD)
            query_pair = query[at, pair]
            found = []
            for e in range(2):
                scores = dot_nt(key_z[e, span, :], query_pair) * SCORE_SCALE + bias[span, :]
                top = jnp.max(scores, axis=0, keepdims=True)
                raised = jnp.exp(scores - top)
                total = jnp.sum(raised, axis=0, keepdims=True)
                found.append(dot_nn(values_t[:, span], raised.astype(BF16)) / total)
                log_totals[2 * m + e : 2 * m + e + 1, at] = top + jnp.log(total)
            attn_v[at, pair] = jnp.concatenate(found, axis=0).T.astype(BF16)

    for step in range(1, seq_size):
        documents_copy(step).start()
    for i, e in enumerate((p.dx, p.dy, p.dd)):
        adapters_copy(i, e).start()
    qkv.start()
    hid.start()
    for copy in stage:
        copy.wait()
    for i in range(5):
        keep[i].start()
    for i in range(5):
        keep[i].wait()
    qkv.recv()
    qkv_plane.start()
    hid.step(1)
    gu[0].start()
    remote(
        documents_all.at[pl.ds(0, seq_size - 1)], documents_all.at[pl.ds(0, seq_size - 1)],
        small_sems.at[0, 0], small_sems.at[1, 0], p.seq(p.sib),
    ).wait_recv()
    for slot in range(seq_size):
        at = pl.ds(tokens * slot, tokens)
        numbers = documents_all[slot].astype(F32)
        seg_row[:, at] = numbers
        seg_col[at, :] = jnp.broadcast_to(numbers[0:1, :], (tokens, tokens)).T
    qkv_plane.forward()
    hid.step(2)
    gu[1].start()
    gu[0].recv()
    gu_planes[0].start()
    qkv_plane.recv()
    keep[5].start()
    keep[5].wait()
    process_distance(0)
    process_distance(1)
    hid.step(3)
    gu[2].start()
    out.start()
    gu[1].recv()
    gu_planes[1].start()
    gu_planes[0].forward()
    process_distance(2)
    process_distance(3)
    gu[3].start()
    out.step(1)
    keep[6].start()
    keep[7].start()
    query_block(0)
    query_block(1)
    gu[2].recv()
    gu_planes[2].start()
    gu_planes[1].forward()
    out.step(2)
    query_block(2)
    query_block(3)
    keep[8].start()
    att.start()
    gu[3].recv()
    gu_planes[3].start()
    gu_planes[2].forward()
    out.step(3)
    out_plane.start()
    att.step(1)
    cot.start()
    down.start()
    gu_planes[3].forward()
    att.step(2)
    out_plane.forward()
    side_copy(0, p.dx).start()
    side_copy(1, p.dy).start()
    cot.step(1)
    att.step(3)
    cot.step(2)
    down.forward()
    out_plane.recv()
    side_copy(2, p.dd).start()
    cot.step(3)
    for i in range(4):
        gu_planes[i].recv()
    down.recv()
    for chain in (out, att, cot):
        for other in range(p.chips):
            chain.side_recv(other)
    for chain in (hid, out, att, cot):
        chain.finish()
    for i, e in enumerate((p.dx, p.dy, p.dd)):
        side_wait(i, e)
    remote(
        adapters_all.at[pl.ds(0, 3)], adapters_all.at[pl.ds(0, 3)],
        small_sems.at[2, 3], small_sems.at[3, 0], p.dp(p.dx),
    ).wait_recv()
    for step in range(1, seq_size):
        documents_copy(step).wait_send()
    for i, e in enumerate((p.dx, p.dy, p.dd)):
        adapters_copy(i, e).wait_send()
        side_copy(i, e).wait_send()
    for group in [qkv, *gu, qkv_plane, down, out_plane, *gu_planes]:
        group.finish()
    for i in (6, 7, 8):
        keep[i].wait()


def front_all(seq_size, ins):
    tokens, width = ins[0].shape
    rows = ins[4].shape[0]
    part = ins[9].shape[0]
    chips = seq_size // 2
    q_width = ins[4].shape[1] // seq_size
    qkv_width = q_width + ins[5].shape[2]
    length = tokens * seq_size
    low_width = ins[11].shape[1]

    def shape(*dims, dtype=BF16):
        return jax.ShapeDtypeStruct(dims, dtype)

    anywhere = pl.BlockSpec(memory_space=pl.ANY)
    vmem = pl.BlockSpec(memory_space=pltpu.VMEM)
    outs = (
        shape(seq_size, tokens, width),
        shape(seq_size, tokens, width),
        shape(4, 8, 128, dtype=jnp.int32),
        shape(4, seq_size * rows, qkv_width),
        shape(4, chips, 2, rows, width),
        shape(4, seq_size * rows, 8 * part),
        shape(4, part, width),
        shape(seq_size, length, q_width),
        shape(seq_size, tokens, width),
        shape(length, q_width),
        shape(length, 2 * HD),
        shape(length, 2 * HD),
        shape(HD, length),
        shape(4, length, dtype=F32),
        shape(8, length, dtype=F32),
        shape(length, tokens, dtype=F32),
        shape(low_width, length),
    )
    return pl.pallas_call(
        functools.partial(front_kernel, seq_size),
        out_shape=outs,
        in_specs=[anywhere] * 10 + [vmem] * 5,
        out_specs=(anywhere,) * 9 + (vmem,) * 8,
        scratch_shapes=[
            pltpu.VMEM((seq_size, 8, tokens), jnp.int32),
            pltpu.SemaphoreType.DMA((4, 4, seq_size)),
            pltpu.SemaphoreType.DMA((3 + PIECES, 2, 4)),
            pltpu.SemaphoreType.DMA((2, 16)),
            pltpu.SemaphoreType.DMA((1 + PIECES, 2)),
            pltpu.SemaphoreType.DMA((4, seq_size)),
            pltpu.SemaphoreType.DMA((2, 3)),
            pltpu.VMEM((seq_size, tokens, width), BF16),
            pltpu.VMEM((seq_size, tokens, width), BF16),
            pltpu.VMEM((tokens, width), BF16),
            pltpu.VMEM((rows, width), BF16),
            pltpu.VMEM((part, width), BF16),
            pltpu.VMEM((rows, qkv_width), BF16),
            pltpu.VMEM((rows, 8 * part), BF16),
            pltpu.VMEM((4, seq_size * rows, qkv_width), BF16),
            pltpu.VMEM((2, length, 2 * HD), BF16),
            pltpu.VMEM((HD, length), BF16),
            pltpu.VMEM((length, QB), F32),
            pltpu.VMEM((length, q_width), BF16),
        ],
        compiler_params=pltpu.CompilerParams(
            collective_id=0, has_side_effects=True, vmem_limit_bytes=60 * 2**20
        ),
        cost_estimate=pl.CostEstimate(
            flops=5 * 10**9, bytes_accessed=60 * 2**20, transcendentals=4 * 2**20
        ),
        name="attend_front",
    )(*ins)


def back_kernel(
    seq_size,
    grad_attn,
    query,
    keys2,
    values2,
    keys_t,
    log_totals,
    seg_row,
    seg_col,
    cos_t,
    sin_t,
    cos_n,
    sin_n,
    qkv_w,
    qkv_in,
    low_map,
    low_qkv_t,
    norm_one,
    ffn_part,
    early_t,
    gu_grad,
    down_grad,
    owners,
    norm_sum,
    ffn_sum,
    share_out,
    gu_out,
    down_out,
    q_out,
    kv_out,
    grads,
    key_z,
    value_z,
    key_acc,
    value_acc,
    bias,
    grad_qkv,
    grad_low,
    qkv_v,
    norm_v,
    ffn_v,
    ffn_side,
    ffn_up,
    ffn_down,
    sum_v,
    sum_side,
    sum_up,
    sum_down,
    share,
    share_in,
    turned,
    gu_in,
    down_in,
    q_got,
    kv_got,
    load_sems,
    swap_sems,
    ffn_sems,
    sum_sems,
    send_sems,
    got_sems,
):
    p = Place(seq_size)
    d, s = p.d, p.s
    length = query.shape[0]
    chips = p.chips
    loads = [
        pltpu.make_async_copy(src, dst, load_sems.at[i])
        for i, (src, dst) in enumerate(
            ((ffn_part, ffn_v), (qkv_w, qkv_v), (norm_one, norm_v), (grad_attn.at[s], grads.at[s]))
        )
    ]
    for copy in loads:
        copy.start()
    barrier = pltpu.get_barrier_semaphore()
    everyone = 4 * seq_size

    def place_of(t):
        return lax.rem(d + t // seq_size, 4), lax.rem(s + lax.rem(t, seq_size), seq_size)

    @pl.loop(1, everyone)
    def _(t):
        pl.semaphore_signal(barrier, 1, device_id=place_of(t), device_id_type=MESH)

    pl.semaphore_wait(barrier, everyone - 1)

    def swap_copy(step):
        return remote(
            grad_attn.at[p.peer(step)], grads.at[s], swap_sems.at[0, step], swap_sems.at[1, 0],
            p.seq(p.peer(step)),
        )

    for step in range(1, seq_size):
        swap_copy(step).start()

    def deliver(src, dst, td, ts, i, wait):
        here = (td == d) & (ts == s)

        @pl.when(jnp.logical_not(here))
        def _():
            copy = remote(src, dst, send_sems.at[i], got_sems.at[i], (td, ts))
            if wait:
                copy.wait_send()
            else:
                copy.start()

        if not wait:

            @pl.when(here)
            def _():
                pltpu.make_async_copy(src, dst, got_sems.at[i]).start()

    def ready(buffer, i):
        remote(buffer, buffer, send_sems.at[i], got_sems.at[i], p.seq(p.sib)).wait_recv()

    block = gu_grad.shape[1] // 8

    def deliver_wide(wait):
        side = pl.ds(pl.multiple_of(block * lax.rem(s, 2), block), block)
        for e in range(4):
            for upper in range(2):
                deliver(
                    gu_grad.at[:, pl.ds((4 * upper + e) * block, block)],
                    gu_in.at[d, :, side],
                    2 * upper + e // 2,
                    lax.rem(e, 2) * (seq_size // 2) + s // 2,
                    0,
                    wait,
                )
            deliver(down_grad.at[:, pl.ds(e * block, block)], down_in.at[d], e, s, 1, wait)

    def deliver_heads(wait):
        for i in range(4):
            m = 4 * s + i
            deliver(
                turned.at[pl.ds(HD * i, HD)], q_got.at[d], m // seq_size, lax.rem(m, seq_size), 2, wait
            )
        for i in range(4):
            m = 2 * seq_size * (i // 2) + 2 * s + i % 2
            deliver(
                turned.at[pl.ds(4 * HD + HD // 2 * i, HD // 2)],
                kv_got.at[d],
                m // seq_size,
                lax.rem(m, seq_size),
                3,
                wait,
            )

    def deliver_share(wait):
        rows = share.shape[0] // everyone

        @pl.loop(0, everyone)
        def _(t):
            td, ts = place_of(t)
            start = pl.multiple_of((td * seq_size + ts) * rows, rows)
            deliver(share.at[pl.ds(start, rows)], share_in.at[d, s], td, ts, 4, wait)

    ffn = ChainSum(p, ffn_v, ffn_side, ffn_up, ffn_down, ffn_sems)
    total = ChainSum(p, sum_v, sum_side, sum_up, sum_down, sum_sems)

    low_lane = lax.broadcasted_iota(jnp.int32, (length, 2 * HD), 1) < HD
    zero = jnp.zeros((length, 2 * HD), BF16)
    key_z[0] = jnp.where(low_lane, keys2[...], zero)
    key_z[1] = jnp.where(low_lane, zero, keys2[...])
    value_z[0] = jnp.where(low_lane, values2[...], zero)
    value_z[1] = jnp.where(low_lane, zero, values2[...])
    key_acc[...] = jnp.zeros_like(key_acc)
    value_acc[...] = jnp.zeros_like(value_acc)
    for copy in loads:
        copy.wait()
    for z in range(chips):
        ffn.side_start(z)
    remote(
        grads.at[pl.ds(0, seq_size - 1)], grads.at[pl.ds(0, seq_size - 1)],
        swap_sems.at[0, 0], swap_sems.at[1, 0], p.seq(p.sib),
    ).wait_recv()
    deliver_wide(False)
    ffn.step(3)

    def query_block(i):
        start = i * QB
        span = pl.ds(0, start + QB)
        rows = pl.ds(start, QB)
        bias[span, :] = mask_bias(seg_col, seg_row, start, QB)
        slots = QB // grads.shape[1]

        for m in range(2):
            pair = pl.ds(2 * HD * m, 2 * HD)
            query_pair = query[rows, pair]
            grad_pair = grads[pl.ds(slots * i, slots), :, pair].reshape(QB, 2 * HD)
            turned_q = []
            for e in range(2):
                h = 2 * m + e
                scores = dot_nt(key_z[e, span, :], query_pair)
                weights = jnp.exp(scores * SCORE_SCALE + bias[span, :] - log_totals[h : h + 1, rows])
                grad_weights = dot_nt(value_z[e, span, :], grad_pair)
                row_dot = jnp.sum(weights * grad_weights, axis=0, keepdims=True)
                grad_scores = (weights * (grad_weights - row_dot)).astype(BF16)
                key_acc[e, span, :] += dot_nn(grad_scores, query_pair)
                value_acc[e, span, :] += dot_nn(weights.astype(BF16), grad_pair)
                grad_q = dot_nn(keys_t[:, span], grad_scores) * SCORE_SCALE
                first, second = grad_q[: HD // 2], grad_q[HD // 2 :]
                cos_part, sin_part = cos_t[:, rows], sin_t[:, rows]
                turned_q.append(first * cos_part + second * sin_part)
                turned_q.append(second * cos_part - first * sin_part)
            grad_qkv[rows, pair] = jnp.concatenate(turned_q, axis=0).T.astype(BF16)

    query_block(0)
    query_block(1)
    query_block(2)
    ffn.step(2)
    query_block(3)

    def folded(acc):
        merged = jnp.where(low_lane, acc[0], acc[1])
        return merged + pltpu.roll(merged, HD, 1)

    grad_key = folded(key_acc) * SCORE_SCALE
    grad_key = grad_key * cos_n[...] - swap_halves(grad_key) * sin_n[...]
    grad_qkv[:, pl.ds(4 * HD, 2 * HD)] = jnp.where(low_lane, grad_key, folded(value_acc)).astype(BF16)
    grad_low[...] = dot_nt(grad_qkv[...], low_map[...]).astype(BF16)
    grad_low_t = dot_nt(low_map[...], grad_qkv[...]).astype(BF16)
    ffn.step(1)

    tokens = sum_v.shape[1]

    def fill(slot):
        rows = pl.ds(pl.multiple_of(slot * tokens, tokens), tokens)
        left, low = grad_qkv[rows, :], grad_low[rows, :]
        for j in range(4):
            cut = pl.ds(512 * j, 512)
            sum_v[slot, :, cut] = (
                dot_nt(left, qkv_v[cut, :]) + dot_nt(low, qkv_in[cut, :])
            ).astype(BF16)

    for k in (3, 2, 1, 0):

        def give(to):
            fill(2 * to)
            fill(2 * to + 1)
            total.side_start(to)

        @pl.when(p.z + k < chips)
        def _():
            give(p.z + k)

        if k:

            @pl.when(p.z >= k)
            def _():
                give(p.z - k)

            total.step(k)
        if k == 2:
            outer = dot_nn(low_qkv_t[...], grad_qkv[...])
            outer = jnp.concatenate([outer, jnp.zeros((80, outer.shape[1]), F32)], axis=0)
            turned[...] = outer.T
            deliver_heads(False)
            for j in range(8):
                cut = pl.ds(256 * j, 256)
                piece = jnp.concatenate(
                    [dot_nn(grad_low_t, norm_v[:, cut]), early_t[:, cut]], axis=0
                )
                share[cut, :] = piece.T.astype(BF16)
            deliver_share(False)
    ffn.last()
    ffn_sum[...] = ffn_v[s].astype(F32)
    for buffer, i in ((gu_in, 0), (down_in, 1), (q_got, 2), (kv_got, 3), (share_in, 4)):
        ready(buffer, i)

    def by_adapter(out, value):
        values = [value(e) for e in range(4)]
        for a in range(4):
            chosen = jnp.zeros_like(values[0])
            for e in range(4):
                chosen = jnp.where(owners[e, 0:1, 0:1] == a, values[e], chosen)
            out[a] = chosen

    by_adapter(gu_out, lambda e: gu_in[e])
    by_adapter(down_out, lambda e: down_in[e])
    by_adapter(q_out, lambda e: q_got[e])
    by_adapter(kv_out, lambda e: kv_got[e])
    by_adapter(share_out, lambda e: jnp.sum(share_in[e].astype(F32), axis=0))
    total.last()
    norm_sum[...] = sum_v[s].astype(F32)
    for step in range(1, seq_size):
        swap_copy(step).wait_send()
    deliver_wide(True)
    deliver_heads(True)
    deliver_share(True)
    ffn.finish()
    total.finish()


def back_all(seq_size, ins):
    (grad_attn, query, keys2) = ins[:3]
    _, tokens, width_q = grad_attn.shape
    length = query.shape[0]
    width = ins[16].shape[1]
    qkv_width = ins[12].shape[1]
    chips = seq_size // 2
    rows = width // (4 * seq_size)
    rank = ins[19].shape[0]
    block = ins[19].shape[1] // 8

    def shape(*dims):
        return jax.ShapeDtypeStruct(dims, F32)

    vmem = pl.BlockSpec(memory_space=pltpu.VMEM)
    anywhere = pl.BlockSpec(memory_space=pl.ANY)
    far = (0, 12, 16, 17)
    outs = (
        shape(tokens, width),
        shape(tokens, width),
        shape(4, rows, 128),
        shape(4, rank, 2 * block),
        shape(4, rank, block),
        shape(4, HD, 128),
        shape(4, HD // 2, 128),
    )
    many = (seq_size, tokens, width)
    few = (chips, tokens, width)
    return pl.pallas_call(
        functools.partial(back_kernel, seq_size),
        out_shape=outs,
        in_specs=[anywhere if i in far else vmem for i in range(len(ins))],
        out_specs=(vmem,) * len(outs),
        scratch_shapes=[
            pltpu.VMEM(grad_attn.shape, BF16),
            pltpu.VMEM((2, length, 2 * HD), BF16),
            pltpu.VMEM((2, length, 2 * HD), BF16),
            pltpu.VMEM((2, length, 2 * HD), F32),
            pltpu.VMEM((2, length, 2 * HD), F32),
            pltpu.VMEM((length, QB), F32),
            pltpu.VMEM((length, qkv_width), BF16),
            pltpu.VMEM((length, 3 * rank), BF16),
            pltpu.VMEM(ins[12].shape, BF16),
            pltpu.VMEM((length, width), BF16),
            pltpu.VMEM(many, BF16),
            pltpu.VMEM(few, BF16),
            pltpu.VMEM(few, BF16),
            pltpu.VMEM(few, BF16),
            pltpu.VMEM(many, BF16),
            pltpu.VMEM(few, BF16),
            pltpu.VMEM(few, BF16),
            pltpu.VMEM(few, BF16),
            pltpu.VMEM((width, 128), BF16),
            pltpu.VMEM((4, seq_size, rows, 128), BF16),
            pltpu.VMEM((qkv_width, 128), F32),
            pltpu.VMEM((4, rank, 2 * block), F32),
            pltpu.VMEM((4, rank, block), F32),
            pltpu.VMEM((4, HD, 128), F32),
            pltpu.VMEM((4, HD // 2, 128), F32),
            pltpu.SemaphoreType.DMA((4,)),
            pltpu.SemaphoreType.DMA((2, seq_size)),
            pltpu.SemaphoreType.DMA((6, chips)),
            pltpu.SemaphoreType.DMA((6, chips)),
            pltpu.SemaphoreType.DMA((5,)),
            pltpu.SemaphoreType.DMA((5,)),
        ],
        compiler_params=pltpu.CompilerParams(
            collective_id=1, has_side_effects=True, vmem_limit_bytes=60 * 2**20
        ),
        cost_estimate=pl.CostEstimate(
            flops=10 * 10**9, bytes_accessed=20 * 2**20, transcendentals=4 * 2**20
        ),
        name="attend_back",
    )(*ins)


def make_local(dp_size, seq_size):
    devices = dp_size * seq_size
    heads = NH // seq_size
    kv_repeat = max(1, seq_size // KVH)
    kernels = dp_size == 4 and seq_size == 8

    def local(
        hidden,
        token_document_numbers,
        sequence_adapter_index,
        cotangent,
        attention_norm_gain,
        feedforward_norm_gain,
        query_weight,
        key_weight,
        value_weight,
        attention_output_weight,
        gate_weight,
        up_weight,
        down_weight,
        adapter_query_key_value_input,
        adapter_query_output,
        adapter_key_value_output,
        adapter_projection_input,
        adapter_projection_output,
        adapter_gate_up_input,
        adapter_gate_up_output,
        adapter_down_input,
        adapter_down_output,
    ):
        tokens, width = hidden.shape[1:]
        length = tokens * seq_size
        rows = query_weight.shape[0]
        key_width = key_weight.shape[1]
        ff_width = gate_weight.shape[1]
        ff_block = ff_width // devices
        rank = adapter_projection_input.shape[2]
        adapters = adapter_projection_input.shape[0]
        me = lax.axis_index("seq")
        q_width = heads * HD

        def across(piece):
            return lax.all_to_all(piece, "seq", split_axis=0, concat_axis=0, tiled=True)

        def gather_dp(block):
            return lax.all_gather(block, "dp", axis=0, tiled=True)

        def gather_seq(block):
            return lax.all_gather(block, "seq", axis=0, tiled=True)

        def scatter_seq(total):
            return lax.psum_scatter(total, "seq", scatter_dimension=0, tiled=True)

        def by_owner(columns):
            return columns.reshape(columns.shape[0], dp_size, seq_size, ff_block)

        hidden_own = hidden[0].astype(F32)
        ff_own = dp_size * ff_block

        adapter = sequence_adapter_index[0]
        qkv_in = adapter_query_key_value_input[adapter]
        q_out = lax.dynamic_slice_in_dim(adapter_query_output[adapter], me * q_width, q_width, 1)
        kv_out = adapter_key_value_output[adapter]
        kv_start = (me // kv_repeat) * HD
        k_out = lax.dynamic_slice_in_dim(kv_out, kv_start, HD, 1)
        v_out = lax.dynamic_slice_in_dim(kv_out, key_width + kv_start, HD, 1)
        o_in = adapter_projection_input[adapter]
        o_out = adapter_projection_output[adapter]
        gu_in = adapter_gate_up_input[adapter]
        gu_all = adapter_gate_up_output[adapter].reshape(rank, 2, dp_size, seq_size, ff_block)
        gu_out = lax.dynamic_index_in_dim(gu_all, me, 3, keepdims=False)
        g_out, u_out = gu_out[:, 0].reshape(rank, ff_own), gu_out[:, 1].reshape(rank, ff_own)
        down_all = adapter_down_input[adapter].reshape(dp_size, seq_size, ff_block, rank)
        down_in = lax.dynamic_index_in_dim(down_all, me, 1, keepdims=False).reshape(ff_own, rank)
        down_out = adapter_down_output[adapter]

        if kernels:
            kv = jnp.concatenate(
                [key_weight.reshape(rows, KVH, HD), value_weight.reshape(rows, KVH, HD)], axis=2
            )
            none_q = jnp.zeros((rank, q_width), BF16)
            none_h = jnp.zeros((rank, HD), BF16)
            low_map = jnp.concatenate(
                [
                    jnp.concatenate([q_out, none_h, none_h], axis=1),
                    jnp.concatenate([none_q, k_out, none_h], axis=1),
                    jnp.concatenate([none_q, none_h, v_out], axis=1),
                ],
                axis=0,
            )
            cos_fixed, sin_fixed = fixed_tables(length)
            (
                hidden_all,
                cotangent_all,
                owners,
                qkv,
                out_full,
                gate_up,
                down,
                attn,
                norm_one,
                query,
                keys2,
                values2,
                keys_t,
                log_totals,
                seg_row,
                seg_col,
                low_t,
            ) = front_all(
                seq_size,
                (
                    hidden[0],
                    cotangent[0],
                    jnp.broadcast_to(token_document_numbers, (8, tokens)),
                    jnp.broadcast_to(sequence_adapter_index[:, None], (8, 128)),
                    query_weight,
                    jnp.swapaxes(kv, 0, 1),
                    attention_output_weight,
                    gate_weight,
                    up_weight,
                    down_weight,
                    attention_norm_gain[None],
                    qkv_in,
                    low_map,
                    jnp.asarray(np.tile(cos_fixed, (1, 4))),
                    jnp.asarray(np.tile(np.concatenate([-sin_fixed, sin_fixed], axis=1), (1, 2))),
                ),
            )
            hidden_all = hidden_all.reshape(length, width)
            cotangent_all = cotangent_all.reshape(length, width)
            norm_one = norm_one.reshape(length, width)
            qkv = qkv.reshape(width, -1)
            out_full = out_full.reshape(width, width)
            gate_up = gate_up.reshape(width, -1)
            down = down.reshape(dp_size * ff_block, width)
            attn = jnp.swapaxes(attn, 0, 1).reshape(length, width)
        else:
            hidden_all = gather_seq(hidden[0])
            segments = gather_seq(token_document_numbers[0])
            kv = jnp.stack([key_weight.reshape(rows, KVH, HD), value_weight.reshape(rows, KVH, HD)], 2)
            kv = jnp.repeat(kv.reshape(rows, KVH, 2 * HD), kv_repeat, axis=1)
            qkv = jnp.concatenate([query_weight.reshape(rows, seq_size, q_width), kv], axis=2)
            qkv = across(jnp.swapaxes(qkv, 0, 1)).reshape(seq_size * rows, q_width + 2 * HD)
            qkv = gather_dp(qkv)
            gate_up = jnp.concatenate([by_owner(gate_weight), by_owner(up_weight)], axis=1)
            gate_up = across(jnp.transpose(gate_up, (2, 0, 1, 3)))
            gate_up = gather_dp(gate_up.reshape(seq_size * rows, 2 * dp_size * ff_block))
            down = gather_dp(down_weight)
            out_full = lax.all_gather(attention_output_weight, ("dp", "seq"), axis=0, tiled=True)
            cotangent_all = gather_seq(cotangent[0])
            owners = lax.all_gather(sequence_adapter_index, "dp", axis=0, tiled=True)
        if not kernels:
            norm_one = rms_scale(hidden_all.astype(F32), attention_norm_gain).astype(BF16)
            low_qkv = mm(norm_one, qkv_in).astype(BF16)
            pre = mm(norm_one, qkv)
            query_pre = pre[:, :q_width] + mm(low_qkv[:, :rank], q_out)
            key_pre = pre[:, q_width : q_width + HD] + mm(low_qkv[:, rank : 2 * rank], k_out)
            value_pre = pre[:, q_width + HD :] + mm(low_qkv[:, 2 * rank :], v_out)
            cos_table, sin_table = angle_tables(jnp.arange(length, dtype=jnp.int32).astype(F32), HD)
            query = rotate(query_pre.reshape(length, heads, HD), cos_table, sin_table).astype(BF16)
            keys = rotate(key_pre.reshape(length, 1, HD), cos_table, sin_table).astype(BF16)[:, 0]
            values = value_pre.astype(BF16)
            attn_heads, log_totals = attend_forward(query, keys, values, segments)
            attn = lax.all_gather(attn_heads, "seq", axis=1, tiled=True)
        low_out = mm(attn, o_in).astype(BF16)
        branch = mm(attn, out_full) + mm(low_out, o_out)
        middle = hidden_all.astype(F32) + RESIDUAL_SCALE * branch
        own_row = me * tokens
        middle_own = lax.dynamic_slice_in_dim(middle, own_row, tokens, 0)
        norm_two = rms_scale(middle, feedforward_norm_gain).astype(BF16)
        low_gu = mm(norm_two, gu_in).astype(BF16)
        wide = mm(norm_two, gate_up)
        gate = wide[:, :ff_own] + mm(low_gu[:, :rank], g_out)
        up_proj = wide[:, ff_own:] + mm(low_gu[:, rank:], u_out)
        sigma = jax.nn.sigmoid(gate)
        activation = (gate * sigma * up_proj).astype(BF16)
        low_down = mm(activation, down_in).astype(BF16)
        ffn_part = (mm(activation, down) + mm(low_down, down_out)).astype(BF16)

        grad_ffn = (RESIDUAL_SCALE * cotangent_all.astype(F32)).astype(BF16)
        grad_low_down = mm_t(grad_ffn, down_out).astype(BF16)
        grad_act = mm_t(grad_ffn, down) + mm_t(grad_low_down, down_in)
        grad_gate = (grad_act * up_proj * sigma * (1.0 + gate * (1.0 - sigma))).astype(BF16)
        grad_up = (grad_act * gate * sigma).astype(BF16)
        grad_low_gu = jnp.concatenate([mm_t(grad_gate, g_out), mm_t(grad_up, u_out)], axis=1)
        grad_low_gu = grad_low_gu.astype(BF16)
        grad_norm_two = scatter_seq(
            (
                mm_t(jnp.concatenate([grad_gate, grad_up], axis=1), gate_up)
                + mm_t(grad_low_gu, gu_in)
            ).astype(BF16)
        )
        grad_middle = cotangent[0].astype(F32) + rms_back(
            middle_own, feedforward_norm_gain, grad_norm_two.astype(F32)
        )
        grad_branch = (RESIDUAL_SCALE * grad_middle).astype(BF16)
        grad_low_out = mm_t(grad_branch, o_out).astype(BF16)
        grad_attn = (mm_t(grad_branch, out_full) + mm_t(grad_low_out, o_in)).astype(BF16)
        attn_own = lax.dynamic_slice_in_dim(attn, own_row, tokens, 0)
        low_out_own = lax.dynamic_slice_in_dim(low_out, own_row, tokens, 0)
        if kernels:
            early = jnp.concatenate(
                [
                    t_mm(grad_low_out, attn_own),
                    t_mm(low_out_own, grad_branch),
                    t_mm(grad_low_gu, norm_two),
                    t_mm(low_down, grad_ffn),
                ],
                axis=0,
            )
            gu_grad = jnp.concatenate(
                [t_mm(low_gu[:, :rank], grad_gate), t_mm(low_gu[:, rank:], grad_up)], axis=1
            )
            sums = back_all(
                seq_size,
                (
                    jnp.swapaxes(grad_attn.reshape(tokens, seq_size, q_width), 0, 1),
                    query,
                    keys2,
                    values2,
                    keys_t,
                    log_totals,
                    seg_row,
                    seg_col,
                    jnp.asarray(np.ascontiguousarray(cos_fixed.T)),
                    jnp.asarray(np.ascontiguousarray(sin_fixed.T)),
                    jnp.asarray(np.tile(cos_fixed, (1, 4))),
                    jnp.asarray(np.tile(np.concatenate([-sin_fixed, sin_fixed], axis=1), (1, 2))),
                    qkv,
                    qkv_in,
                    low_map,
                    low_t,
                    norm_one,
                    ffn_part.reshape(seq_size, tokens, width),
                    early,
                    gu_grad,
                    t_mm(grad_low_down, activation),
                    owners,
                ),
            )
            norm_sum, ffn_sum, share, gu_got, down_got, q_got, kv_got = sums
            mixed = (middle_own + RESIDUAL_SCALE * ffn_sum).astype(BF16)
            grad_hidden = grad_middle + rms_back(hidden_own, attention_norm_gain, norm_sum)
            lower = lax.axis_index("dp") < dp_size // 2
            kv_got = jnp.where(lower, kv_got[:, :, rank : 2 * rank], kv_got[:, :, 2 * rank : 3 * rank])
            share_t = jnp.swapaxes(share, 1, 2)
            return (
                mixed[None],
                grad_hidden.astype(BF16)[None],
                share[:, :, : 3 * rank],
                jnp.swapaxes(q_got[:, :, :rank], 1, 2),
                jnp.swapaxes(kv_got, 1, 2),
                share[:, :, 3 * rank : 4 * rank],
                share_t[:, 4 * rank : 5 * rank],
                share[:, :, 5 * rank : 7 * rank],
                gu_got,
                jnp.swapaxes(down_got, 1, 2),
                share_t[:, 7 * rank :],
            )
        ffn = lax.psum_scatter(ffn_part, "seq", scatter_dimension=0, tiled=True)
        mixed = (middle_own + RESIDUAL_SCALE * ffn.astype(F32)).astype(BF16)
        grad_heads = lax.all_to_all(
            jnp.swapaxes(grad_attn.reshape(tokens, seq_size, q_width), 0, 1),
            "seq",
            split_axis=0,
            concat_axis=0,
            tiled=True,
        ).reshape(length, heads, HD)
        grad_q, grad_k, grad_v = attend_backward(
            query, keys, values, segments, log_totals, grad_heads
        )
        grad_query = rotate(grad_q.astype(F32), cos_table, -sin_table)
        grad_query = grad_query.reshape(length, q_width).astype(BF16)
        grad_key = rotate(grad_k[:, None], cos_table, -sin_table)[:, 0].astype(BF16)
        grad_value = grad_v.astype(BF16)
        grad_low_qkv = jnp.concatenate(
            [mm_t(grad_query, q_out), mm_t(grad_key, k_out), mm_t(grad_value, v_out)], axis=1
        ).astype(BF16)
        grad_qkv = jnp.concatenate([grad_query, grad_key, grad_value], axis=1)
        grad_norm_one = scatter_seq((mm_t(grad_qkv, qkv) + mm_t(grad_low_qkv, qkv_in)).astype(BF16))
        grad_hidden = grad_middle + rms_back(
            hidden_own, attention_norm_gain, grad_norm_one.astype(F32)
        )

        partial = jnp.concatenate(
            [
                t_mm(norm_one, grad_low_qkv),
                t_mm(attn_own, grad_low_out),
                t_mm(grad_branch, low_out_own),
                t_mm(norm_two, grad_low_gu),
                t_mm(grad_ffn, low_down),
            ],
            axis=1,
        ).reshape(dp_size, seq_size, rows, 8 * rank)
        own_q = t_mm(grad_query, low_qkv[:, :rank])
        own_k = t_mm(grad_key, low_qkv[:, rank : 2 * rank])
        own_v = t_mm(grad_value, low_qkv[:, 2 * rank :])
        own_g = t_mm(grad_gate, low_gu[:, :rank]).reshape(dp_size, ff_block, rank)
        own_u = t_mm(grad_up, low_gu[:, rank:]).reshape(dp_size, ff_block, rank)
        own_d = t_mm(activation, grad_low_down).reshape(dp_size, ff_block, rank)

        def placed(block, total, start, axis):
            empty = list(block.shape)
            empty[axis] = total
            return lax.dynamic_update_slice_in_dim(jnp.zeros(empty, F32), block, start, axis)

        def by_target(whole):
            return whole.reshape(dp_size, seq_size, -1)

        full_q = placed(own_q, width, me * q_width, 0)
        full_kv = jnp.concatenate(
            [placed(own_k, key_width, kv_start, 0), placed(own_v, key_width, kv_start, 0)], axis=0
        )
        spot = [placed(v[:, None], seq_size, me, 1) for v in (own_g, own_u, own_d)]
        full_gu = jnp.concatenate([spot[0].reshape(ff_width, rank), spot[1].reshape(ff_width, rank)])
        pieces = [by_target(v) for v in (partial, full_q, full_kv, full_gu, spot[2])]
        send = jnp.concatenate(pieces, axis=2)
        send = jnp.swapaxes(send, 0, 1).reshape(seq_size, -1)
        mine = lax.psum_scatter(send, "seq", scatter_dimension=0, tiled=True)
        mine = lax.all_to_all(
            mine.reshape(dp_size, -1), "dp", split_axis=0, concat_axis=0, tiled=True
        )
        numbers = jnp.arange(adapters, dtype=jnp.int32)
        chooser = (owners[:, None] == numbers[None, :]).astype(F32)
        mine = jnp.einsum("sa,si->ai", chooser, mine, precision=lax.Precision.HIGHEST)
        sizes = [v.shape[2] for v in pieces]
        cuts = [sum(sizes[:i]) for i in range(1, len(sizes))]
        got, got_q, got_kv, got_gu, got_d = jnp.split(mine, cuts, axis=1)
        got = got.reshape(adapters, rows, 8 * rank)

        def turned(flat):
            return jnp.swapaxes(flat.reshape(adapters, -1, rank), 1, 2)

        return (
            mixed[None],
            grad_hidden.astype(BF16)[None],
            got[:, :, : 3 * rank],
            turned(got_q),
            turned(got_kv),
            got[:, :, 3 * rank : 4 * rank],
            jnp.swapaxes(got[:, :, 4 * rank : 5 * rank], 1, 2),
            got[:, :, 5 * rank : 7 * rank],
            turned(got_gu),
            got_d.reshape(adapters, ff_block, rank),
            jnp.swapaxes(got[:, :, 7 * rank :], 1, 2),
        )

    return local


def solution(mesh):
    both = ("dp", "seq")
    tokens = P("dp", "seq", None)
    weight = P(both, None)
    in_specs = (
        (tokens, P("dp", "seq"), P("dp"), tokens, P(), P()) + (weight,) * 7 + (P(),) * 9
    )
    by_row, by_column = P(None, both, None), P(None, None, both)
    out_specs = (
        tokens,
        tokens,
        by_row,
        by_column,
        by_column,
        by_row,
        by_column,
        by_row,
        by_column,
        by_row,
        by_column,
    )
    local = make_local(mesh.shape["dp"], mesh.shape["seq"])
    return jax.shard_map(local, mesh=mesh, in_specs=in_specs, out_specs=out_specs, check_vma=False)
```

```python
import functools
import math

import jax
import jax.numpy as jnp
import numpy as np
from jax import lax
from jax.experimental import pallas as pl
from jax.experimental.pallas import tpu as pltpu
from jax.sharding import PartitionSpec as P

NH = 32
KVH = 8
HD = 64

EPSILON = 1e-05
RESIDUAL_SCALE = 0.22
SCORE_SCALE = 1.0 / 64.0
ROPE_BASE = 10000000.0
BF16 = jnp.bfloat16
F32 = jnp.float32


def mm(a, b):
    return jnp.dot(a, b, preferred_element_type=F32)


def mm_t(a, b):
    return lax.dot_general(a, b, (((1,), (1,)), ((), ())), preferred_element_type=F32)


def t_mm(a, b):
    return lax.dot_general(a, b, (((0,), (0,)), ((), ())), preferred_element_type=F32)


def rms_scale(values, gain):
    mean_square = jnp.mean(values * values, axis=-1, keepdims=True)
    return values * lax.rsqrt(mean_square + EPSILON) * gain


def rms_back(values, gain, grad):
    r = lax.rsqrt(jnp.mean(values * values, axis=-1, keepdims=True) + EPSILON)
    z = grad * gain
    return r * z - r * r * r * values * jnp.mean(z * values, axis=-1, keepdims=True)


def angle_tables(positions, head_size):
    steps = jnp.arange(head_size // 2).astype(F32)
    frequency = jnp.exp(steps * (-2.0 * math.log(ROPE_BASE) / head_size))
    angles = positions[:, None] * frequency[None, :]
    return (jnp.cos(angles), jnp.sin(angles))


def fixed_tables(length):
    steps = np.arange(HD // 2, dtype=np.float32)
    frequency = np.exp(steps * np.float32(-2.0 * math.log(ROPE_BASE) / HD))
    angles = np.arange(length, dtype=np.float32)[:, None] * frequency[None, :]
    return (np.cos(angles), np.sin(angles))


def rotate(values, cos_table, sin_table):
    half_width = values.shape[-1] // 2
    first_half = values[..., :half_width]
    second_half = values[..., half_width:]
    cos_part = cos_table[:, None, :]
    sin_part = sin_table[:, None, :]
    return jnp.concatenate(
        [
            first_half * cos_part - second_half * sin_part,
            second_half * cos_part + first_half * sin_part,
        ],
        axis=-1,
    )


def masked_scores(query_block, keys, seg_block, segments, start_row):
    key_pos = jnp.arange(keys.shape[0], dtype=jnp.int32)
    query_pos = start_row + jnp.arange(query_block.shape[0], dtype=jnp.int32)
    scores = jnp.einsum("qhd,kd->hqk", query_block, keys, preferred_element_type=F32) * SCORE_SCALE
    allowed = (key_pos[None, :] <= query_pos[:, None]) & (seg_block[:, None] == segments[None, :])
    return jnp.where(allowed[None], scores, -1e30)


def attend_forward(query, keys, values, segments):
    length, heads, head_size = query.shape
    rows = min(512, length)

    def one_block(index):
        start = index * rows
        query_block = lax.dynamic_slice_in_dim(query, start, rows, 0)
        seg_block = lax.dynamic_slice_in_dim(segments, start, rows, 0)
        scores = masked_scores(query_block, keys, seg_block, segments, start)
        row_max = jnp.max(scores, axis=-1, keepdims=True)
        weights = jnp.exp(scores - row_max)
        totals = jnp.sum(weights, axis=-1, keepdims=True)
        low = (weights / totals).astype(BF16)
        output = jnp.einsum("hqk,kd->qhd", low, values, preferred_element_type=F32)
        return (output.astype(BF16), (row_max + jnp.log(totals))[..., 0])

    outputs, log_totals = lax.map(one_block, jnp.arange(length // rows, dtype=jnp.int32))
    return (outputs.reshape(length, heads * head_size), log_totals)


def attend_backward(query, keys, values, segments, log_totals, grad):
    length, heads, head_size = query.shape
    rows = min(512, length)

    def one_block(carry, index):
        grad_keys, grad_values = carry
        start = index * rows
        query_block = lax.dynamic_slice_in_dim(query, start, rows, 0)
        seg_block = lax.dynamic_slice_in_dim(segments, start, rows, 0)
        grad_block = lax.dynamic_slice_in_dim(grad, start, rows, 0)
        scores = masked_scores(query_block, keys, seg_block, segments, start)
        weights = jnp.exp(scores - log_totals[index][..., None])
        grad_weights = jnp.einsum("qhd,kd->hqk", grad_block, values, preferred_element_type=F32)
        row_dot = jnp.sum(weights * grad_weights, axis=-1, keepdims=True)
        grad_scores = (weights * (grad_weights - row_dot)).astype(BF16)
        grad_query = jnp.einsum("hqk,kd->qhd", grad_scores, keys, preferred_element_type=F32)
        grad_keys = grad_keys + jnp.einsum(
            "hqk,qhd->kd", grad_scores, query_block, preferred_element_type=F32
        )
        grad_values = grad_values + jnp.einsum(
            "hqk,qhd->kd", weights.astype(BF16), grad_block, preferred_element_type=F32
        )
        return ((grad_keys, grad_values), (grad_query * SCORE_SCALE).astype(BF16))

    zero = jnp.zeros(keys.shape, F32)
    (grad_keys, grad_values), grad_query = lax.scan(
        one_block, (zero, zero), jnp.arange(length // rows, dtype=jnp.int32)
    )
    return (grad_query.reshape(length, heads, head_size), grad_keys * SCORE_SCALE, grad_values)


def make_local(dp_size, seq_size):
    devices = dp_size * seq_size
    heads = NH // seq_size
    kv_repeat = max(1, seq_size // KVH)

    def local(
        hidden,
        token_document_numbers,
        sequence_adapter_index,
        cotangent,
        attention_norm_gain,
        feedforward_norm_gain,
        query_weight,
        key_weight,
        value_weight,
        attention_output_weight,
        gate_weight,
        up_weight,
        down_weight,
        adapter_query_key_value_input,
        adapter_query_output,
        adapter_key_value_output,
        adapter_projection_input,
        adapter_projection_output,
        adapter_gate_up_input,
        adapter_gate_up_output,
        adapter_down_input,
        adapter_down_output,
    ):
        tokens, width = hidden.shape[1:]
        length = tokens * seq_size
        rows = query_weight.shape[0]
        key_width = key_weight.shape[1]
        ff_width = gate_weight.shape[1]
        ff_block = ff_width // devices
        rank = adapter_projection_input.shape[2]
        adapters = adapter_projection_input.shape[0]
        me = lax.axis_index("seq")
        q_width = heads * HD

        def across(piece):
            return lax.all_to_all(piece, "seq", split_axis=0, concat_axis=0, tiled=True)

        def gather_dp(block):
            return lax.all_gather(block, "dp", axis=0, tiled=True)

        def gather_seq(block):
            return lax.all_gather(block, "seq", axis=0, tiled=True)

        def scatter_seq(total):
            return lax.psum_scatter(total, "seq", scatter_dimension=0, tiled=True)

        def by_owner(columns):
            return columns.reshape(columns.shape[0], dp_size, seq_size, ff_block)

        hidden_own = hidden[0].astype(F32)
        hidden_all = gather_seq(hidden[0])
        segments = gather_seq(token_document_numbers[0])
        kv = jnp.stack([key_weight.reshape(rows, KVH, HD), value_weight.reshape(rows, KVH, HD)], 2)
        kv = jnp.repeat(kv.reshape(rows, KVH, 2 * HD), kv_repeat, axis=1)
        qkv = jnp.concatenate([query_weight.reshape(rows, seq_size, q_width), kv], axis=2)
        qkv = across(jnp.swapaxes(qkv, 0, 1)).reshape(seq_size * rows, q_width + 2 * HD)
        qkv = gather_dp(qkv)
        gate_up = jnp.concatenate([by_owner(gate_weight), by_owner(up_weight)], axis=1)
        gate_up = across(jnp.transpose(gate_up, (2, 0, 1, 3)))
        gate_up = gather_dp(gate_up.reshape(seq_size * rows, 2 * dp_size * ff_block))
        down = gather_dp(down_weight)
        out_full = lax.all_gather(attention_output_weight, ("dp", "seq"), axis=0, tiled=True)
        ff_own = dp_size * ff_block

        adapter = sequence_adapter_index[0]
        qkv_in = adapter_query_key_value_input[adapter]
        q_out = lax.dynamic_slice_in_dim(adapter_query_output[adapter], me * q_width, q_width, 1)
        kv_out = adapter_key_value_output[adapter]
        kv_start = (me // kv_repeat) * HD
        k_out = lax.dynamic_slice_in_dim(kv_out, kv_start, HD, 1)
        v_out = lax.dynamic_slice_in_dim(kv_out, key_width + kv_start, HD, 1)
        o_in = adapter_projection_input[adapter]
        o_out = adapter_projection_output[adapter]
        gu_in = adapter_gate_up_input[adapter]
        gu_all = adapter_gate_up_output[adapter].reshape(rank, 2, dp_size, seq_size, ff_block)
        gu_out = lax.dynamic_index_in_dim(gu_all, me, 3, keepdims=False)
        g_out, u_out = gu_out[:, 0].reshape(rank, ff_own), gu_out[:, 1].reshape(rank, ff_own)
        down_all = adapter_down_input[adapter].reshape(dp_size, seq_size, ff_block, rank)
        down_in = lax.dynamic_index_in_dim(down_all, me, 1, keepdims=False).reshape(ff_own, rank)
        down_out = adapter_down_output[adapter]

        norm_one = rms_scale(hidden_all.astype(F32), attention_norm_gain).astype(BF16)
        low_qkv = mm(norm_one, qkv_in).astype(BF16)
        pre = mm(norm_one, qkv)
        query_pre = pre[:, :q_width] + mm(low_qkv[:, :rank], q_out)
        key_pre = pre[:, q_width : q_width + HD] + mm(low_qkv[:, rank : 2 * rank], k_out)
        value_pre = pre[:, q_width + HD :] + mm(low_qkv[:, 2 * rank :], v_out)
        cos_table, sin_table = angle_tables(jnp.arange(length, dtype=jnp.int32).astype(F32), HD)
        query = rotate(query_pre.reshape(length, heads, HD), cos_table, sin_table).astype(BF16)
        keys = rotate(key_pre.reshape(length, 1, HD), cos_table, sin_table).astype(BF16)[:, 0]
        values = value_pre.astype(BF16)
        attn_heads, log_totals = attend_forward(query, keys, values, segments)
        attn = lax.all_gather(attn_heads, "seq", axis=1, tiled=True)
        low_out = mm(attn, o_in).astype(BF16)
        branch = mm(attn, out_full) + mm(low_out, o_out)
        middle = hidden_all.astype(F32) + RESIDUAL_SCALE * branch
        own_row = me * tokens
        middle_own = lax.dynamic_slice_in_dim(middle, own_row, tokens, 0)
        norm_two = rms_scale(middle, feedforward_norm_gain).astype(BF16)
        low_gu = mm(norm_two, gu_in).astype(BF16)
        wide = mm(norm_two, gate_up)
        gate = wide[:, :ff_own] + mm(low_gu[:, :rank], g_out)
        up_proj = wide[:, ff_own:] + mm(low_gu[:, rank:], u_out)
        sigma = jax.nn.sigmoid(gate)
        activation = (gate * sigma * up_proj).astype(BF16)
        low_down = mm(activation, down_in).astype(BF16)
        ffn = scatter_seq((mm(activation, down) + mm(low_down, down_out)).astype(BF16))
        mixed = (middle_own + RESIDUAL_SCALE * ffn.astype(F32)).astype(BF16)

        grad_ffn = gather_seq((RESIDUAL_SCALE * cotangent[0].astype(F32)).astype(BF16))
        grad_low_down = mm_t(grad_ffn, down_out).astype(BF16)
        grad_act = mm_t(grad_ffn, down) + mm_t(grad_low_down, down_in)
        grad_gate = (grad_act * up_proj * sigma * (1.0 + gate * (1.0 - sigma))).astype(BF16)
        grad_up = (grad_act * gate * sigma).astype(BF16)
        grad_low_gu = jnp.concatenate([mm_t(grad_gate, g_out), mm_t(grad_up, u_out)], axis=1)
        grad_low_gu = grad_low_gu.astype(BF16)
        grad_norm_two = scatter_seq(
            (
                mm_t(jnp.concatenate([grad_gate, grad_up], axis=1), gate_up)
                + mm_t(grad_low_gu, gu_in)
            ).astype(BF16)
        )
        grad_middle = cotangent[0].astype(F32) + rms_back(
            middle_own, feedforward_norm_gain, grad_norm_two.astype(F32)
        )
        grad_branch = (RESIDUAL_SCALE * grad_middle).astype(BF16)
        grad_low_out = mm_t(grad_branch, o_out).astype(BF16)
        grad_attn = (mm_t(grad_branch, out_full) + mm_t(grad_low_out, o_in)).astype(BF16)
        grad_heads = lax.all_to_all(
            jnp.swapaxes(grad_attn.reshape(tokens, seq_size, q_width), 0, 1),
            "seq",
            split_axis=0,
            concat_axis=0,
            tiled=True,
        ).reshape(length, heads, HD)
        grad_q, grad_k, grad_v = attend_backward(
            query, keys, values, segments, log_totals, grad_heads
        )
        grad_query = rotate(grad_q.astype(F32), cos_table, -sin_table)
        grad_query = grad_query.reshape(length, q_width).astype(BF16)
        grad_key = rotate(grad_k[:, None], cos_table, -sin_table)[:, 0].astype(BF16)
        grad_value = grad_v.astype(BF16)
        grad_low_qkv = jnp.concatenate(
            [mm_t(grad_query, q_out), mm_t(grad_key, k_out), mm_t(grad_value, v_out)], axis=1
        ).astype(BF16)
        grad_qkv = jnp.concatenate([grad_query, grad_key, grad_value], axis=1)
        grad_norm_one = scatter_seq((mm_t(grad_qkv, qkv) + mm_t(grad_low_qkv, qkv_in)).astype(BF16))
        grad_hidden = grad_middle + rms_back(
            hidden_own, attention_norm_gain, grad_norm_one.astype(F32)
        )

        attn_own = lax.dynamic_slice_in_dim(attn, own_row, tokens, 0)
        low_out_own = lax.dynamic_slice_in_dim(low_out, own_row, tokens, 0)
        partial = jnp.concatenate(
            [
                t_mm(norm_one, grad_low_qkv),
                t_mm(attn_own, grad_low_out),
                t_mm(grad_branch, low_out_own),
                t_mm(norm_two, grad_low_gu),
                t_mm(grad_ffn, low_down),
            ],
            axis=1,
        ).reshape(dp_size, seq_size, rows, 8 * rank)
        own_q = t_mm(grad_query, low_qkv[:, :rank])
        own_k = t_mm(grad_key, low_qkv[:, rank : 2 * rank])
        own_v = t_mm(grad_value, low_qkv[:, 2 * rank :])
        own_g = t_mm(grad_gate, low_gu[:, :rank]).reshape(dp_size, ff_block, rank)
        own_u = t_mm(grad_up, low_gu[:, rank:]).reshape(dp_size, ff_block, rank)
        own_d = t_mm(activation, grad_low_down).reshape(dp_size, ff_block, rank)

        def placed(block, total, start, axis):
            empty = list(block.shape)
            empty[axis] = total
            return lax.dynamic_update_slice_in_dim(jnp.zeros(empty, F32), block, start, axis)

        def by_target(whole):
            return whole.reshape(dp_size, seq_size, -1)

        full_q = placed(own_q, width, me * q_width, 0)
        full_kv = jnp.concatenate(
            [placed(own_k, key_width, kv_start, 0), placed(own_v, key_width, kv_start, 0)], axis=0
        )
        spot = [placed(v[:, None], seq_size, me, 1) for v in (own_g, own_u, own_d)]
        full_gu = jnp.concatenate([spot[0].reshape(ff_width, rank), spot[1].reshape(ff_width, rank)])
        pieces = [by_target(v) for v in (partial, full_q, full_kv, full_gu, spot[2])]
        send = jnp.concatenate(pieces, axis=2)
        send = jnp.swapaxes(send, 0, 1).reshape(seq_size, -1)
        mine = lax.psum_scatter(send, "seq", scatter_dimension=0, tiled=True)
        mine = lax.all_to_all(
            mine.reshape(dp_size, -1), "dp", split_axis=0, concat_axis=0, tiled=True
        )
        owners = lax.all_gather(sequence_adapter_index, "dp", axis=0, tiled=True)
        numbers = jnp.arange(adapters, dtype=jnp.int32)
        chooser = (owners[:, None] == numbers[None, :]).astype(F32)
        mine = jnp.einsum("sa,si->ai", chooser, mine, precision=lax.Precision.HIGHEST)
        sizes = [v.shape[2] for v in pieces]
        cuts = [sum(sizes[:i]) for i in range(1, len(sizes))]
        got, got_q, got_kv, got_gu, got_d = jnp.split(mine, cuts, axis=1)
        got = got.reshape(adapters, rows, 8 * rank)

        def turned(flat):
            return jnp.swapaxes(flat.reshape(adapters, -1, rank), 1, 2)

        return (
            mixed[None],
            grad_hidden.astype(BF16)[None],
            got[:, :, : 3 * rank],
            turned(got_q),
            turned(got_kv),
            got[:, :, 3 * rank : 4 * rank],
            jnp.swapaxes(got[:, :, 4 * rank : 5 * rank], 1, 2),
            got[:, :, 5 * rank : 7 * rank],
            turned(got_gu),
            got_d.reshape(adapters, ff_block, rank),
            jnp.swapaxes(got[:, :, 7 * rank :], 1, 2),
        )

    return local


MESH = pl.DeviceIdType.MESH


def remote(src, dst, send_sem, recv_sem, device):
    return pltpu.make_async_remote_copy(
        src_ref=src,
        dst_ref=dst,
        send_sem=send_sem,
        recv_sem=recv_sem,
        device_id=device,
        device_id_type=MESH,
    )


class Place:
    def __init__(self, seq_size):
        self.d = lax.axis_index("dp")
        self.s = lax.axis_index("seq")
        self.seq_size = seq_size
        self.chips = seq_size // 2
        self.z = self.s // 2
        self.c = self.s % 2
        self.dx = self.d + 1 - 2 * (self.d % 2)
        self.dy = lax.rem(self.d + 2, 4)
        self.dd = lax.rem(self.dx + 2, 4)
        self.sib = self.s + 1 - 2 * self.c

    def seq(self, s):
        return (self.d, s)

    def dp(self, d):
        return (d, self.s)

    def peer(self, step):
        return lax.rem(self.s + step, self.seq_size)

    def greet(self, seq_steps, dp_peers):
        barrier = pltpu.get_barrier_semaphore()
        for step in seq_steps:
            pl.semaphore_signal(
                barrier, 1, device_id=self.seq(self.peer(step)), device_id_type=MESH
            )
        for d in dp_peers:
            pl.semaphore_signal(barrier, 1, device_id=self.dp(d), device_id_type=MESH)
        pl.semaphore_wait(barrier, len(seq_steps) + len(dp_peers))


class Chain:
    def __init__(self, place, own, slot, sems):
        self.p, self.own, self.slot = place, own, slot
        self.up, self.down, self.side, self.got = (sems.at[i] for i in range(4))

    def _up(self, src, i):
        return remote(src, self.slot(i), self.up.at[i], self.got.at[i], self.p.seq(self.p.s + 2))

    def _down(self, src, i):
        return remote(src, self.slot(i), self.down.at[i], self.got.at[i], self.p.seq(self.p.s - 2))

    def _side(self, src, i):
        return remote(src, self.slot(i), self.side.at[i], self.got.at[i], self.p.seq(self.p.sib))

    def start(self):
        p = self.p

        @pl.when(p.z < p.chips - 1)
        def _():
            self._up(self.own, p.s).start()

        @pl.when(p.z > 0)
        def _():
            self._down(self.own, p.s).start()

        self._side(self.own, p.s).start()

    def step(self, k):
        p = self.p
        low, high = p.s - 2 * k, p.s + 2 * k

        @pl.when(p.z >= k)
        def _():
            self._side(self.slot(low), low).wait_recv()

            @pl.when(p.z < p.chips - 1)
            def _():
                self._up(self.slot(low), low).start()

            self._side(self.slot(low), low).start()

        @pl.when(p.z + k < p.chips)
        def _():
            self._side(self.slot(high), high).wait_recv()

            @pl.when(p.z > 0)
            def _():
                self._down(self.slot(high), high).start()

            self._side(self.slot(high), high).start()

    def side_recv(self, z):
        other = 2 * z + 1 - self.p.c
        self._side(self.slot(other), other).wait_recv()

    def finish(self):
        p = self.p

        @pl.when(p.z < p.chips - 1)
        def _():
            self._up(self.own, p.s).wait_send()

        @pl.when(p.z > 0)
        def _():
            self._down(self.own, p.s).wait_send()

        self._side(self.own, p.s).wait_send()
        for k in range(1, p.chips):
            low, high = p.s - 2 * k, p.s + 2 * k

            @pl.when(p.z >= k)
            def _():
                @pl.when(p.z < p.chips - 1)
                def _():
                    self._up(self.slot(low), low).wait_send()

                self._side(self.slot(low), low).wait_send()

            @pl.when(p.z + k < p.chips)
            def _():
                @pl.when(p.z > 0)
                def _():
                    self._down(self.slot(high), high).wait_send()

                self._side(self.slot(high), high).wait_send()


class Plane:
    def __init__(self, place, block, half, sems):
        self.p, self.block, self.half, self.sems = place, block, half, sems

    def _copy(self, ref, i, d):
        return remote(ref, ref, self.sems.at[0, i], self.sems.at[1, i], self.p.dp(d))

    def _all(self):
        p = self.p
        return (
            (self.block(p.d), p.dx),
            (self.block(p.d), p.dy),
            (self.half(p.dx, 0), p.dy),
            (self.half(p.dy, 1), p.dx),
        )

    def start(self):
        for i, (ref, d) in enumerate(self._all()[:2]):
            self._copy(ref, i, d).start()

    def forward(self):
        p = self.p
        everything = self._all()
        for i, came in ((0, p.dx), (1, p.dy)):
            self._copy(self.block(came), i, came).wait_recv()
            ref, d = everything[2 + i]
            self._copy(ref, 2 + i, d).start()

    def recv(self):
        p = self.p
        self._copy(self.half(p.dd, 0), 2, p.dy).wait_recv()
        self._copy(self.half(p.dd, 1), 3, p.dx).wait_recv()

    def finish(self):
        for i, (ref, d) in enumerate(self._all()):
            self._copy(ref, i, d).wait_send()


class Spread:
    def __init__(self, place, pairs, whole, send_sem, recv_sem):
        self.p, self.pairs, self.whole = place, pairs, whole
        self.send_sem, self.recv_sem = send_sem, recv_sem

    def start(self):
        p = self.p
        for step in (1, 2, 3, 4, 5, 6, 7):
            j = p.peer(step)
            for src, dst in self.pairs(j):
                remote(src, dst, self.send_sem, self.recv_sem, p.seq(j)).start()

    def recv(self):
        p = self.p
        for whole in self.whole:
            remote(whole, whole, self.send_sem, self.recv_sem, p.seq(p.sib)).wait_recv()

    def finish(self):
        p = self.p
        for whole in self.whole:
            remote(whole, whole, self.send_sem, self.recv_sem, p.seq(p.sib)).wait_send()


PIECES = 4
QB = 256


def front_kernel(
    seq_size,
    hidden,
    documents,
    adapter_row,
    query_w,
    kv_w,
    out_w,
    gate_w,
    up_w,
    gain,
    qkv_in,
    low_map,
    cos_n,
    sin_n,
    hidden_all,
    adapters_all,
    qkv_all,
    out_all,
    gu_all,
    attn_all,
    norm_all,
    query,
    keys2,
    values2,
    keys_t,
    log_totals,
    seg_row,
    seg_col,
    low_t,
    documents_all,
    chain_sems,
    plane_sems,
    local_sems,
    spread_sems,
    small_sems,
    side_sems,
    hidden_v,
    norm_v,
    out_v,
    qkv_v,
    gu_v,
    weights_v,
    key_z,
    values_t,
    bias,
    attn_v,
):
    p = Place(seq_size)
    d, s, z, c = p.d, p.s, p.z, p.c
    rows = query_w.shape[0]
    part = gate_w.shape[1] // (4 * seq_size)
    tokens = hidden.shape[0]
    half_rows = seq_size * rows // 2
    landing = pl.ds(pl.multiple_of(rows * s, rows), rows)
    q_width = query_w.shape[1] // seq_size

    def column_block(number, size):
        return pl.ds(pl.multiple_of(number * size, size), size)

    stage = [
        (hidden, hidden_v.at[s]),
        (out_w, out_v),
        (query_w.at[:, column_block(s, q_width)], qkv_v.at[:, pl.ds(0, q_width)]),
        (kv_w.at[s], qkv_v.at[:, pl.ds(q_width, kv_w.shape[2])]),
        (documents, documents_all.at[s]),
        (adapter_row, adapters_all.at[d]),
    ]
    for i in range(8):
        matrix = (gate_w, up_w)[i // 4]
        block = matrix.at[:, column_block(seq_size * (i % 4) + s, part)]
        stage.append((block, gu_v.at[:, pl.ds(part * i, part)]))
    stage = [
        pltpu.make_async_copy(src, dst, local_sems.at[0, i]) for i, (src, dst) in enumerate(stage)
    ]
    keep = [
        pltpu.make_async_copy(src, dst, local_sems.at[1, i])
        for i, (src, dst) in enumerate(
            (
                (out_v, out_all.at[d, z, c]),
                (qkv_v, qkv_all.at[d, landing]),
                (gu_v, gu_all.at[d, landing]),
                (qkv_all, weights_v),
                (hidden_v, hidden_all),
                (norm_v, norm_all),
                (attn_v, attn_all.at[s]),
            )
        )
    ]
    for copy in stage:
        copy.start()
    p.greet(range(1, seq_size), (p.dx, p.dy, p.dd))

    hid = Chain(p, hidden, lambda i: hidden_v.at[i], chain_sems.at[0])
    out = Chain(p, out_w, lambda i: out_all.at[d, i // 2, i % 2], chain_sems.at[2])
    att = Chain(p, attn_v, lambda i: attn_all.at[i], chain_sems.at[3])

    def qkv_pairs(j):
        return (
            (query_w.at[:, column_block(j, q_width)], qkv_all.at[d, landing, pl.ds(0, q_width)]),
            (kv_w.at[j], qkv_all.at[d, landing, pl.ds(q_width, kv_w.shape[2])]),
        )

    def gu_pairs(piece):
        matrix = (gate_w, up_w)[piece // 2]

        def pairs(j):
            found = []
            for block in (2 * (piece % 2), 2 * (piece % 2) + 1):
                at = part * (4 * (piece // 2) + block)
                source = matrix.at[:, column_block(seq_size * block + j, part)]
                found.append((source, gu_all.at[d, landing, pl.ds(at, part)]))
            return found

        return pairs

    others = pl.ds(0, rows * (seq_size - 1))
    qkv = Spread(
        p, qkv_pairs, [qkv_all.at[d, others]], spread_sems.at[0, 0], spread_sems.at[0, 1]
    )
    gu = []
    gu_planes = []
    for i in range(PIECES):
        cut = pl.ds(2 * part * i, 2 * part)
        gu.append(
            Spread(
                p, gu_pairs(i), [gu_all.at[d, others, cut]], spread_sems.at[1 + i, 0],
                spread_sems.at[1 + i, 1],
            )
        )
        gu_planes.append(
            Plane(
                p,
                lambda e, cut=cut: gu_all.at[e, :, cut],
                lambda e, h, cut=cut: gu_all.at[e, pl.ds(half_rows * h, half_rows), cut],
                plane_sems.at[3 + i],
            )
        )
    qkv_plane = Plane(
        p,
        lambda e: qkv_all.at[e],
        lambda e, h: qkv_all.at[e, pl.ds(half_rows * h, half_rows)],
        plane_sems.at[0],
    )
    half_chips = p.chips // 2
    out_plane = Plane(
        p,
        lambda e: out_all.at[e, :, c],
        lambda e, h: out_all.at[e, pl.ds(half_chips * h, half_chips), c],
        plane_sems.at[2],
    )

    def documents_copy(step):
        return remote(
            documents, documents_all.at[s], small_sems.at[0, step], small_sems.at[1, 0],
            p.seq(p.peer(step)),
        )

    def adapters_copy(i, e):
        return remote(
            adapter_row, adapters_all.at[d], small_sems.at[2, i], small_sems.at[3, 0], p.dp(e)
        )

    def side_copy(i, e):
        ref = out_all.at[e, :, c]
        return remote(ref, ref, side_sems.at[0, i], side_sems.at[1, i], p.seq(p.sib))

    def side_wait(i, e):
        ref = out_all.at[e, :, 1 - c]
        remote(ref, ref, side_sems.at[0, i], side_sems.at[1, i], p.seq(p.sib)).wait_recv()

    low_lane = lax.broadcasted_iota(jnp.int32, (tokens, 2 * HD), 1) < HD
    weights = weights_v.reshape(4 * seq_size * rows, qkv_v.shape[1])

    def process(slot):
        at = pl.ds(pl.multiple_of(slot * tokens, tokens), tokens)
        cos_part, sin_part = cos_n[at, :], sin_n[at, :]
        normed = rms_scale(hidden_v[slot].astype(F32), gain[...]).astype(BF16)
        norm_v[slot] = normed
        low = dot_nn(normed, qkv_in[...]).astype(BF16)
        pre = dot_nn(normed, weights[...]) + dot_nn(low, low_map[...])
        padded = jnp.concatenate(
            [low.astype(F32), jnp.zeros((tokens, 128 - low.shape[1]), F32)], axis=1
        )
        low_t[:, at] = padded.T[: low.shape[1]].astype(BF16)
        for m in range(2):
            pair = pre[:, 2 * HD * m : 2 * HD * (m + 1)]
            turned = pair * cos_part + swap_halves(pair) * sin_part
            query[at, pl.ds(2 * HD * m, 2 * HD)] = turned.astype(BF16)
        pair = pre[:, 4 * HD :]
        turned = pair * cos_part + swap_halves(pair) * sin_part
        both = jnp.where(low_lane, turned, pair)
        crossed = pltpu.roll(both, HD, 1)
        keys2[at, :] = jnp.where(low_lane, both, crossed).astype(BF16)
        values2[at, :] = jnp.where(low_lane, crossed, both).astype(BF16)
        zero = jnp.zeros_like(both)
        key_z[0, at, :] = jnp.where(low_lane, both, zero).astype(BF16)
        key_z[1, at, :] = jnp.where(low_lane, zero, crossed).astype(BF16)
        both_t = both.T
        keys_t[:, at] = both_t[:HD].astype(BF16)
        values_t[:, at] = both_t[HD:].astype(BF16)

    def process_distance(k):
        @pl.when(p.z >= k)
        def _():
            hid.side_recv(p.z - k)

            @pl.loop(0, 2)
            def _(core):
                process(2 * (p.z - k) + core)

        if k:

            @pl.when(p.z + k < p.chips)
            def _():
                hid.side_recv(p.z + k)

                @pl.loop(0, 2)
                def _(core):
                    process(2 * (p.z + k) + core)

    def query_block(i):
        start = i * QB
        span = pl.ds(0, start + QB)
        at = pl.ds(start, QB)
        bias[span, :] = mask_bias(seg_col, seg_row, start, QB)

        for m in range(2):
            pair = pl.ds(2 * HD * m, 2 * HD)
            query_pair = query[at, pair]
            found = []
            for e in range(2):
                scores = dot_nt(key_z[e, span, :], query_pair) * SCORE_SCALE + bias[span, :]
                top = jnp.max(scores, axis=0, keepdims=True)
                raised = jnp.exp(scores - top)
                total = jnp.sum(raised, axis=0, keepdims=True)
                found.append(dot_nn(values_t[:, span], raised.astype(BF16)) / total)
                log_totals[2 * m + e : 2 * m + e + 1, at] = top + jnp.log(total)
            attn_v[at, pair] = jnp.concatenate(found, axis=0).T.astype(BF16)

    for step in range(1, seq_size):
        documents_copy(step).start()
    for i, e in enumerate((p.dx, p.dy, p.dd)):
        adapters_copy(i, e).start()
    qkv.start()
    hid.start()
    for copy in stage:
        copy.wait()
    for i in range(3):
        keep[i].start()
    for i in range(3):
        keep[i].wait()
    qkv.recv()
    qkv_plane.start()
    hid.step(1)
    gu[0].start()
    remote(
        documents_all.at[pl.ds(0, seq_size - 1)], documents_all.at[pl.ds(0, seq_size - 1)],
        small_sems.at[0, 0], small_sems.at[1, 0], p.seq(p.sib),
    ).wait_recv()
    for slot in range(seq_size):
        at = pl.ds(tokens * slot, tokens)
        numbers = documents_all[slot].astype(F32)
        seg_row[:, at] = numbers
        seg_col[at, :] = jnp.broadcast_to(numbers[0:1, :], (tokens, tokens)).T
    qkv_plane.forward()
    hid.step(2)
    gu[1].start()
    gu[0].recv()
    gu_planes[0].start()
    qkv_plane.recv()
    keep[3].start()
    keep[3].wait()
    process_distance(0)
    process_distance(1)
    hid.step(3)
    gu[2].start()
    out.start()
    gu[1].recv()
    gu_planes[1].start()
    gu_planes[0].forward()
    process_distance(2)
    process_distance(3)
    gu[3].start()
    out.step(1)
    keep[4].start()
    keep[5].start()
    query_block(0)
    query_block(1)
    gu[2].recv()
    gu_planes[2].start()
    gu_planes[1].forward()
    out.step(2)
    query_block(2)
    query_block(3)
    keep[6].start()
    att.start()
    gu[3].recv()
    gu_planes[3].start()
    gu_planes[2].forward()
    out.step(3)
    out_plane.start()
    att.step(1)
    gu_planes[3].forward()
    att.step(2)
    out_plane.forward()
    side_copy(0, p.dx).start()
    side_copy(1, p.dy).start()
    att.step(3)
    out_plane.recv()
    side_copy(2, p.dd).start()
    for i in range(4):
        gu_planes[i].recv()
    for chain in (out, att):
        for other in range(p.chips):
            chain.side_recv(other)
    for chain in (hid, out, att):
        chain.finish()
    for i, e in enumerate((p.dx, p.dy, p.dd)):
        side_wait(i, e)
    remote(
        adapters_all.at[pl.ds(0, 3)], adapters_all.at[pl.ds(0, 3)],
        small_sems.at[2, 3], small_sems.at[3, 0], p.dp(p.dx),
    ).wait_recv()
    for step in range(1, seq_size):
        documents_copy(step).wait_send()
    for i, e in enumerate((p.dx, p.dy, p.dd)):
        adapters_copy(i, e).wait_send()
        side_copy(i, e).wait_send()
    for group in [qkv, *gu, qkv_plane, out_plane, *gu_planes]:
        group.finish()
    for i in (4, 5, 6):
        keep[i].wait()


def front_all(seq_size, ins):
    tokens, width = ins[0].shape
    rows = ins[3].shape[0]
    part = ins[6].shape[1] // (4 * seq_size)
    chips = seq_size // 2
    q_width = ins[3].shape[1] // seq_size
    qkv_width = q_width + ins[4].shape[2]
    length = tokens * seq_size
    low_width = ins[9].shape[1]

    def shape(*dims, dtype=BF16):
        return jax.ShapeDtypeStruct(dims, dtype)

    anywhere = pl.BlockSpec(memory_space=pl.ANY)
    vmem = pl.BlockSpec(memory_space=pltpu.VMEM)
    outs = (
        shape(seq_size, tokens, width),
        shape(4, 8, 128, dtype=jnp.int32),
        shape(4, seq_size * rows, qkv_width),
        shape(4, chips, 2, rows, width),
        shape(4, seq_size * rows, 8 * part),
        shape(seq_size, length, q_width),
        shape(seq_size, tokens, width),
        shape(length, q_width),
        shape(length, 2 * HD),
        shape(length, 2 * HD),
        shape(HD, length),
        shape(4, length, dtype=F32),
        shape(8, length, dtype=F32),
        shape(length, tokens, dtype=F32),
        shape(low_width, length),
    )
    return pl.pallas_call(
        functools.partial(front_kernel, seq_size),
        out_shape=outs,
        in_specs=[anywhere] * 8 + [vmem] * 5,
        out_specs=(anywhere,) * 7 + (vmem,) * 8,
        scratch_shapes=[
            pltpu.VMEM((seq_size, 8, tokens), jnp.int32),
            pltpu.SemaphoreType.DMA((4, 4, seq_size)),
            pltpu.SemaphoreType.DMA((3 + PIECES, 2, 4)),
            pltpu.SemaphoreType.DMA((2, 16)),
            pltpu.SemaphoreType.DMA((1 + PIECES, 2)),
            pltpu.SemaphoreType.DMA((4, seq_size)),
            pltpu.SemaphoreType.DMA((2, 3)),
            pltpu.VMEM((seq_size, tokens, width), BF16),
            pltpu.VMEM((seq_size, tokens, width), BF16),
            pltpu.VMEM((rows, width), BF16),
            pltpu.VMEM((rows, qkv_width), BF16),
            pltpu.VMEM((rows, 8 * part), BF16),
            pltpu.VMEM((4, seq_size * rows, qkv_width), BF16),
            pltpu.VMEM((2, length, 2 * HD), BF16),
            pltpu.VMEM((HD, length), BF16),
            pltpu.VMEM((length, QB), F32),
            pltpu.VMEM((length, q_width), BF16),
        ],
        compiler_params=pltpu.CompilerParams(
            collective_id=0, has_side_effects=True, vmem_limit_bytes=60 * 2**20
        ),
        cost_estimate=pl.CostEstimate(
            flops=5 * 10**9, bytes_accessed=60 * 2**20, transcendentals=4 * 2**20
        ),
        name="attend_front",
    )(*ins)


def dot_nn(a, b):
    return lax.dot_general(a, b, (((1,), (0,)), ((), ())), preferred_element_type=F32)


def dot_nt(a, b):
    return lax.dot_general(a, b, (((1,), (1,)), ((), ())), preferred_element_type=F32)


class ChainSum:
    def __init__(self, place, part, side_in, up_in, down_in, sems):
        self.p, self.part = place, part
        self.side_in, self.up_in, self.down_in = side_in, up_in, down_in
        self.sems = sems

    def _side(self, z):
        p = self.p
        return remote(
            self.part.at[2 * z + 1 - p.c], self.side_in.at[z],
            self.sems.at[0, z], self.sems.at[1, z], p.seq(p.sib),
        )

    def _up(self, z):
        p = self.p
        return remote(
            self.part.at[2 * z + p.c], self.up_in.at[z],
            self.sems.at[2, z], self.sems.at[3, z], p.seq(p.s + 2),
        )

    def _down(self, z):
        p = self.p
        return remote(
            self.part.at[2 * z + p.c], self.down_in.at[z],
            self.sems.at[4, z], self.sems.at[5, z], p.seq(p.s - 2),
        )

    def _add(self, z, incoming):
        slot = 2 * z + self.p.c
        rows = self.part.shape[1]

        @pl.loop(0, rows // 16)
        def _(i):
            cut = pl.ds(pl.multiple_of(i * 16, 16), 16)
            total = self.part[slot, cut].astype(F32) + incoming[z, cut].astype(F32)
            self.part[slot, cut] = total.astype(BF16)

    def side_start(self, z):
        self._side(z).start()

    def side_add(self, z):
        self._side(z).wait_recv()
        self._add(z, self.side_in)

    def step(self, k):
        p = self.p

        @pl.when(p.z + k < p.chips)
        def _():
            to = p.z + k
            self.side_add(to)

            @pl.when(p.z > 0)
            def _():
                self._up(to).wait_recv()
                self._add(to, self.up_in)

            self._up(to).start()

        @pl.when(p.z >= k)
        def _():
            to = p.z - k
            self.side_add(to)

            @pl.when(p.z < p.chips - 1)
            def _():
                self._down(to).wait_recv()
                self._add(to, self.down_in)

            self._down(to).start()

    def last(self):
        p = self.p
        self.side_add(p.z)

        @pl.when(p.z > 0)
        def _():
            self._up(p.z).wait_recv()
            self._add(p.z, self.up_in)

        @pl.when(p.z < p.chips - 1)
        def _():
            self._down(p.z).wait_recv()
            self._add(p.z, self.down_in)

    def finish(self):
        p = self.p
        for z in range(p.chips):
            self._side(z).wait_send()
        for k in range(1, p.chips):

            @pl.when(p.z + k < p.chips)
            def _():
                self._up(p.z + k).wait_send()

            @pl.when(p.z >= k)
            def _():
                self._down(p.z - k).wait_send()


def chain_order(z):
    second = jnp.where(z == 0, 2, jnp.where(z == 1, 0, jnp.where(z == 2, 3, 1)))
    return (jnp.where(z < 2, 3, 0), second, jnp.where(z % 2 == 0, 1, 2), z)


def swap_halves(values):
    lane = lax.broadcasted_iota(jnp.int32, values.shape, 1)
    return jnp.where(
        lane % HD < HD // 2,
        pltpu.roll(values, values.shape[1] - HD // 2, 1),
        pltpu.roll(values, HD // 2, 1),
    )


def mask_bias(seg_col, seg_row, start, size):
    length = start + size
    key_pos = lax.broadcasted_iota(jnp.int32, (length, size), 0)
    query_pos = start + lax.broadcasted_iota(jnp.int32, (length, size), 1)
    same = seg_col[pl.ds(0, length), 0:1] == seg_row[0:1, pl.ds(start, size)]
    return jnp.where((key_pos <= query_pos) & same, 0.0, -1e30).astype(F32)


def back_kernel(
    seq_size,
    grad_attn,
    query,
    keys2,
    values2,
    keys_t,
    log_totals,
    seg_row,
    seg_col,
    cos_t,
    sin_t,
    cos_n,
    sin_n,
    qkv_w,
    qkv_in,
    low_map,
    low_qkv_t,
    norm_one,
    ffn_part,
    early_t,
    gu_grad,
    down_grad,
    owners,
    norm_sum,
    ffn_sum,
    share_out,
    gu_out,
    down_out,
    q_out,
    kv_out,
    grads,
    key_z,
    value_z,
    key_acc,
    value_acc,
    bias,
    grad_qkv,
    grad_low,
    qkv_v,
    norm_v,
    ffn_v,
    ffn_side,
    ffn_up,
    ffn_down,
    sum_v,
    sum_side,
    sum_up,
    sum_down,
    share,
    share_in,
    turned,
    gu_in,
    down_in,
    q_got,
    kv_got,
    load_sems,
    swap_sems,
    ffn_sems,
    sum_sems,
    send_sems,
    got_sems,
):
    p = Place(seq_size)
    d, s = p.d, p.s
    length = query.shape[0]
    chips = p.chips
    loads = [
        pltpu.make_async_copy(src, dst, load_sems.at[i])
        for i, (src, dst) in enumerate(
            ((ffn_part, ffn_v), (qkv_w, qkv_v), (norm_one, norm_v), (grad_attn.at[s], grads.at[s]))
        )
    ]
    for copy in loads:
        copy.start()
    barrier = pltpu.get_barrier_semaphore()
    everyone = 4 * seq_size

    def place_of(t):
        return lax.rem(d + t // seq_size, 4), lax.rem(s + lax.rem(t, seq_size), seq_size)

    @pl.loop(1, everyone)
    def _(t):
        pl.semaphore_signal(barrier, 1, device_id=place_of(t), device_id_type=MESH)

    pl.semaphore_wait(barrier, everyone - 1)

    def swap_copy(step):
        return remote(
            grad_attn.at[p.peer(step)], grads.at[s], swap_sems.at[0, step], swap_sems.at[1, 0],
            p.seq(p.peer(step)),
        )

    for step in range(1, seq_size):
        swap_copy(step).start()

    def deliver(src, dst, td, ts, i, wait):
        here = (td == d) & (ts == s)

        @pl.when(jnp.logical_not(here))
        def _():
            copy = remote(src, dst, send_sems.at[i], got_sems.at[i], (td, ts))
            if wait:
                copy.wait_send()
            else:
                copy.start()

        if not wait:

            @pl.when(here)
            def _():
                pltpu.make_async_copy(src, dst, got_sems.at[i]).start()

    def ready(buffer, i):
        remote(buffer, buffer, send_sems.at[i], got_sems.at[i], p.seq(p.sib)).wait_recv()

    block = gu_grad.shape[1] // 8

    def deliver_wide(wait):
        side = pl.ds(pl.multiple_of(block * lax.rem(s, 2), block), block)
        for e in range(4):
            for upper in range(2):
                deliver(
                    gu_grad.at[:, pl.ds((4 * upper + e) * block, block)],
                    gu_in.at[d, :, side],
                    2 * upper + e // 2,
                    lax.rem(e, 2) * (seq_size // 2) + s // 2,
                    0,
                    wait,
                )
            deliver(down_grad.at[:, pl.ds(e * block, block)], down_in.at[d], e, s, 1, wait)

    def deliver_heads(wait):
        for i in range(4):
            m = 4 * s + i
            deliver(
                turned.at[pl.ds(HD * i, HD)], q_got.at[d], m // seq_size, lax.rem(m, seq_size), 2, wait
            )
        for i in range(4):
            m = 2 * seq_size * (i // 2) + 2 * s + i % 2
            deliver(
                turned.at[pl.ds(4 * HD + HD // 2 * i, HD // 2)],
                kv_got.at[d],
                m // seq_size,
                lax.rem(m, seq_size),
                3,
                wait,
            )

    def deliver_share(wait):
        rows = share.shape[0] // everyone

        @pl.loop(0, everyone)
        def _(t):
            td, ts = place_of(t)
            start = pl.multiple_of((td * seq_size + ts) * rows, rows)
            deliver(share.at[pl.ds(start, rows)], share_in.at[d, s], td, ts, 4, wait)

    ffn = ChainSum(p, ffn_v, ffn_side, ffn_up, ffn_down, ffn_sems)
    total = ChainSum(p, sum_v, sum_side, sum_up, sum_down, sum_sems)

    low_lane = lax.broadcasted_iota(jnp.int32, (length, 2 * HD), 1) < HD
    zero = jnp.zeros((length, 2 * HD), BF16)
    key_z[0] = jnp.where(low_lane, keys2[...], zero)
    key_z[1] = jnp.where(low_lane, zero, keys2[...])
    value_z[0] = jnp.where(low_lane, values2[...], zero)
    value_z[1] = jnp.where(low_lane, zero, values2[...])
    key_acc[...] = jnp.zeros_like(key_acc)
    value_acc[...] = jnp.zeros_like(value_acc)
    for copy in loads:
        copy.wait()
    for z in range(chips):
        ffn.side_start(z)
    remote(
        grads.at[pl.ds(0, seq_size - 1)], grads.at[pl.ds(0, seq_size - 1)],
        swap_sems.at[0, 0], swap_sems.at[1, 0], p.seq(p.sib),
    ).wait_recv()
    deliver_wide(False)
    ffn.step(3)

    def query_block(i):
        start = i * QB
        span = pl.ds(0, start + QB)
        rows = pl.ds(start, QB)
        bias[span, :] = mask_bias(seg_col, seg_row, start, QB)
        slots = QB // grads.shape[1]

        for m in range(2):
            pair = pl.ds(2 * HD * m, 2 * HD)
            query_pair = query[rows, pair]
            grad_pair = grads[pl.ds(slots * i, slots), :, pair].reshape(QB, 2 * HD)
            turned_q = []
            for e in range(2):
                h = 2 * m + e
                scores = dot_nt(key_z[e, span, :], query_pair)
                weights = jnp.exp(scores * SCORE_SCALE + bias[span, :] - log_totals[h : h + 1, rows])
                grad_weights = dot_nt(value_z[e, span, :], grad_pair)
                row_dot = jnp.sum(weights * grad_weights, axis=0, keepdims=True)
                grad_scores = (weights * (grad_weights - row_dot)).astype(BF16)
                key_acc[e, span, :] += dot_nn(grad_scores, query_pair)
                value_acc[e, span, :] += dot_nn(weights.astype(BF16), grad_pair)
                grad_q = dot_nn(keys_t[:, span], grad_scores) * SCORE_SCALE
                first, second = grad_q[: HD // 2], grad_q[HD // 2 :]
                cos_part, sin_part = cos_t[:, rows], sin_t[:, rows]
                turned_q.append(first * cos_part + second * sin_part)
                turned_q.append(second * cos_part - first * sin_part)
            grad_qkv[rows, pair] = jnp.concatenate(turned_q, axis=0).T.astype(BF16)

    query_block(0)
    query_block(1)
    query_block(2)
    ffn.step(2)
    query_block(3)

    def folded(acc):
        merged = jnp.where(low_lane, acc[0], acc[1])
        return merged + pltpu.roll(merged, HD, 1)

    grad_key = folded(key_acc) * SCORE_SCALE
    grad_key = grad_key * cos_n[...] - swap_halves(grad_key) * sin_n[...]
    grad_qkv[:, pl.ds(4 * HD, 2 * HD)] = jnp.where(low_lane, grad_key, folded(value_acc)).astype(BF16)
    grad_low[...] = dot_nt(grad_qkv[...], low_map[...]).astype(BF16)
    grad_low_t = dot_nt(low_map[...], grad_qkv[...]).astype(BF16)
    ffn.step(1)

    tokens = sum_v.shape[1]

    def give(to):
        rows = pl.ds(pl.multiple_of(2 * to * tokens, 2 * tokens), 2 * tokens)
        left, low = grad_qkv[rows, :], grad_low[rows, :]
        for j in range(4):
            cut = pl.ds(512 * j, 512)
            value = dot_nt(left, qkv_v[cut, :]) + dot_nt(low, qkv_in[cut, :])
            sum_v[2 * to, :, cut] = value[:tokens].astype(BF16)
            sum_v[2 * to + 1, :, cut] = value[tokens:].astype(BF16)
        total.side_start(to)

    order = chain_order(p.z)
    give(order[0])
    total.step(3)
    give(order[1])
    give(order[2])
    give(order[3])
    outer = dot_nn(low_qkv_t[...], grad_qkv[...])
    outer = jnp.concatenate([outer, jnp.zeros((80, outer.shape[1]), F32)], axis=0)
    turned[...] = outer.T
    deliver_heads(False)
    total.step(2)
    for j in range(8):
        cut = pl.ds(256 * j, 256)
        piece = jnp.concatenate([dot_nn(grad_low_t, norm_v[:, cut]), early_t[:, cut]], axis=0)
        share[cut, :] = piece.T.astype(BF16)
    deliver_share(False)
    total.step(1)
    ffn.last()
    ffn_sum[...] = ffn_v[s].astype(F32)
    for buffer, i in ((gu_in, 0), (down_in, 1), (q_got, 2), (kv_got, 3), (share_in, 4)):
        ready(buffer, i)

    def by_adapter(out, value):
        values = [value(e) for e in range(4)]
        for a in range(4):
            chosen = jnp.zeros_like(values[0])
            for e in range(4):
                chosen = jnp.where(owners[e, 0:1, 0:1] == a, values[e], chosen)
            out[a] = chosen

    by_adapter(gu_out, lambda e: gu_in[e])
    by_adapter(down_out, lambda e: down_in[e])
    by_adapter(q_out, lambda e: q_got[e])
    by_adapter(kv_out, lambda e: kv_got[e])
    by_adapter(share_out, lambda e: jnp.sum(share_in[e].astype(F32), axis=0))
    total.last()
    norm_sum[...] = sum_v[s].astype(F32)
    for step in range(1, seq_size):
        swap_copy(step).wait_send()
    deliver_wide(True)
    deliver_heads(True)
    deliver_share(True)
    ffn.finish()
    total.finish()


def back_all(seq_size, ins):
    (grad_attn, query, keys2) = ins[:3]
    _, tokens, width_q = grad_attn.shape
    length = query.shape[0]
    width = ins[16].shape[1]
    qkv_width = ins[12].shape[1]
    chips = seq_size // 2
    rows = width // (4 * seq_size)
    rank = ins[19].shape[0]
    block = ins[19].shape[1] // 8

    def shape(*dims):
        return jax.ShapeDtypeStruct(dims, F32)

    vmem = pl.BlockSpec(memory_space=pltpu.VMEM)
    anywhere = pl.BlockSpec(memory_space=pl.ANY)
    far = (0, 12, 16, 17)
    outs = (
        shape(tokens, width),
        shape(tokens, width),
        shape(4, rows, 128),
        shape(4, rank, 2 * block),
        shape(4, rank, block),
        shape(4, HD, 128),
        shape(4, HD // 2, 128),
    )
    many = (seq_size, tokens, width)
    few = (chips, tokens, width)
    return pl.pallas_call(
        functools.partial(back_kernel, seq_size),
        out_shape=outs,
        in_specs=[anywhere if i in far else vmem for i in range(len(ins))],
        out_specs=(vmem,) * len(outs),
        scratch_shapes=[
            pltpu.VMEM(grad_attn.shape, BF16),
            pltpu.VMEM((2, length, 2 * HD), BF16),
            pltpu.VMEM((2, length, 2 * HD), BF16),
            pltpu.VMEM((2, length, 2 * HD), F32),
            pltpu.VMEM((2, length, 2 * HD), F32),
            pltpu.VMEM((length, QB), F32),
            pltpu.VMEM((length, qkv_width), BF16),
            pltpu.VMEM((length, 3 * rank), BF16),
            pltpu.VMEM(ins[12].shape, BF16),
            pltpu.VMEM((length, width), BF16),
            pltpu.VMEM(many, BF16),
            pltpu.VMEM(few, BF16),
            pltpu.VMEM(few, BF16),
            pltpu.VMEM(few, BF16),
            pltpu.VMEM(many, BF16),
            pltpu.VMEM(few, BF16),
            pltpu.VMEM(few, BF16),
            pltpu.VMEM(few, BF16),
            pltpu.VMEM((width, 128), BF16),
            pltpu.VMEM((4, seq_size, rows, 128), BF16),
            pltpu.VMEM((qkv_width, 128), F32),
            pltpu.VMEM((4, rank, 2 * block), F32),
            pltpu.VMEM((4, rank, block), F32),
            pltpu.VMEM((4, HD, 128), F32),
            pltpu.VMEM((4, HD // 2, 128), F32),
            pltpu.SemaphoreType.DMA((4,)),
            pltpu.SemaphoreType.DMA((2, seq_size)),
            pltpu.SemaphoreType.DMA((6, chips)),
            pltpu.SemaphoreType.DMA((6, chips)),
            pltpu.SemaphoreType.DMA((5,)),
            pltpu.SemaphoreType.DMA((5,)),
        ],
        compiler_params=pltpu.CompilerParams(
            collective_id=1, has_side_effects=True, vmem_limit_bytes=60 * 2**20
        ),
        cost_estimate=pl.CostEstimate(
            flops=10 * 10**9, bytes_accessed=20 * 2**20, transcendentals=4 * 2**20
        ),
        name="attend_back",
    )(*ins)


def mid_kernel(
    seq_size,
    attn_all,
    hidden_all,
    out_all,
    gu_all,
    cotangent,
    down_w,
    gain,
    o_in,
    o_out,
    gu_in,
    gu_map,
    down_in,
    down_out,
    ffn_part,
    middle_own,
    grad_middle,
    grad_attn,
    early_t,
    gu_grad,
    down_grad,
    out_v,
    gu_v,
    down_v,
    cot_v,
    norm_v,
    both_v,
    wide,
    act_v,
    sum_v,
    sum_side,
    sum_up,
    sum_down,
    attn_own,
    low_own,
    lows,
    lows_t,
    chain_sems,
    plane_sems,
    sum_sems,
    local_sems,
):
    p = Place(seq_size)
    d, s, z, c = p.d, p.s, p.z, p.c
    tokens, width = cotangent.shape
    part = down_w.shape[0]
    span = 2 * tokens
    hidden_width = 4 * part
    rank = o_in.shape[1]
    heads_width = attn_all.shape[2]
    step_width = 512
    loads = [
        pltpu.make_async_copy(src, dst, local_sems.at[0, i])
        for i, (src, dst) in enumerate(
            [(down_w, down_v.at[d]), (cotangent, cot_v.at[s]), (hidden_all, norm_v), (out_all, out_v)]
            + [
                (attn_all.at[j], both_v.at[:, pl.ds(heads_width * j, heads_width)])
                for j in range(seq_size)
            ]
            + [(gu_all, gu_v)]
        )
    ]
    for copy in loads:
        copy.start()
    barrier = pltpu.get_barrier_semaphore()
    p_up, p_down = p.z < p.chips - 1, p.z > 0

    @pl.when(p_up)
    def _():
        pl.semaphore_signal(barrier, 1, device_id=p.seq(s + 2), device_id_type=MESH)

    @pl.when(p_down)
    def _():
        pl.semaphore_signal(barrier, 1, device_id=p.seq(s - 2), device_id_type=MESH)

    for place in (p.seq(p.sib), p.dp(p.dx), p.dp(p.dy)):
        pl.semaphore_signal(barrier, 1, device_id=place, device_id_type=MESH)

    @pl.when(p_up & p_down)
    def _():
        pl.semaphore_wait(barrier, 5)

    @pl.when(jnp.logical_not(p_up & p_down))
    def _():
        pl.semaphore_wait(barrier, 4)

    cot = Chain(p, cotangent, lambda i: cot_v.at[i], chain_sems)
    down = Plane(
        p,
        lambda e: down_v.at[e],
        lambda e, h: down_v.at[e, pl.ds(part // 2 * h, part // 2)],
        plane_sems,
    )
    total = ChainSum(p, sum_v, sum_side, sum_up, sum_down, sum_sems)
    down_all = down_v.reshape(4 * part, width)
    cot.start()
    loads[0].wait()
    down.start()
    for copy in loads[1:-1]:
        copy.wait()

    def columns(body, count):
        @pl.loop(0, count)
        def _(n):
            body(pl.ds(pl.multiple_of(n * step_width, step_width), step_width))

    def flat(ref, zz, cut=slice(None)):
        return ref[pl.ds(2 * zz, 2), :, cut].reshape(span, -1)

    lows[...] = jnp.zeros_like(lows)

    def forward(zz):
        rows = pl.ds(span * zz, span)
        low = dot_nn(both_v[rows, :], o_in[...]).astype(BF16)

        def branch(cut):
            value = dot_nn(both_v[rows, :], out_v[:, cut]) + dot_nn(low, o_out[:, cut])
            wide[rows, cut] = flat(norm_v, zz, cut).astype(F32) + RESIDUAL_SCALE * value

        columns(branch, width // step_width)

        @pl.when(z == zz)
        def _():
            mine = pl.ds(pl.multiple_of(s * tokens, tokens), tokens)
            middle_own[...] = wide[mine, :]
            attn_own[...] = both_v[mine, :]
            low_own[...] = dot_nn(attn_own[...], o_in[...]).astype(BF16)

        middle = wide[rows, :]
        normed = rms_scale(middle, gain[...]).astype(BF16)
        norm_v[2 * zz] = normed[:tokens]
        norm_v[2 * zz + 1] = normed[tokens:]
        low_gu = dot_nn(normed, gu_in[...]).astype(BF16)
        lows[rows, 0 : 2 * rank] = low_gu.astype(F32)

        def gate_up(cut):
            value = dot_nn(flat(norm_v, zz), gu_v[:, cut]) + dot_nn(low_gu, gu_map[:, cut])
            wide[rows, cut] = value

        columns(gate_up, 2 * hidden_width // step_width)

    for zz in range(p.chips):
        if zz == 0:
            loads[-1].wait()
        forward(zz)
        if zz == 0:
            cot.step(1)
        if zz == 2:
            cot.step(2)
            down.forward()
    cot.step(3)
    down.recv()
    for zz in range(p.chips):
        cot.side_recv(zz)

    def backward(zz):
        rows = pl.ds(pl.multiple_of(span * zz, span), span)
        grad = flat(cot_v, zz)
        low = dot_nt(grad, down_out[...]).astype(BF16)
        lows[rows, 5 * rank : 6 * rank] = low.astype(F32)

        def hidden_part(n):
            cut = pl.ds(pl.multiple_of(n * step_width, step_width), step_width)
            upper = pl.ds(pl.multiple_of(hidden_width + n * step_width, step_width), step_width)
            grad_act = RESIDUAL_SCALE * (
                dot_nt(flat(cot_v, zz), down_all[cut, :]) + dot_nt(low, down_in[cut, :])
            )
            gate, up = wide[rows, cut], wide[rows, upper]
            sigma = 1.0 / (1.0 + jnp.exp(-gate))
            raised = gate * sigma
            act_v[rows, cut] = (raised * up).astype(BF16)
            both_v[rows, cut] = (grad_act * up * sigma * (1.0 + gate * (1.0 - sigma))).astype(BF16)
            both_v[rows, upper] = (grad_act * raised).astype(BF16)

        pl.loop(0, hidden_width // step_width)(hidden_part)
        low_gu = dot_nt(both_v[rows, :], gu_map[...]).astype(BF16)
        lows[rows, 2 * rank : 4 * rank] = low_gu.astype(F32)

        def model_part(cut):
            value = dot_nt(both_v[rows, :], gu_v[cut, :]) + dot_nt(low_gu, gu_in[cut, :])
            sum_v[2 * zz, :, cut] = value[:tokens].astype(BF16)
            sum_v[2 * zz + 1, :, cut] = value[tokens:].astype(BF16)

        columns(model_part, width // step_width)
        total.side_start(zz)

    order = chain_order(z)
    backward(order[0])
    total.step(3)
    backward(order[1])
    backward(order[2])
    total.step(2)
    backward(order[3])
    lows[:, 4 * rank : 5 * rank] = dot_nn(act_v[...], down_in[...])
    for zz in range(p.chips):
        lows_t[:, pl.ds(span * zz, span)] = lows[pl.ds(span * zz, span), :].T.astype(BF16)
    total.step(1)
    length = seq_size * tokens

    for n in range(width // step_width):
        cut = pl.ds(step_width * n, step_width)
        early_t[2 * rank : 4 * rank, cut] = dot_nn(
            lows_t[2 * rank : 4 * rank, :], norm_v[:, :, cut].reshape(length, step_width)
        )
        early_t[4 * rank : 5 * rank, cut] = RESIDUAL_SCALE * dot_nn(
            lows_t[4 * rank : 5 * rank, :], cot_v[:, :, cut].reshape(length, step_width)
        )
        source = pl.ds(0, rank) if n < hidden_width // step_width else pl.ds(rank, rank)
        gu_grad[:, cut] = dot_nn(lows_t[source, :], both_v[:, cut])
        if n < hidden_width // step_width:
            down_grad[:, cut] = RESIDUAL_SCALE * dot_nn(
                lows_t[5 * rank : 6 * rank, :], act_v[:, cut]
            )

    @pl.loop(0, p.chips)
    def _(zz):
        rows = pl.ds(pl.multiple_of(span * zz, span), span)
        low = lows[rows, 4 * rank : 5 * rank].astype(BF16)

        def block(cut):
            value = dot_nn(act_v[rows, :], down_all[:, cut]) + dot_nn(low, down_out[:, cut])
            norm_v[2 * zz, :, cut] = value[:tokens].astype(BF16)
            norm_v[2 * zz + 1, :, cut] = value[tokens:].astype(BF16)

        columns(block, width // step_width)

    store = pltpu.make_async_copy(norm_v, ffn_part, local_sems.at[1, 0])
    store.start()
    total.last()
    middle = middle_own[...]
    mean = jnp.mean(middle * middle, axis=-1, keepdims=True)
    r = lax.rsqrt(mean + EPSILON)
    scaled = sum_v[s].astype(F32) * gain[...]
    inner = jnp.mean(scaled * middle, axis=-1, keepdims=True)
    grad_mid = cot_v[s].astype(F32) + r * scaled - r * r * r * inner * middle
    grad_middle[...] = grad_mid
    branch = (RESIDUAL_SCALE * grad_mid).astype(BF16)
    low = dot_nt(branch, o_out[...]).astype(BF16)
    for j in range(seq_size):
        cut = pl.ds(heads_width * j, heads_width)
        grad_attn[j] = (dot_nt(branch, out_v[cut, :]) + dot_nt(low, o_in[cut, :])).astype(BF16)
    pair = jnp.concatenate(
        [low.astype(F32), low_own[...].astype(F32), jnp.zeros((tokens, 128 - 2 * rank), F32)], axis=1
    )
    pair = pair.T.astype(BF16)
    early_t[0:rank, :] = dot_nn(pair[0:rank], attn_own[...])
    early_t[rank : 2 * rank, :] = dot_nn(pair[rank : 2 * rank], branch)
    cot.finish()
    down.finish()
    total.finish()
    store.wait()


def mid_all(seq_size, ins):
    tokens, width = ins[4].shape
    part = ins[5].shape[0]
    length = seq_size * tokens
    rank = ins[7].shape[1]
    chips = seq_size // 2
    heads_width = ins[0].shape[2]

    def shape(*dims, dtype=F32):
        return jax.ShapeDtypeStruct(dims, dtype)

    vmem = pl.BlockSpec(memory_space=pltpu.VMEM)
    anywhere = pl.BlockSpec(memory_space=pl.ANY)
    many, few = (seq_size, tokens, width), (chips, tokens, width)
    outs = (
        shape(*many, dtype=BF16),
        shape(tokens, width),
        shape(tokens, width),
        shape(seq_size, tokens, heads_width, dtype=BF16),
        shape(5 * rank, width),
        shape(rank, 8 * part),
        shape(rank, 4 * part),
    )
    return pl.pallas_call(
        functools.partial(mid_kernel, seq_size),
        out_shape=outs,
        in_specs=[anywhere] * 6 + [vmem] * 7,
        out_specs=(anywhere,) + (vmem,) * 6,
        scratch_shapes=[
            pltpu.VMEM((width, width), BF16),
            pltpu.VMEM((width, 8 * part), BF16),
            pltpu.VMEM((4, part, width), BF16),
            pltpu.VMEM(many, BF16),
            pltpu.VMEM(many, BF16),
            pltpu.VMEM((length, width), BF16),
            pltpu.VMEM((length, 8 * part), F32),
            pltpu.VMEM((length, 4 * part), BF16),
            pltpu.VMEM(many, BF16),
            pltpu.VMEM(few, BF16),
            pltpu.VMEM(few, BF16),
            pltpu.VMEM(few, BF16),
            pltpu.VMEM((tokens, width), BF16),
            pltpu.VMEM((tokens, rank), BF16),
            pltpu.VMEM((length, 128), F32),
            pltpu.VMEM((128, length), BF16),
            pltpu.SemaphoreType.DMA((4, seq_size)),
            pltpu.SemaphoreType.DMA((2, 4)),
            pltpu.SemaphoreType.DMA((6, chips)),
            pltpu.SemaphoreType.DMA((2, 13)),
        ],
        compiler_params=pltpu.CompilerParams(
            collective_id=2, has_side_effects=True, vmem_limit_bytes=63 * 2**20
        ),
        cost_estimate=pl.CostEstimate(
            flops=40 * 10**9, bytes_accessed=40 * 2**20, transcendentals=4 * 2**20
        ),
        name="feed_forward",
    )(*ins)


def make_kernel_local(dp_size, seq_size):
    heads = NH // seq_size

    def local(
        hidden,
        token_document_numbers,
        sequence_adapter_index,
        cotangent,
        attention_norm_gain,
        feedforward_norm_gain,
        query_weight,
        key_weight,
        value_weight,
        attention_output_weight,
        gate_weight,
        up_weight,
        down_weight,
        adapter_query_key_value_input,
        adapter_query_output,
        adapter_key_value_output,
        adapter_projection_input,
        adapter_projection_output,
        adapter_gate_up_input,
        adapter_gate_up_output,
        adapter_down_input,
        adapter_down_output,
    ):
        tokens, width = hidden.shape[1:]
        length = tokens * seq_size
        rows = query_weight.shape[0]
        key_width = key_weight.shape[1]
        ff_block = gate_weight.shape[1] // (dp_size * seq_size)
        ff_own = dp_size * ff_block
        rank = adapter_projection_input.shape[2]
        q_width = heads * HD
        me = lax.axis_index("seq")
        adapter = sequence_adapter_index[0]

        def pick(maps):
            return lax.dynamic_index_in_dim(maps, adapter, 0, keepdims=False)

        def pick_columns(maps, start, size):
            return lax.dynamic_slice(maps, (adapter, 0, start), (1, rank, size))[0]

        qkv_in = pick(adapter_query_key_value_input)
        q_out = pick_columns(adapter_query_output, me * q_width, q_width)
        k_out = pick_columns(adapter_key_value_output, me * HD, HD)
        v_out = pick_columns(adapter_key_value_output, key_width + me * HD, HD)
        none_q, none_h = jnp.zeros((rank, q_width), BF16), jnp.zeros((rank, HD), BF16)
        low_map = jnp.concatenate(
            [
                jnp.concatenate([q_out, none_h, none_h], axis=1),
                jnp.concatenate([none_q, k_out, none_h], axis=1),
                jnp.concatenate([none_q, none_h, v_out], axis=1),
            ],
            axis=0,
        )
        kv = jnp.concatenate(
            [key_weight.reshape(rows, KVH, HD), value_weight.reshape(rows, KVH, HD)], axis=2
        )
        cos_fixed, sin_fixed = fixed_tables(length)
        cos_n = jnp.asarray(np.tile(cos_fixed, (1, 4)))
        sin_n = jnp.asarray(np.tile(np.concatenate([-sin_fixed, sin_fixed], axis=1), (1, 2)))
        (
            hidden_all,
            owners,
            qkv,
            out_full,
            gate_up,
            attn,
            norm_one,
            query,
            keys2,
            values2,
            keys_t,
            log_totals,
            seg_row,
            seg_col,
            low_t,
        ) = front_all(
            seq_size,
            (
                hidden[0],
                jnp.broadcast_to(token_document_numbers, (8, tokens)),
                jnp.broadcast_to(sequence_adapter_index[:, None], (8, 128)),
                query_weight,
                jnp.swapaxes(kv, 0, 1),
                attention_output_weight,
                gate_weight,
                up_weight,
                attention_norm_gain[None],
                qkv_in,
                low_map,
                cos_n,
                sin_n,
            ),
        )
        gu_out = pick(adapter_gate_up_output).reshape(rank, 2, dp_size, seq_size, ff_block)
        gu_out = lax.dynamic_index_in_dim(gu_out, me, 3, keepdims=False).reshape(rank, 2, ff_own)
        none_f = jnp.zeros((rank, ff_own), BF16)
        gu_map = jnp.concatenate(
            [
                jnp.concatenate([gu_out[:, 0], none_f], axis=1),
                jnp.concatenate([none_f, gu_out[:, 1]], axis=1),
            ],
            axis=0,
        )
        down_in = pick(adapter_down_input).reshape(dp_size, seq_size, ff_block, rank)
        down_in = lax.dynamic_index_in_dim(down_in, me, 1, keepdims=False).reshape(ff_own, rank)
        ffn_part, middle, grad_middle, grad_attn, early, gu_grad, down_grad = mid_all(
            seq_size,
            (
                attn,
                hidden_all,
                out_full.reshape(width, width),
                gate_up.reshape(width, 2 * ff_own),
                cotangent[0],
                down_weight,
                feedforward_norm_gain[None],
                pick(adapter_projection_input),
                pick(adapter_projection_output),
                pick(adapter_gate_up_input),
                gu_map,
                down_in,
                pick(adapter_down_output),
            ),
        )
        norm_sum, ffn_sum, share, gu_got, down_got, q_got, kv_got = back_all(
            seq_size,
            (
                grad_attn,
                query,
                keys2,
                values2,
                keys_t,
                log_totals,
                seg_row,
                seg_col,
                jnp.asarray(np.ascontiguousarray(cos_fixed.T)),
                jnp.asarray(np.ascontiguousarray(sin_fixed.T)),
                cos_n,
                sin_n,
                qkv.reshape(width, -1),
                qkv_in,
                low_map,
                low_t,
                norm_one.reshape(length, width),
                ffn_part,
                early,
                gu_grad,
                down_grad,
                owners,
            ),
        )
        mixed = (middle + RESIDUAL_SCALE * ffn_sum).astype(BF16)
        grad_hidden = grad_middle + rms_back(hidden[0].astype(F32), attention_norm_gain, norm_sum)
        lower = lax.axis_index("dp") < dp_size // 2
        kv_got = jnp.where(lower, kv_got[:, :, rank : 2 * rank], kv_got[:, :, 2 * rank : 3 * rank])
        share_t = jnp.swapaxes(share, 1, 2)
        return (
            mixed[None],
            grad_hidden.astype(BF16)[None],
            share[:, :, : 3 * rank],
            jnp.swapaxes(q_got[:, :, :rank], 1, 2),
            jnp.swapaxes(kv_got, 1, 2),
            share[:, :, 3 * rank : 4 * rank],
            share_t[:, 4 * rank : 5 * rank],
            share[:, :, 5 * rank : 7 * rank],
            gu_got,
            jnp.swapaxes(down_got, 1, 2),
            share_t[:, 7 * rank :],
        )

    return local


def solution(mesh):
    both = ("dp", "seq")
    tokens = P("dp", "seq", None)
    weight = P(both, None)
    in_specs = (
        (tokens, P("dp", "seq"), P("dp"), tokens, P(), P()) + (weight,) * 7 + (P(),) * 9
    )
    by_row, by_column = P(None, both, None), P(None, None, both)
    out_specs = (
        tokens,
        tokens,
        by_row,
        by_column,
        by_column,
        by_row,
        by_column,
        by_row,
        by_column,
        by_row,
        by_column,
    )
    dp_size, seq_size = mesh.shape["dp"], mesh.shape["seq"]
    if dp_size == 4 and seq_size == KVH:
        local = make_kernel_local(dp_size, seq_size)
    else:
        local = make_local(dp_size, seq_size)
    return jax.shard_map(local, mesh=mesh, in_specs=in_specs, out_specs=out_specs, check_vma=False)
```

```python
import functools
import math

import jax
import jax.numpy as jnp
import numpy as np
from jax import lax
from jax.experimental import pallas as pl
from jax.experimental.pallas import tpu as pltpu
from jax.sharding import PartitionSpec as P

NH = 32
KVH = 8
HD = 64

EPSILON = 1e-05
RESIDUAL_SCALE = 0.22
SCORE_SCALE = 1.0 / 64.0
ROPE_BASE = 10000000.0
BF16 = jnp.bfloat16
F32 = jnp.float32


def mm(a, b):
    return jnp.dot(a, b, preferred_element_type=F32)


def mm_t(a, b):
    return lax.dot_general(a, b, (((1,), (1,)), ((), ())), preferred_element_type=F32)


def t_mm(a, b):
    return lax.dot_general(a, b, (((0,), (0,)), ((), ())), preferred_element_type=F32)


def rms_scale(values, gain):
    mean_square = jnp.mean(values * values, axis=-1, keepdims=True)
    return values * lax.rsqrt(mean_square + EPSILON) * gain


def rms_back(values, gain, grad):
    r = lax.rsqrt(jnp.mean(values * values, axis=-1, keepdims=True) + EPSILON)
    z = grad * gain
    return r * z - r * r * r * values * jnp.mean(z * values, axis=-1, keepdims=True)


def angle_tables(positions, head_size):
    steps = jnp.arange(head_size // 2).astype(F32)
    frequency = jnp.exp(steps * (-2.0 * math.log(ROPE_BASE) / head_size))
    angles = positions[:, None] * frequency[None, :]
    return (jnp.cos(angles), jnp.sin(angles))


def fixed_tables(length):
    steps = np.arange(HD // 2, dtype=np.float32)
    frequency = np.exp(steps * np.float32(-2.0 * math.log(ROPE_BASE) / HD))
    angles = np.arange(length, dtype=np.float32)[:, None] * frequency[None, :]
    return (np.cos(angles), np.sin(angles))


def rotate(values, cos_table, sin_table):
    half_width = values.shape[-1] // 2
    first_half = values[..., :half_width]
    second_half = values[..., half_width:]
    cos_part = cos_table[:, None, :]
    sin_part = sin_table[:, None, :]
    return jnp.concatenate(
        [
            first_half * cos_part - second_half * sin_part,
            second_half * cos_part + first_half * sin_part,
        ],
        axis=-1,
    )


def masked_scores(query_block, keys, seg_block, segments, start_row):
    key_pos = jnp.arange(keys.shape[0], dtype=jnp.int32)
    query_pos = start_row + jnp.arange(query_block.shape[0], dtype=jnp.int32)
    scores = jnp.einsum("qhd,kd->hqk", query_block, keys, preferred_element_type=F32) * SCORE_SCALE
    allowed = (key_pos[None, :] <= query_pos[:, None]) & (seg_block[:, None] == segments[None, :])
    return jnp.where(allowed[None], scores, -1e30)


def attend_forward(query, keys, values, segments):
    length, heads, head_size = query.shape
    rows = min(512, length)

    def one_block(index):
        start = index * rows
        query_block = lax.dynamic_slice_in_dim(query, start, rows, 0)
        seg_block = lax.dynamic_slice_in_dim(segments, start, rows, 0)
        scores = masked_scores(query_block, keys, seg_block, segments, start)
        row_max = jnp.max(scores, axis=-1, keepdims=True)
        weights = jnp.exp(scores - row_max)
        totals = jnp.sum(weights, axis=-1, keepdims=True)
        low = (weights / totals).astype(BF16)
        output = jnp.einsum("hqk,kd->qhd", low, values, preferred_element_type=F32)
        return (output.astype(BF16), (row_max + jnp.log(totals))[..., 0])

    outputs, log_totals = lax.map(one_block, jnp.arange(length // rows, dtype=jnp.int32))
    return (outputs.reshape(length, heads * head_size), log_totals)


def attend_backward(query, keys, values, segments, log_totals, grad):
    length, heads, head_size = query.shape
    rows = min(512, length)

    def one_block(carry, index):
        grad_keys, grad_values = carry
        start = index * rows
        query_block = lax.dynamic_slice_in_dim(query, start, rows, 0)
        seg_block = lax.dynamic_slice_in_dim(segments, start, rows, 0)
        grad_block = lax.dynamic_slice_in_dim(grad, start, rows, 0)
        scores = masked_scores(query_block, keys, seg_block, segments, start)
        weights = jnp.exp(scores - log_totals[index][..., None])
        grad_weights = jnp.einsum("qhd,kd->hqk", grad_block, values, preferred_element_type=F32)
        row_dot = jnp.sum(weights * grad_weights, axis=-1, keepdims=True)
        grad_scores = (weights * (grad_weights - row_dot)).astype(BF16)
        grad_query = jnp.einsum("hqk,kd->qhd", grad_scores, keys, preferred_element_type=F32)
        grad_keys = grad_keys + jnp.einsum(
            "hqk,qhd->kd", grad_scores, query_block, preferred_element_type=F32
        )
        grad_values = grad_values + jnp.einsum(
            "hqk,qhd->kd", weights.astype(BF16), grad_block, preferred_element_type=F32
        )
        return ((grad_keys, grad_values), (grad_query * SCORE_SCALE).astype(BF16))

    zero = jnp.zeros(keys.shape, F32)
    (grad_keys, grad_values), grad_query = lax.scan(
        one_block, (zero, zero), jnp.arange(length // rows, dtype=jnp.int32)
    )
    return (grad_query.reshape(length, heads, head_size), grad_keys * SCORE_SCALE, grad_values)


def make_local(dp_size, seq_size):
    devices = dp_size * seq_size
    heads = NH // seq_size
    kv_repeat = max(1, seq_size // KVH)

    def local(
        hidden,
        token_document_numbers,
        sequence_adapter_index,
        cotangent,
        attention_norm_gain,
        feedforward_norm_gain,
        query_weight,
        key_weight,
        value_weight,
        attention_output_weight,
        gate_weight,
        up_weight,
        down_weight,
        adapter_query_key_value_input,
        adapter_query_output,
        adapter_key_value_output,
        adapter_projection_input,
        adapter_projection_output,
        adapter_gate_up_input,
        adapter_gate_up_output,
        adapter_down_input,
        adapter_down_output,
    ):
        tokens, width = hidden.shape[1:]
        length = tokens * seq_size
        rows = query_weight.shape[0]
        key_width = key_weight.shape[1]
        ff_width = gate_weight.shape[1]
        ff_block = ff_width // devices
        rank = adapter_projection_input.shape[2]
        adapters = adapter_projection_input.shape[0]
        me = lax.axis_index("seq")
        q_width = heads * HD

        def across(piece):
            return lax.all_to_all(piece, "seq", split_axis=0, concat_axis=0, tiled=True)

        def gather_dp(block):
            return lax.all_gather(block, "dp", axis=0, tiled=True)

        def gather_seq(block):
            return lax.all_gather(block, "seq", axis=0, tiled=True)

        def scatter_seq(total):
            return lax.psum_scatter(total, "seq", scatter_dimension=0, tiled=True)

        def by_owner(columns):
            return columns.reshape(columns.shape[0], dp_size, seq_size, ff_block)

        hidden_own = hidden[0].astype(F32)
        hidden_all = gather_seq(hidden[0])
        segments = gather_seq(token_document_numbers[0])
        kv = jnp.stack([key_weight.reshape(rows, KVH, HD), value_weight.reshape(rows, KVH, HD)], 2)
        kv = jnp.repeat(kv.reshape(rows, KVH, 2 * HD), kv_repeat, axis=1)
        qkv = jnp.concatenate([query_weight.reshape(rows, seq_size, q_width), kv], axis=2)
        qkv = across(jnp.swapaxes(qkv, 0, 1)).reshape(seq_size * rows, q_width + 2 * HD)
        qkv = gather_dp(qkv)
        gate_up = jnp.concatenate([by_owner(gate_weight), by_owner(up_weight)], axis=1)
        gate_up = across(jnp.transpose(gate_up, (2, 0, 1, 3)))
        gate_up = gather_dp(gate_up.reshape(seq_size * rows, 2 * dp_size * ff_block))
        down = gather_dp(down_weight)
        out_full = lax.all_gather(attention_output_weight, ("dp", "seq"), axis=0, tiled=True)
        ff_own = dp_size * ff_block

        adapter = sequence_adapter_index[0]
        qkv_in = adapter_query_key_value_input[adapter]
        q_out = lax.dynamic_slice_in_dim(adapter_query_output[adapter], me * q_width, q_width, 1)
        kv_out = adapter_key_value_output[adapter]
        kv_start = (me // kv_repeat) * HD
        k_out = lax.dynamic_slice_in_dim(kv_out, kv_start, HD, 1)
        v_out = lax.dynamic_slice_in_dim(kv_out, key_width + kv_start, HD, 1)
        o_in = adapter_projection_input[adapter]
        o_out = adapter_projection_output[adapter]
        gu_in = adapter_gate_up_input[adapter]
        gu_all = adapter_gate_up_output[adapter].reshape(rank, 2, dp_size, seq_size, ff_block)
        gu_out = lax.dynamic_index_in_dim(gu_all, me, 3, keepdims=False)
        g_out, u_out = gu_out[:, 0].reshape(rank, ff_own), gu_out[:, 1].reshape(rank, ff_own)
        down_all = adapter_down_input[adapter].reshape(dp_size, seq_size, ff_block, rank)
        down_in = lax.dynamic_index_in_dim(down_all, me, 1, keepdims=False).reshape(ff_own, rank)
        down_out = adapter_down_output[adapter]

        norm_one = rms_scale(hidden_all.astype(F32), attention_norm_gain).astype(BF16)
        low_qkv = mm(norm_one, qkv_in).astype(BF16)
        pre = mm(norm_one, qkv)
        query_pre = pre[:, :q_width] + mm(low_qkv[:, :rank], q_out)
        key_pre = pre[:, q_width : q_width + HD] + mm(low_qkv[:, rank : 2 * rank], k_out)
        value_pre = pre[:, q_width + HD :] + mm(low_qkv[:, 2 * rank :], v_out)
        cos_table, sin_table = angle_tables(jnp.arange(length, dtype=jnp.int32).astype(F32), HD)
        query = rotate(query_pre.reshape(length, heads, HD), cos_table, sin_table).astype(BF16)
        keys = rotate(key_pre.reshape(length, 1, HD), cos_table, sin_table).astype(BF16)[:, 0]
        values = value_pre.astype(BF16)
        attn_heads, log_totals = attend_forward(query, keys, values, segments)
        attn = lax.all_gather(attn_heads, "seq", axis=1, tiled=True)
        low_out = mm(attn, o_in).astype(BF16)
        branch = mm(attn, out_full) + mm(low_out, o_out)
        middle = hidden_all.astype(F32) + RESIDUAL_SCALE * branch
        own_row = me * tokens
        middle_own = lax.dynamic_slice_in_dim(middle, own_row, tokens, 0)
        norm_two = rms_scale(middle, feedforward_norm_gain).astype(BF16)
        low_gu = mm(norm_two, gu_in).astype(BF16)
        wide = mm(norm_two, gate_up)
        gate = wide[:, :ff_own] + mm(low_gu[:, :rank], g_out)
        up_proj = wide[:, ff_own:] + mm(low_gu[:, rank:], u_out)
        sigma = jax.nn.sigmoid(gate)
        activation = (gate * sigma * up_proj).astype(BF16)
        low_down = mm(activation, down_in).astype(BF16)
        ffn = scatter_seq((mm(activation, down) + mm(low_down, down_out)).astype(BF16))
        mixed = (middle_own + RESIDUAL_SCALE * ffn.astype(F32)).astype(BF16)

        grad_ffn = gather_seq((RESIDUAL_SCALE * cotangent[0].astype(F32)).astype(BF16))
        grad_low_down = mm_t(grad_ffn, down_out).astype(BF16)
        grad_act = mm_t(grad_ffn, down) + mm_t(grad_low_down, down_in)
        grad_gate = (grad_act * up_proj * sigma * (1.0 + gate * (1.0 - sigma))).astype(BF16)
        grad_up = (grad_act * gate * sigma).astype(BF16)
        grad_low_gu = jnp.concatenate([mm_t(grad_gate, g_out), mm_t(grad_up, u_out)], axis=1)
        grad_low_gu = grad_low_gu.astype(BF16)
        grad_norm_two = scatter_seq(
            (
                mm_t(jnp.concatenate([grad_gate, grad_up], axis=1), gate_up)
                + mm_t(grad_low_gu, gu_in)
            ).astype(BF16)
        )
        grad_middle = cotangent[0].astype(F32) + rms_back(
            middle_own, feedforward_norm_gain, grad_norm_two.astype(F32)
        )
        grad_branch = (RESIDUAL_SCALE * grad_middle).astype(BF16)
        grad_low_out = mm_t(grad_branch, o_out).astype(BF16)
        grad_attn = (mm_t(grad_branch, out_full) + mm_t(grad_low_out, o_in)).astype(BF16)
        grad_heads = lax.all_to_all(
            jnp.swapaxes(grad_attn.reshape(tokens, seq_size, q_width), 0, 1),
            "seq",
            split_axis=0,
            concat_axis=0,
            tiled=True,
        ).reshape(length, heads, HD)
        grad_q, grad_k, grad_v = attend_backward(
            query, keys, values, segments, log_totals, grad_heads
        )
        grad_query = rotate(grad_q.astype(F32), cos_table, -sin_table)
        grad_query = grad_query.reshape(length, q_width).astype(BF16)
        grad_key = rotate(grad_k[:, None], cos_table, -sin_table)[:, 0].astype(BF16)
        grad_value = grad_v.astype(BF16)
        grad_low_qkv = jnp.concatenate(
            [mm_t(grad_query, q_out), mm_t(grad_key, k_out), mm_t(grad_value, v_out)], axis=1
        ).astype(BF16)
        grad_qkv = jnp.concatenate([grad_query, grad_key, grad_value], axis=1)
        grad_norm_one = scatter_seq((mm_t(grad_qkv, qkv) + mm_t(grad_low_qkv, qkv_in)).astype(BF16))
        grad_hidden = grad_middle + rms_back(
            hidden_own, attention_norm_gain, grad_norm_one.astype(F32)
        )

        attn_own = lax.dynamic_slice_in_dim(attn, own_row, tokens, 0)
        low_out_own = lax.dynamic_slice_in_dim(low_out, own_row, tokens, 0)
        partial = jnp.concatenate(
            [
                t_mm(norm_one, grad_low_qkv),
                t_mm(attn_own, grad_low_out),
                t_mm(grad_branch, low_out_own),
                t_mm(norm_two, grad_low_gu),
                t_mm(grad_ffn, low_down),
            ],
            axis=1,
        ).reshape(dp_size, seq_size, rows, 8 * rank)
        own_q = t_mm(grad_query, low_qkv[:, :rank])
        own_k = t_mm(grad_key, low_qkv[:, rank : 2 * rank])
        own_v = t_mm(grad_value, low_qkv[:, 2 * rank :])
        own_g = t_mm(grad_gate, low_gu[:, :rank]).reshape(dp_size, ff_block, rank)
        own_u = t_mm(grad_up, low_gu[:, rank:]).reshape(dp_size, ff_block, rank)
        own_d = t_mm(activation, grad_low_down).reshape(dp_size, ff_block, rank)

        def placed(block, total, start, axis):
            empty = list(block.shape)
            empty[axis] = total
            return lax.dynamic_update_slice_in_dim(jnp.zeros(empty, F32), block, start, axis)

        def by_target(whole):
            return whole.reshape(dp_size, seq_size, -1)

        full_q = placed(own_q, width, me * q_width, 0)
        full_kv = jnp.concatenate(
            [placed(own_k, key_width, kv_start, 0), placed(own_v, key_width, kv_start, 0)], axis=0
        )
        spot = [placed(v[:, None], seq_size, me, 1) for v in (own_g, own_u, own_d)]
        full_gu = jnp.concatenate([spot[0].reshape(ff_width, rank), spot[1].reshape(ff_width, rank)])
        pieces = [by_target(v) for v in (partial, full_q, full_kv, full_gu, spot[2])]
        send = jnp.concatenate(pieces, axis=2)
        send = jnp.swapaxes(send, 0, 1).reshape(seq_size, -1)
        mine = lax.psum_scatter(send, "seq", scatter_dimension=0, tiled=True)
        mine = lax.all_to_all(
            mine.reshape(dp_size, -1), "dp", split_axis=0, concat_axis=0, tiled=True
        )
        owners = lax.all_gather(sequence_adapter_index, "dp", axis=0, tiled=True)
        numbers = jnp.arange(adapters, dtype=jnp.int32)
        chooser = (owners[:, None] == numbers[None, :]).astype(F32)
        mine = jnp.einsum("sa,si->ai", chooser, mine, precision=lax.Precision.HIGHEST)
        sizes = [v.shape[2] for v in pieces]
        cuts = [sum(sizes[:i]) for i in range(1, len(sizes))]
        got, got_q, got_kv, got_gu, got_d = jnp.split(mine, cuts, axis=1)
        got = got.reshape(adapters, rows, 8 * rank)

        def turned(flat):
            return jnp.swapaxes(flat.reshape(adapters, -1, rank), 1, 2)

        return (
            mixed[None],
            grad_hidden.astype(BF16)[None],
            got[:, :, : 3 * rank],
            turned(got_q),
            turned(got_kv),
            got[:, :, 3 * rank : 4 * rank],
            jnp.swapaxes(got[:, :, 4 * rank : 5 * rank], 1, 2),
            got[:, :, 5 * rank : 7 * rank],
            turned(got_gu),
            got_d.reshape(adapters, ff_block, rank),
            jnp.swapaxes(got[:, :, 7 * rank :], 1, 2),
        )

    return local


MESH = pl.DeviceIdType.MESH


def remote(src, dst, send_sem, recv_sem, device):
    return pltpu.make_async_remote_copy(
        src_ref=src,
        dst_ref=dst,
        send_sem=send_sem,
        recv_sem=recv_sem,
        device_id=device,
        device_id_type=MESH,
    )


class Place:
    def __init__(self, seq_size):
        self.d = lax.axis_index("dp")
        self.s = lax.axis_index("seq")
        self.seq_size = seq_size
        self.chips = seq_size // 2
        self.z = self.s // 2
        self.c = self.s % 2
        self.dx = self.d + 1 - 2 * (self.d % 2)
        self.dy = lax.rem(self.d + 2, 4)
        self.dd = lax.rem(self.dx + 2, 4)
        self.sib = self.s + 1 - 2 * self.c

    def seq(self, s):
        return (self.d, s)

    def dp(self, d):
        return (d, self.s)

    def peer(self, step):
        return lax.rem(self.s + step, self.seq_size)

    def greet(self, seq_steps, dp_peers):
        barrier = pltpu.get_barrier_semaphore()
        for step in seq_steps:
            pl.semaphore_signal(
                barrier, 1, device_id=self.seq(self.peer(step)), device_id_type=MESH
            )
        for d in dp_peers:
            pl.semaphore_signal(barrier, 1, device_id=self.dp(d), device_id_type=MESH)
        pl.semaphore_wait(barrier, len(seq_steps) + len(dp_peers))


class Chain:
    def __init__(self, place, own, slot, sems):
        self.p, self.own, self.slot = place, own, slot
        self.up, self.down, self.side, self.got = (sems.at[i] for i in range(4))

    def _up(self, src, i):
        return remote(src, self.slot(i), self.up.at[i], self.got.at[i], self.p.seq(self.p.s + 2))

    def _down(self, src, i):
        return remote(src, self.slot(i), self.down.at[i], self.got.at[i], self.p.seq(self.p.s - 2))

    def _side(self, src, i):
        return remote(src, self.slot(i), self.side.at[i], self.got.at[i], self.p.seq(self.p.sib))

    def start(self):
        p = self.p

        @pl.when(p.z < p.chips - 1)
        def _():
            self._up(self.own, p.s).start()

        @pl.when(p.z > 0)
        def _():
            self._down(self.own, p.s).start()

        self._side(self.own, p.s).start()

    def step(self, k):
        p = self.p
        low, high = p.s - 2 * k, p.s + 2 * k

        @pl.when(p.z >= k)
        def _():
            self._side(self.slot(low), low).wait_recv()

            @pl.when(p.z < p.chips - 1)
            def _():
                self._up(self.slot(low), low).start()

            self._side(self.slot(low), low).start()

        @pl.when(p.z + k < p.chips)
        def _():
            self._side(self.slot(high), high).wait_recv()

            @pl.when(p.z > 0)
            def _():
                self._down(self.slot(high), high).start()

            self._side(self.slot(high), high).start()

    def side_recv(self, z):
        other = 2 * z + 1 - self.p.c
        self._side(self.slot(other), other).wait_recv()

    def finish(self):
        p = self.p

        @pl.when(p.z < p.chips - 1)
        def _():
            self._up(self.own, p.s).wait_send()

        @pl.when(p.z > 0)
        def _():
            self._down(self.own, p.s).wait_send()

        self._side(self.own, p.s).wait_send()
        for k in range(1, p.chips):
            low, high = p.s - 2 * k, p.s + 2 * k

            @pl.when(p.z >= k)
            def _():
                @pl.when(p.z < p.chips - 1)
                def _():
                    self._up(self.slot(low), low).wait_send()

                self._side(self.slot(low), low).wait_send()

            @pl.when(p.z + k < p.chips)
            def _():
                @pl.when(p.z > 0)
                def _():
                    self._down(self.slot(high), high).wait_send()

                self._side(self.slot(high), high).wait_send()


class Chains:
    def __init__(self, place, own, slot, rows, sems, parts=2):
        size = rows // parts
        self.all = [
            Chain(
                place,
                own.at[pl.ds(size * i, size)],
                lambda n, i=i: slot(n).at[pl.ds(size * i, size)],
                sems.at[i],
            )
            for i in range(parts)
        ]

    def start(self):
        for chain in self.all:
            chain.start()

    def step(self, k):
        for chain in self.all:
            chain.step(k)

    def side_recv(self, z):
        for chain in self.all:
            chain.side_recv(z)

    def finish(self):
        for chain in self.all:
            chain.finish()


class Plane:
    def __init__(self, place, block, half, sems):
        self.p, self.block, self.half, self.sems = place, block, half, sems

    def _copy(self, ref, i, d):
        return remote(ref, ref, self.sems.at[0, i], self.sems.at[1, i], self.p.dp(d))

    def _all(self):
        p = self.p
        return (
            (self.block(p.d), p.dx),
            (self.block(p.d), p.dy),
            (self.half(p.dx, 0), p.dy),
            (self.half(p.dy, 1), p.dx),
        )

    def start(self):
        for i, (ref, d) in enumerate(self._all()[:2]):
            self._copy(ref, i, d).start()

    def forward(self):
        p = self.p
        everything = self._all()
        for i, came in ((0, p.dx), (1, p.dy)):
            self._copy(self.block(came), i, came).wait_recv()
            ref, d = everything[2 + i]
            self._copy(ref, 2 + i, d).start()

    def recv(self):
        p = self.p
        self._copy(self.half(p.dd, 0), 2, p.dy).wait_recv()
        self._copy(self.half(p.dd, 1), 3, p.dx).wait_recv()

    def finish(self):
        for i, (ref, d) in enumerate(self._all()):
            self._copy(ref, i, d).wait_send()


class Spread:
    def __init__(self, place, pairs, whole, send_sem, recv_sem):
        self.p, self.pairs, self.whole = place, pairs, whole
        self.send_sem, self.recv_sem = send_sem, recv_sem

    def start(self):
        p = self.p
        for step in (1, 2, 3, 4, 5, 6, 7):
            j = p.peer(step)
            for src, dst in self.pairs(j):
                remote(src, dst, self.send_sem, self.recv_sem, p.seq(j)).start()

    def recv(self):
        p = self.p
        for whole in self.whole:
            remote(whole, whole, self.send_sem, self.recv_sem, p.seq(p.sib)).wait_recv()

    def finish(self):
        p = self.p
        for whole in self.whole:
            remote(whole, whole, self.send_sem, self.recv_sem, p.seq(p.sib)).wait_send()


PIECES = 4
QB = 256


def front_kernel(
    seq_size,
    hidden,
    numbers,
    query_w,
    kv_w,
    out_w,
    gate_w,
    up_w,
    gain,
    maps,
    cos_n,
    sin_n,
    hidden_all,
    adapters_all,
    qkv_all,
    out_all,
    gu_all,
    attn_all,
    norm_all,
    query,
    keys2,
    values2,
    keys_t,
    log_totals,
    seg_row,
    seg_col,
    low_t,
    documents_all,
    chain_sems,
    plane_sems,
    local_sems,
    spread_sems,
    small_sems,
    side_sems,
    hidden_v,
    norm_v,
    out_v,
    qkv_v,
    gu_v,
    weights_v,
    key_z,
    values_t,
    bias,
    attn_v,
):
    p = Place(seq_size)
    d, s, z, c = p.d, p.s, p.z, p.c
    rows = query_w.shape[0]
    documents, adapter_row = numbers.at[0], numbers.at[1]
    low_rows = maps.shape[0] // 2
    qkv_in = maps.at[pl.ds(0, low_rows)]
    part = gate_w.shape[1] // (4 * seq_size)
    tokens = hidden.shape[0]
    half_rows = seq_size * rows // 2
    landing = pl.ds(pl.multiple_of(rows * s, rows), rows)
    q_width = query_w.shape[1] // seq_size
    low_map = maps.at[pl.ds(low_rows, low_rows), pl.ds(0, qkv_v.shape[1])]

    def column_block(number, size):
        return pl.ds(pl.multiple_of(number * size, size), size)

    stage = [
        (hidden, hidden_v.at[s]),
        (out_w, out_v),
        (query_w.at[:, column_block(s, q_width)], qkv_v.at[:, pl.ds(0, q_width)]),
        (kv_w.at[s], qkv_v.at[:, pl.ds(q_width, kv_w.shape[2])]),
        (documents, documents_all.at[s]),
        (adapter_row, adapters_all.at[d]),
    ]
    for i in range(8):
        matrix = (gate_w, up_w)[i // 4]
        block = matrix.at[:, column_block(seq_size * (i % 4) + s, part)]
        stage.append((block, gu_v.at[:, pl.ds(part * i, part)]))
    stage = [
        pltpu.make_async_copy(src, dst, local_sems.at[0, i]) for i, (src, dst) in enumerate(stage)
    ]
    keep = [
        pltpu.make_async_copy(src, dst, local_sems.at[1, i])
        for i, (src, dst) in enumerate(
            (
                (out_v, out_all.at[d, z, c]),
                (qkv_v, qkv_all.at[d, landing]),
                (gu_v, gu_all.at[d, landing]),
                (qkv_all, weights_v),
                (hidden_v, hidden_all),
                (norm_v, norm_all),
                (attn_v, attn_all.at[s]),
            )
        )
    ]
    for copy in stage:
        copy.start()
    p.greet(range(1, seq_size), (p.dx, p.dy, p.dd))

    hid = Chains(p, hidden, lambda i: hidden_v.at[i], tokens, chain_sems.at[0])
    out = Chain(p, out_w, lambda i: out_all.at[d, i // 2, i % 2], chain_sems.at[1, 0])
    att = Chains(p, attn_v, lambda i: attn_all.at[i], attn_v.shape[0], chain_sems.at[2])

    def qkv_pairs(j):
        return (
            (query_w.at[:, column_block(j, q_width)], qkv_all.at[d, landing, pl.ds(0, q_width)]),
            (kv_w.at[j], qkv_all.at[d, landing, pl.ds(q_width, kv_w.shape[2])]),
        )

    def gu_pairs(piece):
        matrix = (gate_w, up_w)[piece // 2]

        def pairs(j):
            found = []
            for block in (2 * (piece % 2), 2 * (piece % 2) + 1):
                at = part * (4 * (piece // 2) + block)
                source = matrix.at[:, column_block(seq_size * block + j, part)]
                found.append((source, gu_all.at[d, landing, pl.ds(at, part)]))
            return found

        return pairs

    others = pl.ds(0, rows * (seq_size - 1))
    qkv = Spread(
        p, qkv_pairs, [qkv_all.at[d, others]], spread_sems.at[0, 0], spread_sems.at[0, 1]
    )
    gu = []
    gu_planes = []
    for i in range(PIECES):
        cut = pl.ds(2 * part * i, 2 * part)
        gu.append(
            Spread(
                p, gu_pairs(i), [gu_all.at[d, others, cut]], spread_sems.at[1 + i, 0],
                spread_sems.at[1 + i, 1],
            )
        )
        gu_planes.append(
            Plane(
                p,
                lambda e, cut=cut: gu_all.at[e, :, cut],
                lambda e, h, cut=cut: gu_all.at[e, pl.ds(half_rows * h, half_rows), cut],
                plane_sems.at[3 + i],
            )
        )
    qkv_plane = Plane(
        p,
        lambda e: qkv_all.at[e],
        lambda e, h: qkv_all.at[e, pl.ds(half_rows * h, half_rows)],
        plane_sems.at[0],
    )
    half_chips = p.chips // 2
    out_plane = Plane(
        p,
        lambda e: out_all.at[e, :, c],
        lambda e, h: out_all.at[e, pl.ds(half_chips * h, half_chips), c],
        plane_sems.at[2],
    )

    def documents_copy(step):
        return remote(
            documents, documents_all.at[s], small_sems.at[0, step], small_sems.at[1, 0],
            p.seq(p.peer(step)),
        )

    def adapters_copy(i, e):
        return remote(
            adapter_row, adapters_all.at[d], small_sems.at[2, i], small_sems.at[3, 0], p.dp(e)
        )

    def side_copy(i, e):
        ref = out_all.at[e, :, c]
        return remote(ref, ref, side_sems.at[0, i], side_sems.at[1, i], p.seq(p.sib))

    def side_wait(i, e):
        ref = out_all.at[e, :, 1 - c]
        remote(ref, ref, side_sems.at[0, i], side_sems.at[1, i], p.seq(p.sib)).wait_recv()

    low_lane = lax.broadcasted_iota(jnp.int32, (tokens, 2 * HD), 1) < HD
    weights = weights_v.reshape(4 * seq_size * rows, qkv_v.shape[1])

    def process(slot):
        at = pl.ds(pl.multiple_of(slot * tokens, tokens), tokens)
        cos_part, sin_part = cos_n[at, :], sin_n[at, :]
        normed = rms_scale(hidden_v[slot].astype(F32), gain[...]).astype(BF16)
        norm_v[slot] = normed
        low = dot_nt(normed, qkv_in[...]).astype(BF16)
        pre = dot_nn(normed, weights[...]) + dot_nn(low, low_map[...])
        padded = jnp.concatenate(
            [low.astype(F32), jnp.zeros((tokens, 128 - low.shape[1]), F32)], axis=1
        )
        low_t[:, at] = padded.T[: low.shape[1]].astype(BF16)
        for m in range(2):
            pair = pre[:, 2 * HD * m : 2 * HD * (m + 1)]
            turned = pair * cos_part + swap_halves(pair) * sin_part
            query[at, pl.ds(2 * HD * m, 2 * HD)] = turned.astype(BF16)
        pair = pre[:, 4 * HD :]
        turned = pair * cos_part + swap_halves(pair) * sin_part
        both = jnp.where(low_lane, turned, pair)
        crossed = pltpu.roll(both, HD, 1)
        keys2[at, :] = jnp.where(low_lane, both, crossed).astype(BF16)
        values2[at, :] = jnp.where(low_lane, crossed, both).astype(BF16)
        zero = jnp.zeros_like(both)
        key_z[0, at, :] = jnp.where(low_lane, both, zero).astype(BF16)
        key_z[1, at, :] = jnp.where(low_lane, zero, crossed).astype(BF16)
        both_t = both.T
        keys_t[:, at] = both_t[:HD].astype(BF16)
        values_t[:, at] = both_t[HD:].astype(BF16)

    def process_distance(k):
        @pl.when(p.z >= k)
        def _():
            hid.side_recv(p.z - k)

            @pl.loop(0, 2)
            def _(core):
                process(2 * (p.z - k) + core)

        if k:

            @pl.when(p.z + k < p.chips)
            def _():
                hid.side_recv(p.z + k)

                @pl.loop(0, 2)
                def _(core):
                    process(2 * (p.z + k) + core)

    def query_block(i):
        start = i * QB
        span = pl.ds(0, start + QB)
        at = pl.ds(start, QB)
        bias[span, :] = mask_bias(seg_col, seg_row, start, QB)

        for m in range(2):
            pair = pl.ds(2 * HD * m, 2 * HD)
            query_pair = query[at, pair]
            found = []
            for e in range(2):
                scores = dot_nt(key_z[e, span, :], query_pair) * SCORE_SCALE + bias[span, :]
                top = jnp.max(scores, axis=0, keepdims=True)
                raised = jnp.exp(scores - top)
                total = jnp.sum(raised, axis=0, keepdims=True)
                found.append(dot_nn(values_t[:, span], raised.astype(BF16)) / total)
                log_totals[2 * m + e : 2 * m + e + 1, at] = top + jnp.log(total)
            attn_v[at, pair] = jnp.concatenate(found, axis=0).T.astype(BF16)

    for step in range(1, seq_size):
        documents_copy(step).start()
    for i, e in enumerate((p.dx, p.dy, p.dd)):
        adapters_copy(i, e).start()
    qkv.start()
    out.start()
    hid.start()
    for copy in stage:
        copy.wait()
    for i in range(3):
        keep[i].start()
    for i in range(3):
        keep[i].wait()
    qkv.recv()
    qkv_plane.start()
    out.step(1)
    hid.step(1)
    out.step(2)
    remote(
        documents_all.at[pl.ds(0, seq_size - 1)], documents_all.at[pl.ds(0, seq_size - 1)],
        small_sems.at[0, 0], small_sems.at[1, 0], p.seq(p.sib),
    ).wait_recv()
    for slot in range(seq_size):
        at = pl.ds(tokens * slot, tokens)
        numbers = documents_all[slot].astype(F32)
        seg_row[:, at] = numbers
        seg_col[at, :] = jnp.broadcast_to(numbers[0:1, :], (tokens, tokens)).T
    qkv_plane.forward()
    out.step(3)
    out_plane.start()
    hid.step(2)
    gu[0].start()
    qkv_plane.recv()
    keep[3].start()
    keep[3].wait()
    process_distance(0)
    process_distance(1)
    out_plane.forward()
    side_copy(0, p.dx).start()
    side_copy(1, p.dy).start()
    hid.step(3)
    gu[1].start()
    gu[2].start()
    process_distance(2)
    process_distance(3)
    gu[0].recv()
    gu_planes[0].start()
    gu[3].start()
    out_plane.recv()
    side_copy(2, p.dd).start()
    keep[4].start()
    keep[5].start()
    query_block(0)
    query_block(1)
    gu[1].recv()
    gu_planes[1].start()
    gu_planes[0].forward()
    query_block(2)
    query_block(3)
    keep[6].start()
    att.start()
    gu[2].recv()
    gu_planes[2].start()
    gu_planes[1].forward()
    gu[3].recv()
    gu_planes[3].start()
    att.step(1)
    gu_planes[2].forward()
    att.step(2)
    gu_planes[3].forward()
    att.step(3)
    for i in range(4):
        gu_planes[i].recv()
    for chain in (out, att):
        for other in range(p.chips):
            chain.side_recv(other)
    for chain in (hid, out, att):
        chain.finish()
    for i, e in enumerate((p.dx, p.dy, p.dd)):
        side_wait(i, e)
    remote(
        adapters_all.at[pl.ds(0, 3)], adapters_all.at[pl.ds(0, 3)],
        small_sems.at[2, 3], small_sems.at[3, 0], p.dp(p.dx),
    ).wait_recv()
    for step in range(1, seq_size):
        documents_copy(step).wait_send()
    for i, e in enumerate((p.dx, p.dy, p.dd)):
        adapters_copy(i, e).wait_send()
        side_copy(i, e).wait_send()
    for group in [qkv, *gu, qkv_plane, out_plane, *gu_planes]:
        group.finish()
    for i in (4, 5, 6):
        keep[i].wait()


def front_all(seq_size, ins):
    tokens, width = ins[0].shape
    rows = ins[2].shape[0]
    part = ins[5].shape[1] // (4 * seq_size)
    chips = seq_size // 2
    q_width = ins[2].shape[1] // seq_size
    qkv_width = q_width + ins[3].shape[2]
    length = tokens * seq_size
    low_width = ins[8].shape[0] // 2

    def shape(*dims, dtype=BF16):
        return jax.ShapeDtypeStruct(dims, dtype)

    anywhere = pl.BlockSpec(memory_space=pl.ANY)
    vmem = pl.BlockSpec(memory_space=pltpu.VMEM)
    outs = (
        shape(seq_size, tokens, width),
        shape(4, 8, 128, dtype=jnp.int32),
        shape(4, seq_size * rows, qkv_width),
        shape(4, chips, 2, rows, width),
        shape(4, seq_size * rows, 8 * part),
        shape(seq_size, length, q_width),
        shape(seq_size, tokens, width),
        shape(length, q_width),
        shape(length, 2 * HD),
        shape(length, 2 * HD),
        shape(HD, length),
        shape(4, length, dtype=F32),
        shape(8, length, dtype=F32),
        shape(length, tokens, dtype=F32),
        shape(low_width, length),
    )
    return pl.pallas_call(
        functools.partial(front_kernel, seq_size),
        out_shape=outs,
        in_specs=[anywhere] * 7 + [vmem] * 4,
        out_specs=(anywhere,) * 7 + (vmem,) * 8,
        scratch_shapes=[
            pltpu.VMEM((seq_size, 8, tokens), jnp.int32),
            pltpu.SemaphoreType.DMA((3, 2, 4, seq_size)),
            pltpu.SemaphoreType.DMA((3 + PIECES, 2, 4)),
            pltpu.SemaphoreType.DMA((2, 16)),
            pltpu.SemaphoreType.DMA((1 + PIECES, 2)),
            pltpu.SemaphoreType.DMA((4, seq_size)),
            pltpu.SemaphoreType.DMA((2, 3)),
            pltpu.VMEM((seq_size, tokens, width), BF16),
            pltpu.VMEM((seq_size, tokens, width), BF16),
            pltpu.VMEM((rows, width), BF16),
            pltpu.VMEM((rows, qkv_width), BF16),
            pltpu.VMEM((rows, 8 * part), BF16),
            pltpu.VMEM((4, seq_size * rows, qkv_width), BF16),
            pltpu.VMEM((2, length, 2 * HD), BF16),
            pltpu.VMEM((HD, length), BF16),
            pltpu.VMEM((length, QB), F32),
            pltpu.VMEM((length, q_width), BF16),
        ],
        compiler_params=pltpu.CompilerParams(
            collective_id=0, has_side_effects=True, vmem_limit_bytes=60 * 2**20
        ),
        cost_estimate=pl.CostEstimate(
            flops=5 * 10**9, bytes_accessed=60 * 2**20, transcendentals=4 * 2**20
        ),
        name="attend_front",
    )(*ins)


def dot_nn(a, b):
    return lax.dot_general(a, b, (((1,), (0,)), ((), ())), preferred_element_type=F32)


def dot_nt(a, b):
    return lax.dot_general(a, b, (((1,), (1,)), ((), ())), preferred_element_type=F32)


class ChainSum:
    def __init__(self, place, part, side_in, up_in, down_in, sems, first, size):
        self.p, self.part = place, part
        self.first, self.size = first, size
        self.cut = pl.ds(first, size)
        self.side_in, self.up_in, self.down_in = side_in, up_in, down_in
        self.sems = sems

    def _side(self, z):
        p = self.p
        return remote(
            self.part.at[2 * z + 1 - p.c, self.cut], self.side_in.at[z, self.cut],
            self.sems.at[0, z], self.sems.at[1, z], p.seq(p.sib),
        )

    def _up(self, z):
        p = self.p
        return remote(
            self.part.at[2 * z + p.c, self.cut], self.up_in.at[z, self.cut],
            self.sems.at[2, z], self.sems.at[3, z], p.seq(p.s + 2),
        )

    def _down(self, z):
        p = self.p
        return remote(
            self.part.at[2 * z + p.c, self.cut], self.down_in.at[z, self.cut],
            self.sems.at[4, z], self.sems.at[5, z], p.seq(p.s - 2),
        )

    def _add(self, z, incoming):
        slot = 2 * z + self.p.c

        @pl.loop(0, self.size // 16)
        def _(i):
            cut = pl.ds(pl.multiple_of(self.first + i * 16, 16), 16)
            total = self.part[slot, cut].astype(F32) + incoming[z, cut].astype(F32)
            self.part[slot, cut] = total.astype(BF16)

    def side_start(self, z):
        self._side(z).start()

    def side_add(self, z):
        self._side(z).wait_recv()
        self._add(z, self.side_in)

    def step(self, k):
        p = self.p

        @pl.when(p.z + k < p.chips)
        def _():
            to = p.z + k
            self.side_add(to)

            @pl.when(p.z > 0)
            def _():
                self._up(to).wait_recv()
                self._add(to, self.up_in)

            self._up(to).start()

        @pl.when(p.z >= k)
        def _():
            to = p.z - k
            self.side_add(to)

            @pl.when(p.z < p.chips - 1)
            def _():
                self._down(to).wait_recv()
                self._add(to, self.down_in)

            self._down(to).start()

    def last(self):
        p = self.p
        self.side_add(p.z)

        @pl.when(p.z > 0)
        def _():
            self._up(p.z).wait_recv()
            self._add(p.z, self.up_in)

        @pl.when(p.z < p.chips - 1)
        def _():
            self._down(p.z).wait_recv()
            self._add(p.z, self.down_in)

    def finish(self):
        p = self.p
        for z in range(p.chips):
            self._side(z).wait_send()
        for k in range(1, p.chips):

            @pl.when(p.z + k < p.chips)
            def _():
                self._up(p.z + k).wait_send()

            @pl.when(p.z >= k)
            def _():
                self._down(p.z - k).wait_send()


class ChainSums:
    def __init__(self, place, part, side_in, up_in, down_in, sems, parts=2):
        size = part.shape[1] // parts
        self.all = [
            ChainSum(place, part, side_in, up_in, down_in, sems.at[i], size * i, size)
            for i in range(parts)
        ]

    def side_start(self, z):
        for chain in self.all:
            chain.side_start(z)

    def step(self, k):
        for chain in self.all:
            chain.step(k)

    def last(self):
        for chain in self.all:
            chain.last()

    def finish(self):
        for chain in self.all:
            chain.finish()


def chain_order(z):
    second = jnp.where(z == 0, 2, jnp.where(z == 1, 0, jnp.where(z == 2, 3, 1)))
    return (jnp.where(z < 2, 3, 0), second, jnp.where(z % 2 == 0, 1, 2), z)


def swap_halves(values):
    lane = lax.broadcasted_iota(jnp.int32, values.shape, 1)
    return jnp.where(
        lane % HD < HD // 2,
        pltpu.roll(values, values.shape[1] - HD // 2, 1),
        pltpu.roll(values, HD // 2, 1),
    )


def mask_bias(seg_col, seg_row, start, size):
    length = start + size
    key_pos = lax.broadcasted_iota(jnp.int32, (length, size), 0)
    query_pos = start + lax.broadcasted_iota(jnp.int32, (length, size), 1)
    same = seg_col[pl.ds(0, length), 0:1] == seg_row[0:1, pl.ds(start, size)]
    return jnp.where((key_pos <= query_pos) & same, 0.0, -1e30).astype(F32)


def back_kernel(
    seq_size,
    grad_attn,
    query,
    keys2,
    values2,
    keys_t,
    log_totals,
    seg_row,
    seg_col,
    cos_t,
    sin_t,
    cos_n,
    sin_n,
    qkv_w,
    maps,
    low_qkv_t,
    norm_one,
    ffn_part,
    early_t,
    gu_grad,
    down_grad,
    owners,
    norm_sum,
    ffn_sum,
    share_out,
    gu_out,
    down_out,
    q_out,
    kv_out,
    grads,
    key_z,
    value_z,
    key_acc,
    value_acc,
    bias,
    grad_qkv,
    grad_low,
    qkv_v,
    norm_v,
    ffn_v,
    ffn_side,
    ffn_up,
    ffn_down,
    sum_v,
    sum_side,
    sum_up,
    sum_down,
    share,
    share_in,
    turned,
    gu_in,
    down_in,
    q_got,
    kv_got,
    load_sems,
    swap_sems,
    ffn_sems,
    sum_sems,
    send_sems,
    got_sems,
):
    p = Place(seq_size)
    d, s = p.d, p.s
    length = query.shape[0]
    low_rows = maps.shape[0] // 2
    qkv_in = maps.at[pl.ds(0, low_rows)]
    low_map = maps.at[pl.ds(low_rows, low_rows), pl.ds(0, qkv_w.shape[1])]
    chips = p.chips
    loads = [
        pltpu.make_async_copy(src, dst, load_sems.at[i])
        for i, (src, dst) in enumerate(
            ((ffn_part, ffn_v), (qkv_w, qkv_v), (norm_one, norm_v), (grad_attn.at[s], grads.at[s]))
        )
    ]
    for copy in loads:
        copy.start()
    barrier = pltpu.get_barrier_semaphore()
    everyone = 4 * seq_size

    def place_of(t):
        return lax.rem(d + t // seq_size, 4), lax.rem(s + lax.rem(t, seq_size), seq_size)

    @pl.loop(1, everyone)
    def _(t):
        pl.semaphore_signal(barrier, 1, device_id=place_of(t), device_id_type=MESH)

    pl.semaphore_wait(barrier, everyone - 1)

    def swap_copy(step):
        return remote(
            grad_attn.at[p.peer(step)], grads.at[s], swap_sems.at[0, step], swap_sems.at[1, 0],
            p.seq(p.peer(step)),
        )

    for step in range(1, seq_size):
        swap_copy(step).start()

    def deliver(src, dst, td, ts, i, wait):
        here = (td == d) & (ts == s)

        @pl.when(jnp.logical_not(here))
        def _():
            copy = remote(src, dst, send_sems.at[i], got_sems.at[i], (td, ts))
            if wait:
                copy.wait_send()
            else:
                copy.start()

        if not wait:

            @pl.when(here)
            def _():
                pltpu.make_async_copy(src, dst, got_sems.at[i]).start()

    def ready(buffer, i):
        remote(buffer, buffer, send_sems.at[i], got_sems.at[i], p.seq(p.sib)).wait_recv()

    block = gu_grad.shape[1] // 8

    def deliver_wide(wait):
        side = pl.ds(pl.multiple_of(block * lax.rem(s, 2), block), block)
        for e in range(4):
            for upper in range(2):
                deliver(
                    gu_grad.at[:, pl.ds((4 * upper + e) * block, block)],
                    gu_in.at[d, :, side],
                    2 * upper + e // 2,
                    lax.rem(e, 2) * (seq_size // 2) + s // 2,
                    0,
                    wait,
                )
            deliver(down_grad.at[:, pl.ds(e * block, block)], down_in.at[d], e, s, 1, wait)

    def deliver_heads(wait):
        for i in range(4):
            m = 4 * s + i
            deliver(
                turned.at[pl.ds(HD * i, HD)], q_got.at[d], m // seq_size, lax.rem(m, seq_size), 2, wait
            )
        for i in range(4):
            m = 2 * seq_size * (i // 2) + 2 * s + i % 2
            deliver(
                turned.at[pl.ds(4 * HD + HD // 2 * i, HD // 2)],
                kv_got.at[d],
                m // seq_size,
                lax.rem(m, seq_size),
                3,
                wait,
            )

    def deliver_share(wait):
        rows = share.shape[0] // everyone

        @pl.loop(0, everyone)
        def _(t):
            td, ts = place_of(t)
            start = pl.multiple_of((td * seq_size + ts) * rows, rows)
            deliver(share.at[pl.ds(start, rows)], share_in.at[d, s], td, ts, 4, wait)

    ffn = ChainSums(p, ffn_v, ffn_side, ffn_up, ffn_down, ffn_sems)
    total = ChainSums(p, sum_v, sum_side, sum_up, sum_down, sum_sems)

    low_lane = lax.broadcasted_iota(jnp.int32, (length, 2 * HD), 1) < HD
    zero = jnp.zeros((length, 2 * HD), BF16)
    key_z[0] = jnp.where(low_lane, keys2[...], zero)
    key_z[1] = jnp.where(low_lane, zero, keys2[...])
    value_z[0] = jnp.where(low_lane, values2[...], zero)
    value_z[1] = jnp.where(low_lane, zero, values2[...])
    key_acc[...] = jnp.zeros_like(key_acc)
    value_acc[...] = jnp.zeros_like(value_acc)
    for copy in loads:
        copy.wait()
    for z in range(chips):
        ffn.side_start(z)
    remote(
        grads.at[pl.ds(0, seq_size - 1)], grads.at[pl.ds(0, seq_size - 1)],
        swap_sems.at[0, 0], swap_sems.at[1, 0], p.seq(p.sib),
    ).wait_recv()
    deliver_wide(False)
    ffn.step(3)

    def query_block(i):
        start = i * QB
        span = pl.ds(0, start + QB)
        rows = pl.ds(start, QB)
        bias[span, :] = mask_bias(seg_col, seg_row, start, QB)
        slots = QB // grads.shape[1]

        for m in range(2):
            pair = pl.ds(2 * HD * m, 2 * HD)
            query_pair = query[rows, pair]
            grad_pair = grads[pl.ds(slots * i, slots), :, pair].reshape(QB, 2 * HD)
            turned_q = []
            for e in range(2):
                h = 2 * m + e
                scores = dot_nt(key_z[e, span, :], query_pair)
                weights = jnp.exp(scores * SCORE_SCALE + bias[span, :] - log_totals[h : h + 1, rows])
                grad_weights = dot_nt(value_z[e, span, :], grad_pair)
                row_dot = jnp.sum(weights * grad_weights, axis=0, keepdims=True)
                grad_scores = (weights * (grad_weights - row_dot)).astype(BF16)
                key_acc[e, span, :] += dot_nn(grad_scores, query_pair)
                value_acc[e, span, :] += dot_nn(weights.astype(BF16), grad_pair)
                grad_q = dot_nn(keys_t[:, span], grad_scores) * SCORE_SCALE
                first, second = grad_q[: HD // 2], grad_q[HD // 2 :]
                cos_part, sin_part = cos_t[:, rows], sin_t[:, rows]
                turned_q.append(first * cos_part + second * sin_part)
                turned_q.append(second * cos_part - first * sin_part)
            grad_qkv[rows, pair] = jnp.concatenate(turned_q, axis=0).T.astype(BF16)

    query_block(0)
    query_block(1)
    query_block(2)
    ffn.step(2)
    query_block(3)

    def folded(acc):
        merged = jnp.where(low_lane, acc[0], acc[1])
        return merged + pltpu.roll(merged, HD, 1)

    grad_key = folded(key_acc) * SCORE_SCALE
    grad_key = grad_key * cos_n[...] - swap_halves(grad_key) * sin_n[...]
    grad_qkv[:, pl.ds(4 * HD, 2 * HD)] = jnp.where(low_lane, grad_key, folded(value_acc)).astype(BF16)
    grad_low[...] = dot_nt(grad_qkv[...], low_map[...]).astype(BF16)
    grad_low_t = dot_nt(low_map[...], grad_qkv[...]).astype(BF16)
    ffn.step(1)

    tokens = sum_v.shape[1]

    def give(to):
        rows = pl.ds(pl.multiple_of(2 * to * tokens, 2 * tokens), 2 * tokens)
        left, low = grad_qkv[rows, :], grad_low[rows, :]
        for j in range(4):
            cut = pl.ds(512 * j, 512)
            value = dot_nt(left, qkv_v[cut, :]) + dot_nn(low, qkv_in[:, cut])
            sum_v[2 * to, :, cut] = value[:tokens].astype(BF16)
            sum_v[2 * to + 1, :, cut] = value[tokens:].astype(BF16)
        total.side_start(to)

    order = chain_order(p.z)
    give(order[0])
    total.step(3)
    give(order[1])
    give(order[2])
    give(order[3])
    outer = dot_nn(low_qkv_t[...], grad_qkv[...])
    outer = jnp.concatenate([outer, jnp.zeros((80, outer.shape[1]), F32)], axis=0)
    turned[...] = outer.T
    deliver_heads(False)
    total.step(2)
    for j in range(8):
        cut = pl.ds(256 * j, 256)
        piece = jnp.concatenate([dot_nn(grad_low_t, norm_v[:, cut]), early_t[:, cut]], axis=0)
        share[cut, :] = piece.T.astype(BF16)
    deliver_share(False)
    total.step(1)
    ffn.last()
    ffn_sum[...] = ffn_v[s].astype(F32)
    for buffer, i in ((gu_in, 0), (down_in, 1), (q_got, 2), (kv_got, 3), (share_in, 4)):
        ready(buffer, i)

    def by_adapter(out, value):
        values = [value(e) for e in range(4)]
        for a in range(4):
            chosen = jnp.zeros_like(values[0])
            for e in range(4):
                chosen = jnp.where(owners[e, 0:1, 0:1] == a, values[e], chosen)
            out[a] = chosen

    by_adapter(gu_out, lambda e: gu_in[e])
    by_adapter(down_out, lambda e: down_in[e])
    by_adapter(q_out, lambda e: q_got[e])
    by_adapter(kv_out, lambda e: kv_got[e])
    by_adapter(share_out, lambda e: jnp.sum(share_in[e].astype(F32), axis=0))
    total.last()
    norm_sum[...] = sum_v[s].astype(F32)
    for step in range(1, seq_size):
        swap_copy(step).wait_send()
    deliver_wide(True)
    deliver_heads(True)
    deliver_share(True)
    ffn.finish()
    total.finish()


def back_all(seq_size, ins):
    (grad_attn, query, keys2) = ins[:3]
    _, tokens, width_q = grad_attn.shape
    length = query.shape[0]
    width = ins[15].shape[1]
    qkv_width = ins[12].shape[1]
    chips = seq_size // 2
    rows = width // (4 * seq_size)
    rank = ins[18].shape[0]
    block = ins[18].shape[1] // 8

    def shape(*dims):
        return jax.ShapeDtypeStruct(dims, F32)

    vmem = pl.BlockSpec(memory_space=pltpu.VMEM)
    anywhere = pl.BlockSpec(memory_space=pl.ANY)
    far = (0, 12, 15, 16)
    outs = (
        shape(tokens, width),
        shape(tokens, width),
        shape(4, rows, 128),
        shape(4, rank, 2 * block),
        shape(4, rank, block),
        shape(4, HD, 128),
        shape(4, HD // 2, 128),
    )
    many = (seq_size, tokens, width)
    few = (chips, tokens, width)
    return pl.pallas_call(
        functools.partial(back_kernel, seq_size),
        out_shape=outs,
        in_specs=[anywhere if i in far else vmem for i in range(len(ins))],
        out_specs=(vmem,) * len(outs),
        scratch_shapes=[
            pltpu.VMEM(grad_attn.shape, BF16),
            pltpu.VMEM((2, length, 2 * HD), BF16),
            pltpu.VMEM((2, length, 2 * HD), BF16),
            pltpu.VMEM((2, length, 2 * HD), F32),
            pltpu.VMEM((2, length, 2 * HD), F32),
            pltpu.VMEM((length, QB), F32),
            pltpu.VMEM((length, qkv_width), BF16),
            pltpu.VMEM((length, 3 * rank), BF16),
            pltpu.VMEM(ins[12].shape, BF16),
            pltpu.VMEM((length, width), BF16),
            pltpu.VMEM(many, BF16),
            pltpu.VMEM(few, BF16),
            pltpu.VMEM(few, BF16),
            pltpu.VMEM(few, BF16),
            pltpu.VMEM(many, BF16),
            pltpu.VMEM(few, BF16),
            pltpu.VMEM(few, BF16),
            pltpu.VMEM(few, BF16),
            pltpu.VMEM((width, 128), BF16),
            pltpu.VMEM((4, seq_size, rows, 128), BF16),
            pltpu.VMEM((qkv_width, 128), F32),
            pltpu.VMEM((4, rank, 2 * block), F32),
            pltpu.VMEM((4, rank, block), F32),
            pltpu.VMEM((4, HD, 128), F32),
            pltpu.VMEM((4, HD // 2, 128), F32),
            pltpu.SemaphoreType.DMA((4,)),
            pltpu.SemaphoreType.DMA((2, seq_size)),
            pltpu.SemaphoreType.DMA((2, 6, chips)),
            pltpu.SemaphoreType.DMA((2, 6, chips)),
            pltpu.SemaphoreType.DMA((5,)),
            pltpu.SemaphoreType.DMA((5,)),
        ],
        compiler_params=pltpu.CompilerParams(
            collective_id=1, has_side_effects=True, vmem_limit_bytes=60 * 2**20
        ),
        cost_estimate=pl.CostEstimate(
            flops=10 * 10**9, bytes_accessed=20 * 2**20, transcendentals=4 * 2**20
        ),
        name="attend_back",
    )(*ins)


def mid_kernel(
    seq_size,
    attn_all,
    hidden_all,
    out_all,
    gu_all,
    cotangent,
    down_w,
    gain,
    maps,
    ffn_part,
    middle_own,
    grad_middle,
    grad_attn,
    early_t,
    gu_grad,
    down_grad,
    out_v,
    gu_v,
    down_v,
    cot_v,
    norm_v,
    both_v,
    wide,
    act_v,
    sum_v,
    sum_side,
    sum_up,
    sum_down,
    attn_own,
    low_own,
    lows,
    lows_t,
    chain_sems,
    plane_sems,
    sum_sems,
    local_sems,
):
    p = Place(seq_size)
    d, s, z, c = p.d, p.s, p.z, p.c
    tokens, width = cotangent.shape
    part = down_w.shape[0]
    span = 2 * tokens
    hidden_width = 4 * part
    rank = maps.shape[0] // 8
    o_in, o_out, gu_in, gu_map, down_out, down_in = mid_views(maps)
    down_in = down_in.at[:, pl.ds(0, hidden_width)]
    heads_width = attn_all.shape[2]
    step_width = 512
    loads = [
        pltpu.make_async_copy(src, dst, local_sems.at[0, i])
        for i, (src, dst) in enumerate(
            [(down_w, down_v.at[d]), (cotangent, cot_v.at[s]), (hidden_all, norm_v), (out_all, out_v)]
            + [
                (attn_all.at[j], both_v.at[:, pl.ds(heads_width * j, heads_width)])
                for j in range(seq_size)
            ]
            + [(gu_all, gu_v)]
        )
    ]
    for copy in loads:
        copy.start()
    barrier = pltpu.get_barrier_semaphore()
    p_up, p_down = p.z < p.chips - 1, p.z > 0

    @pl.when(p_up)
    def _():
        pl.semaphore_signal(barrier, 1, device_id=p.seq(s + 2), device_id_type=MESH)

    @pl.when(p_down)
    def _():
        pl.semaphore_signal(barrier, 1, device_id=p.seq(s - 2), device_id_type=MESH)

    for place in (p.seq(p.sib), p.dp(p.dx), p.dp(p.dy)):
        pl.semaphore_signal(barrier, 1, device_id=place, device_id_type=MESH)

    @pl.when(p_up & p_down)
    def _():
        pl.semaphore_wait(barrier, 5)

    @pl.when(jnp.logical_not(p_up & p_down))
    def _():
        pl.semaphore_wait(barrier, 4)

    cot = Chains(p, cotangent, lambda i: cot_v.at[i], tokens, chain_sems)
    down = Plane(
        p,
        lambda e: down_v.at[e],
        lambda e, h: down_v.at[e, pl.ds(part // 2 * h, part // 2)],
        plane_sems,
    )
    total = ChainSums(p, sum_v, sum_side, sum_up, sum_down, sum_sems)
    down_all = down_v.reshape(4 * part, width)
    cot.start()
    loads[0].wait()
    down.start()
    for copy in loads[1:-1]:
        copy.wait()

    def columns(body, count):
        for n in range(count):
            body(pl.ds(n * step_width, step_width))

    def tiles(body, count):
        for zz in range(p.chips):
            for n in range(count):
                body(pl.ds(span * zz, span), pl.ds(n * step_width, step_width))

    length = seq_size * tokens
    norm_rows = norm_v.reshape(length, width)
    cot_rows = cot_v.reshape(length, width)
    sum_rows = sum_v.reshape(length, width)
    lows[...] = jnp.zeros_like(lows)
    mine = pl.ds(pl.multiple_of(s * tokens, tokens), tokens)
    lows[:, 0:rank] = dot_nt(both_v[...], o_in[...])

    def branch(rows, cut):
        low = lows[rows, 0:rank].astype(BF16)
        value = dot_nn(both_v[rows, :], out_v[:, cut]) + dot_nn(low, o_out[:, cut])
        wide[rows, cut] = norm_rows[rows, cut].astype(F32) + RESIDUAL_SCALE * value

    tiles(branch, width // step_width)
    middle_own[...] = wide[mine, :]
    attn_own[...] = both_v[mine, :]
    low_own[...] = dot_nt(attn_own[...], o_in[...]).astype(BF16)
    cot.step(1)
    down.forward()

    @pl.loop(0, length // 64)
    def _(i):
        rows = pl.ds(pl.multiple_of(i * 64, 64), 64)
        norm_rows[rows, :] = rms_scale(wide[rows, :], gain[...]).astype(BF16)

    loads[-1].wait()
    lows[:, 0 : 2 * rank] = dot_nt(norm_rows[...], gu_in[...])
    cot.step(2)

    def gate_up(rows, cut):
        low = lows[rows, 0 : 2 * rank].astype(BF16)
        wide[rows, cut] = dot_nn(norm_rows[rows, :], gu_v[:, cut]) + dot_nn(low, gu_map[:, cut])

    tiles(gate_up, 2 * hidden_width // step_width)
    cot.step(3)
    down.recv()
    for zz in range(p.chips):
        cot.side_recv(zz)

    def backward(zz):
        rows = pl.ds(pl.multiple_of(span * zz, span), span)
        low = dot_nt(cot_rows[rows, :], down_out[...]).astype(BF16)
        lows[rows, 5 * rank : 6 * rank] = low.astype(F32)

        for n in range(hidden_width // step_width):
            cut = pl.ds(n * step_width, step_width)
            upper = pl.ds(hidden_width + n * step_width, step_width)
            grad_act = RESIDUAL_SCALE * (
                dot_nt(cot_rows[rows, :], down_all[cut, :]) + dot_nn(low, down_in[:, cut])
            )
            gate, up = wide[rows, cut], wide[rows, upper]
            sigma = 1.0 / (1.0 + jnp.exp(-gate))
            raised = gate * sigma
            act_v[rows, cut] = (raised * up).astype(BF16)
            both_v[rows, cut] = (grad_act * up * sigma * (1.0 + gate * (1.0 - sigma))).astype(BF16)
            both_v[rows, upper] = (grad_act * raised).astype(BF16)

        low_gu = dot_nt(both_v[rows, :], gu_map[...]).astype(BF16)
        lows[rows, 2 * rank : 4 * rank] = low_gu.astype(F32)

        def model_part(cut):
            value = dot_nt(both_v[rows, :], gu_v[cut, :]) + dot_nn(low_gu, gu_in[:, cut])
            sum_rows[rows, cut] = value.astype(BF16)

        columns(model_part, width // step_width)
        total.side_start(zz)

    order = chain_order(z)
    backward(order[0])
    total.step(3)
    backward(order[1])
    backward(order[2])
    total.step(2)
    backward(order[3])
    lows[:, 4 * rank : 5 * rank] = dot_nt(act_v[...], down_in[...])
    for zz in range(p.chips):
        lows_t[:, pl.ds(span * zz, span)] = lows[pl.ds(span * zz, span), :].T.astype(BF16)
    total.step(1)

    for n in range(width // step_width):
        cut = pl.ds(step_width * n, step_width)
        early_t[2 * rank : 4 * rank, cut] = dot_nn(
            lows_t[2 * rank : 4 * rank, :], norm_rows[:, cut]
        )
        early_t[4 * rank : 5 * rank, cut] = RESIDUAL_SCALE * dot_nn(
            lows_t[4 * rank : 5 * rank, :], cot_rows[:, cut]
        )
        source = pl.ds(0, rank) if n < hidden_width // step_width else pl.ds(rank, rank)
        gu_grad[:, cut] = dot_nn(lows_t[source, :], both_v[:, cut])
        if n < hidden_width // step_width:
            down_grad[:, cut] = RESIDUAL_SCALE * dot_nn(
                lows_t[5 * rank : 6 * rank, :], act_v[:, cut]
            )


    def feed_forward(rows, cut):
        low = lows[rows, 4 * rank : 5 * rank].astype(BF16)
        value = dot_nn(act_v[rows, :], down_all[:, cut]) + dot_nn(low, down_out[:, cut])
        norm_rows[rows, cut] = value.astype(BF16)

    tiles(feed_forward, width // step_width)
    store = pltpu.make_async_copy(norm_v, ffn_part, local_sems.at[1, 0])
    store.start()
    total.last()
    middle = middle_own[...]
    mean = jnp.mean(middle * middle, axis=-1, keepdims=True)
    r = lax.rsqrt(mean + EPSILON)
    scaled = sum_v[s].astype(F32) * gain[...]
    inner = jnp.mean(scaled * middle, axis=-1, keepdims=True)
    grad_mid = cot_v[s].astype(F32) + r * scaled - r * r * r * inner * middle
    grad_middle[...] = grad_mid
    branch = (RESIDUAL_SCALE * grad_mid).astype(BF16)
    low = dot_nt(branch, o_out[...]).astype(BF16)
    for j in range(seq_size):
        cut = pl.ds(heads_width * j, heads_width)
        grad_attn[j] = (dot_nt(branch, out_v[cut, :]) + dot_nn(low, o_in[:, cut])).astype(BF16)
    pair = jnp.concatenate(
        [low.astype(F32), low_own[...].astype(F32), jnp.zeros((tokens, 128 - 2 * rank), F32)], axis=1
    )
    pair = pair.T.astype(BF16)
    early_t[0:rank, :] = dot_nn(pair[0:rank], attn_own[...])
    early_t[rank : 2 * rank, :] = dot_nn(pair[rank : 2 * rank], branch)
    cot.finish()
    down.finish()
    total.finish()
    store.wait()


def mid_all(seq_size, ins):
    tokens, width = ins[4].shape
    part = ins[5].shape[0]
    length = seq_size * tokens
    rank = ins[7].shape[0] // 8
    chips = seq_size // 2
    heads_width = ins[0].shape[2]

    def shape(*dims, dtype=F32):
        return jax.ShapeDtypeStruct(dims, dtype)

    vmem = pl.BlockSpec(memory_space=pltpu.VMEM)
    anywhere = pl.BlockSpec(memory_space=pl.ANY)
    many, few = (seq_size, tokens, width), (chips, tokens, width)
    outs = (
        shape(*many, dtype=BF16),
        shape(tokens, width),
        shape(tokens, width),
        shape(seq_size, tokens, heads_width, dtype=BF16),
        shape(5 * rank, width),
        shape(rank, 8 * part),
        shape(rank, 4 * part),
    )
    return pl.pallas_call(
        functools.partial(mid_kernel, seq_size),
        out_shape=outs,
        in_specs=[anywhere] * 6 + [vmem] * 2,
        out_specs=(anywhere,) + (vmem,) * 6,
        scratch_shapes=[
            pltpu.VMEM((width, width), BF16),
            pltpu.VMEM((width, 8 * part), BF16),
            pltpu.VMEM((4, part, width), BF16),
            pltpu.VMEM(many, BF16),
            pltpu.VMEM(many, BF16),
            pltpu.VMEM((length, width), BF16),
            pltpu.VMEM((length, 8 * part), F32),
            pltpu.VMEM((length, 4 * part), BF16),
            pltpu.VMEM(many, BF16),
            pltpu.VMEM(few, BF16),
            pltpu.VMEM(few, BF16),
            pltpu.VMEM(few, BF16),
            pltpu.VMEM((tokens, width), BF16),
            pltpu.VMEM((tokens, rank), BF16),
            pltpu.VMEM((length, 128), F32),
            pltpu.VMEM((128, length), BF16),
            pltpu.SemaphoreType.DMA((2, 4, seq_size)),
            pltpu.SemaphoreType.DMA((2, 4)),
            pltpu.SemaphoreType.DMA((2, 6, chips)),
            pltpu.SemaphoreType.DMA((2, 13)),
        ],
        compiler_params=pltpu.CompilerParams(
            collective_id=2, has_side_effects=True, vmem_limit_bytes=63 * 2**20
        ),
        cost_estimate=pl.CostEstimate(
            flops=40 * 10**9, bytes_accessed=40 * 2**20, transcendentals=4 * 2**20
        ),
        name="feed_forward",
    )(*ins)


def mid_views(maps):
    rank = maps.shape[0] // 8
    starts = (0, 1, 2, 4, 6, 7, 8)
    return [
        maps.at[pl.ds(rank * a, rank * (b - a))] for a, b in zip(starts[:-1], starts[1:], strict=True)
    ]


def prepare_kernel(
    seq_size,
    adapter_ref,
    documents,
    key_w,
    value_w,
    qkv_in_all,
    q_out_all,
    kv_out_all,
    o_in_all,
    o_out_all,
    gu_in_all,
    gu_out_all,
    down_in_all,
    down_out_all,
    numbers,
    kv,
    front_maps,
    mid_maps,
    heads_v,
    sems,
):
    me = lax.axis_index("seq")
    adapter = adapter_ref[0]
    rank = o_out_all.shape[1]
    q_width = q_out_all.shape[2] // seq_size
    part = down_in_all.shape[2] // (4 * seq_size)
    qkv_in = front_maps.at[pl.ds(0, 3 * rank)]
    low_map = front_maps.at[pl.ds(3 * rank, 3 * rank)]
    o_in, o_out, gu_in, gu_map, down_out, down_in = mid_views(mid_maps)
    low_map[...] = jnp.zeros(low_map.shape, BF16)
    gu_map[...] = jnp.zeros(gu_map.shape, BF16)
    down_in[...] = jnp.zeros(down_in.shape, BF16)

    def block(number, size):
        return pl.ds(pl.multiple_of(number * size, size), size)

    moves = [
        (qkv_in_all.at[adapter], qkv_in),
        (o_in_all.at[adapter], o_in),
        (o_out_all.at[adapter], o_out),
        (gu_in_all.at[adapter], gu_in),
        (down_out_all.at[adapter], down_out),
        (q_out_all.at[adapter, :, block(me, q_width)], low_map.at[pl.ds(0, rank), pl.ds(0, q_width)]),
        (kv_out_all.at[adapter, :, block(me // 2, 2 * HD)], heads_v.at[0]),
        (kv_out_all.at[adapter, :, block(seq_size // 2 + me // 2, 2 * HD)], heads_v.at[1]),
    ]
    for e in range(4):
        moves.append(
            (
                down_in_all.at[adapter, :, block(seq_size * e + me, part)],
                down_in.at[:, pl.ds(part * e, part)],
            )
        )
        for upper in range(2):
            moves.append(
                (
                    gu_out_all.at[adapter, :, block(seq_size * (4 * upper + e) + me, part)],
                    gu_map.at[pl.ds(rank * upper, rank), pl.ds(part * (4 * upper + e), part)],
                )
            )
    moves = [pltpu.make_async_copy(a, b, sems.at[i]) for i, (a, b) in enumerate(moves)]
    for move in moves:
        move.start()
    numbers[0] = jnp.broadcast_to(documents[...], numbers.shape[1:])
    numbers[1] = jnp.full(numbers.shape[1:], adapter, jnp.int32)
    rows = key_w.shape[0]
    low_lane = lax.broadcasted_iota(jnp.int32, (rows, 2 * HD), 1) < HD
    for j in range(seq_size // 2):
        cut = pl.ds(2 * HD * j, 2 * HD)
        left, right = key_w[:, cut].astype(F32), value_w[:, cut].astype(F32)
        kv[2 * j] = jnp.where(low_lane, left, pltpu.roll(right, HD, 1)).astype(BF16)
        kv[2 * j + 1] = jnp.where(low_lane, pltpu.roll(left, HD, 1), right).astype(BF16)
    for move in moves:
        move.wait()
    low_lane = lax.broadcasted_iota(jnp.int32, (rank, 2 * HD), 1) < HD
    odd = me % 2 == 1
    for i in range(2):
        value = heads_v[i].astype(F32)
        turned = pltpu.roll(value, HD, 1)
        value = jnp.where(odd, turned, value) if i == 0 else jnp.where(odd, value, turned)
        kept = low_lane if i == 0 else jnp.logical_not(low_lane)
        low_map[pl.ds(rank * (1 + i), rank), pl.ds(q_width, 2 * HD)] = jnp.where(
            kept, value, 0.0
        ).astype(BF16)


def prepare_all(seq_size, adapter_index, documents, key_w, value_w, maps):
    q_out = maps[1]
    rank = q_out.shape[1]
    rows = key_w.shape[0]
    tokens = documents.shape[1]

    def shape(*dims, dtype=BF16):
        return jax.ShapeDtypeStruct(dims, dtype)

    vmem = pl.BlockSpec(memory_space=pltpu.VMEM)
    width = q_out.shape[2]
    outs = (
        shape(2, 8, tokens, dtype=jnp.int32),
        shape(seq_size, rows, 2 * HD),
        shape(6 * rank, width),
        shape(8 * rank, width),
    )
    return pl.pallas_call(
        functools.partial(prepare_kernel, seq_size),
        out_shape=outs,
        in_specs=[pl.BlockSpec(memory_space=pltpu.SMEM), vmem, vmem, vmem]
        + [pl.BlockSpec(memory_space=pl.ANY)] * 9,
        out_specs=(vmem,) * len(outs),
        scratch_shapes=[pltpu.VMEM((2, rank, 2 * HD), BF16), pltpu.SemaphoreType.DMA((20,))],
        compiler_params=pltpu.CompilerParams(vmem_limit_bytes=62 * 2**20),
        name="prepare",
    )(adapter_index, documents, key_w, value_w, *maps)


def finish_kernel(count, *refs):
    far, outs = refs[:count], refs[count : count + 11]
    near, sems = refs[count + 11 : 2 * count + 11], refs[-1]
    loads = [pltpu.make_async_copy(a, b, sems.at[i]) for i, (a, b) in enumerate(zip(far, near, strict=True))]
    for load in loads:
        load.start()
    middle, ffn_sum, grad_middle, norm_sum, hidden, gain, share, gu_got, down_got, q_got, kv_got = near
    mixed, grad_hidden, qkv_in, q_out, kv_out, o_in, o_out, gu_in, gu_out, down_in, down_out = outs
    rank = o_in.shape[1]
    lower = lax.axis_index("dp") < 2
    for load in loads:
        load.wait()
    for a in range(share.shape[0]):
        own = share[a].T
        qkv_in[a] = own[: 3 * rank]
        o_in[a] = own[3 * rank : 4 * rank]
        o_out[a] = own[4 * rank : 5 * rank]
        gu_in[a] = own[5 * rank : 7 * rank]
        down_out[a] = own[7 * rank :]
        gu_out[a] = gu_got[a]
        down_in[a] = down_got[a]
        q_out[a] = q_got[a].T[:rank]
        turned = kv_got[a].T
        kv_out[a] = jnp.where(lower, turned[rank : 2 * rank], turned[2 * rank : 3 * rank])

    @pl.loop(0, middle.shape[0] // 32)
    def _(i):
        rows = pl.ds(pl.multiple_of(i * 32, 32), 32)
        mixed[0, rows, :] = (middle[rows, :] + RESIDUAL_SCALE * ffn_sum[rows, :]).astype(BF16)
        back = rms_back(hidden[rows, :].astype(F32), gain[...], norm_sum[rows, :])
        grad_hidden[0, rows, :] = (grad_middle[rows, :] + back).astype(BF16)


def finish_all(ins):
    tokens, width = ins[0].shape
    adapters, rows = ins[6].shape[:2]
    rank = ins[7].shape[1]

    def shape(*dims, dtype=F32):
        return jax.ShapeDtypeStruct(dims, dtype)

    vmem = pl.BlockSpec(memory_space=pltpu.VMEM)
    outs = (
        shape(1, tokens, width, dtype=BF16),
        shape(1, tokens, width, dtype=BF16),
        shape(adapters, 3 * rank, rows),
        shape(adapters, rank, rows),
        shape(adapters, rank, rows // 2),
        shape(adapters, rank, rows),
        shape(adapters, rank, rows),
        shape(adapters, 2 * rank, rows),
        shape(*ins[7].shape),
        shape(*ins[8].shape),
        shape(adapters, rank, rows),
    )
    made = pl.pallas_call(
        functools.partial(finish_kernel, len(ins)),
        out_shape=outs,
        in_specs=[pl.BlockSpec(memory_space=pltpu.HBM)] * len(ins),
        out_specs=(vmem,) * len(outs),
        scratch_shapes=[pltpu.VMEM(v.shape, v.dtype) for v in ins]
        + [pltpu.SemaphoreType.DMA((len(ins),))],
        compiler_params=pltpu.CompilerParams(vmem_limit_bytes=62 * 2**20),
        name="finish",
    )(*ins)
    made = list(made)
    for i in (2, 5, 7, 9):
        made[i] = jnp.swapaxes(made[i], 1, 2)
    return tuple(made)


def make_kernel_local(dp_size, seq_size):
    def local(
        hidden,
        token_document_numbers,
        sequence_adapter_index,
        cotangent,
        attention_norm_gain,
        feedforward_norm_gain,
        query_weight,
        key_weight,
        value_weight,
        attention_output_weight,
        gate_weight,
        up_weight,
        down_weight,
        adapter_query_key_value_input,
        adapter_query_output,
        adapter_key_value_output,
        adapter_projection_input,
        adapter_projection_output,
        adapter_gate_up_input,
        adapter_gate_up_output,
        adapter_down_input,
        adapter_down_output,
    ):
        tokens, width = hidden.shape[1:]
        length = tokens * seq_size
        numbers, kv, front_maps, mid_maps = (
            prepare_all(
                seq_size,
                sequence_adapter_index,
                token_document_numbers,
                key_weight,
                value_weight,
                (
                    jnp.swapaxes(adapter_query_key_value_input, 1, 2),
                    adapter_query_output,
                    adapter_key_value_output,
                    jnp.swapaxes(adapter_projection_input, 1, 2),
                    adapter_projection_output,
                    jnp.swapaxes(adapter_gate_up_input, 1, 2),
                    adapter_gate_up_output,
                    jnp.swapaxes(adapter_down_input, 1, 2),
                    adapter_down_output,
                ),
            )
        )
        cos_fixed, sin_fixed = fixed_tables(length)
        cos_n = jnp.asarray(np.tile(cos_fixed, (1, 4)))
        sin_n = jnp.asarray(np.tile(np.concatenate([-sin_fixed, sin_fixed], axis=1), (1, 2)))
        (
            hidden_all,
            owners,
            qkv,
            out_full,
            gate_up,
            attn,
            norm_one,
            query,
            keys2,
            values2,
            keys_t,
            log_totals,
            seg_row,
            seg_col,
            low_t,
        ) = front_all(
            seq_size,
            (
                hidden[0],
                numbers,
                query_weight,
                kv,
                attention_output_weight,
                gate_weight,
                up_weight,
                attention_norm_gain[None],
                front_maps,
                cos_n,
                sin_n,
            ),
        )
        ffn_part, middle, grad_middle, grad_attn, early, gu_grad, down_grad = mid_all(
            seq_size,
            (
                attn,
                hidden_all,
                out_full.reshape(width, width),
                gate_up.reshape(width, -1),
                cotangent[0],
                down_weight,
                feedforward_norm_gain[None],
                mid_maps,
            ),
        )
        norm_sum, ffn_sum, share, gu_got, down_got, q_got, kv_got = back_all(
            seq_size,
            (
                grad_attn,
                query,
                keys2,
                values2,
                keys_t,
                log_totals,
                seg_row,
                seg_col,
                jnp.asarray(np.ascontiguousarray(cos_fixed.T)),
                jnp.asarray(np.ascontiguousarray(sin_fixed.T)),
                cos_n,
                sin_n,
                qkv.reshape(width, -1),
                front_maps,
                low_t,
                norm_one.reshape(length, width),
                ffn_part,
                early,
                gu_grad,
                down_grad,
                owners,
            ),
        )
        return finish_all(
            (
                middle,
                ffn_sum,
                grad_middle,
                norm_sum,
                hidden[0],
                attention_norm_gain[None],
                share,
                gu_got,
                down_got,
                q_got,
                kv_got,
            )
        )

    return local


def solution(mesh):
    both = ("dp", "seq")
    tokens = P("dp", "seq", None)
    weight = P(both, None)
    in_specs = (
        (tokens, P("dp", "seq"), P("dp"), tokens, P(), P()) + (weight,) * 7 + (P(),) * 9
    )
    by_row, by_column = P(None, both, None), P(None, None, both)
    out_specs = (
        tokens,
        tokens,
        by_row,
        by_column,
        by_column,
        by_row,
        by_column,
        by_row,
        by_column,
        by_row,
        by_column,
    )
    dp_size, seq_size = mesh.shape["dp"], mesh.shape["seq"]
    if dp_size == 4 and seq_size == KVH:
        local = make_kernel_local(dp_size, seq_size)
    else:
        local = make_local(dp_size, seq_size)
    return jax.shard_map(local, mesh=mesh, in_specs=in_specs, out_specs=out_specs, check_vma=False)
```

```python
import functools
import math

import jax
import jax.numpy as jnp
import numpy as np
from jax import lax
from jax.experimental import pallas as pl
from jax.experimental.pallas import tpu as pltpu
from jax.sharding import PartitionSpec as P

NH = 32
KVH = 8
HD = 64

EPSILON = 1e-05
RESIDUAL_SCALE = 0.22
SCORE_SCALE = 1.0 / 64.0
ROPE_BASE = 10000000.0
BF16 = jnp.bfloat16
F32 = jnp.float32


def mm(a, b):
    return jnp.dot(a, b, preferred_element_type=F32)


def mm_t(a, b):
    return lax.dot_general(a, b, (((1,), (1,)), ((), ())), preferred_element_type=F32)


def t_mm(a, b):
    return lax.dot_general(a, b, (((0,), (0,)), ((), ())), preferred_element_type=F32)


def rms_scale(values, gain):
    mean_square = jnp.mean(values * values, axis=-1, keepdims=True)
    return values * lax.rsqrt(mean_square + EPSILON) * gain


def rms_back(values, gain, grad):
    r = lax.rsqrt(jnp.mean(values * values, axis=-1, keepdims=True) + EPSILON)
    z = grad * gain
    return r * z - r * r * r * values * jnp.mean(z * values, axis=-1, keepdims=True)


def angle_tables(positions, head_size):
    steps = jnp.arange(head_size // 2).astype(F32)
    frequency = jnp.exp(steps * (-2.0 * math.log(ROPE_BASE) / head_size))
    angles = positions[:, None] * frequency[None, :]
    return (jnp.cos(angles), jnp.sin(angles))


def fixed_tables(length):
    steps = np.arange(HD // 2, dtype=np.float32)
    frequency = np.exp(steps * np.float32(-2.0 * math.log(ROPE_BASE) / HD))
    angles = np.arange(length, dtype=np.float32)[:, None] * frequency[None, :]
    return (np.cos(angles), np.sin(angles))


def rotate(values, cos_table, sin_table):
    half_width = values.shape[-1] // 2
    first_half = values[..., :half_width]
    second_half = values[..., half_width:]
    cos_part = cos_table[:, None, :]
    sin_part = sin_table[:, None, :]
    return jnp.concatenate(
        [
            first_half * cos_part - second_half * sin_part,
            second_half * cos_part + first_half * sin_part,
        ],
        axis=-1,
    )


def masked_scores(query_block, keys, seg_block, segments, start_row):
    key_pos = jnp.arange(keys.shape[0], dtype=jnp.int32)
    query_pos = start_row + jnp.arange(query_block.shape[0], dtype=jnp.int32)
    scores = jnp.einsum("qhd,kd->hqk", query_block, keys, preferred_element_type=F32) * SCORE_SCALE
    allowed = (key_pos[None, :] <= query_pos[:, None]) & (seg_block[:, None] == segments[None, :])
    return jnp.where(allowed[None], scores, -1e30)


def attend_forward(query, keys, values, segments):
    length, heads, head_size = query.shape
    rows = min(512, length)

    def one_block(index):
        start = index * rows
        query_block = lax.dynamic_slice_in_dim(query, start, rows, 0)
        seg_block = lax.dynamic_slice_in_dim(segments, start, rows, 0)
        scores = masked_scores(query_block, keys, seg_block, segments, start)
        row_max = jnp.max(scores, axis=-1, keepdims=True)
        weights = jnp.exp(scores - row_max)
        totals = jnp.sum(weights, axis=-1, keepdims=True)
        low = (weights / totals).astype(BF16)
        output = jnp.einsum("hqk,kd->qhd", low, values, preferred_element_type=F32)
        return (output.astype(BF16), (row_max + jnp.log(totals))[..., 0])

    outputs, log_totals = lax.map(one_block, jnp.arange(length // rows, dtype=jnp.int32))
    return (outputs.reshape(length, heads * head_size), log_totals)


def attend_backward(query, keys, values, segments, log_totals, grad):
    length, heads, head_size = query.shape
    rows = min(512, length)

    def one_block(carry, index):
        grad_keys, grad_values = carry
        start = index * rows
        query_block = lax.dynamic_slice_in_dim(query, start, rows, 0)
        seg_block = lax.dynamic_slice_in_dim(segments, start, rows, 0)
        grad_block = lax.dynamic_slice_in_dim(grad, start, rows, 0)
        scores = masked_scores(query_block, keys, seg_block, segments, start)
        weights = jnp.exp(scores - log_totals[index][..., None])
        grad_weights = jnp.einsum("qhd,kd->hqk", grad_block, values, preferred_element_type=F32)
        row_dot = jnp.sum(weights * grad_weights, axis=-1, keepdims=True)
        grad_scores = (weights * (grad_weights - row_dot)).astype(BF16)
        grad_query = jnp.einsum("hqk,kd->qhd", grad_scores, keys, preferred_element_type=F32)
        grad_keys = grad_keys + jnp.einsum(
            "hqk,qhd->kd", grad_scores, query_block, preferred_element_type=F32
        )
        grad_values = grad_values + jnp.einsum(
            "hqk,qhd->kd", weights.astype(BF16), grad_block, preferred_element_type=F32
        )
        return ((grad_keys, grad_values), (grad_query * SCORE_SCALE).astype(BF16))

    zero = jnp.zeros(keys.shape, F32)
    (grad_keys, grad_values), grad_query = lax.scan(
        one_block, (zero, zero), jnp.arange(length // rows, dtype=jnp.int32)
    )
    return (grad_query.reshape(length, heads, head_size), grad_keys * SCORE_SCALE, grad_values)


def make_local(dp_size, seq_size):
    devices = dp_size * seq_size
    heads = NH // seq_size
    kv_repeat = max(1, seq_size // KVH)

    def local(
        hidden,
        token_document_numbers,
        sequence_adapter_index,
        cotangent,
        attention_norm_gain,
        feedforward_norm_gain,
        query_weight,
        key_weight,
        value_weight,
        attention_output_weight,
        gate_weight,
        up_weight,
        down_weight,
        adapter_query_key_value_input,
        adapter_query_output,
        adapter_key_value_output,
        adapter_projection_input,
        adapter_projection_output,
        adapter_gate_up_input,
        adapter_gate_up_output,
        adapter_down_input,
        adapter_down_output,
    ):
        tokens, width = hidden.shape[1:]
        length = tokens * seq_size
        rows = query_weight.shape[0]
        key_width = key_weight.shape[1]
        ff_width = gate_weight.shape[1]
        ff_block = ff_width // devices
        rank = adapter_projection_input.shape[2]
        adapters = adapter_projection_input.shape[0]
        me = lax.axis_index("seq")
        q_width = heads * HD

        def across(piece):
            return lax.all_to_all(piece, "seq", split_axis=0, concat_axis=0, tiled=True)

        def gather_dp(block):
            return lax.all_gather(block, "dp", axis=0, tiled=True)

        def gather_seq(block):
            return lax.all_gather(block, "seq", axis=0, tiled=True)

        def scatter_seq(total):
            return lax.psum_scatter(total, "seq", scatter_dimension=0, tiled=True)

        def by_owner(columns):
            return columns.reshape(columns.shape[0], dp_size, seq_size, ff_block)

        hidden_own = hidden[0].astype(F32)
        hidden_all = gather_seq(hidden[0])
        segments = gather_seq(token_document_numbers[0])
        kv = jnp.stack([key_weight.reshape(rows, KVH, HD), value_weight.reshape(rows, KVH, HD)], 2)
        kv = jnp.repeat(kv.reshape(rows, KVH, 2 * HD), kv_repeat, axis=1)
        qkv = jnp.concatenate([query_weight.reshape(rows, seq_size, q_width), kv], axis=2)
        qkv = across(jnp.swapaxes(qkv, 0, 1)).reshape(seq_size * rows, q_width + 2 * HD)
        qkv = gather_dp(qkv)
        gate_up = jnp.concatenate([by_owner(gate_weight), by_owner(up_weight)], axis=1)
        gate_up = across(jnp.transpose(gate_up, (2, 0, 1, 3)))
        gate_up = gather_dp(gate_up.reshape(seq_size * rows, 2 * dp_size * ff_block))
        down = gather_dp(down_weight)
        out_full = lax.all_gather(attention_output_weight, ("dp", "seq"), axis=0, tiled=True)
        ff_own = dp_size * ff_block

        adapter = sequence_adapter_index[0]
        qkv_in = adapter_query_key_value_input[adapter]
        q_out = lax.dynamic_slice_in_dim(adapter_query_output[adapter], me * q_width, q_width, 1)
        kv_out = adapter_key_value_output[adapter]
        kv_start = (me // kv_repeat) * HD
        k_out = lax.dynamic_slice_in_dim(kv_out, kv_start, HD, 1)
        v_out = lax.dynamic_slice_in_dim(kv_out, key_width + kv_start, HD, 1)
        o_in = adapter_projection_input[adapter]
        o_out = adapter_projection_output[adapter]
        gu_in = adapter_gate_up_input[adapter]
        gu_all = adapter_gate_up_output[adapter].reshape(rank, 2, dp_size, seq_size, ff_block)
        gu_out = lax.dynamic_index_in_dim(gu_all, me, 3, keepdims=False)
        g_out, u_out = gu_out[:, 0].reshape(rank, ff_own), gu_out[:, 1].reshape(rank, ff_own)
        down_all = adapter_down_input[adapter].reshape(dp_size, seq_size, ff_block, rank)
        down_in = lax.dynamic_index_in_dim(down_all, me, 1, keepdims=False).reshape(ff_own, rank)
        down_out = adapter_down_output[adapter]

        norm_one = rms_scale(hidden_all.astype(F32), attention_norm_gain).astype(BF16)
        low_qkv = mm(norm_one, qkv_in).astype(BF16)
        pre = mm(norm_one, qkv)
        query_pre = pre[:, :q_width] + mm(low_qkv[:, :rank], q_out)
        key_pre = pre[:, q_width : q_width + HD] + mm(low_qkv[:, rank : 2 * rank], k_out)
        value_pre = pre[:, q_width + HD :] + mm(low_qkv[:, 2 * rank :], v_out)
        cos_table, sin_table = angle_tables(jnp.arange(length, dtype=jnp.int32).astype(F32), HD)
        query = rotate(query_pre.reshape(length, heads, HD), cos_table, sin_table).astype(BF16)
        keys = rotate(key_pre.reshape(length, 1, HD), cos_table, sin_table).astype(BF16)[:, 0]
        values = value_pre.astype(BF16)
        attn_heads, log_totals = attend_forward(query, keys, values, segments)
        attn = lax.all_gather(attn_heads, "seq", axis=1, tiled=True)
        low_out = mm(attn, o_in).astype(BF16)
        branch = mm(attn, out_full) + mm(low_out, o_out)
        middle = hidden_all.astype(F32) + RESIDUAL_SCALE * branch
        own_row = me * tokens
        middle_own = lax.dynamic_slice_in_dim(middle, own_row, tokens, 0)
        norm_two = rms_scale(middle, feedforward_norm_gain).astype(BF16)
        low_gu = mm(norm_two, gu_in).astype(BF16)
        wide = mm(norm_two, gate_up)
        gate = wide[:, :ff_own] + mm(low_gu[:, :rank], g_out)
        up_proj = wide[:, ff_own:] + mm(low_gu[:, rank:], u_out)
        sigma = jax.nn.sigmoid(gate)
        activation = (gate * sigma * up_proj).astype(BF16)
        low_down = mm(activation, down_in).astype(BF16)
        ffn = scatter_seq((mm(activation, down) + mm(low_down, down_out)).astype(BF16))
        mixed = (middle_own + RESIDUAL_SCALE * ffn.astype(F32)).astype(BF16)

        grad_ffn = gather_seq((RESIDUAL_SCALE * cotangent[0].astype(F32)).astype(BF16))
        grad_low_down = mm_t(grad_ffn, down_out).astype(BF16)
        grad_act = mm_t(grad_ffn, down) + mm_t(grad_low_down, down_in)
        grad_gate = (grad_act * up_proj * sigma * (1.0 + gate * (1.0 - sigma))).astype(BF16)
        grad_up = (grad_act * gate * sigma).astype(BF16)
        grad_low_gu = jnp.concatenate([mm_t(grad_gate, g_out), mm_t(grad_up, u_out)], axis=1)
        grad_low_gu = grad_low_gu.astype(BF16)
        grad_norm_two = scatter_seq(
            (
                mm_t(jnp.concatenate([grad_gate, grad_up], axis=1), gate_up)
                + mm_t(grad_low_gu, gu_in)
            ).astype(BF16)
        )
        grad_middle = cotangent[0].astype(F32) + rms_back(
            middle_own, feedforward_norm_gain, grad_norm_two.astype(F32)
        )
        grad_branch = (RESIDUAL_SCALE * grad_middle).astype(BF16)
        grad_low_out = mm_t(grad_branch, o_out).astype(BF16)
        grad_attn = (mm_t(grad_branch, out_full) + mm_t(grad_low_out, o_in)).astype(BF16)
        grad_heads = lax.all_to_all(
            jnp.swapaxes(grad_attn.reshape(tokens, seq_size, q_width), 0, 1),
            "seq",
            split_axis=0,
            concat_axis=0,
            tiled=True,
        ).reshape(length, heads, HD)
        grad_q, grad_k, grad_v = attend_backward(
            query, keys, values, segments, log_totals, grad_heads
        )
        grad_query = rotate(grad_q.astype(F32), cos_table, -sin_table)
        grad_query = grad_query.reshape(length, q_width).astype(BF16)
        grad_key = rotate(grad_k[:, None], cos_table, -sin_table)[:, 0].astype(BF16)
        grad_value = grad_v.astype(BF16)
        grad_low_qkv = jnp.concatenate(
            [mm_t(grad_query, q_out), mm_t(grad_key, k_out), mm_t(grad_value, v_out)], axis=1
        ).astype(BF16)
        grad_qkv = jnp.concatenate([grad_query, grad_key, grad_value], axis=1)
        grad_norm_one = scatter_seq((mm_t(grad_qkv, qkv) + mm_t(grad_low_qkv, qkv_in)).astype(BF16))
        grad_hidden = grad_middle + rms_back(
            hidden_own, attention_norm_gain, grad_norm_one.astype(F32)
        )

        attn_own = lax.dynamic_slice_in_dim(attn, own_row, tokens, 0)
        low_out_own = lax.dynamic_slice_in_dim(low_out, own_row, tokens, 0)
        partial = jnp.concatenate(
            [
                t_mm(norm_one, grad_low_qkv),
                t_mm(attn_own, grad_low_out),
                t_mm(grad_branch, low_out_own),
                t_mm(norm_two, grad_low_gu),
                t_mm(grad_ffn, low_down),
            ],
            axis=1,
        ).reshape(dp_size, seq_size, rows, 8 * rank)
        own_q = t_mm(grad_query, low_qkv[:, :rank])
        own_k = t_mm(grad_key, low_qkv[:, rank : 2 * rank])
        own_v = t_mm(grad_value, low_qkv[:, 2 * rank :])
        own_g = t_mm(grad_gate, low_gu[:, :rank]).reshape(dp_size, ff_block, rank)
        own_u = t_mm(grad_up, low_gu[:, rank:]).reshape(dp_size, ff_block, rank)
        own_d = t_mm(activation, grad_low_down).reshape(dp_size, ff_block, rank)

        def placed(block, total, start, axis):
            empty = list(block.shape)
            empty[axis] = total
            return lax.dynamic_update_slice_in_dim(jnp.zeros(empty, F32), block, start, axis)

        def by_target(whole):
            return whole.reshape(dp_size, seq_size, -1)

        full_q = placed(own_q, width, me * q_width, 0)
        full_kv = jnp.concatenate(
            [placed(own_k, key_width, kv_start, 0), placed(own_v, key_width, kv_start, 0)], axis=0
        )
        spot = [placed(v[:, None], seq_size, me, 1) for v in (own_g, own_u, own_d)]
        full_gu = jnp.concatenate([spot[0].reshape(ff_width, rank), spot[1].reshape(ff_width, rank)])
        pieces = [by_target(v) for v in (partial, full_q, full_kv, full_gu, spot[2])]
        send = jnp.concatenate(pieces, axis=2)
        send = jnp.swapaxes(send, 0, 1).reshape(seq_size, -1)
        mine = lax.psum_scatter(send, "seq", scatter_dimension=0, tiled=True)
        mine = lax.all_to_all(
            mine.reshape(dp_size, -1), "dp", split_axis=0, concat_axis=0, tiled=True
        )
        owners = lax.all_gather(sequence_adapter_index, "dp", axis=0, tiled=True)
        numbers = jnp.arange(adapters, dtype=jnp.int32)
        chooser = (owners[:, None] == numbers[None, :]).astype(F32)
        mine = jnp.einsum("sa,si->ai", chooser, mine, precision=lax.Precision.HIGHEST)
        sizes = [v.shape[2] for v in pieces]
        cuts = [sum(sizes[:i]) for i in range(1, len(sizes))]
        got, got_q, got_kv, got_gu, got_d = jnp.split(mine, cuts, axis=1)
        got = got.reshape(adapters, rows, 8 * rank)

        def turned(flat):
            return jnp.swapaxes(flat.reshape(adapters, -1, rank), 1, 2)

        return (
            mixed[None],
            grad_hidden.astype(BF16)[None],
            got[:, :, : 3 * rank],
            turned(got_q),
            turned(got_kv),
            got[:, :, 3 * rank : 4 * rank],
            jnp.swapaxes(got[:, :, 4 * rank : 5 * rank], 1, 2),
            got[:, :, 5 * rank : 7 * rank],
            turned(got_gu),
            got_d.reshape(adapters, ff_block, rank),
            jnp.swapaxes(got[:, :, 7 * rank :], 1, 2),
        )

    return local


MESH = pl.DeviceIdType.MESH


def remote(src, dst, send_sem, recv_sem, device):
    return pltpu.make_async_remote_copy(
        src_ref=src,
        dst_ref=dst,
        send_sem=send_sem,
        recv_sem=recv_sem,
        device_id=device,
        device_id_type=MESH,
    )


class Place:
    def __init__(self, seq_size):
        self.d = lax.axis_index("dp")
        self.s = lax.axis_index("seq")
        self.seq_size = seq_size
        self.chips = seq_size // 2
        self.z = self.s // 2
        self.c = self.s % 2
        self.dx = self.d + 1 - 2 * (self.d % 2)
        self.dy = lax.rem(self.d + 2, 4)
        self.dd = lax.rem(self.dx + 2, 4)
        self.sib = self.s + 1 - 2 * self.c

    def seq(self, s):
        return (self.d, s)

    def dp(self, d):
        return (d, self.s)

    def peer(self, step):
        return lax.rem(self.s + step, self.seq_size)

    def greet(self, seq_steps, dp_peers):
        barrier = pltpu.get_barrier_semaphore()
        for step in seq_steps:
            pl.semaphore_signal(
                barrier, 1, device_id=self.seq(self.peer(step)), device_id_type=MESH
            )
        for d in dp_peers:
            pl.semaphore_signal(barrier, 1, device_id=self.dp(d), device_id_type=MESH)
        pl.semaphore_wait(barrier, len(seq_steps) + len(dp_peers))


class Chain:
    def __init__(self, place, own, slot, sems):
        self.p, self.own, self.slot = place, own, slot
        self.up, self.down, self.side, self.got = (sems.at[i] for i in range(4))

    def _up(self, src, i):
        return remote(src, self.slot(i), self.up.at[i], self.got.at[i], self.p.seq(self.p.s + 2))

    def _down(self, src, i):
        return remote(src, self.slot(i), self.down.at[i], self.got.at[i], self.p.seq(self.p.s - 2))

    def _side(self, src, i):
        return remote(src, self.slot(i), self.side.at[i], self.got.at[i], self.p.seq(self.p.sib))

    def start(self):
        p = self.p

        @pl.when(p.z < p.chips - 1)
        def _():
            self._up(self.own, p.s).start()

        @pl.when(p.z > 0)
        def _():
            self._down(self.own, p.s).start()

        self._side(self.own, p.s).start()

    def step(self, k):
        p = self.p
        low, high = p.s - 2 * k, p.s + 2 * k

        @pl.when(p.z >= k)
        def _():
            self._side(self.slot(low), low).wait_recv()

            @pl.when(p.z < p.chips - 1)
            def _():
                self._up(self.slot(low), low).start()

            self._side(self.slot(low), low).start()

        @pl.when(p.z + k < p.chips)
        def _():
            self._side(self.slot(high), high).wait_recv()

            @pl.when(p.z > 0)
            def _():
                self._down(self.slot(high), high).start()

            self._side(self.slot(high), high).start()

    def side_recv(self, z):
        other = 2 * z + 1 - self.p.c
        self._side(self.slot(other), other).wait_recv()

    def finish(self):
        p = self.p

        @pl.when(p.z < p.chips - 1)
        def _():
            self._up(self.own, p.s).wait_send()

        @pl.when(p.z > 0)
        def _():
            self._down(self.own, p.s).wait_send()

        self._side(self.own, p.s).wait_send()
        for k in range(1, p.chips):
            low, high = p.s - 2 * k, p.s + 2 * k

            @pl.when(p.z >= k)
            def _():
                @pl.when(p.z < p.chips - 1)
                def _():
                    self._up(self.slot(low), low).wait_send()

                self._side(self.slot(low), low).wait_send()

            @pl.when(p.z + k < p.chips)
            def _():
                @pl.when(p.z > 0)
                def _():
                    self._down(self.slot(high), high).wait_send()

                self._side(self.slot(high), high).wait_send()


class Chains:
    def __init__(self, place, own, slot, rows, sems, parts=2):
        size = rows // parts
        self.all = [
            Chain(
                place,
                own.at[pl.ds(size * i, size)],
                lambda n, i=i: slot(n).at[pl.ds(size * i, size)],
                sems.at[i],
            )
            for i in range(parts)
        ]

    def start(self):
        for chain in self.all:
            chain.start()

    def step(self, k):
        for chain in self.all:
            chain.step(k)

    def side_recv(self, z):
        for chain in self.all:
            chain.side_recv(z)

    def finish(self):
        for chain in self.all:
            chain.finish()


class Plane:
    def __init__(self, place, block, half, sems):
        self.p, self.block, self.half, self.sems = place, block, half, sems

    def _copy(self, ref, i, d):
        return remote(ref, ref, self.sems.at[0, i], self.sems.at[1, i], self.p.dp(d))

    def _all(self):
        p = self.p
        return (
            (self.block(p.d), p.dx),
            (self.block(p.d), p.dy),
            (self.half(p.dx, 0), p.dy),
            (self.half(p.dy, 1), p.dx),
        )

    def start(self):
        for i, (ref, d) in enumerate(self._all()[:2]):
            self._copy(ref, i, d).start()

    def forward(self):
        p = self.p
        everything = self._all()
        for i, came in ((0, p.dx), (1, p.dy)):
            self._copy(self.block(came), i, came).wait_recv()
            ref, d = everything[2 + i]
            self._copy(ref, 2 + i, d).start()

    def recv(self):
        p = self.p
        self._copy(self.half(p.dd, 0), 2, p.dy).wait_recv()
        self._copy(self.half(p.dd, 1), 3, p.dx).wait_recv()

    def finish(self):
        for i, (ref, d) in enumerate(self._all()):
            self._copy(ref, i, d).wait_send()


class Spread:
    def __init__(self, place, pairs, whole, send_sem, recv_sem):
        self.p, self.pairs, self.whole = place, pairs, whole
        self.send_sem, self.recv_sem = send_sem, recv_sem

    def start(self):
        p = self.p
        for step in (1, 2, 3, 4, 5, 6, 7):
            j = p.peer(step)
            for src, dst in self.pairs(j):
                remote(src, dst, self.send_sem, self.recv_sem, p.seq(j)).start()

    def recv(self):
        p = self.p
        for whole in self.whole:
            remote(whole, whole, self.send_sem, self.recv_sem, p.seq(p.sib)).wait_recv()

    def finish(self):
        p = self.p
        for whole in self.whole:
            remote(whole, whole, self.send_sem, self.recv_sem, p.seq(p.sib)).wait_send()


PIECES = 4
QB = 256


def front_kernel(
    seq_size,
    hidden,
    numbers,
    query_w,
    kv_w,
    out_w,
    gate_w,
    up_w,
    gain,
    maps,
    cos_n,
    sin_n,
    hidden_all,
    adapters_all,
    qkv_all,
    out_all,
    gu_all,
    attn_all,
    norm_all,
    query,
    keys2,
    values2,
    keys_t,
    log_totals,
    seg_row,
    seg_col,
    low_t,
    documents_all,
    chain_sems,
    plane_sems,
    local_sems,
    spread_sems,
    small_sems,
    side_sems,
    hidden_v,
    norm_v,
    out_v,
    qkv_v,
    gu_v,
    weights_v,
    key_z,
    values_t,
    bias,
    attn_v,
):
    p = Place(seq_size)
    d, s, z, c = p.d, p.s, p.z, p.c
    rows = query_w.shape[0]
    documents, adapter_row = numbers.at[0], numbers.at[1]
    low_rows = maps.shape[0] // 2
    qkv_in = maps.at[pl.ds(0, low_rows)]
    part = gate_w.shape[1] // (4 * seq_size)
    tokens = hidden.shape[0]
    half_rows = seq_size * rows // 2
    landing = pl.ds(pl.multiple_of(rows * s, rows), rows)
    q_width = query_w.shape[1] // seq_size
    low_map = maps.at[pl.ds(low_rows, low_rows), pl.ds(0, qkv_v.shape[1])]

    def column_block(number, size):
        return pl.ds(pl.multiple_of(number * size, size), size)

    stage = [
        (hidden, hidden_v.at[s]),
        (out_w, out_v),
        (query_w.at[:, column_block(s, q_width)], qkv_v.at[:, pl.ds(0, q_width)]),
        (kv_w.at[s], qkv_v.at[:, pl.ds(q_width, kv_w.shape[2])]),
        (documents, documents_all.at[s]),
        (adapter_row, adapters_all.at[d]),
    ]
    for i in range(8):
        matrix = (gate_w, up_w)[i // 4]
        block = matrix.at[:, column_block(seq_size * (i % 4) + s, part)]
        stage.append((block, gu_v.at[:, pl.ds(part * i, part)]))
    stage = [
        pltpu.make_async_copy(src, dst, local_sems.at[0, i]) for i, (src, dst) in enumerate(stage)
    ]
    keep = [
        pltpu.make_async_copy(src, dst, local_sems.at[1, i])
        for i, (src, dst) in enumerate(
            (
                (out_v, out_all.at[d, z, c]),
                (qkv_v, qkv_all.at[d, landing]),
                (gu_v, gu_all.at[d, landing]),
                (qkv_all, weights_v),
                (hidden_v, hidden_all),
                (norm_v, norm_all),
                (attn_v, attn_all.at[s]),
            )
        )
    ]
    for copy in stage:
        copy.start()
    p.greet(range(1, seq_size), (p.dx, p.dy, p.dd))

    hid = Chains(p, hidden, lambda i: hidden_v.at[i], tokens, chain_sems.at[0])
    out = Chain(p, out_w, lambda i: out_all.at[d, i // 2, i % 2], chain_sems.at[1, 0])
    att = Chains(p, attn_v, lambda i: attn_all.at[i], attn_v.shape[0], chain_sems.at[2])

    def qkv_pairs(j):
        return (
            (query_w.at[:, column_block(j, q_width)], qkv_all.at[d, landing, pl.ds(0, q_width)]),
            (kv_w.at[j], qkv_all.at[d, landing, pl.ds(q_width, kv_w.shape[2])]),
        )

    def gu_pairs(piece):
        matrix = (gate_w, up_w)[piece // 2]

        def pairs(j):
            found = []
            for block in (2 * (piece % 2), 2 * (piece % 2) + 1):
                at = part * (4 * (piece // 2) + block)
                source = matrix.at[:, column_block(seq_size * block + j, part)]
                found.append((source, gu_all.at[d, landing, pl.ds(at, part)]))
            return found

        return pairs

    others = pl.ds(0, rows * (seq_size - 1))
    qkv = Spread(
        p, qkv_pairs, [qkv_all.at[d, others]], spread_sems.at[0, 0], spread_sems.at[0, 1]
    )
    gu = []
    gu_planes = []
    for i in range(PIECES):
        cut = pl.ds(2 * part * i, 2 * part)
        gu.append(
            Spread(
                p, gu_pairs(i), [gu_all.at[d, others, cut]], spread_sems.at[1 + i, 0],
                spread_sems.at[1 + i, 1],
            )
        )
        gu_planes.append(
            Plane(
                p,
                lambda e, cut=cut: gu_all.at[e, :, cut],
                lambda e, h, cut=cut: gu_all.at[e, pl.ds(half_rows * h, half_rows), cut],
                plane_sems.at[3 + i],
            )
        )
    qkv_plane = Plane(
        p,
        lambda e: qkv_all.at[e],
        lambda e, h: qkv_all.at[e, pl.ds(half_rows * h, half_rows)],
        plane_sems.at[0],
    )
    half_chips = p.chips // 2
    out_plane = Plane(
        p,
        lambda e: out_all.at[e, :, c],
        lambda e, h: out_all.at[e, pl.ds(half_chips * h, half_chips), c],
        plane_sems.at[2],
    )

    def documents_copy(step):
        return remote(
            documents, documents_all.at[s], small_sems.at[0, step], small_sems.at[1, 0],
            p.seq(p.peer(step)),
        )

    def adapters_copy(i, e):
        return remote(
            adapter_row, adapters_all.at[d], small_sems.at[2, i], small_sems.at[3, 0], p.dp(e)
        )

    def side_copy(i, e):
        ref = out_all.at[e, :, c]
        return remote(ref, ref, side_sems.at[0, i], side_sems.at[1, i], p.seq(p.sib))

    def side_wait(i, e):
        ref = out_all.at[e, :, 1 - c]
        remote(ref, ref, side_sems.at[0, i], side_sems.at[1, i], p.seq(p.sib)).wait_recv()

    low_lane = lax.broadcasted_iota(jnp.int32, (tokens, 2 * HD), 1) < HD
    weights = weights_v.reshape(4 * seq_size * rows, qkv_v.shape[1])

    def process(slot):
        at = pl.ds(pl.multiple_of(slot * tokens, tokens), tokens)
        cos_part, sin_part = cos_n[at, :], sin_n[at, :]
        normed = rms_scale(hidden_v[slot].astype(F32), gain[...]).astype(BF16)
        norm_v[slot] = normed
        low = dot_nt(normed, qkv_in[...]).astype(BF16)
        pre = dot_nn(normed, weights[...]) + dot_nn(low, low_map[...])
        padded = jnp.concatenate(
            [low.astype(F32), jnp.zeros((tokens, 128 - low.shape[1]), F32)], axis=1
        )
        low_t[:, at] = padded.T[: low.shape[1]].astype(BF16)
        for m in range(2):
            pair = pre[:, 2 * HD * m : 2 * HD * (m + 1)]
            turned = pair * cos_part + swap_halves(pair) * sin_part
            query[at, pl.ds(2 * HD * m, 2 * HD)] = turned.astype(BF16)
        pair = pre[:, 4 * HD :]
        turned = pair * cos_part + swap_halves(pair) * sin_part
        both = jnp.where(low_lane, turned, pair)
        crossed = pltpu.roll(both, HD, 1)
        keys2[at, :] = jnp.where(low_lane, both, crossed).astype(BF16)
        values2[at, :] = jnp.where(low_lane, crossed, both).astype(BF16)
        zero = jnp.zeros_like(both)
        key_z[0, at, :] = jnp.where(low_lane, both, zero).astype(BF16)
        key_z[1, at, :] = jnp.where(low_lane, zero, crossed).astype(BF16)
        both_t = both.T
        keys_t[:, at] = both_t[:HD].astype(BF16)
        values_t[:, at] = both_t[HD:].astype(BF16)

    def process_distance(k):
        @pl.when(p.z >= k)
        def _():
            hid.side_recv(p.z - k)

            @pl.loop(0, 2)
            def _(core):
                process(2 * (p.z - k) + core)

        if k:

            @pl.when(p.z + k < p.chips)
            def _():
                hid.side_recv(p.z + k)

                @pl.loop(0, 2)
                def _(core):
                    process(2 * (p.z + k) + core)

    def query_block(i):
        start = i * QB
        span = pl.ds(0, start + QB)
        at = pl.ds(start, QB)
        bias[span, :] = mask_bias(seg_col, seg_row, start, QB)

        for m in range(2):
            pair = pl.ds(2 * HD * m, 2 * HD)
            query_pair = query[at, pair]
            found = []
            for e in range(2):
                scores = dot_nt(key_z[e, span, :], query_pair) * SCORE_SCALE + bias[span, :]
                top = jnp.max(scores, axis=0, keepdims=True)
                raised = jnp.exp(scores - top)
                total = jnp.sum(raised, axis=0, keepdims=True)
                found.append(dot_nn(values_t[:, span], raised.astype(BF16)) / total)
                log_totals[2 * m + e : 2 * m + e + 1, at] = top + jnp.log(total)
            attn_v[at, pair] = jnp.concatenate(found, axis=0).T.astype(BF16)

    for step in range(1, seq_size):
        documents_copy(step).start()
    for i, e in enumerate((p.dx, p.dy, p.dd)):
        adapters_copy(i, e).start()
    qkv.start()
    out.start()
    hid.start()
    for copy in stage:
        copy.wait()
    for i in range(3):
        keep[i].start()
    for i in range(3):
        keep[i].wait()
    qkv.recv()
    qkv_plane.start()
    out.step(1)
    hid.step(1)
    out.step(2)
    remote(
        documents_all.at[pl.ds(0, seq_size - 1)], documents_all.at[pl.ds(0, seq_size - 1)],
        small_sems.at[0, 0], small_sems.at[1, 0], p.seq(p.sib),
    ).wait_recv()
    for slot in range(seq_size):
        at = pl.ds(tokens * slot, tokens)
        numbers = documents_all[slot].astype(F32)
        seg_row[:, at] = numbers
        seg_col[at, :] = jnp.broadcast_to(numbers[0:1, :], (tokens, tokens)).T
    qkv_plane.forward()
    out.step(3)
    out_plane.start()
    hid.step(2)
    qkv_plane.recv()
    keep[3].start()
    keep[3].wait()
    process_distance(0)
    process_distance(1)
    out_plane.forward()
    side_copy(0, p.dx).start()
    side_copy(1, p.dy).start()
    hid.step(3)
    gu[0].start()
    gu[1].start()
    gu[2].start()
    process_distance(2)
    process_distance(3)
    gu[0].recv()
    gu_planes[0].start()
    gu[3].start()
    out_plane.recv()
    side_copy(2, p.dd).start()
    keep[4].start()
    keep[5].start()
    query_block(0)
    query_block(1)
    gu[1].recv()
    gu_planes[1].start()
    gu_planes[0].forward()
    query_block(2)
    query_block(3)
    keep[6].start()
    att.start()
    gu[2].recv()
    gu_planes[2].start()
    gu_planes[1].forward()
    gu[3].recv()
    gu_planes[3].start()
    att.step(1)
    gu_planes[2].forward()
    att.step(2)
    gu_planes[3].forward()
    att.step(3)
    for i in range(4):
        gu_planes[i].recv()
    for chain in (out, att):
        for other in range(p.chips):
            chain.side_recv(other)
    for chain in (hid, out, att):
        chain.finish()
    for i, e in enumerate((p.dx, p.dy, p.dd)):
        side_wait(i, e)
    remote(
        adapters_all.at[pl.ds(0, 3)], adapters_all.at[pl.ds(0, 3)],
        small_sems.at[2, 3], small_sems.at[3, 0], p.dp(p.dx),
    ).wait_recv()
    for step in range(1, seq_size):
        documents_copy(step).wait_send()
    for i, e in enumerate((p.dx, p.dy, p.dd)):
        adapters_copy(i, e).wait_send()
        side_copy(i, e).wait_send()
    for group in [qkv, *gu, qkv_plane, out_plane, *gu_planes]:
        group.finish()
    for i in (4, 5, 6):
        keep[i].wait()


def front_all(seq_size, ins):
    tokens, width = ins[0].shape
    rows = ins[2].shape[0]
    part = ins[5].shape[1] // (4 * seq_size)
    chips = seq_size // 2
    q_width = ins[2].shape[1] // seq_size
    qkv_width = q_width + ins[3].shape[2]
    length = tokens * seq_size
    low_width = ins[8].shape[0] // 2

    def shape(*dims, dtype=BF16):
        return jax.ShapeDtypeStruct(dims, dtype)

    anywhere = pl.BlockSpec(memory_space=pl.ANY)
    vmem = pl.BlockSpec(memory_space=pltpu.VMEM)
    outs = (
        shape(seq_size, tokens, width),
        shape(4, 8, 128, dtype=jnp.int32),
        shape(4, seq_size * rows, qkv_width),
        shape(4, chips, 2, rows, width),
        shape(4, seq_size * rows, 8 * part),
        shape(seq_size, length, q_width),
        shape(seq_size, tokens, width),
        shape(length, q_width),
        shape(length, 2 * HD),
        shape(length, 2 * HD),
        shape(HD, length),
        shape(4, length, dtype=F32),
        shape(8, length, dtype=F32),
        shape(length, tokens, dtype=F32),
        shape(low_width, length),
    )
    return pl.pallas_call(
        functools.partial(front_kernel, seq_size),
        out_shape=outs,
        in_specs=[anywhere] * 7 + [vmem] * 4,
        out_specs=(anywhere,) * 7 + (vmem,) * 8,
        scratch_shapes=[
            pltpu.VMEM((seq_size, 8, tokens), jnp.int32),
            pltpu.SemaphoreType.DMA((3, 2, 4, seq_size)),
            pltpu.SemaphoreType.DMA((3 + PIECES, 2, 4)),
            pltpu.SemaphoreType.DMA((2, 16)),
            pltpu.SemaphoreType.DMA((1 + PIECES, 2)),
            pltpu.SemaphoreType.DMA((4, seq_size)),
            pltpu.SemaphoreType.DMA((2, 3)),
            pltpu.VMEM((seq_size, tokens, width), BF16),
            pltpu.VMEM((seq_size, tokens, width), BF16),
            pltpu.VMEM((rows, width), BF16),
            pltpu.VMEM((rows, qkv_width), BF16),
            pltpu.VMEM((rows, 8 * part), BF16),
            pltpu.VMEM((4, seq_size * rows, qkv_width), BF16),
            pltpu.VMEM((2, length, 2 * HD), BF16),
            pltpu.VMEM((HD, length), BF16),
            pltpu.VMEM((length, QB), F32),
            pltpu.VMEM((length, q_width), BF16),
        ],
        compiler_params=pltpu.CompilerParams(
            collective_id=0, has_side_effects=True, vmem_limit_bytes=60 * 2**20
        ),
        cost_estimate=pl.CostEstimate(
            flops=5 * 10**9, bytes_accessed=60 * 2**20, transcendentals=4 * 2**20
        ),
        name="attend_front",
    )(*ins)


def dot_nn(a, b):
    return lax.dot_general(a, b, (((1,), (0,)), ((), ())), preferred_element_type=F32)


def dot_nt(a, b):
    return lax.dot_general(a, b, (((1,), (1,)), ((), ())), preferred_element_type=F32)


class ChainSum:
    def __init__(self, place, part, side_in, up_in, down_in, sems, first, size):
        self.p, self.part = place, part
        self.first, self.size = first, size
        self.cut = pl.ds(first, size)
        self.side_in, self.up_in, self.down_in = side_in, up_in, down_in
        self.sems = sems

    def _side(self, z):
        p = self.p
        return remote(
            self.part.at[2 * z + 1 - p.c, self.cut], self.side_in.at[z, self.cut],
            self.sems.at[0, z], self.sems.at[1, z], p.seq(p.sib),
        )

    def _up(self, z):
        p = self.p
        return remote(
            self.part.at[2 * z + p.c, self.cut], self.up_in.at[z, self.cut],
            self.sems.at[2, z], self.sems.at[3, z], p.seq(p.s + 2),
        )

    def _down(self, z):
        p = self.p
        return remote(
            self.part.at[2 * z + p.c, self.cut], self.down_in.at[z, self.cut],
            self.sems.at[4, z], self.sems.at[5, z], p.seq(p.s - 2),
        )

    def _add(self, z, incoming):
        slot = 2 * z + self.p.c

        @pl.loop(0, self.size // 16)
        def _(i):
            cut = pl.ds(pl.multiple_of(self.first + i * 16, 16), 16)
            total = self.part[slot, cut].astype(F32) + incoming[z, cut].astype(F32)
            self.part[slot, cut] = total.astype(BF16)

    def side_start(self, z):
        self._side(z).start()

    def side_add(self, z):
        self._side(z).wait_recv()
        self._add(z, self.side_in)

    def step(self, k):
        p = self.p

        @pl.when(p.z + k < p.chips)
        def _():
            to = p.z + k
            self.side_add(to)

            @pl.when(p.z > 0)
            def _():
                self._up(to).wait_recv()
                self._add(to, self.up_in)

            self._up(to).start()

        @pl.when(p.z >= k)
        def _():
            to = p.z - k
            self.side_add(to)

            @pl.when(p.z < p.chips - 1)
            def _():
                self._down(to).wait_recv()
                self._add(to, self.down_in)

            self._down(to).start()

    def last(self):
        p = self.p
        self.side_add(p.z)

        @pl.when(p.z > 0)
        def _():
            self._up(p.z).wait_recv()
            self._add(p.z, self.up_in)

        @pl.when(p.z < p.chips - 1)
        def _():
            self._down(p.z).wait_recv()
            self._add(p.z, self.down_in)

    def finish(self):
        p = self.p
        for z in range(p.chips):
            self._side(z).wait_send()
        for k in range(1, p.chips):

            @pl.when(p.z + k < p.chips)
            def _():
                self._up(p.z + k).wait_send()

            @pl.when(p.z >= k)
            def _():
                self._down(p.z - k).wait_send()


class ChainSums:
    def __init__(self, place, part, side_in, up_in, down_in, sems, parts=2):
        size = part.shape[1] // parts
        self.all = [
            ChainSum(place, part, side_in, up_in, down_in, sems.at[i], size * i, size)
            for i in range(parts)
        ]

    def side_start(self, z):
        for chain in self.all:
            chain.side_start(z)

    def step(self, k):
        for chain in self.all:
            chain.step(k)

    def last(self):
        for chain in self.all:
            chain.last()

    def finish(self):
        for chain in self.all:
            chain.finish()


def chain_order(z):
    second = jnp.where(z == 0, 2, jnp.where(z == 1, 0, jnp.where(z == 2, 3, 1)))
    return (jnp.where(z < 2, 3, 0), second, jnp.where(z % 2 == 0, 1, 2), z)


def swap_halves(values):
    lane = lax.broadcasted_iota(jnp.int32, values.shape, 1)
    return jnp.where(
        lane % HD < HD // 2,
        pltpu.roll(values, values.shape[1] - HD // 2, 1),
        pltpu.roll(values, HD // 2, 1),
    )


def mask_bias(seg_col, seg_row, start, size):
    length = start + size
    key_pos = lax.broadcasted_iota(jnp.int32, (length, size), 0)
    query_pos = start + lax.broadcasted_iota(jnp.int32, (length, size), 1)
    same = seg_col[pl.ds(0, length), 0:1] == seg_row[0:1, pl.ds(start, size)]
    return jnp.where((key_pos <= query_pos) & same, 0.0, -1e30).astype(F32)


def back_kernel(
    seq_size,
    grad_attn,
    query,
    keys2,
    values2,
    keys_t,
    log_totals,
    seg_row,
    seg_col,
    cos_t,
    sin_t,
    cos_n,
    sin_n,
    qkv_w,
    maps,
    low_qkv_t,
    norm_one,
    ffn_part,
    early_t,
    gu_grad,
    down_grad,
    owners,
    norm_sum,
    ffn_sum,
    share_out,
    gu_out,
    down_out,
    q_out,
    kv_out,
    grads,
    key_z,
    value_z,
    key_acc,
    value_acc,
    bias,
    grad_qkv,
    grad_low,
    qkv_v,
    norm_v,
    ffn_v,
    ffn_side,
    ffn_up,
    ffn_down,
    sum_v,
    sum_side,
    sum_up,
    sum_down,
    share,
    share_in,
    turned,
    gu_in,
    down_in,
    q_got,
    kv_got,
    load_sems,
    swap_sems,
    ffn_sems,
    sum_sems,
    send_sems,
    got_sems,
):
    p = Place(seq_size)
    d, s = p.d, p.s
    length = query.shape[0]
    low_rows = maps.shape[0] // 2
    qkv_in = maps.at[pl.ds(0, low_rows)]
    low_map = maps.at[pl.ds(low_rows, low_rows), pl.ds(0, qkv_w.shape[1])]
    chips = p.chips
    loads = [
        pltpu.make_async_copy(src, dst, load_sems.at[i])
        for i, (src, dst) in enumerate(
            ((ffn_part, ffn_v), (qkv_w, qkv_v), (norm_one, norm_v), (grad_attn.at[s], grads.at[s]))
        )
    ]
    for copy in loads:
        copy.start()
    barrier = pltpu.get_barrier_semaphore()
    everyone = 4 * seq_size

    def place_of(t):
        return lax.rem(d + t // seq_size, 4), lax.rem(s + lax.rem(t, seq_size), seq_size)

    @pl.loop(1, everyone)
    def _(t):
        pl.semaphore_signal(barrier, 1, device_id=place_of(t), device_id_type=MESH)

    pl.semaphore_wait(barrier, everyone - 1)

    def swap_copy(step):
        return remote(
            grad_attn.at[p.peer(step)], grads.at[s], swap_sems.at[0, step], swap_sems.at[1, 0],
            p.seq(p.peer(step)),
        )

    for step in range(1, seq_size):
        swap_copy(step).start()

    def deliver(src, dst, td, ts, i, wait):
        here = (td == d) & (ts == s)

        @pl.when(jnp.logical_not(here))
        def _():
            copy = remote(src, dst, send_sems.at[i], got_sems.at[i], (td, ts))
            if wait:
                copy.wait_send()
            else:
                copy.start()

        if not wait:

            @pl.when(here)
            def _():
                pltpu.make_async_copy(src, dst, got_sems.at[i]).start()

    def ready(buffer, i):
        remote(buffer, buffer, send_sems.at[i], got_sems.at[i], p.seq(p.sib)).wait_recv()

    block = gu_grad.shape[1] // 8

    def deliver_wide(wait):
        side = pl.ds(pl.multiple_of(block * lax.rem(s, 2), block), block)
        for e in range(4):
            for upper in range(2):
                deliver(
                    gu_grad.at[:, pl.ds((4 * upper + e) * block, block)],
                    gu_in.at[d, :, side],
                    2 * upper + e // 2,
                    lax.rem(e, 2) * (seq_size // 2) + s // 2,
                    0,
                    wait,
                )
            deliver(down_grad.at[:, pl.ds(e * block, block)], down_in.at[d], e, s, 1, wait)

    def deliver_heads(wait):
        for i in range(4):
            m = 4 * s + i
            deliver(
                turned.at[pl.ds(HD * i, HD)], q_got.at[d], m // seq_size, lax.rem(m, seq_size), 2, wait
            )
        for i in range(4):
            m = 2 * seq_size * (i // 2) + 2 * s + i % 2
            deliver(
                turned.at[pl.ds(4 * HD + HD // 2 * i, HD // 2)],
                kv_got.at[d],
                m // seq_size,
                lax.rem(m, seq_size),
                3,
                wait,
            )

    def deliver_share(wait):
        rows = share.shape[0] // everyone

        @pl.loop(0, everyone)
        def _(t):
            td, ts = place_of(t)
            start = pl.multiple_of((td * seq_size + ts) * rows, rows)
            deliver(share.at[pl.ds(start, rows)], share_in.at[d, s], td, ts, 4, wait)

    ffn = ChainSums(p, ffn_v, ffn_side, ffn_up, ffn_down, ffn_sems)
    total = ChainSums(p, sum_v, sum_side, sum_up, sum_down, sum_sems)

    low_lane = lax.broadcasted_iota(jnp.int32, (length, 2 * HD), 1) < HD
    zero = jnp.zeros((length, 2 * HD), BF16)
    key_z[0] = jnp.where(low_lane, keys2[...], zero)
    key_z[1] = jnp.where(low_lane, zero, keys2[...])
    value_z[0] = jnp.where(low_lane, values2[...], zero)
    value_z[1] = jnp.where(low_lane, zero, values2[...])
    key_acc[...] = jnp.zeros_like(key_acc)
    value_acc[...] = jnp.zeros_like(value_acc)
    for copy in loads:
        copy.wait()
    for z in range(chips):
        ffn.side_start(z)
    remote(
        grads.at[pl.ds(0, seq_size - 1)], grads.at[pl.ds(0, seq_size - 1)],
        swap_sems.at[0, 0], swap_sems.at[1, 0], p.seq(p.sib),
    ).wait_recv()
    deliver_wide(False)
    ffn.step(3)

    def query_block(i):
        start = i * QB
        span = pl.ds(0, start + QB)
        rows = pl.ds(start, QB)
        bias[span, :] = mask_bias(seg_col, seg_row, start, QB)
        slots = QB // grads.shape[1]

        for m in range(2):
            pair = pl.ds(2 * HD * m, 2 * HD)
            query_pair = query[rows, pair]
            grad_pair = grads[pl.ds(slots * i, slots), :, pair].reshape(QB, 2 * HD)
            turned_q = []
            for e in range(2):
                h = 2 * m + e
                scores = dot_nt(key_z[e, span, :], query_pair)
                weights = jnp.exp(scores * SCORE_SCALE + bias[span, :] - log_totals[h : h + 1, rows])
                grad_weights = dot_nt(value_z[e, span, :], grad_pair)
                row_dot = jnp.sum(weights * grad_weights, axis=0, keepdims=True)
                grad_scores = (weights * (grad_weights - row_dot)).astype(BF16)
                key_acc[e, span, :] += dot_nn(grad_scores, query_pair)
                value_acc[e, span, :] += dot_nn(weights.astype(BF16), grad_pair)
                grad_q = dot_nn(keys_t[:, span], grad_scores) * SCORE_SCALE
                first, second = grad_q[: HD // 2], grad_q[HD // 2 :]
                cos_part, sin_part = cos_t[:, rows], sin_t[:, rows]
                turned_q.append(first * cos_part + second * sin_part)
                turned_q.append(second * cos_part - first * sin_part)
            grad_qkv[rows, pair] = jnp.concatenate(turned_q, axis=0).T.astype(BF16)

    query_block(0)
    query_block(1)
    query_block(2)
    ffn.step(2)
    query_block(3)

    def folded(acc):
        merged = jnp.where(low_lane, acc[0], acc[1])
        return merged + pltpu.roll(merged, HD, 1)

    grad_key = folded(key_acc) * SCORE_SCALE
    grad_key = grad_key * cos_n[...] - swap_halves(grad_key) * sin_n[...]
    grad_qkv[:, pl.ds(4 * HD, 2 * HD)] = jnp.where(low_lane, grad_key, folded(value_acc)).astype(BF16)
    grad_low[...] = dot_nt(grad_qkv[...], low_map[...]).astype(BF16)
    grad_low_t = dot_nt(low_map[...], grad_qkv[...]).astype(BF16)
    ffn.step(1)

    tokens = sum_v.shape[1]

    def give(to):
        rows = pl.ds(pl.multiple_of(2 * to * tokens, 2 * tokens), 2 * tokens)
        left, low = grad_qkv[rows, :], grad_low[rows, :]
        for j in range(4):
            cut = pl.ds(512 * j, 512)
            value = dot_nt(left, qkv_v[cut, :]) + dot_nn(low, qkv_in[:, cut])
            sum_v[2 * to, :, cut] = value[:tokens].astype(BF16)
            sum_v[2 * to + 1, :, cut] = value[tokens:].astype(BF16)
        total.side_start(to)

    order = chain_order(p.z)
    give(order[0])
    total.step(3)
    give(order[1])
    give(order[2])
    give(order[3])
    outer = dot_nn(low_qkv_t[...], grad_qkv[...])
    outer = jnp.concatenate([outer, jnp.zeros((80, outer.shape[1]), F32)], axis=0)
    turned[...] = outer.T
    deliver_heads(False)
    total.step(2)
    for j in range(8):
        cut = pl.ds(256 * j, 256)
        piece = jnp.concatenate([dot_nn(grad_low_t, norm_v[:, cut]), early_t[:, cut]], axis=0)
        share[cut, :] = piece.T.astype(BF16)
    deliver_share(False)
    total.step(1)
    ffn.last()
    ffn_sum[...] = ffn_v[s].astype(F32)
    for buffer, i in ((gu_in, 0), (down_in, 1), (q_got, 2), (kv_got, 3), (share_in, 4)):
        ready(buffer, i)

    def by_adapter(out, value):
        values = [value(e) for e in range(4)]
        for a in range(4):
            chosen = jnp.zeros_like(values[0])
            for e in range(4):
                chosen = jnp.where(owners[e, 0:1, 0:1] == a, values[e], chosen)
            out[a] = chosen

    by_adapter(gu_out, lambda e: gu_in[e])
    by_adapter(down_out, lambda e: down_in[e])
    by_adapter(q_out, lambda e: q_got[e])
    by_adapter(kv_out, lambda e: kv_got[e])
    by_adapter(share_out, lambda e: jnp.sum(share_in[e].astype(F32), axis=0))
    total.last()
    norm_sum[...] = sum_v[s].astype(F32)
    for step in range(1, seq_size):
        swap_copy(step).wait_send()
    deliver_wide(True)
    deliver_heads(True)
    deliver_share(True)
    ffn.finish()
    total.finish()


def back_all(seq_size, ins):
    (grad_attn, query, keys2) = ins[:3]
    _, tokens, width_q = grad_attn.shape
    length = query.shape[0]
    width = ins[15].shape[1]
    qkv_width = ins[12].shape[1]
    chips = seq_size // 2
    rows = width // (4 * seq_size)
    rank = ins[18].shape[0]
    block = ins[18].shape[1] // 8

    def shape(*dims):
        return jax.ShapeDtypeStruct(dims, F32)

    vmem = pl.BlockSpec(memory_space=pltpu.VMEM)
    anywhere = pl.BlockSpec(memory_space=pl.ANY)
    far = (0, 12, 15, 16)
    outs = (
        shape(tokens, width),
        shape(tokens, width),
        shape(4, rows, 128),
        shape(4, rank, 2 * block),
        shape(4, rank, block),
        shape(4, HD, 128),
        shape(4, HD // 2, 128),
    )
    many = (seq_size, tokens, width)
    few = (chips, tokens, width)
    return pl.pallas_call(
        functools.partial(back_kernel, seq_size),
        out_shape=outs,
        in_specs=[anywhere if i in far else vmem for i in range(len(ins))],
        out_specs=(vmem,) * len(outs),
        scratch_shapes=[
            pltpu.VMEM(grad_attn.shape, BF16),
            pltpu.VMEM((2, length, 2 * HD), BF16),
            pltpu.VMEM((2, length, 2 * HD), BF16),
            pltpu.VMEM((2, length, 2 * HD), F32),
            pltpu.VMEM((2, length, 2 * HD), F32),
            pltpu.VMEM((length, QB), F32),
            pltpu.VMEM((length, qkv_width), BF16),
            pltpu.VMEM((length, 3 * rank), BF16),
            pltpu.VMEM(ins[12].shape, BF16),
            pltpu.VMEM((length, width), BF16),
            pltpu.VMEM(many, BF16),
            pltpu.VMEM(few, BF16),
            pltpu.VMEM(few, BF16),
            pltpu.VMEM(few, BF16),
            pltpu.VMEM(many, BF16),
            pltpu.VMEM(few, BF16),
            pltpu.VMEM(few, BF16),
            pltpu.VMEM(few, BF16),
            pltpu.VMEM((width, 128), BF16),
            pltpu.VMEM((4, seq_size, rows, 128), BF16),
            pltpu.VMEM((qkv_width, 128), F32),
            pltpu.VMEM((4, rank, 2 * block), F32),
            pltpu.VMEM((4, rank, block), F32),
            pltpu.VMEM((4, HD, 128), F32),
            pltpu.VMEM((4, HD // 2, 128), F32),
            pltpu.SemaphoreType.DMA((4,)),
            pltpu.SemaphoreType.DMA((2, seq_size)),
            pltpu.SemaphoreType.DMA((2, 6, chips)),
            pltpu.SemaphoreType.DMA((2, 6, chips)),
            pltpu.SemaphoreType.DMA((5,)),
            pltpu.SemaphoreType.DMA((5,)),
        ],
        compiler_params=pltpu.CompilerParams(
            collective_id=1, has_side_effects=True, vmem_limit_bytes=60 * 2**20
        ),
        cost_estimate=pl.CostEstimate(
            flops=10 * 10**9, bytes_accessed=20 * 2**20, transcendentals=4 * 2**20
        ),
        name="attend_back",
    )(*ins)


def mid_kernel(
    seq_size,
    attn_all,
    hidden_all,
    out_all,
    gu_all,
    cotangent,
    down_w,
    gain,
    maps,
    ffn_part,
    middle_own,
    grad_middle,
    grad_attn,
    early_t,
    gu_grad,
    down_grad,
    out_v,
    gu_v,
    down_v,
    cot_v,
    norm_v,
    both_v,
    wide,
    act_v,
    sum_v,
    sum_side,
    sum_up,
    sum_down,
    attn_own,
    low_own,
    lows,
    lows_t,
    chain_sems,
    plane_sems,
    sum_sems,
    local_sems,
):
    p = Place(seq_size)
    d, s, z, c = p.d, p.s, p.z, p.c
    tokens, width = cotangent.shape
    part = down_w.shape[0]
    span = 2 * tokens
    hidden_width = 4 * part
    rank = maps.shape[0] // 8
    o_in, o_out, gu_in, gu_map, down_out, down_in = mid_views(maps)
    down_in = down_in.at[:, pl.ds(0, hidden_width)]
    heads_width = attn_all.shape[2]
    step_width = 512
    loads = [
        pltpu.make_async_copy(src, dst, local_sems.at[0, i])
        for i, (src, dst) in enumerate(
            [(down_w, down_v.at[d]), (cotangent, cot_v.at[s]), (hidden_all, norm_v), (out_all, out_v)]
            + [
                (attn_all.at[j], both_v.at[:, pl.ds(heads_width * j, heads_width)])
                for j in range(seq_size)
            ]
            + [(gu_all, gu_v)]
        )
    ]
    for copy in loads:
        copy.start()
    barrier = pltpu.get_barrier_semaphore()
    p_up, p_down = p.z < p.chips - 1, p.z > 0

    @pl.when(p_up)
    def _():
        pl.semaphore_signal(barrier, 1, device_id=p.seq(s + 2), device_id_type=MESH)

    @pl.when(p_down)
    def _():
        pl.semaphore_signal(barrier, 1, device_id=p.seq(s - 2), device_id_type=MESH)

    for place in (p.seq(p.sib), p.dp(p.dx), p.dp(p.dy)):
        pl.semaphore_signal(barrier, 1, device_id=place, device_id_type=MESH)

    @pl.when(p_up & p_down)
    def _():
        pl.semaphore_wait(barrier, 5)

    @pl.when(jnp.logical_not(p_up & p_down))
    def _():
        pl.semaphore_wait(barrier, 4)

    cot = Chains(p, cotangent, lambda i: cot_v.at[i], tokens, chain_sems)
    down = Plane(
        p,
        lambda e: down_v.at[e],
        lambda e, h: down_v.at[e, pl.ds(part // 2 * h, part // 2)],
        plane_sems,
    )
    total = ChainSums(p, sum_v, sum_side, sum_up, sum_down, sum_sems)
    down_all = down_v.reshape(4 * part, width)
    cot.start()
    loads[0].wait()
    down.start()
    for copy in loads[1:-1]:
        copy.wait()

    def columns(body, count):
        for n in range(count):
            body(pl.ds(n * step_width, step_width))

    def tiles(body, count):
        for zz in range(p.chips):
            for n in range(count):
                body(pl.ds(span * zz, span), pl.ds(n * step_width, step_width))

    length = seq_size * tokens
    norm_rows = norm_v.reshape(length, width)
    cot_rows = cot_v.reshape(length, width)
    sum_rows = sum_v.reshape(length, width)
    lows[...] = jnp.zeros_like(lows)
    mine = pl.ds(pl.multiple_of(s * tokens, tokens), tokens)
    lows[:, 0:rank] = dot_nt(both_v[...], o_in[...])

    def branch(rows, cut):
        low = lows[rows, 0:rank].astype(BF16)
        value = dot_nn(both_v[rows, :], out_v[:, cut]) + dot_nn(low, o_out[:, cut])
        wide[rows, cut] = norm_rows[rows, cut].astype(F32) + RESIDUAL_SCALE * value

    tiles(branch, width // step_width)
    middle_own[...] = wide[mine, :]
    attn_own[...] = both_v[mine, :]
    low_own[...] = dot_nt(attn_own[...], o_in[...]).astype(BF16)
    cot.step(1)
    down.forward()

    @pl.loop(0, length // 64)
    def _(i):
        rows = pl.ds(pl.multiple_of(i * 64, 64), 64)
        norm_rows[rows, :] = rms_scale(wide[rows, :], gain[...]).astype(BF16)

    loads[-1].wait()
    lows[:, 0 : 2 * rank] = dot_nt(norm_rows[...], gu_in[...])
    cot.step(2)

    def gate_up(rows, cut):
        low = lows[rows, 0 : 2 * rank].astype(BF16)
        wide[rows, cut] = dot_nn(norm_rows[rows, :], gu_v[:, cut]) + dot_nn(low, gu_map[:, cut])

    tiles(gate_up, 2 * hidden_width // step_width)
    cot.step(3)
    down.recv()
    for zz in range(p.chips):
        cot.side_recv(zz)

    def backward(zz):
        rows = pl.ds(pl.multiple_of(span * zz, span), span)
        low = dot_nt(cot_rows[rows, :], down_out[...]).astype(BF16)
        lows[rows, 5 * rank : 6 * rank] = low.astype(F32)

        for n in range(hidden_width // step_width):
            cut = pl.ds(n * step_width, step_width)
            upper = pl.ds(hidden_width + n * step_width, step_width)
            grad_act = RESIDUAL_SCALE * (
                dot_nt(cot_rows[rows, :], down_all[cut, :]) + dot_nn(low, down_in[:, cut])
            )
            gate, up = wide[rows, cut], wide[rows, upper]
            sigma = 1.0 / (1.0 + jnp.exp(-gate))
            raised = gate * sigma
            act_v[rows, cut] = (raised * up).astype(BF16)
            both_v[rows, cut] = (grad_act * up * sigma * (1.0 + gate * (1.0 - sigma))).astype(BF16)
            both_v[rows, upper] = (grad_act * raised).astype(BF16)

        low_gu = dot_nt(both_v[rows, :], gu_map[...]).astype(BF16)
        lows[rows, 2 * rank : 4 * rank] = low_gu.astype(F32)

        def model_part(cut):
            value = dot_nt(both_v[rows, :], gu_v[cut, :]) + dot_nn(low_gu, gu_in[:, cut])
            sum_rows[rows, cut] = value.astype(BF16)

        columns(model_part, width // step_width)
        total.side_start(zz)

    order = chain_order(z)
    backward(order[0])
    total.step(3)
    backward(order[1])
    backward(order[2])
    total.step(2)
    backward(order[3])
    lows[:, 4 * rank : 5 * rank] = dot_nt(act_v[...], down_in[...])
    for zz in range(p.chips):
        lows_t[:, pl.ds(span * zz, span)] = lows[pl.ds(span * zz, span), :].T.astype(BF16)
    total.step(1)

    for n in range(width // step_width):
        cut = pl.ds(step_width * n, step_width)
        early_t[2 * rank : 4 * rank, cut] = dot_nn(
            lows_t[2 * rank : 4 * rank, :], norm_rows[:, cut]
        )
        early_t[4 * rank : 5 * rank, cut] = RESIDUAL_SCALE * dot_nn(
            lows_t[4 * rank : 5 * rank, :], cot_rows[:, cut]
        )
        source = pl.ds(0, rank) if n < hidden_width // step_width else pl.ds(rank, rank)
        gu_grad[:, cut] = dot_nn(lows_t[source, :], both_v[:, cut])
        if n < hidden_width // step_width:
            down_grad[:, cut] = RESIDUAL_SCALE * dot_nn(
                lows_t[5 * rank : 6 * rank, :], act_v[:, cut]
            )


    def feed_forward(rows, cut):
        low = lows[rows, 4 * rank : 5 * rank].astype(BF16)
        value = dot_nn(act_v[rows, :], down_all[:, cut]) + dot_nn(low, down_out[:, cut])
        norm_rows[rows, cut] = value.astype(BF16)

    tiles(feed_forward, width // step_width)
    store = pltpu.make_async_copy(norm_v, ffn_part, local_sems.at[1, 0])
    store.start()
    total.last()
    middle = middle_own[...]
    mean = jnp.mean(middle * middle, axis=-1, keepdims=True)
    r = lax.rsqrt(mean + EPSILON)
    scaled = sum_v[s].astype(F32) * gain[...]
    inner = jnp.mean(scaled * middle, axis=-1, keepdims=True)
    grad_mid = cot_v[s].astype(F32) + r * scaled - r * r * r * inner * middle
    grad_middle[...] = grad_mid
    branch = (RESIDUAL_SCALE * grad_mid).astype(BF16)
    low = dot_nt(branch, o_out[...]).astype(BF16)
    for j in range(seq_size):
        cut = pl.ds(heads_width * j, heads_width)
        grad_attn[j] = (dot_nt(branch, out_v[cut, :]) + dot_nn(low, o_in[:, cut])).astype(BF16)
    pair = jnp.concatenate(
        [low.astype(F32), low_own[...].astype(F32), jnp.zeros((tokens, 128 - 2 * rank), F32)], axis=1
    )
    pair = pair.T.astype(BF16)
    early_t[0:rank, :] = dot_nn(pair[0:rank], attn_own[...])
    early_t[rank : 2 * rank, :] = dot_nn(pair[rank : 2 * rank], branch)
    cot.finish()
    down.finish()
    total.finish()
    store.wait()


def mid_all(seq_size, ins):
    tokens, width = ins[4].shape
    part = ins[5].shape[0]
    length = seq_size * tokens
    rank = ins[7].shape[0] // 8
    chips = seq_size // 2
    heads_width = ins[0].shape[2]

    def shape(*dims, dtype=F32):
        return jax.ShapeDtypeStruct(dims, dtype)

    vmem = pl.BlockSpec(memory_space=pltpu.VMEM)
    anywhere = pl.BlockSpec(memory_space=pl.ANY)
    many, few = (seq_size, tokens, width), (chips, tokens, width)
    outs = (
        shape(*many, dtype=BF16),
        shape(tokens, width),
        shape(tokens, width),
        shape(seq_size, tokens, heads_width, dtype=BF16),
        shape(5 * rank, width),
        shape(rank, 8 * part),
        shape(rank, 4 * part),
    )
    return pl.pallas_call(
        functools.partial(mid_kernel, seq_size),
        out_shape=outs,
        in_specs=[anywhere] * 6 + [vmem] * 2,
        out_specs=(anywhere,) + (vmem,) * 6,
        scratch_shapes=[
            pltpu.VMEM((width, width), BF16),
            pltpu.VMEM((width, 8 * part), BF16),
            pltpu.VMEM((4, part, width), BF16),
            pltpu.VMEM(many, BF16),
            pltpu.VMEM(many, BF16),
            pltpu.VMEM((length, width), BF16),
            pltpu.VMEM((length, 8 * part), F32),
            pltpu.VMEM((length, 4 * part), BF16),
            pltpu.VMEM(many, BF16),
            pltpu.VMEM(few, BF16),
            pltpu.VMEM(few, BF16),
            pltpu.VMEM(few, BF16),
            pltpu.VMEM((tokens, width), BF16),
            pltpu.VMEM((tokens, rank), BF16),
            pltpu.VMEM((length, 128), F32),
            pltpu.VMEM((128, length), BF16),
            pltpu.SemaphoreType.DMA((2, 4, seq_size)),
            pltpu.SemaphoreType.DMA((2, 4)),
            pltpu.SemaphoreType.DMA((2, 6, chips)),
            pltpu.SemaphoreType.DMA((2, 13)),
        ],
        compiler_params=pltpu.CompilerParams(
            collective_id=2, has_side_effects=True, vmem_limit_bytes=63 * 2**20
        ),
        cost_estimate=pl.CostEstimate(
            flops=40 * 10**9, bytes_accessed=40 * 2**20, transcendentals=4 * 2**20
        ),
        name="feed_forward",
    )(*ins)


def mid_views(maps):
    rank = maps.shape[0] // 8
    starts = (0, 1, 2, 4, 6, 7, 8)
    return [
        maps.at[pl.ds(rank * a, rank * (b - a))] for a, b in zip(starts[:-1], starts[1:], strict=True)
    ]


def prepare_kernel(
    seq_size,
    adapter_ref,
    documents,
    key_w,
    value_w,
    qkv_in_all,
    q_out_all,
    kv_out_all,
    o_in_all,
    o_out_all,
    gu_in_all,
    gu_out_all,
    down_in_all,
    down_out_all,
    numbers,
    kv,
    front_maps,
    mid_maps,
    heads_v,
    sems,
):
    me = lax.axis_index("seq")
    adapter = adapter_ref[0]
    rank = o_out_all.shape[1]
    q_width = q_out_all.shape[2] // seq_size
    part = down_in_all.shape[2] // (4 * seq_size)
    qkv_in = front_maps.at[pl.ds(0, 3 * rank)]
    low_map = front_maps.at[pl.ds(3 * rank, 3 * rank)]
    o_in, o_out, gu_in, gu_map, down_out, down_in = mid_views(mid_maps)
    low_map[...] = jnp.zeros(low_map.shape, BF16)
    gu_map[...] = jnp.zeros(gu_map.shape, BF16)
    down_in[...] = jnp.zeros(down_in.shape, BF16)

    def block(number, size):
        return pl.ds(pl.multiple_of(number * size, size), size)

    moves = [
        (qkv_in_all.at[adapter], qkv_in),
        (o_in_all.at[adapter], o_in),
        (o_out_all.at[adapter], o_out),
        (gu_in_all.at[adapter], gu_in),
        (down_out_all.at[adapter], down_out),
        (q_out_all.at[adapter, :, block(me, q_width)], low_map.at[pl.ds(0, rank), pl.ds(0, q_width)]),
        (kv_out_all.at[adapter, :, block(me // 2, 2 * HD)], heads_v.at[0]),
        (kv_out_all.at[adapter, :, block(seq_size // 2 + me // 2, 2 * HD)], heads_v.at[1]),
    ]
    for e in range(4):
        moves.append(
            (
                down_in_all.at[adapter, :, block(seq_size * e + me, part)],
                down_in.at[:, pl.ds(part * e, part)],
            )
        )
        for upper in range(2):
            moves.append(
                (
                    gu_out_all.at[adapter, :, block(seq_size * (4 * upper + e) + me, part)],
                    gu_map.at[pl.ds(rank * upper, rank), pl.ds(part * (4 * upper + e), part)],
                )
            )
    moves = [pltpu.make_async_copy(a, b, sems.at[i]) for i, (a, b) in enumerate(moves)]
    for move in moves:
        move.start()
    numbers[0] = jnp.broadcast_to(documents[...], numbers.shape[1:])
    numbers[1] = jnp.full(numbers.shape[1:], adapter, jnp.int32)
    rows = key_w.shape[0]
    low_lane = lax.broadcasted_iota(jnp.int32, (rows, 2 * HD), 1) < HD
    for j in range(seq_size // 2):
        cut = pl.ds(2 * HD * j, 2 * HD)
        left, right = key_w[:, cut].astype(F32), value_w[:, cut].astype(F32)
        kv[2 * j] = jnp.where(low_lane, left, pltpu.roll(right, HD, 1)).astype(BF16)
        kv[2 * j + 1] = jnp.where(low_lane, pltpu.roll(left, HD, 1), right).astype(BF16)
    for move in moves:
        move.wait()
    low_lane = lax.broadcasted_iota(jnp.int32, (rank, 2 * HD), 1) < HD
    odd = me % 2 == 1
    for i in range(2):
        value = heads_v[i].astype(F32)
        turned = pltpu.roll(value, HD, 1)
        value = jnp.where(odd, turned, value) if i == 0 else jnp.where(odd, value, turned)
        kept = low_lane if i == 0 else jnp.logical_not(low_lane)
        low_map[pl.ds(rank * (1 + i), rank), pl.ds(q_width, 2 * HD)] = jnp.where(
            kept, value, 0.0
        ).astype(BF16)


def prepare_all(seq_size, adapter_index, documents, key_w, value_w, maps):
    q_out = maps[1]
    rank = q_out.shape[1]
    rows = key_w.shape[0]
    tokens = documents.shape[1]

    def shape(*dims, dtype=BF16):
        return jax.ShapeDtypeStruct(dims, dtype)

    vmem = pl.BlockSpec(memory_space=pltpu.VMEM)
    width = q_out.shape[2]
    outs = (
        shape(2, 8, tokens, dtype=jnp.int32),
        shape(seq_size, rows, 2 * HD),
        shape(6 * rank, width),
        shape(8 * rank, width),
    )
    return pl.pallas_call(
        functools.partial(prepare_kernel, seq_size),
        out_shape=outs,
        in_specs=[pl.BlockSpec(memory_space=pltpu.SMEM), vmem, vmem, vmem]
        + [pl.BlockSpec(memory_space=pl.ANY)] * 9,
        out_specs=(vmem,) * len(outs),
        scratch_shapes=[pltpu.VMEM((2, rank, 2 * HD), BF16), pltpu.SemaphoreType.DMA((20,))],
        compiler_params=pltpu.CompilerParams(vmem_limit_bytes=62 * 2**20),
        name="prepare",
    )(adapter_index, documents, key_w, value_w, *maps)


def finish_kernel(count, *refs):
    far, outs = refs[:count], refs[count : count + 11]
    near, sems = refs[count + 11 : 2 * count + 11], refs[-1]
    loads = [pltpu.make_async_copy(a, b, sems.at[i]) for i, (a, b) in enumerate(zip(far, near, strict=True))]
    for load in loads:
        load.start()
    middle, ffn_sum, grad_middle, norm_sum, hidden, gain, share, gu_got, down_got, q_got, kv_got = near
    mixed, grad_hidden, qkv_in, q_out, kv_out, o_in, o_out, gu_in, gu_out, down_in, down_out = outs
    rank = o_in.shape[1]
    lower = lax.axis_index("dp") < 2
    for load in loads:
        load.wait()
    for a in range(share.shape[0]):
        own = share[a].T
        qkv_in[a] = own[: 3 * rank]
        o_in[a] = own[3 * rank : 4 * rank]
        o_out[a] = own[4 * rank : 5 * rank]
        gu_in[a] = own[5 * rank : 7 * rank]
        down_out[a] = own[7 * rank :]
        gu_out[a] = gu_got[a]
        down_in[a] = down_got[a]
        q_out[a] = q_got[a].T[:rank]
        turned = kv_got[a].T
        kv_out[a] = jnp.where(lower, turned[rank : 2 * rank], turned[2 * rank : 3 * rank])

    @pl.loop(0, middle.shape[0] // 32)
    def _(i):
        rows = pl.ds(pl.multiple_of(i * 32, 32), 32)
        mixed[0, rows, :] = (middle[rows, :] + RESIDUAL_SCALE * ffn_sum[rows, :]).astype(BF16)
        back = rms_back(hidden[rows, :].astype(F32), gain[...], norm_sum[rows, :])
        grad_hidden[0, rows, :] = (grad_middle[rows, :] + back).astype(BF16)


def finish_all(ins):
    tokens, width = ins[0].shape
    adapters, rows = ins[6].shape[:2]
    rank = ins[7].shape[1]

    def shape(*dims, dtype=F32):
        return jax.ShapeDtypeStruct(dims, dtype)

    vmem = pl.BlockSpec(memory_space=pltpu.VMEM)
    outs = (
        shape(1, tokens, width, dtype=BF16),
        shape(1, tokens, width, dtype=BF16),
        shape(adapters, 3 * rank, rows),
        shape(adapters, rank, rows),
        shape(adapters, rank, rows // 2),
        shape(adapters, rank, rows),
        shape(adapters, rank, rows),
        shape(adapters, 2 * rank, rows),
        shape(*ins[7].shape),
        shape(*ins[8].shape),
        shape(adapters, rank, rows),
    )
    made = pl.pallas_call(
        functools.partial(finish_kernel, len(ins)),
        out_shape=outs,
        in_specs=[pl.BlockSpec(memory_space=pltpu.HBM)] * len(ins),
        out_specs=(vmem,) * len(outs),
        scratch_shapes=[pltpu.VMEM(v.shape, v.dtype) for v in ins]
        + [pltpu.SemaphoreType.DMA((len(ins),))],
        compiler_params=pltpu.CompilerParams(vmem_limit_bytes=62 * 2**20),
        name="finish",
    )(*ins)
    made = list(made)
    for i in (2, 5, 7, 9):
        made[i] = jnp.swapaxes(made[i], 1, 2)
    return tuple(made)


def make_kernel_local(dp_size, seq_size):
    def local(
        hidden,
        token_document_numbers,
        sequence_adapter_index,
        cotangent,
        attention_norm_gain,
        feedforward_norm_gain,
        query_weight,
        key_weight,
        value_weight,
        attention_output_weight,
        gate_weight,
        up_weight,
        down_weight,
        adapter_query_key_value_input,
        adapter_query_output,
        adapter_key_value_output,
        adapter_projection_input,
        adapter_projection_output,
        adapter_gate_up_input,
        adapter_gate_up_output,
        adapter_down_input,
        adapter_down_output,
    ):
        tokens, width = hidden.shape[1:]
        length = tokens * seq_size
        numbers, kv, front_maps, mid_maps = (
            prepare_all(
                seq_size,
                sequence_adapter_index,
                token_document_numbers,
                key_weight,
                value_weight,
                (
                    jnp.swapaxes(adapter_query_key_value_input, 1, 2),
                    adapter_query_output,
                    adapter_key_value_output,
                    jnp.swapaxes(adapter_projection_input, 1, 2),
                    adapter_projection_output,
                    jnp.swapaxes(adapter_gate_up_input, 1, 2),
                    adapter_gate_up_output,
                    jnp.swapaxes(adapter_down_input, 1, 2),
                    adapter_down_output,
                ),
            )
        )
        cos_fixed, sin_fixed = fixed_tables(length)
        cos_n = jnp.asarray(np.tile(cos_fixed, (1, 4)))
        sin_n = jnp.asarray(np.tile(np.concatenate([-sin_fixed, sin_fixed], axis=1), (1, 2)))
        (
            hidden_all,
            owners,
            qkv,
            out_full,
            gate_up,
            attn,
            norm_one,
            query,
            keys2,
            values2,
            keys_t,
            log_totals,
            seg_row,
            seg_col,
            low_t,
        ) = front_all(
            seq_size,
            (
                hidden[0],
                numbers,
                query_weight,
                kv,
                attention_output_weight,
                gate_weight,
                up_weight,
                attention_norm_gain[None],
                front_maps,
                cos_n,
                sin_n,
            ),
        )
        ffn_part, middle, grad_middle, grad_attn, early, gu_grad, down_grad = mid_all(
            seq_size,
            (
                attn,
                hidden_all,
                out_full.reshape(width, width),
                gate_up.reshape(width, -1),
                cotangent[0],
                down_weight,
                feedforward_norm_gain[None],
                mid_maps,
            ),
        )
        norm_sum, ffn_sum, share, gu_got, down_got, q_got, kv_got = back_all(
            seq_size,
            (
                grad_attn,
                query,
                keys2,
                values2,
                keys_t,
                log_totals,
                seg_row,
                seg_col,
                jnp.asarray(np.ascontiguousarray(cos_fixed.T)),
                jnp.asarray(np.ascontiguousarray(sin_fixed.T)),
                cos_n,
                sin_n,
                qkv.reshape(width, -1),
                front_maps,
                low_t,
                norm_one.reshape(length, width),
                ffn_part,
                early,
                gu_grad,
                down_grad,
                owners,
            ),
        )
        return finish_all(
            (
                middle,
                ffn_sum,
                grad_middle,
                norm_sum,
                hidden[0],
                attention_norm_gain[None],
                share,
                gu_got,
                down_got,
                q_got,
                kv_got,
            )
        )

    return local


def solution(mesh):
    both = ("dp", "seq")
    tokens = P("dp", "seq", None)
    weight = P(both, None)
    in_specs = (
        (tokens, P("dp", "seq"), P("dp"), tokens, P(), P()) + (weight,) * 7 + (P(),) * 9
    )
    by_row, by_column = P(None, both, None), P(None, None, both)
    out_specs = (
        tokens,
        tokens,
        by_row,
        by_column,
        by_column,
        by_row,
        by_column,
        by_row,
        by_column,
        by_row,
        by_column,
    )
    dp_size, seq_size = mesh.shape["dp"], mesh.shape["seq"]
    if dp_size == 4 and seq_size == KVH:
        local = make_kernel_local(dp_size, seq_size)
    else:
        local = make_local(dp_size, seq_size)
    return jax.shard_map(local, mesh=mesh, in_specs=in_specs, out_specs=out_specs, check_vma=False)
```
